32 devices in a mesh: dp: 8 (over z, x), tensor: 4 (over y, core).
Axes of the slice: x: 2, y: 2, z: 4, core: 2. Of those that a mesh axis runs over, the one named last changes fastest.
Arguments:
- tokens: bfloat16 [32768, 768], P(('dp', 'tensor')), may hold values from -6 to 6
- qkv_weight: bfloat16 [3, 768, 768], replicated, may hold values from -0.21875 to 0.21875
- out_weight: bfloat16 [768, 768], replicated, may hold values from -0.625 to 0.625
- in_weight: bfloat16 [768, 3072], P(None, 'tensor'), may hold values from -0.21875 to 0.21875
- back_weight: bfloat16 [3072, 768], P('tensor'), may hold values from -0.109375 to 0.109375
- rel_embed: bfloat16 [512, 768], replicated, may hold values from -6 to 6
- gain_one: float32 [768], replicated, may hold values from 0.5 to 1.5
- shift_one: float32 [768], replicated, may hold values from -1 to 1
- gain_two: float32 [768], replicated, may hold values from 0.5 to 1.5
- shift_two: float32 [768], replicated, may hold values from -1 to 1
- adapt_down: bfloat16 [5, 12, 768], replicated, may hold values from -0.21875 to 0.21875
- adapt_up: bfloat16 [5, 12, 768], replicated, may hold values from -1.75 to 1.75
- hidden_up: bfloat16 [12, 3072], P(None, 'tensor'), may hold values from -1.75 to 1.75
- hidden_down: bfloat16 [12, 3072], P(None, 'tensor'), may hold values from -0.109375 to 0.109375
- adapt_scale: float32 [6, 12], replicated, may hold values from -3 to 3
- seq_lengths: int32 [32, 4], P(('dp', 'tensor')), may hold values from 65 to 512, as said below
- seq_counts: int32 [32, 3], P(('dp', 'tensor')), may hold values from 0 to 2, as said below
- rel_bucket: int32 [1023], replicated, may hold values from 1 to 511, as said below
- out_grad: bfloat16 [32768, 768], P(('dp', 'tensor')), may hold values from -6 to 6
Outputs:
- mixed: bfloat16 [32768, 768], P(('dp', 'tensor'))
- in_grad: float32 [32768, 768], P(('dp', 'tensor'))
- down_grad: float32 [5, 12, 768], replicated
- up_grad: float32 [5, 12, 768], replicated
- hidden_up_grad: float32 [12, 3072], P(None, 'tensor')
- hidden_down_grad: float32 [12, 3072], P(None, 'tensor')
- scale_grad: float32 [6, 12], replicated
The draws below stay inside these ranges and needn't reach their ends.
Inputs may be any that keep to these rules, and one draw needn't show every extreme that they name: `seq_lengths`: column s of row g is the length of slot s of row group g; a slot of 128, 256 or 512 rows has a length from half its rows plus one to its rows; in every draw some row group has all its slots full. `seq_counts`: column b of row g counts the used slots of bucket b (2 slots of 128 rows, 1 of 256, 1 of 512) in row group g; the used slots are the first of their bucket in row order; column 0 is 1 or more; in every draw some row group uses all its slots. `rel_bucket`: entry 511 + d is the bucket of relative position d: 256 + sign(d) m(|d|), where m never decreases, m(0) = 0 and m(|d|) = |d| for |d| up to 64.
All inputs are finite; a program needn't handle non-finite values.
Results may differ from the reference program's by a relative error of at most 0.018.
Values may be sent and summed in bfloat16 or wider, within the bound.
A program may use at most 256 MiB of HBM per device.

```python
import jax
import jax.numpy as jnp
from jax import lax

D = 768
H = 12
DH = 64
FF = 3072
SPAN = 256
R = 12
LEN1 = 128
LEN2 = 256
LEN3 = 512
GROUPS = 1
TOKENS = 32768
N_DP = 8
N_TENSOR = 4


def draw_seq_lengths(key, part):
    key = jax.random.fold_in(key, 11)
    device_count = N_DP * N_TENSOR
    slot_rows = jnp.tile(jnp.array([LEN1, LEN1, LEN2, LEN3], dtype=jnp.int32), GROUPS)
    random_bits = jax.random.randint(jax.random.fold_in(key, 1), (device_count, 4 * GROUPS), 0, 1 << 20, dtype=jnp.int32)
    shorten = random_bits % (slot_rows[None, :] // 2)
    chosen = jax.random.randint(jax.random.fold_in(key, 2), (), 0, device_count, dtype=jnp.int32)
    full_group = jnp.arange(device_count, dtype=jnp.int32)[:, None] == chosen
    return jnp.where(full_group, slot_rows[None, :], slot_rows[None, :] - shorten).astype(jnp.int32)


def draw_seq_counts(key, part):
    key = jax.random.fold_in(key, 12)
    device_count = N_DP * N_TENSOR
    limits = jnp.array([2 * GROUPS, GROUPS, GROUPS], dtype=jnp.int32)
    lowest = jnp.array([1, 0, 0], dtype=jnp.int32)
    random_bits = jax.random.randint(jax.random.fold_in(key, 1), (device_count, 3), 0, 1 << 20, dtype=jnp.int32)
    counts = lowest[None, :] + random_bits % (limits + 1 - lowest)[None, :]
    chosen = jax.random.randint(jax.random.fold_in(key, 2), (), 0, device_count, dtype=jnp.int32)
    full_group = jnp.arange(device_count, dtype=jnp.int32)[:, None] == chosen
    return jnp.where(full_group, limits[None, :], counts).astype(jnp.int32)


def draw_rel_bucket(key, part):
    key = jax.random.fold_in(key, 13)
    magnitude = jnp.arange(LEN3, dtype=jnp.int32)
    coin_flips = jax.random.randint(key, (LEN3,), 0, 2, dtype=jnp.int32)
    increments = jnp.where(magnitude == 0, 0, jnp.where(magnitude <= SPAN // 4, 1, coin_flips))
    distance = jnp.minimum(jnp.cumsum(increments).astype(jnp.int32), SPAN - 1)
    distance = jnp.where(magnitude == LEN3 - 1, SPAN - 1, distance)
    offsets = jnp.arange(2 * LEN3 - 1, dtype=jnp.int32) - (LEN3 - 1)
    return (SPAN + jnp.sign(offsets) * distance[jnp.abs(offsets)]).astype(jnp.int32)


def levels(stream_key, dims, split, low, largest):
    level, own = 1.0, jax.random.fold_in(stream_key, 6)
    for axis_at, blocks in split:
        steps = jnp.exp(jax.random.uniform(jax.random.fold_in(own, axis_at), (blocks,), jnp.float32, low / len(split), largest / len(split)))
        level = level * jnp.repeat(steps, dims[axis_at] // blocks).reshape([-1 if axis == axis_at else 1 for axis in range(len(dims))])
    return level


def bell_draw(stream_key, shape, scale, most, cuts=(), kind=jnp.bfloat16):
    factor_of = levels(stream_key, shape, cuts, -0.22, 0.18) if cuts else 1.0
    values = jax.random.normal(stream_key, shape, jnp.float32) * scale * factor_of
    return jnp.minimum(jnp.maximum(values, -most), most).astype(kind)


def setup_inputs(seed: int = 0) -> dict:
    keys = jax.random.split(jax.random.key(seed), 20)
    tokens = bell_draw(keys[0], (TOKENS, D), 1.0, 6.0, ((0, 32),))
    qkv_weight = bell_draw(keys[1], (3, D, D), D ** -0.5, 0.21875)
    out_weight = bell_draw(keys[2], (D, D), (D // 8) ** -0.5, 0.625)
    in_weight = bell_draw(keys[3], (D, FF), D ** -0.5, 0.21875, ((1, 4),))
    back_weight = bell_draw(keys[4], (FF, D), FF ** -0.5, 0.109375, ((0, 4),))
    rel_embed = bell_draw(keys[5], (2 * SPAN, D), 1.0, 6.0)
    gain_one = jnp.clip(1.0 + 0.1 * jax.random.normal(keys[6], (D,), jnp.float32), 0.5, 1.5)
    shift_one = bell_draw(keys[7], (D,), 0.2, 1.0, (), jnp.float32)
    gain_two = jnp.clip(1.0 + 0.1 * jax.random.normal(keys[8], (D,), jnp.float32), 0.5, 1.5)
    shift_two = bell_draw(keys[9], (D,), 0.2, 1.0, (), jnp.float32)
    adapt_down = bell_draw(keys[10], (5, R, D), D ** -0.5, 0.21875)
    adapt_up = bell_draw(keys[11], (5, R, D), R ** -0.5, 1.75)
    hidden_up = bell_draw(keys[12], (R, FF), R ** -0.5, 1.75, ((1, 4),))
    hidden_down = bell_draw(keys[13], (R, FF), FF ** -0.5, 0.109375, ((1, 4),))
    adapt_scale = bell_draw(keys[14], (6, R), 0.7, 3.0, (), jnp.float32)
    seq_lengths = draw_seq_lengths(jax.random.fold_in(keys[19], 71), 0)
    seq_counts = draw_seq_counts(jax.random.fold_in(keys[19], 71), 0)
    rel_bucket = draw_rel_bucket(jax.random.fold_in(keys[19], 71), 0)
    out_grad = bell_draw(keys[18], (TOKENS, D), 1.0, 6.0, ((0, 32),))
    return {"tokens": tokens, "qkv_weight": qkv_weight, "out_weight": out_weight, "in_weight": in_weight, "back_weight": back_weight, "rel_embed": rel_embed, "gain_one": gain_one, "shift_one": shift_one, "gain_two": gain_two, "shift_two": shift_two, "adapt_down": adapt_down, "adapt_up": adapt_up, "hidden_up": hidden_up, "hidden_down": hidden_down, "adapt_scale": adapt_scale, "seq_lengths": seq_lengths, "seq_counts": seq_counts, "rel_bucket": rel_bucket, "out_grad": out_grad}


@jax.custom_vjp
def low(v):
    return lax.optimization_barrier(v.astype(jnp.bfloat16)).astype(jnp.float32)

@jax.custom_vjp
def low_back(v):
    return v

def low_keep(v):
    return (low(v), None)

def low_pass(kept, grad):
    return (grad,)

def back_keep(v):
    return (v, None)

def back_low(kept, grad):
    return (low(grad),)
low.defvjp(low_keep, low_pass)
low_back.defvjp(back_keep, back_low)
norm_epsilon = 1e-07
masked_score = -1e+30

def exact_dot(left, right):
    return jnp.dot(left, right, precision=lax.Precision.HIGHEST)

def row_layout(row_count, lengths, counts):
    row_index = jnp.arange(row_count, dtype=jnp.int32)
    group_id = row_index // (2 * LEN3)
    within_set = row_index % (2 * LEN3)
    second = within_set >= LEN3
    inner_row = within_set % LEN3
    first_slot = jnp.minimum(inner_row // LEN1, 2)
    slot_kind = jnp.where(second, 3, first_slot)
    position = inner_row - jnp.where(second, 0, first_slot * LEN1)
    slot_id = group_id * 4 + slot_kind
    bucket = jnp.maximum(slot_kind - 1, 0)
    bucket_rank = jnp.where(slot_kind < 2, 2 * group_id + slot_kind, group_id)
    used_slots = lax.optimization_barrier(jnp.sum(jnp.where(bucket[:, None] == jnp.arange(3, dtype=jnp.int32)[None, :], counts[None, :], 0), axis=1))
    slot_length = lax.optimization_barrier(jnp.sum(jnp.where(slot_id[:, None] == jnp.arange(lengths.shape[0], dtype=jnp.int32)[None, :], lengths[None, :], 0), axis=1))
    is_live = (bucket_rank < used_slots) & (position < slot_length)
    return (slot_id, position, is_live)

def adapted(inputs, weight, downward, upward, scaling):
    coefficient = exact_dot(inputs, downward.T) * scaling
    return exact_dot(inputs, weight) + exact_dot(coefficient, upward)

def layer_norm(values, norm_gain, norm_shift):
    centered = values - lax.optimization_barrier(jnp.mean(values, axis=-1, keepdims=True))
    variance = lax.optimization_barrier(jnp.mean(centered * centered, axis=-1, keepdims=True))
    return centered * lax.rsqrt(variance + norm_epsilon) * norm_gain + norm_shift

def attend_block(block_queries, block_keys, block_values, pos_key, pos_query, slot_id, position, is_live, rel_bucket):
    topmost_precision = lax.Precision.HIGHEST
    query_per_head = block_queries.reshape(LEN3, H, DH)
    head_key = block_keys.reshape(LEN3, H, DH)
    head_value = block_values.reshape(LEN3, H, DH)
    relative_key_rows = pos_key.reshape(2 * SPAN, H, DH)
    rel_query = pos_query.reshape(2 * SPAN, H, DH)
    content = jnp.einsum('ihd,jhd->hij', query_per_head, head_key, precision=topmost_precision)
    target_position = jnp.einsum('ukq,fkq->kuf', query_per_head, relative_key_rows, precision=topmost_precision)
    from_pos = jnp.einsum('jhd,bhd->hjb', head_key, rel_query, precision=topmost_precision)
    offsets = position[:, None] - position[None, :] + LEN3 - 1
    bucket_of = jnp.broadcast_to(rel_bucket[offsets][None], (H, LEN3, LEN3))
    relative = jnp.take_along_axis(target_position, bucket_of, axis=2) + jnp.swapaxes(jnp.take_along_axis(from_pos, bucket_of, axis=2), 1, 2)
    raw_scores = low_back(content + relative)
    allowed = (slot_id[:, None] == slot_id[None, :]) & is_live[None, :]
    scores = jnp.where(allowed[None], raw_scores * (3.0 * DH) ** (-0.5), masked_score)
    prob_low = low(jax.nn.softmax(scores, axis=2))
    context = jnp.einsum('hij,jhd->ihd', prob_low, head_value, precision=topmost_precision)
    return context.reshape(LEN3, D)

def device_forward(frozen, trained, rel_bucket, inputs, lengths, counts):
    qkv_weight, out_weight, in_weight, back_weight, rel_embed, gain_one, shift_one, gain_two, shift_two = frozen
    adapt_down, adapt_up, hidden_up, hidden_down, adapt_scale = trained
    row_count = inputs.shape[0]
    slot_id, position, is_live = row_layout(row_count, lengths, counts)

    def project(source, member):
        return low_back(low(adapted(source, qkv_weight[member], adapt_down[member], adapt_up[member], adapt_scale[member])))
    queries = project(inputs, 0)
    every_key_rows = project(inputs, 1)
    values_all = project(inputs, 2)
    pos_key = project(rel_embed, 1)
    pos_query = project(rel_embed, 0)
    blocks = row_count // LEN3
    context = jax.vmap(attend_block, in_axes=(0, 0, 0, None, None, 0, 0, 0, None))(queries.reshape(blocks, LEN3, D), every_key_rows.reshape(blocks, LEN3, D), values_all.reshape(blocks, LEN3, D), pos_key, pos_query, slot_id.reshape(blocks, LEN3), position.reshape(blocks, LEN3), is_live.reshape(blocks, LEN3), rel_bucket)
    context = low_back(low(context.reshape(row_count, D)))
    attended = low_back(adapted(context, out_weight, adapt_down[3], adapt_up[3], adapt_scale[3]))
    normed = layer_norm(inputs + attended, gain_one, shift_one)
    hidden = low_back(adapted(low(normed), in_weight, adapt_down[4], hidden_up, adapt_scale[4]))
    active = low(jax.nn.gelu(hidden, approximate=False))
    mlp_out = low_back(adapted(active, back_weight, hidden_down, adapt_up[4], adapt_scale[5]))
    result = layer_norm(normed + mlp_out, gain_two, shift_two)
    return result * is_live[:, None].astype(result.dtype)

def reference(tokens, qkv_weight, out_weight, in_weight, back_weight, rel_embed, gain_one, shift_one, gain_two, shift_two, adapt_down, adapt_up, hidden_up, hidden_down, adapt_scale, seq_lengths, seq_counts, rel_bucket, out_grad):
    device_count = N_DP * N_TENSOR
    frozen = tuple((source.astype(jnp.float32) for source in (qkv_weight, out_weight, in_weight, back_weight, rel_embed, gain_one, shift_one, gain_two, shift_two)))
    trained = tuple((source.astype(jnp.float32) for source in (adapt_down, adapt_up, hidden_up, hidden_down, adapt_scale)))
    inputs = tokens.astype(jnp.float32).reshape(device_count, -1, D)

    def forward_all(inputs, trained):

        def device_step(unused, pieces):
            return (unused, jax.checkpoint(device_forward)(frozen, trained, rel_bucket, pieces[0], pieces[1], pieces[2]))
        unused, outputs = lax.scan(device_step, jnp.zeros((), jnp.int32), (inputs, seq_lengths, seq_counts))
        return outputs
    outputs, pullback = jax.vjp(forward_all, inputs, trained)
    grad_inputs, grad_trained = pullback(out_grad.astype(jnp.float32).reshape(device_count, -1, D))
    mixed = outputs.reshape(-1, D).astype(jnp.bfloat16)
    return (mixed, grad_inputs.reshape(-1, D), grad_trained[0], grad_trained[1], grad_trained[2], grad_trained[3], grad_trained[4])
```

```python
import jax
import jax.numpy as jnp
from jax import lax
from jax.experimental import pallas as pl
from jax.experimental.pallas import tpu as pltpu
from jax.sharding import PartitionSpec as P

D = 768
H = 12
DH = 64
PAIR = 2 * DH
SPAN = 256
RANK = 12
PAD = 16
ROWS = 1024
LEN1 = 128
LEN3 = 512
OFFSETS = 2 * LEN3
TILE = 128
BLOCK = 256
SLOTS = ((0, 128), (128, 128), (256, 256), (512, 512))
PACKED = 2 * D + 2 * PAD
norm_epsilon = 1e-07
masked_score = -1e30
bf16 = jnp.bfloat16
f32 = jnp.float32
MEMORY = 60 * 1024 * 1024


def dot_nn(a, b):
    return jnp.dot(a, b, preferred_element_type=f32)


def dot_nt(a, b):
    return lax.dot_general(a, b, (((1,), (1,)), ((), ())), preferred_element_type=f32)


def dot_tn(a, b):
    return lax.dot_general(a, b, (((0,), (0,)), ((), ())), preferred_element_type=f32)


def two_parts(wide):
    high = wide.astype(bf16)
    rest = (wide - high.astype(f32)).astype(bf16)
    return jnp.concatenate([high, rest], axis=0)


def add_parts(stacked):
    return stacked[:PAD] + stacked[PAD:]


def merged(weight, down, up, scale):
    twice = jnp.concatenate([up, up], axis=0)
    extra = dot_tn(two_parts(down.astype(f32) * scale), twice)
    return (weight.astype(f32) + extra).astype(bf16)


def live_counts(lengths_ref, counts_ref):
    ranks = ((0, 0), (0, 1), (1, 0), (2, 0))
    return [
        jnp.where(rank < counts_ref[0, bucket], lengths_ref[0, slot], 0)
        for slot, (bucket, rank) in enumerate(ranks)
    ]


def pack_kernel(in_ref, back_ref, factor_ref, scale_ref, packed_ref):
    packed_ref[:D] = merged(in_ref[...], factor_ref[4], factor_ref[10], scale_ref[:, 4:5])
    packed_ref[D : 2 * D] = merged(back_ref[...], factor_ref[11], factor_ref[9], scale_ref[:, 5:6])
    packed_ref[2 * D : 2 * D + PAD] = factor_ref[10]
    packed_ref[2 * D + PAD :] = factor_ref[11]


def pack_weights(in_weight, back_weight, factors, scales):
    return pl.pallas_call(
        pack_kernel,
        out_shape=jax.ShapeDtypeStruct((PACKED, D), bf16),
        compiler_params=pltpu.CompilerParams(vmem_limit_bytes=MEMORY),
        name="pack_weights",
    )(in_weight, back_weight, factors, scales)


def project_kernel(
    tokens_ref,
    qkv_ref,
    out_ref,
    rel_ref,
    index_ref,
    factor_ref,
    scale_ref,
    q_ref,
    k_ref,
    v_ref,
    ek_ref,
    eq_ref,
    fq_ref,
    merged_ref,
    coeff_ref,
    rel_coeff_ref,
    pos_scr,
):
    step = pl.program_id(0)

    @pl.when(step == 0)
    def _():
        for member in range(3):
            merged_ref[member] = merged(
                qkv_ref[member],
                factor_ref[member],
                factor_ref[5 + member],
                scale_ref[:, member : member + 1],
            )
        merged_ref[3] = merged(out_ref[...], factor_ref[3], factor_ref[8], scale_ref[:, 3:4])
        rel = rel_ref[...]
        for member in range(2):
            pos_scr[member] = dot_nn(rel, merged_ref[member]).astype(bf16)
            rel_coeff_ref[member] = dot_nt(factor_ref[member], rel)

    tokens = tokens_ref[...]
    for member, ref in enumerate((q_ref, k_ref, v_ref)):
        ref[...] = dot_nn(tokens, merged_ref[member]).astype(bf16)
        coeff_ref[member] = dot_nt(factor_ref[member], tokens)
    bucket = lax.broadcasted_iota(jnp.int32, (2 * SPAN, BLOCK), 0)
    for ref, row, member in ((ek_ref, 0, 1), (eq_ref, 0, 0), (fq_ref, 1, 0)):
        chosen = jnp.where(bucket == index_ref[row : row + 1, :], 1.0, 0.0).astype(bf16)
        ref[...] = dot_tn(chosen, pos_scr[member]).astype(bf16)


def whole(*shape):
    return pl.BlockSpec(shape, lambda *at: (0,) * len(shape))


def project(tokens, qkv_weight, out_weight, rel_embed, index_rows, factors, scales):
    tile = pl.BlockSpec((BLOCK, D), lambda i: (i, 0))
    rows = jax.ShapeDtypeStruct((ROWS, D), bf16)
    return pl.pallas_call(
        project_kernel,
        grid=(ROWS // BLOCK,),
        in_specs=[
            tile,
            whole(3, D, D),
            whole(D, D),
            whole(2 * SPAN, D),
            pl.BlockSpec((2, BLOCK), lambda i: (0, i)),
            whole(12, PAD, D),
            whole(PAD, 128),
        ],
        out_specs=[tile] * 6
        + [
            whole(4, D, D),
            pl.BlockSpec((3, PAD, BLOCK), lambda i: (0, 0, i)),
            whole(2, PAD, 2 * SPAN),
        ],
        out_shape=[rows] * 6
        + [
            jax.ShapeDtypeStruct((4, D, D), bf16),
            jax.ShapeDtypeStruct((3, PAD, ROWS), f32),
            jax.ShapeDtypeStruct((2, PAD, 2 * SPAN), f32),
        ],
        scratch_shapes=[pltpu.VMEM((2, 2 * SPAN, D), bf16)],
        compiler_params=pltpu.CompilerParams(vmem_limit_bytes=MEMORY),
        name="project",
    )(tokens, qkv_weight, out_weight, rel_embed, index_rows, factors, scales)


def unit_matrix(flipped):
    row = lax.broadcasted_iota(jnp.int32, (TILE, TILE), 0)
    col = lax.broadcasted_iota(jnp.int32, (TILE, TILE), 1)
    return jnp.where(row == (TILE - 1 - col if flipped else col), 1.0, 0.0).astype(bf16)


def head_lanes(member):
    lane = lax.broadcasted_iota(jnp.int32, (1, PAIR), 1)
    return jnp.where(lane // DH == member, 1.0, 0.0).astype(bf16)


def skew(table, length):
    return pltpu.roll(table, length + 1, 1, stride=1, stride_axis=0)[:, :length]


def unskew(scores):
    wide = jnp.concatenate([scores, jnp.zeros((TILE, TILE), f32)], axis=1)
    return pltpu.roll(wide, 0, 1, stride=1, stride_axis=0)


def add_pair(ref, member, start, value):
    here = pl.ds(start, value.shape[0])

    @pl.when(member == 0)
    def _():
        ref[here, :] = value

    @pl.when(member == 1)
    def _():
        ref[here, :] = ref[here, :] + value


def forward_kernel(
    lengths_ref,
    counts_ref,
    q_ref,
    k_ref,
    v_ref,
    ek_ref,
    eq_ref,
    context_ref,
    p1_ref,
    p2_ref,
    p3_ref,
    shift_scr,
):
    member = pl.program_id(1)
    mask = head_lanes(member)
    eye = unit_matrix(False)
    anti = unit_matrix(True)
    factor = (3.0 * DH) ** -0.5
    counts = live_counts(lengths_ref, counts_ref)
    for slot, (start, length) in enumerate(SLOTS):
        keys = k_ref[start : start + length, :] * mask
        values = v_ref[start : start + length, :] * mask
        live = lax.broadcasted_iota(jnp.int32, (1, length), 1) < counts[slot]
        for t in range(length // TILE):
            low = LEN3 - TILE - TILE * t
            table = dot_nt(keys[t * TILE : (t + 1) * TILE], eq_ref[low : low + length + TILE, :])
            shift_scr[t * TILE : (t + 1) * TILE, :length] = skew(table, length).astype(bf16)
        for t in range(length // TILE):
            low = LEN3 - TILE - TILE * t
            row = start + t * TILE
            queries = q_ref[row : row + TILE, :] * mask
            relative = skew(dot_nt(queries, ek_ref[low : low + length + TILE, :]), length)
            left = jnp.concatenate([queries, eye], axis=1)
            right = jnp.concatenate(
                [keys, shift_scr[:length, t * TILE : (t + 1) * TILE]], axis=1
            )
            scores = jnp.where(live, (dot_nt(left, right) + relative) * factor, masked_score)
            weights = jnp.exp(scores - jnp.max(scores, axis=1, keepdims=True))
            prob = (weights * (1.0 / jnp.sum(weights, axis=1, keepdims=True))).astype(bf16)
            add_pair(context_ref, member, row, dot_nn(prob, values).astype(bf16))
            turned = dot_nn(anti, prob).astype(bf16)
            if length == LEN1:
                p1_ref[0, row : row + TILE, :] = turned
            elif length == LEN3:
                p3_ref[0, t * TILE : (t + 1) * TILE, :] = turned
            else:
                p2_ref[0, t * TILE : (t + 1) * TILE, :] = turned


PAIR_SPEC = pl.BlockSpec((ROWS, PAIR), lambda p, e: (0, p))
PROB_SIZES = ((256, 128), (256, 256), (512, 512))
PROB_SPECS = [pl.BlockSpec((1, *size), lambda p, e: (2 * p + e, 0, 0)) for size in PROB_SIZES]


def attend_forward(lengths, counts, q, k, v, ek, eq):
    return pl.pallas_call(
        forward_kernel,
        grid=(H // 2, 2),
        in_specs=[pl.BlockSpec(memory_space=pltpu.SMEM)] * 2 + [PAIR_SPEC] * 5,
        out_specs=[PAIR_SPEC] + PROB_SPECS,
        out_shape=[jax.ShapeDtypeStruct((ROWS, D), bf16)]
        + [jax.ShapeDtypeStruct((H, *size), bf16) for size in PROB_SIZES],
        scratch_shapes=[pltpu.VMEM((LEN3, LEN3), bf16)],
        compiler_params=pltpu.CompilerParams(vmem_limit_bytes=MEMORY),
        name="attention_forward",
    )(lengths, counts, q, k, v, ek, eq)


def backward_kernel(
    q_ref,
    k_ref,
    v_ref,
    g_ref,
    ek_ref,
    fq_ref,
    p1_ref,
    p2_ref,
    p3_ref,
    gq_ref,
    gk_ref,
    gv_ref,
    gek_ref,
    gfq_ref,
    grad_scr,
    turned_scr,
    values_scr,
):
    member = pl.program_id(1)
    mask = head_lanes(member)
    eye = unit_matrix(False)
    anti = unit_matrix(True)
    factor = (3.0 * DH) ** -0.5

    @pl.when(member == 0)
    def _():
        gek_ref[...] = jnp.zeros_like(gek_ref)
        gfq_ref[...] = jnp.zeros_like(gfq_ref)

    for start, length in SLOTS:
        count = length // TILE
        keys = k_ref[start : start + length, :] * mask
        values = v_ref[start : start + length, :] * mask
        value_grad = jnp.zeros((PAIR, length), f32)
        for t in range(count):
            low = LEN3 - TILE - TILE * t
            row = start + t * TILE
            queries = dot_nn(anti, q_ref[row : row + TILE, :] * mask).astype(bf16)
            grads = dot_nn(anti, g_ref[row : row + TILE, :] * mask).astype(bf16)
            if length == LEN1:
                prob = p1_ref[0, row : row + TILE, :]
            elif length == LEN3:
                prob = p3_ref[0, t * TILE : (t + 1) * TILE, :]
            else:
                prob = p2_ref[0, t * TILE : (t + 1) * TILE, :]
            grad_prob = dot_nt(grads, values)
            wide = prob.astype(f32)
            delta = jnp.sum(wide * grad_prob, axis=1, keepdims=True)
            raw = (wide * ((grad_prob - delta) * factor)).astype(bf16)
            place = (count - 1 - t) * TILE
            grad_scr[place : place + TILE, :length] = raw
            turned_scr[place : place + TILE, :] = queries
            spread = unskew(raw.astype(f32)).astype(bf16)
            window = ek_ref[low : low + length + TILE, :] * mask
            query_grad = dot_nn(
                jnp.concatenate([raw, spread], axis=1), jnp.concatenate([keys, window], axis=0)
            )
            add_pair(gq_ref, member, row, dot_nn(anti, query_grad.astype(bf16)).astype(bf16))
            gek_ref[:, low : low + length + TILE] += dot_tn(queries, spread)
            value_grad = value_grad + dot_tn(grads, prob)
        values_scr[:, start : start + length] = value_grad
        turned = turned_scr[:length, :]
        for t in range(count):
            low = LEN3 - length + TILE * t
            row = start + t * TILE
            raw = dot_nt(eye, grad_scr[:length, t * TILE : (t + 1) * TILE])
            spread = unskew(raw).astype(bf16)
            window = fq_ref[low : low + length + TILE, :] * mask
            key_grad = dot_nn(
                jnp.concatenate([raw.astype(bf16), spread], axis=1),
                jnp.concatenate([turned, window], axis=0),
            )
            add_pair(gk_ref, member, row, key_grad.astype(bf16))
            gfq_ref[:, low : low + length + TILE] += dot_tn(
                keys[t * TILE : (t + 1) * TILE], spread
            )
    add_pair(gv_ref, member, 0, values_scr[...].T.astype(bf16))


def attend_backward(q, k, v, g, ek, fq, p1, p2, p3):
    table = pl.BlockSpec((PAIR, OFFSETS), lambda p, e: (p, 0))
    return pl.pallas_call(
        backward_kernel,
        grid=(H // 2, 2),
        in_specs=[PAIR_SPEC] * 6 + PROB_SPECS,
        out_specs=[PAIR_SPEC] * 3 + [table] * 2,
        out_shape=[jax.ShapeDtypeStruct((ROWS, D), bf16)] * 3
        + [jax.ShapeDtypeStruct((D, OFFSETS), f32)] * 2,
        scratch_shapes=[
            pltpu.VMEM((LEN3, LEN3), bf16),
            pltpu.VMEM((LEN3, PAIR), bf16),
            pltpu.VMEM((PAIR, ROWS), f32),
        ],
        compiler_params=pltpu.CompilerParams(vmem_limit_bytes=MEMORY),
        name="attention_backward",
    )(q, k, v, g, ek, fq, p1, p2, p3)


def gelu_pair(hidden):
    z = jnp.abs(hidden) * 0.7071067811865476
    t = 1.0 / (1.0 + 0.3275911 * z)
    poly = t * (
        0.127414796
        + t * (-0.142248368 + t * (0.7107068705 + t * (-0.7265760135 + t * 0.5307027145)))
    )
    bell = jnp.exp(-z * z)
    tail = poly * bell
    below = jnp.where(hidden >= 0, 1.0 - tail, tail)
    return hidden * below, below + hidden * (bell * 0.3989422804014327)


def norm_forward(values, gain, shift):
    centered = values - jnp.mean(values, axis=1, keepdims=True)
    inverse = lax.rsqrt(jnp.mean(centered * centered, axis=1, keepdims=True) + norm_epsilon)
    normal = centered * inverse
    return (normal * gain + shift, normal, inverse)


def norm_backward(grad_out, normal, inverse, gain):
    scaled = grad_out * gain
    return inverse * (
        scaled
        - jnp.mean(scaled, axis=1, keepdims=True)
        - normal * jnp.mean(scaled * normal, axis=1, keepdims=True)
    )


def middle_kernel(
    lengths_ref,
    counts_ref,
    tokens_ref,
    context_ref,
    out_grad_ref,
    weight_ref,
    packed_ref,
    factor_ref,
    scale_ref,
    norm_ref,
    mixed_ref,
    grad_one_ref,
    context_grad_ref,
    small_ref,
    hidden_ref,
    scale_grad_ref,
    active_scr,
    slope_scr,
):
    step = pl.program_id(0)
    chunks = packed_ref.shape[0]

    @pl.when(step == 0)
    def _():
        small_ref[...] = jnp.zeros_like(small_ref)
        hidden_ref[...] = jnp.zeros_like(hidden_ref)
        scale_grad_ref[...] = jnp.zeros_like(scale_grad_ref)

    row = lax.broadcasted_iota(jnp.int32, (BLOCK, 1), 0) + step * BLOCK
    live = jnp.zeros((BLOCK, 1), f32)
    for (start, length), used in zip(SLOTS, live_counts(lengths_ref, counts_ref)):
        live = jnp.where((row >= start) & (row < start + used), 1.0, live)
    gain_one, shift_one, gain_two, shift_two = (norm_ref[i : i + 1, :] for i in range(4))

    context = context_ref[...]
    weight = weight_ref[0]
    attended = dot_nn(context, weight)
    normed, normal_one, inverse_one = norm_forward(
        tokens_ref[...].astype(f32) + attended, gain_one, shift_one
    )
    normed_low = normed.astype(bf16)
    mlp = jnp.zeros((BLOCK, D), f32)
    back_coeff = jnp.zeros((PAD, BLOCK), f32)
    for c in range(chunks):
        hidden = dot_nn(normed_low, packed_ref[c, :D, :])
        active, slope = gelu_pair(hidden)
        active = active.astype(bf16)
        active_scr[c] = active
        slope_scr[c] = slope
        mlp = mlp + dot_nn(active, packed_ref[c, D : 2 * D, :])
        back_coeff = back_coeff + dot_nt(packed_ref[c, 2 * D + PAD :, :], active)
    result, normal_two, inverse_two = norm_forward(normed + mlp, gain_two, shift_two)
    mixed_ref[...] = (result * live).astype(bf16)
    grad_two = norm_backward(
        out_grad_ref[...].astype(f32) * live, normal_two, inverse_two, gain_two
    )
    grad_mlp = grad_two.astype(bf16)

    back_slope = dot_nt(factor_ref[9], grad_mlp)
    small_ref[3] += add_parts(dot_nn(two_parts(back_coeff * scale_ref[:, 5:6]), grad_mlp))
    scale_grad_ref[:, 5:6] += jnp.sum(back_coeff * back_slope, axis=1, keepdims=True)
    back_through = two_parts(back_slope * scale_ref[:, 5:6])
    in_coeff = dot_nt(factor_ref[4], normed_low)
    in_scaled = two_parts(in_coeff * scale_ref[:, 4:5])
    in_slope = jnp.zeros((PAD, BLOCK), f32)
    grad_normed = grad_two
    for c in range(chunks):
        grad_active = dot_nt(grad_mlp, packed_ref[c, D : 2 * D, :])
        grad_hidden = (grad_active * slope_scr[c]).astype(bf16)
        grad_normed = grad_normed + dot_nt(grad_hidden, packed_ref[c, :D, :])
        in_slope = in_slope + dot_nt(packed_ref[c, 2 * D : 2 * D + PAD, :], grad_hidden)
        hidden_ref[c] += add_parts(dot_nn(in_scaled, grad_hidden))
        hidden_ref[chunks + c] += add_parts(dot_nn(back_through, active_scr[c]))
    scale_grad_ref[:, 4:5] += jnp.sum(in_coeff * in_slope, axis=1, keepdims=True)
    small_ref[2] += add_parts(dot_nn(two_parts(in_slope * scale_ref[:, 4:5]), normed_low))

    grad_one = norm_backward(grad_normed, normal_one, inverse_one, gain_one)
    grad_one_ref[...] = grad_one
    grad_attended = grad_one.astype(bf16)
    context_grad_ref[...] = dot_nt(grad_attended, weight).astype(bf16)
    out_coeff = dot_nt(factor_ref[3], context)
    out_slope = dot_nt(factor_ref[8], grad_attended)
    small_ref[1] += add_parts(dot_nn(two_parts(out_coeff * scale_ref[:, 3:4]), grad_attended))
    small_ref[0] += add_parts(dot_nn(two_parts(out_slope * scale_ref[:, 3:4]), context))
    scale_grad_ref[:, 3:4] += jnp.sum(out_coeff * out_slope, axis=1, keepdims=True)


def middle(lengths, counts, tokens, context, out_grad, weights, packed, factors, scales, norms):
    chunks = packed.shape[0]
    tile = pl.BlockSpec((BLOCK, D), lambda i: (i, 0))
    return pl.pallas_call(
        middle_kernel,
        grid=(ROWS // BLOCK,),
        in_specs=[pl.BlockSpec(memory_space=pltpu.SMEM)] * 2
        + [tile] * 3
        + [
            pl.BlockSpec((1, D, D), lambda i: (3, 0, 0)),
            pl.BlockSpec(
                (chunks, PACKED, D), lambda i: (0, 0, 0), pipeline_mode=pl.Buffered(1)
            ),
            whole(12, PAD, D),
            whole(PAD, 128),
            whole(4, D),
        ],
        out_specs=[tile] * 3
        + [whole(4, PAD, D), whole(2 * chunks, PAD, D), whole(PAD, 128)],
        out_shape=[
            jax.ShapeDtypeStruct((ROWS, D), bf16),
            jax.ShapeDtypeStruct((ROWS, D), f32),
            jax.ShapeDtypeStruct((ROWS, D), bf16),
            jax.ShapeDtypeStruct((4, PAD, D), f32),
            jax.ShapeDtypeStruct((2 * chunks, PAD, D), f32),
            jax.ShapeDtypeStruct((PAD, 128), f32),
        ],
        scratch_shapes=[
            pltpu.VMEM((chunks, BLOCK, D), bf16),
            pltpu.VMEM((chunks, BLOCK, D), f32),
        ],
        compiler_params=pltpu.CompilerParams(vmem_limit_bytes=MEMORY),
        name="middle",
    )(lengths, counts, tokens, context, out_grad, weights, packed, factors, scales, norms)


def last_kernel(
    tokens_ref,
    gq_ref,
    gk_ref,
    gv_ref,
    grad_one_ref,
    coeff_ref,
    merged_ref,
    rel_ref,
    index_ref,
    rel_coeff_ref,
    gek_ref,
    gfq_ref,
    factor_ref,
    scale_ref,
    in_grad_ref,
    down_ref,
    up_ref,
    scale_grad_ref,
):
    step = pl.program_id(0)

    @pl.when(step == 0)
    def _():
        rel = rel_ref[...]
        scale_grad_ref[...] = jnp.zeros_like(scale_grad_ref)
        down_ref[2] = jnp.zeros((PAD, D), f32)
        up_ref[2] = jnp.zeros((PAD, D), f32)
        bucket = lax.broadcasted_iota(jnp.int32, (2 * SPAN, OFFSETS), 0)
        for member, ref, row in ((0, gfq_ref, 1), (1, gek_ref, 0)):
            scale = scale_ref[:, member : member + 1]
            chosen = jnp.where(bucket == index_ref[row : row + 1, :], 1.0, 0.0).astype(bf16)
            grad = dot_nt(ref[...].astype(bf16), chosen).astype(bf16)
            coeff = rel_coeff_ref[member]
            slope = dot_nn(factor_ref[5 + member], grad)
            up_ref[member] = add_parts(dot_nt(two_parts(coeff * scale), grad))
            down_ref[member] = add_parts(dot_nn(two_parts(slope * scale), rel))
            scale_grad_ref[:, member : member + 1] += jnp.sum(
                coeff * slope, axis=1, keepdims=True
            )

    tokens = tokens_ref[...]
    in_grad = grad_one_ref[...]
    for member, ref in enumerate((gq_ref, gk_ref, gv_ref)):
        grad = ref[...]
        scale = scale_ref[:, member : member + 1]
        in_grad = in_grad + dot_nt(grad, merged_ref[member])
        coeff = coeff_ref[member]
        slope = dot_nt(factor_ref[5 + member], grad)
        up_ref[member] += add_parts(dot_nn(two_parts(coeff * scale), grad))
        down_ref[member] += add_parts(dot_nn(two_parts(slope * scale), tokens))
        scale_grad_ref[:, member : member + 1] += jnp.sum(coeff * slope, axis=1, keepdims=True)
    in_grad_ref[...] = in_grad


def last(tokens, gq, gk, gv, grad_one, coeff, weights, rel, index, rel_coeff, gek, gfq, factors, scales):
    tile = pl.BlockSpec((BLOCK, D), lambda i: (i, 0))
    return pl.pallas_call(
        last_kernel,
        grid=(ROWS // BLOCK,),
        in_specs=[tile] * 5
        + [
            pl.BlockSpec((3, PAD, BLOCK), lambda i: (0, 0, i)),
            whole(3, D, D),
            whole(2 * SPAN, D),
            whole(2, OFFSETS),
            whole(2, PAD, 2 * SPAN),
            whole(D, OFFSETS),
            whole(D, OFFSETS),
            whole(12, PAD, D),
            whole(PAD, 128),
        ],
        out_specs=[tile, whole(3, PAD, D), whole(3, PAD, D), whole(PAD, 128)],
        out_shape=[
            jax.ShapeDtypeStruct((ROWS, D), f32),
            jax.ShapeDtypeStruct((3, PAD, D), f32),
            jax.ShapeDtypeStruct((3, PAD, D), f32),
            jax.ShapeDtypeStruct((PAD, 128), f32),
        ],
        compiler_params=pltpu.CompilerParams(vmem_limit_bytes=MEMORY),
        name="last",
    )(tokens, gq, gk, gv, grad_one, coeff, weights, rel, index, rel_coeff, gek, gfq, factors, scales)


def devices():
    return lax.axis_size("dp") * lax.axis_size("tensor")


def share_kernel(
    down_ref,
    up_ref,
    last_ref,
    middle_ref,
    early_ref,
    down_out,
    up_out,
    scale_out,
    stage_scr,
    mine_scr,
    land_scr,
    all_scr,
    send_sem,
    land_sem,
    spread_sem,
    all_sem,
):
    count = devices()
    inner = lax.axis_size("tensor")
    me = lax.axis_index("dp") * inner + lax.axis_index("tensor")

    def partner(off):
        other = lax.rem(me + off, count)
        return other, (other // inner, lax.rem(other, inner))

    barrier = pltpu.get_barrier_semaphore()

    @pl.loop(1, count)
    def _(off):
        pl.semaphore_signal(
            barrier, inc=1, device_id=partner(off)[1], device_id_type=pl.DeviceIdType.MESH
        )

    stage_scr[...] = jnp.zeros_like(stage_scr)
    for number in range(6):
        ref = down_ref if number < 3 else up_ref
        for block in range(D // 128):
            at = (number * (D // 128) + block) * RANK
            stage_scr[at : at + RANK, :] = ref[number % 3, :RANK, block * 128 : block * 128 + 128]
    at = 6 * (D // 128) * RANK
    stage_scr[at : at + PAD, :] = last_ref[...] + middle_ref[...]
    mine_scr[...] = stage_scr[...].astype(bf16).reshape(count, PAD, 128)
    pl.semaphore_wait(barrier, count - 1)

    def first(off):
        other, where = partner(off)
        return pltpu.make_async_remote_copy(
            src_ref=mine_scr.at[other],
            dst_ref=land_scr.at[off],
            send_sem=send_sem.at[off],
            recv_sem=land_sem.at[off],
            device_id=where,
            device_id_type=pl.DeviceIdType.MESH,
        )

    def second(off):
        other, where = partner(off)
        return pltpu.make_async_remote_copy(
            src_ref=all_scr.at[me],
            dst_ref=all_scr.at[me],
            send_sem=spread_sem.at[off],
            recv_sem=all_sem.at[off],
            device_id=where,
            device_id_type=pl.DeviceIdType.MESH,
        )

    def second_arrival(off):
        origin = lax.rem(me + count - off, count)
        return pltpu.make_async_remote_copy(
            src_ref=all_scr.at[origin],
            dst_ref=all_scr.at[origin],
            send_sem=spread_sem.at[off],
            recv_sem=all_sem.at[off],
            device_id=partner(off)[1],
            device_id_type=pl.DeviceIdType.MESH,
        )

    @pl.loop(1, count)
    def _(off):
        first(off).start()

    land_scr[0] = mine_scr[me]

    @pl.loop(1, count)
    def _(off):
        first(off).wait_recv()

    all_scr[me] = jnp.sum(land_scr[...].astype(f32), axis=0).astype(bf16)

    @pl.loop(1, count)
    def _(off):
        second(off).start()

    for index, place in ((0, 3), (2, 4)):
        down_out[place] = early_ref[index]
        up_out[place] = early_ref[index + 1]

    @pl.loop(1, count)
    def _(off):
        second_arrival(off).wait_recv()

    stage_scr[...] = all_scr[...].astype(f32).reshape(count * PAD, 128)
    for number in range(6):
        ref = down_out if number < 3 else up_out
        for block in range(D // 128):
            at = (number * (D // 128) + block) * RANK
            ref[number % 3, :, block * 128 : block * 128 + 128] = stage_scr[at : at + RANK, :]
    at = 6 * (D // 128) * RANK
    scale_out[...] = stage_scr[at : at + PAD, :].T[:6, :RANK]

    @pl.loop(1, count)
    def _(off):
        first(off).wait_send()
        second(off).wait_send()


def share(down, up, last_scale, middle_scale, early):
    count = devices()
    factor = jax.ShapeDtypeStruct((5, RANK, D), f32)
    return pl.pallas_call(
        share_kernel,
        in_specs=[pl.BlockSpec(memory_space=pltpu.VMEM)] * 5,
        out_specs=[pl.BlockSpec(memory_space=pltpu.VMEM)] * 3,
        out_shape=[factor, factor, jax.ShapeDtypeStruct((6, RANK), f32)],
        scratch_shapes=[
            pltpu.VMEM((count * PAD, 128), f32),
            pltpu.VMEM((count, PAD, 128), bf16),
            pltpu.VMEM((count, PAD, 128), bf16),
            pltpu.VMEM((count, PAD, 128), bf16),
        ]
        + [pltpu.SemaphoreType.DMA((count,))] * 4,
        compiler_params=pltpu.CompilerParams(
            collective_id=0, has_side_effects=True, vmem_limit_bytes=MEMORY
        ),
        name="share",
    )(down, up, last_scale, middle_scale, early)


def on_device(
    tokens,
    qkv_weight,
    out_weight,
    in_weight,
    back_weight,
    rel_embed,
    gain_one,
    shift_one,
    gain_two,
    shift_two,
    adapt_down,
    adapt_up,
    hidden_up,
    hidden_down,
    adapt_scale,
    seq_lengths,
    seq_counts,
    rel_bucket,
    out_grad,
):
    factors = jnp.pad(
        jnp.concatenate([adapt_down, adapt_up, hidden_up[None], hidden_down[None]], axis=0),
        ((0, 0), (0, PAD - RANK), (0, 0)),
    )
    scales = jnp.pad(adapt_scale.T, ((0, PAD - RANK), (0, 128 - 6)))
    index_rows = jnp.pad(
        jnp.stack([rel_bucket[::-1], rel_bucket]), ((0, 0), (0, 1)), constant_values=-1
    )
    norms = jnp.stack([gain_one, shift_one, gain_two, shift_two])
    packed = lax.all_gather(
        pack_weights(in_weight, back_weight, factors, scales), "tensor", axis=0
    )
    q, k, v, ek, eq, fq, weights, coeff, rel_coeff = project(
        tokens, qkv_weight, out_weight, rel_embed, index_rows, factors, scales
    )
    context, p1, p2, p3 = attend_forward(seq_lengths, seq_counts, q, k, v, ek, eq)
    mixed, grad_one, context_grad, small, hidden, middle_scale = middle(
        seq_lengths, seq_counts, tokens, context, out_grad, weights, packed, factors, scales, norms
    )
    chunks = packed.shape[0]
    small, hidden = lax.psum(
        (small[:, :RANK], hidden[:, :RANK].reshape(2, chunks, RANK, D)), ("dp", "tensor")
    )
    hidden = hidden[:, lax.axis_index("tensor")]
    gq, gk, gv, gek, gfq = attend_backward(q, k, v, context_grad, ek, fq, p1, p2, p3)
    in_grad, down, up, last_scale = last(
        tokens, gq, gk, gv, grad_one, coeff, weights, rel_embed, index_rows, rel_coeff, gek, gfq, factors, scales
    )
    down_grad, up_grad, scale_grad = share(down, up, last_scale, middle_scale, small)
    return (mixed, in_grad, down_grad, up_grad, hidden[0], hidden[1], scale_grad)


def solution(mesh):
    rows = P(("dp", "tensor"), None)
    return jax.shard_map(
        on_device,
        mesh=mesh,
        in_specs=(
            rows,
            P(),
            P(),
            P(None, "tensor"),
            P("tensor", None),
            P(),
            P(),
            P(),
            P(),
            P(),
            P(),
            P(),
            P(None, "tensor"),
            P(None, "tensor"),
            P(),
            rows,
            rows,
            P(),
            rows,
        ),
        out_specs=(rows, rows, P(), P(), P(None, "tensor"), P(None, "tensor"), P()),
        check_vma=False,
    )
```

```python
import jax
import jax.numpy as jnp
from jax import lax
from jax.experimental import pallas as pl
from jax.experimental.pallas import tpu as pltpu
from jax.sharding import PartitionSpec as P

D = 768
H = 12
DH = 64
PAIR = 2 * DH
SPAN = 256
RANK = 12
PAD = 16
ROWS = 1024
LEN1 = 128
LEN3 = 512
OFFSETS = 2 * LEN3
TILE = 128
BLOCK = 256
SLOTS = ((0, 128), (128, 128), (256, 256), (512, 512))
PACKED = 2 * D + 2 * PAD
norm_epsilon = 1e-07
masked_score = -1e30
bf16 = jnp.bfloat16
f32 = jnp.float32
MEMORY = 60 * 1024 * 1024


def dot_nn(a, b):
    return jnp.dot(a, b, preferred_element_type=f32)


def dot_nt(a, b):
    return lax.dot_general(a, b, (((1,), (1,)), ((), ())), preferred_element_type=f32)


def dot_tn(a, b):
    return lax.dot_general(a, b, (((0,), (0,)), ((), ())), preferred_element_type=f32)


def two_parts(wide):
    high = wide.astype(bf16)
    rest = (wide - high.astype(f32)).astype(bf16)
    return jnp.concatenate([high, rest], axis=0)


def add_parts(stacked):
    return stacked[:PAD] + stacked[PAD:]


def merged(weight, down, up, scale):
    twice = jnp.concatenate([up, up], axis=0)
    extra = dot_tn(two_parts(down.astype(f32) * scale), twice)
    return (weight.astype(f32) + extra).astype(bf16)


def live_counts(lengths_ref, counts_ref):
    ranks = ((0, 0), (0, 1), (1, 0), (2, 0))
    return [
        jnp.where(rank < counts_ref[0, bucket], lengths_ref[0, slot], 0)
        for slot, (bucket, rank) in enumerate(ranks)
    ]


def pack_kernel(in_ref, back_ref, factor_ref, scale_ref, packed_ref):
    packed_ref[:D] = merged(in_ref[...], factor_ref[4], factor_ref[10], scale_ref[:, 4:5])
    packed_ref[D : 2 * D] = merged(back_ref[...], factor_ref[11], factor_ref[9], scale_ref[:, 5:6])
    packed_ref[2 * D : 2 * D + PAD] = factor_ref[10]
    packed_ref[2 * D + PAD :] = factor_ref[11]


def pack_weights(in_weight, back_weight, factors, scales):
    return pl.pallas_call(
        pack_kernel,
        out_shape=jax.ShapeDtypeStruct((PACKED, D), bf16),
        compiler_params=pltpu.CompilerParams(vmem_limit_bytes=MEMORY),
        name="pack_weights",
    )(in_weight, back_weight, factors, scales)


def project_kernel(
    tokens_ref,
    qkv_ref,
    out_ref,
    rel_ref,
    index_ref,
    factor_ref,
    scale_ref,
    q_ref,
    k_ref,
    v_ref,
    ek_ref,
    fq_ref,
    ekt_ref,
    eqt_ref,
    merged_ref,
    coeff_ref,
    rel_coeff_ref,
    pos_scr,
):
    step = pl.program_id(0)

    @pl.when(step == 0)
    def _():
        for member in range(3):
            merged_ref[member] = merged(
                qkv_ref[member],
                factor_ref[member],
                factor_ref[5 + member],
                scale_ref[:, member : member + 1],
            )
        merged_ref[3] = merged(out_ref[...], factor_ref[3], factor_ref[8], scale_ref[:, 3:4])
        rel = rel_ref[...]
        for member in range(2):
            pos_scr[member] = dot_nn(rel, merged_ref[member]).astype(bf16)
            rel_coeff_ref[member] = dot_nt(factor_ref[member], rel)

    tokens = tokens_ref[...]
    for member, ref in enumerate((q_ref, k_ref, v_ref)):
        ref[...] = dot_nn(tokens, merged_ref[member]).astype(bf16)
        coeff_ref[member] = dot_nt(factor_ref[member], tokens)
    bucket = lax.broadcasted_iota(jnp.int32, (2 * SPAN, BLOCK), 0)
    back, forth = (
        jnp.where(bucket == index_ref[row : row + 1, :], 1.0, 0.0).astype(bf16) for row in range(2)
    )
    ek_ref[...] = dot_tn(back, pos_scr[1]).astype(bf16)
    fq_ref[...] = dot_tn(forth, pos_scr[0]).astype(bf16)
    ekt_ref[...] = dot_tn(pos_scr[1], back).astype(bf16)
    eqt_ref[...] = dot_tn(pos_scr[0], back).astype(bf16)


def whole(*shape):
    return pl.BlockSpec(shape, lambda *at: (0,) * len(shape))


def project(tokens, qkv_weight, out_weight, rel_embed, index_rows, factors, scales):
    tile = pl.BlockSpec((BLOCK, D), lambda i: (i, 0))
    rows = jax.ShapeDtypeStruct((ROWS, D), bf16)
    return pl.pallas_call(
        project_kernel,
        grid=(ROWS // BLOCK,),
        in_specs=[
            tile,
            whole(3, D, D),
            whole(D, D),
            whole(2 * SPAN, D),
            pl.BlockSpec((2, BLOCK), lambda i: (0, i)),
            whole(12, PAD, D),
            whole(PAD, 128),
        ],
        out_specs=[tile] * 5
        + [pl.BlockSpec((D, BLOCK), lambda i: (0, i))] * 2
        + [
            whole(4, D, D),
            pl.BlockSpec((3, PAD, BLOCK), lambda i: (0, 0, i)),
            whole(2, PAD, 2 * SPAN),
        ],
        out_shape=[rows] * 5
        + [jax.ShapeDtypeStruct((D, OFFSETS), bf16)] * 2
        + [
            jax.ShapeDtypeStruct((4, D, D), bf16),
            jax.ShapeDtypeStruct((3, PAD, ROWS), f32),
            jax.ShapeDtypeStruct((2, PAD, 2 * SPAN), f32),
        ],
        scratch_shapes=[pltpu.VMEM((2, 2 * SPAN, D), bf16)],
        compiler_params=pltpu.CompilerParams(vmem_limit_bytes=MEMORY),
        name="project",
    )(tokens, qkv_weight, out_weight, rel_embed, index_rows, factors, scales)


def unit_matrix(flipped):
    row = lax.broadcasted_iota(jnp.int32, (TILE, TILE), 0)
    col = lax.broadcasted_iota(jnp.int32, (TILE, TILE), 1)
    return jnp.where(row == (TILE - 1 - col if flipped else col), 1.0, 0.0).astype(bf16)


def head_lanes(member):
    lane = lax.broadcasted_iota(jnp.int32, (1, PAIR), 1)
    return jnp.where(lane // DH == member, 1.0, 0.0).astype(bf16)


def each_head(rows):
    return jnp.concatenate([rows * head_lanes(0), rows * head_lanes(1)], axis=0)


def own_lanes(stacked):
    lane = lax.broadcasted_iota(jnp.int32, (TILE, PAIR), 1)
    return jnp.where(lane < DH, stacked[:TILE], stacked[TILE:])


def lane_and_row():
    lane = lax.broadcasted_iota(jnp.int32, (8, 128), 1)
    return lane, lax.broadcasted_iota(jnp.int32, (8, 128), 0)


def turn(block, shift):
    return pltpu.roll(block, shift % 128, 1, stride=1, stride_axis=0)


def skew(table, length):
    lane, row = lane_and_row()
    count = length // 128
    done = []
    for at in range(0, TILE, 8):
        blocks = [table[at : at + 8, 128 * c : 128 * c + 128] for c in range(count + 1)]
        blocks[0] = jnp.where(lane + row >= 127 - at, blocks[0], blocks[count])
        moved = [turn(block, at + 1) for block in blocks[:count]]
        if count > 1:
            inside = lane - row <= at
            moved = [
                jnp.where(inside, moved[c], moved[(c + 1) % count]) for c in range(count)
            ]
        done.append(jnp.concatenate(moved, axis=1))
    return jnp.concatenate(done, axis=0)


def unskew(scores, length):
    lane, row = lane_and_row()
    zero = jnp.zeros((8, 128), f32)
    done = []
    for at in range(0, TILE, 8):
        moved = [
            turn(scores[at : at + 8, 128 * c : 128 * c + 128], at) for c in range(length // 128)
        ]
        before = lane - row < at
        done.append(
            jnp.concatenate(
                [jnp.where(before, x, y) for x, y in zip([zero] + moved, moved + [zero])], axis=1
            )
        )
    return jnp.concatenate(done, axis=0)


def forward_kernel(
    lengths_ref,
    counts_ref,
    q_ref,
    k_ref,
    v_ref,
    ek_ref,
    eq_ref,
    context_ref,
    p1_ref,
    p2_ref,
    p3_ref,
    shift_scr,
):
    eye = unit_matrix(False)
    anti = unit_matrix(True)
    factor = (3.0 * DH) ** -0.5
    counts = live_counts(lengths_ref, counts_ref)
    for slot, (start, length) in enumerate(SLOTS):
        keys = k_ref[start : start + length, :]
        values = v_ref[start : start + length, :]
        live = lax.broadcasted_iota(jnp.int32, (1, length), 1) < counts[slot]
        for t in range(length // TILE):
            low = LEN3 - TILE - TILE * t
            here = keys[t * TILE : (t + 1) * TILE]
            table = dot_nn(each_head(here), eq_ref[:, low : low + length + TILE])
            for member in range(2):
                shift_scr[member, start + t * TILE : start + (t + 1) * TILE, :length] = skew(
                    table[member * TILE : (member + 1) * TILE], length
                ).astype(bf16)
        for t in range(length // TILE):
            low = LEN3 - TILE - TILE * t
            row = start + t * TILE
            queries = each_head(q_ref[row : row + TILE, :])
            table = dot_nn(queries, ek_ref[:, low : low + length + TILE])
            probs = []
            for member in range(2):
                mine = slice(member * TILE, (member + 1) * TILE)
                left = jnp.concatenate([queries[mine], eye], axis=1)
                shifted = shift_scr[
                    member, start : start + length, t * TILE : (t + 1) * TILE
                ]
                right = jnp.concatenate([keys, shifted], axis=1)
                scores = dot_nt(left, right) + skew(table[mine], length)
                scores = jnp.where(live, scores * factor, masked_score)
                weights = jnp.exp(scores - jnp.max(scores, axis=1, keepdims=True))
                prob = weights * (1.0 / jnp.sum(weights, axis=1, keepdims=True))
                probs.append(prob.astype(bf16))
            context = dot_nn(jnp.concatenate(probs, axis=0), values)
            context_ref[row : row + TILE, :] = own_lanes(context).astype(bf16)
            for member in range(2):
                turned = dot_nn(anti, probs[member]).astype(bf16)
                if length == LEN1:
                    p1_ref[member, row : row + TILE, :] = turned
                elif length == LEN3:
                    p3_ref[member, t * TILE : (t + 1) * TILE, :] = turned
                else:
                    p2_ref[member, t * TILE : (t + 1) * TILE, :] = turned


PAIR_SPEC = pl.BlockSpec((ROWS, PAIR), lambda p: (0, p))
TABLE_SPEC = pl.BlockSpec((PAIR, OFFSETS), lambda p: (p, 0))
PROB_SIZES = ((256, 128), (256, 256), (512, 512))
PROB_SPECS = [pl.BlockSpec((2, *size), lambda p: (p, 0, 0)) for size in PROB_SIZES]


def attend_forward(lengths, counts, q, k, v, ek, eq):
    return pl.pallas_call(
        forward_kernel,
        grid=(H // 2,),
        in_specs=[pl.BlockSpec(memory_space=pltpu.SMEM)] * 2
        + [PAIR_SPEC] * 3
        + [TABLE_SPEC] * 2,
        out_specs=[PAIR_SPEC] + PROB_SPECS,
        out_shape=[jax.ShapeDtypeStruct((ROWS, D), bf16)]
        + [jax.ShapeDtypeStruct((H, *size), bf16) for size in PROB_SIZES],
        scratch_shapes=[pltpu.VMEM((2, ROWS, LEN3), bf16)],
        compiler_params=pltpu.CompilerParams(vmem_limit_bytes=MEMORY),
        name="attention_forward",
    )(lengths, counts, q, k, v, ek, eq)


def backward_kernel(
    q_ref,
    k_ref,
    v_ref,
    g_ref,
    ek_ref,
    fq_ref,
    p1_ref,
    p2_ref,
    p3_ref,
    gq_ref,
    gk_ref,
    gv_ref,
    gek_ref,
    gfq_ref,
    grad_scr,
    turned_scr,
    values_scr,
):
    eye = unit_matrix(False)
    anti = unit_matrix(True)
    factor = (3.0 * DH) ** -0.5
    gek_ref[...] = jnp.zeros_like(gek_ref)
    gfq_ref[...] = jnp.zeros_like(gfq_ref)
    for start, length in SLOTS:
        count = length // TILE
        keys = k_ref[start : start + length, :]
        values = v_ref[start : start + length, :]
        value_grad = jnp.zeros((PAIR, length), f32)
        for t in range(count):
            low = LEN3 - TILE - TILE * t
            row = start + t * TILE
            place = start + (count - 1 - t) * TILE
            both = jnp.concatenate([q_ref[row : row + TILE, :], g_ref[row : row + TILE, :]], axis=1)
            both = dot_nn(anti, both).astype(bf16)
            turned_scr[place : place + TILE, :] = both[:, :PAIR]
            queries = each_head(both[:, :PAIR])
            grads = each_head(both[:, PAIR:])
            grad_prob = dot_nt(grads, values)
            probs, raws, spreads = [], [], []
            for member in range(2):
                if length == LEN1:
                    prob = p1_ref[member, row : row + TILE, :]
                elif length == LEN3:
                    prob = p3_ref[member, t * TILE : (t + 1) * TILE, :]
                else:
                    prob = p2_ref[member, t * TILE : (t + 1) * TILE, :]
                mine = grad_prob[member * TILE : (member + 1) * TILE]
                wide = prob.astype(f32)
                delta = jnp.sum(wide * mine, axis=1, keepdims=True)
                raw = (wide * ((mine - delta) * factor)).astype(bf16)
                grad_scr[member, place : place + TILE, :length] = raw
                probs.append(prob)
                raws.append(raw)
                spreads.append(unskew(raw.astype(f32), length).astype(bf16))
            raw = jnp.concatenate(raws, axis=0)
            spread = jnp.concatenate(spreads, axis=0)
            query_grad = own_lanes(
                dot_nn(
                    jnp.concatenate([raw, spread], axis=1),
                    jnp.concatenate([keys, ek_ref[low : low + length + TILE, :]], axis=0),
                )
            )
            gq_ref[row : row + TILE, :] = dot_nn(anti, query_grad.astype(bf16)).astype(bf16)
            gek_ref[:, low : low + length + TILE] += dot_tn(queries, spread)
            value_grad = value_grad + dot_tn(grads, jnp.concatenate(probs, axis=0))
        values_scr[:, start : start + length] = value_grad
        turned = turned_scr[start : start + length, :]
        for t in range(count):
            low = LEN3 - length + TILE * t
            row = start + t * TILE
            raws, spreads = [], []
            for member in range(2):
                raw = dot_nt(
                    eye, grad_scr[member, start : start + length, t * TILE : (t + 1) * TILE]
                )
                raws.append(raw.astype(bf16))
                spreads.append(unskew(raw, length).astype(bf16))
            raw = jnp.concatenate(raws, axis=0)
            spread = jnp.concatenate(spreads, axis=0)
            key_grad = own_lanes(
                dot_nn(
                    jnp.concatenate([raw, spread], axis=1),
                    jnp.concatenate([turned, fq_ref[low : low + length + TILE, :]], axis=0),
                )
            )
            gk_ref[row : row + TILE, :] = key_grad.astype(bf16)
            gfq_ref[:, low : low + length + TILE] += dot_tn(
                each_head(k_ref[row : row + TILE, :]), spread
            )
    gv_ref[...] = values_scr[...].T.astype(bf16)


def attend_backward(q, k, v, g, ek, fq, p1, p2, p3):
    return pl.pallas_call(
        backward_kernel,
        grid=(H // 2,),
        in_specs=[PAIR_SPEC] * 6 + PROB_SPECS,
        out_specs=[PAIR_SPEC] * 3 + [TABLE_SPEC] * 2,
        out_shape=[jax.ShapeDtypeStruct((ROWS, D), bf16)] * 3
        + [jax.ShapeDtypeStruct((D, OFFSETS), f32)] * 2,
        scratch_shapes=[
            pltpu.VMEM((2, ROWS, LEN3), bf16),
            pltpu.VMEM((ROWS, PAIR), bf16),
            pltpu.VMEM((PAIR, ROWS), f32),
        ],
        compiler_params=pltpu.CompilerParams(vmem_limit_bytes=MEMORY),
        name="attention_backward",
    )(q, k, v, g, ek, fq, p1, p2, p3)


def gelu_pair(hidden):
    z = jnp.abs(hidden) * 0.7071067811865476
    t = 1.0 / (1.0 + 0.3275911 * z)
    poly = t * (
        0.127414796
        + t * (-0.142248368 + t * (0.7107068705 + t * (-0.7265760135 + t * 0.5307027145)))
    )
    bell = jnp.exp(-z * z)
    tail = poly * bell
    below = jnp.where(hidden >= 0, 1.0 - tail, tail)
    return hidden * below, below + hidden * (bell * 0.3989422804014327)


def norm_forward(values, gain, shift):
    centered = values - jnp.mean(values, axis=1, keepdims=True)
    inverse = lax.rsqrt(jnp.mean(centered * centered, axis=1, keepdims=True) + norm_epsilon)
    normal = centered * inverse
    return (normal * gain + shift, normal, inverse)


def norm_backward(grad_out, normal, inverse, gain):
    scaled = grad_out * gain
    return inverse * (
        scaled
        - jnp.mean(scaled, axis=1, keepdims=True)
        - normal * jnp.mean(scaled * normal, axis=1, keepdims=True)
    )


def middle_kernel(
    lengths_ref,
    counts_ref,
    tokens_ref,
    context_ref,
    out_grad_ref,
    weight_ref,
    packed_ref,
    factor_ref,
    scale_ref,
    norm_ref,
    mixed_ref,
    grad_one_ref,
    context_grad_ref,
    small_ref,
    hidden_ref,
    scale_grad_ref,
    active_scr,
    slope_scr,
):
    step = pl.program_id(0)
    chunks = packed_ref.shape[0]

    @pl.when(step == 0)
    def _():
        small_ref[...] = jnp.zeros_like(small_ref)
        hidden_ref[...] = jnp.zeros_like(hidden_ref)
        scale_grad_ref[...] = jnp.zeros_like(scale_grad_ref)

    row = lax.broadcasted_iota(jnp.int32, (BLOCK, 1), 0) + step * BLOCK
    live = jnp.zeros((BLOCK, 1), f32)
    for (start, length), used in zip(SLOTS, live_counts(lengths_ref, counts_ref)):
        live = jnp.where((row >= start) & (row < start + used), 1.0, live)
    gain_one, shift_one, gain_two, shift_two = (norm_ref[i : i + 1, :] for i in range(4))

    context = context_ref[...]
    weight = weight_ref[0]
    attended = dot_nn(context, weight)
    normed, normal_one, inverse_one = norm_forward(
        tokens_ref[...].astype(f32) + attended, gain_one, shift_one
    )
    normed_low = normed.astype(bf16)
    mlp = jnp.zeros((BLOCK, D), f32)
    back_coeff = jnp.zeros((PAD, BLOCK), f32)
    for c in range(chunks):
        hidden = dot_nn(normed_low, packed_ref[c, :D, :])
        active, slope = gelu_pair(hidden)
        active = active.astype(bf16)
        active_scr[c] = active
        slope_scr[c] = slope
        mlp = mlp + dot_nn(active, packed_ref[c, D : 2 * D, :])
        back_coeff = back_coeff + dot_nt(packed_ref[c, 2 * D + PAD :, :], active)
    result, normal_two, inverse_two = norm_forward(normed + mlp, gain_two, shift_two)
    mixed_ref[...] = (result * live).astype(bf16)
    grad_two = norm_backward(
        out_grad_ref[...].astype(f32) * live, normal_two, inverse_two, gain_two
    )
    grad_mlp = grad_two.astype(bf16)

    back_slope = dot_nt(factor_ref[9], grad_mlp)
    small_ref[3] += add_parts(dot_nn(two_parts(back_coeff * scale_ref[:, 5:6]), grad_mlp))
    scale_grad_ref[:, 5:6] += jnp.sum(back_coeff * back_slope, axis=1, keepdims=True)
    back_through = two_parts(back_slope * scale_ref[:, 5:6])
    in_coeff = dot_nt(factor_ref[4], normed_low)
    in_scaled = two_parts(in_coeff * scale_ref[:, 4:5])
    in_slope = jnp.zeros((PAD, BLOCK), f32)
    grad_normed = grad_two
    for c in range(chunks):
        grad_active = dot_nt(grad_mlp, packed_ref[c, D : 2 * D, :])
        grad_hidden = (grad_active * slope_scr[c]).astype(bf16)
        grad_normed = grad_normed + dot_nt(grad_hidden, packed_ref[c, :D, :])
        in_slope = in_slope + dot_nt(packed_ref[c, 2 * D : 2 * D + PAD, :], grad_hidden)
        hidden_ref[c] += add_parts(dot_nn(in_scaled, grad_hidden))
        hidden_ref[chunks + c] += add_parts(dot_nn(back_through, active_scr[c]))
    scale_grad_ref[:, 4:5] += jnp.sum(in_coeff * in_slope, axis=1, keepdims=True)
    small_ref[2] += add_parts(dot_nn(two_parts(in_slope * scale_ref[:, 4:5]), normed_low))

    grad_one = norm_backward(grad_normed, normal_one, inverse_one, gain_one)
    grad_one_ref[...] = grad_one
    grad_attended = grad_one.astype(bf16)
    context_grad_ref[...] = dot_nt(grad_attended, weight).astype(bf16)
    out_coeff = dot_nt(factor_ref[3], context)
    out_slope = dot_nt(factor_ref[8], grad_attended)
    small_ref[1] += add_parts(dot_nn(two_parts(out_coeff * scale_ref[:, 3:4]), grad_attended))
    small_ref[0] += add_parts(dot_nn(two_parts(out_slope * scale_ref[:, 3:4]), context))
    scale_grad_ref[:, 3:4] += jnp.sum(out_coeff * out_slope, axis=1, keepdims=True)


def middle(lengths, counts, tokens, context, out_grad, weights, packed, factors, scales, norms):
    chunks = packed.shape[0]
    tile = pl.BlockSpec((BLOCK, D), lambda i: (i, 0))
    return pl.pallas_call(
        middle_kernel,
        grid=(ROWS // BLOCK,),
        in_specs=[pl.BlockSpec(memory_space=pltpu.SMEM)] * 2
        + [tile] * 3
        + [
            pl.BlockSpec((1, D, D), lambda i: (3, 0, 0)),
            pl.BlockSpec(
                (chunks, PACKED, D), lambda i: (0, 0, 0), pipeline_mode=pl.Buffered(1)
            ),
            whole(12, PAD, D),
            whole(PAD, 128),
            whole(4, D),
        ],
        out_specs=[tile] * 3
        + [whole(4, PAD, D), whole(2 * chunks, PAD, D), whole(PAD, 128)],
        out_shape=[
            jax.ShapeDtypeStruct((ROWS, D), bf16),
            jax.ShapeDtypeStruct((ROWS, D), f32),
            jax.ShapeDtypeStruct((ROWS, D), bf16),
            jax.ShapeDtypeStruct((4, PAD, D), f32),
            jax.ShapeDtypeStruct((2 * chunks, PAD, D), f32),
            jax.ShapeDtypeStruct((PAD, 128), f32),
        ],
        scratch_shapes=[
            pltpu.VMEM((chunks, BLOCK, D), bf16),
            pltpu.VMEM((chunks, BLOCK, D), f32),
        ],
        compiler_params=pltpu.CompilerParams(vmem_limit_bytes=MEMORY),
        name="middle",
    )(lengths, counts, tokens, context, out_grad, weights, packed, factors, scales, norms)


def last_kernel(
    tokens_ref,
    gq_ref,
    gk_ref,
    gv_ref,
    grad_one_ref,
    coeff_ref,
    merged_ref,
    rel_ref,
    index_ref,
    rel_coeff_ref,
    gek_ref,
    gfq_ref,
    factor_ref,
    scale_ref,
    in_grad_ref,
    down_ref,
    up_ref,
    scale_grad_ref,
):
    step = pl.program_id(0)

    @pl.when(step == 0)
    def _():
        rel = rel_ref[...]
        scale_grad_ref[...] = jnp.zeros_like(scale_grad_ref)
        down_ref[2] = jnp.zeros((PAD, D), f32)
        up_ref[2] = jnp.zeros((PAD, D), f32)
        bucket = lax.broadcasted_iota(jnp.int32, (2 * SPAN, OFFSETS), 0)
        for member, ref, row in ((0, gfq_ref, 1), (1, gek_ref, 0)):
            scale = scale_ref[:, member : member + 1]
            chosen = jnp.where(bucket == index_ref[row : row + 1, :], 1.0, 0.0).astype(bf16)
            grad = dot_nt(ref[...].astype(bf16), chosen).astype(bf16)
            coeff = rel_coeff_ref[member]
            slope = dot_nn(factor_ref[5 + member], grad)
            up_ref[member] = add_parts(dot_nt(two_parts(coeff * scale), grad))
            down_ref[member] = add_parts(dot_nn(two_parts(slope * scale), rel))
            scale_grad_ref[:, member : member + 1] += jnp.sum(
                coeff * slope, axis=1, keepdims=True
            )

    tokens = tokens_ref[...]
    in_grad = grad_one_ref[...]
    for member, ref in enumerate((gq_ref, gk_ref, gv_ref)):
        grad = ref[...]
        scale = scale_ref[:, member : member + 1]
        in_grad = in_grad + dot_nt(grad, merged_ref[member])
        coeff = coeff_ref[member]
        slope = dot_nt(factor_ref[5 + member], grad)
        up_ref[member] += add_parts(dot_nn(two_parts(coeff * scale), grad))
        down_ref[member] += add_parts(dot_nn(two_parts(slope * scale), tokens))
        scale_grad_ref[:, member : member + 1] += jnp.sum(coeff * slope, axis=1, keepdims=True)
    in_grad_ref[...] = in_grad


def last(tokens, gq, gk, gv, grad_one, coeff, weights, rel, index, rel_coeff, gek, gfq, factors, scales):
    tile = pl.BlockSpec((BLOCK, D), lambda i: (i, 0))
    return pl.pallas_call(
        last_kernel,
        grid=(ROWS // BLOCK,),
        in_specs=[tile] * 5
        + [
            pl.BlockSpec((3, PAD, BLOCK), lambda i: (0, 0, i)),
            whole(3, D, D),
            whole(2 * SPAN, D),
            whole(2, OFFSETS),
            whole(2, PAD, 2 * SPAN),
            whole(D, OFFSETS),
            whole(D, OFFSETS),
            whole(12, PAD, D),
            whole(PAD, 128),
        ],
        out_specs=[tile, whole(3, PAD, D), whole(3, PAD, D), whole(PAD, 128)],
        out_shape=[
            jax.ShapeDtypeStruct((ROWS, D), f32),
            jax.ShapeDtypeStruct((3, PAD, D), f32),
            jax.ShapeDtypeStruct((3, PAD, D), f32),
            jax.ShapeDtypeStruct((PAD, 128), f32),
        ],
        compiler_params=pltpu.CompilerParams(vmem_limit_bytes=MEMORY),
        name="last",
    )(tokens, gq, gk, gv, grad_one, coeff, weights, rel, index, rel_coeff, gek, gfq, factors, scales)


def devices():
    return lax.axis_size("dp") * lax.axis_size("tensor")


def share_kernel(
    down_ref,
    up_ref,
    last_ref,
    middle_ref,
    early_ref,
    down_out,
    up_out,
    scale_out,
    stage_scr,
    mine_scr,
    land_scr,
    all_scr,
    send_sem,
    land_sem,
    spread_sem,
    all_sem,
):
    count = devices()
    inner = lax.axis_size("tensor")
    me = lax.axis_index("dp") * inner + lax.axis_index("tensor")

    def partner(off):
        other = lax.rem(me + off, count)
        return other, (other // inner, lax.rem(other, inner))

    barrier = pltpu.get_barrier_semaphore()

    @pl.loop(1, count)
    def _(off):
        pl.semaphore_signal(
            barrier, inc=1, device_id=partner(off)[1], device_id_type=pl.DeviceIdType.MESH
        )

    stage_scr[...] = jnp.zeros_like(stage_scr)
    for number in range(6):
        ref = down_ref if number < 3 else up_ref
        for block in range(D // 128):
            at = (number * (D // 128) + block) * RANK
            stage_scr[at : at + RANK, :] = ref[number % 3, :RANK, block * 128 : block * 128 + 128]
    at = 6 * (D // 128) * RANK
    stage_scr[at : at + PAD, :] = last_ref[...] + middle_ref[...]
    mine_scr[...] = stage_scr[...].astype(bf16).reshape(count, PAD, 128)
    pl.semaphore_wait(barrier, count - 1)

    def first(off):
        other, where = partner(off)
        return pltpu.make_async_remote_copy(
            src_ref=mine_scr.at[other],
            dst_ref=land_scr.at[off],
            send_sem=send_sem.at[off],
            recv_sem=land_sem.at[off],
            device_id=where,
            device_id_type=pl.DeviceIdType.MESH,
        )

    def second(off):
        other, where = partner(off)
        return pltpu.make_async_remote_copy(
            src_ref=all_scr.at[me],
            dst_ref=all_scr.at[me],
            send_sem=spread_sem.at[off],
            recv_sem=all_sem.at[off],
            device_id=where,
            device_id_type=pl.DeviceIdType.MESH,
        )

    def second_arrival(off):
        origin = lax.rem(me + count - off, count)
        return pltpu.make_async_remote_copy(
            src_ref=all_scr.at[origin],
            dst_ref=all_scr.at[origin],
            send_sem=spread_sem.at[off],
            recv_sem=all_sem.at[off],
            device_id=partner(off)[1],
            device_id_type=pl.DeviceIdType.MESH,
        )

    @pl.loop(1, count)
    def _(off):
        first(off).start()

    land_scr[0] = mine_scr[me]

    @pl.loop(1, count)
    def _(off):
        first(off).wait_recv()

    all_scr[me] = jnp.sum(land_scr[...].astype(f32), axis=0).astype(bf16)

    @pl.loop(1, count)
    def _(off):
        second(off).start()

    for index, place in ((0, 3), (2, 4)):
        down_out[place] = early_ref[index]
        up_out[place] = early_ref[index + 1]

    @pl.loop(1, count)
    def _(off):
        second_arrival(off).wait_recv()

    stage_scr[...] = all_scr[...].astype(f32).reshape(count * PAD, 128)
    for number in range(6):
        ref = down_out if number < 3 else up_out
        for block in range(D // 128):
            at = (number * (D // 128) + block) * RANK
            ref[number % 3, :, block * 128 : block * 128 + 128] = stage_scr[at : at + RANK, :]
    at = 6 * (D // 128) * RANK
    scale_out[...] = stage_scr[at : at + PAD, :].T[:6, :RANK]

    @pl.loop(1, count)
    def _(off):
        first(off).wait_send()
        second(off).wait_send()


def share(down, up, last_scale, middle_scale, early):
    count = devices()
    factor = jax.ShapeDtypeStruct((5, RANK, D), f32)
    return pl.pallas_call(
        share_kernel,
        in_specs=[pl.BlockSpec(memory_space=pltpu.VMEM)] * 5,
        out_specs=[pl.BlockSpec(memory_space=pltpu.VMEM)] * 3,
        out_shape=[factor, factor, jax.ShapeDtypeStruct((6, RANK), f32)],
        scratch_shapes=[
            pltpu.VMEM((count * PAD, 128), f32),
            pltpu.VMEM((count, PAD, 128), bf16),
            pltpu.VMEM((count, PAD, 128), bf16),
            pltpu.VMEM((count, PAD, 128), bf16),
        ]
        + [pltpu.SemaphoreType.DMA((count,))] * 4,
        compiler_params=pltpu.CompilerParams(
            collective_id=0, has_side_effects=True, vmem_limit_bytes=MEMORY
        ),
        name="share",
    )(down, up, last_scale, middle_scale, early)


def on_device(
    tokens,
    qkv_weight,
    out_weight,
    in_weight,
    back_weight,
    rel_embed,
    gain_one,
    shift_one,
    gain_two,
    shift_two,
    adapt_down,
    adapt_up,
    hidden_up,
    hidden_down,
    adapt_scale,
    seq_lengths,
    seq_counts,
    rel_bucket,
    out_grad,
):
    factors = jnp.pad(
        jnp.concatenate([adapt_down, adapt_up, hidden_up[None], hidden_down[None]], axis=0),
        ((0, 0), (0, PAD - RANK), (0, 0)),
    )
    scales = jnp.pad(adapt_scale.T, ((0, PAD - RANK), (0, 128 - 6)))
    index_rows = jnp.pad(
        jnp.stack([rel_bucket[::-1], rel_bucket]), ((0, 0), (0, 1)), constant_values=-1
    )
    norms = jnp.stack([gain_one, shift_one, gain_two, shift_two])
    packed = lax.all_gather(
        pack_weights(in_weight, back_weight, factors, scales), "tensor", axis=0
    )
    q, k, v, ek, fq, ekt, eqt, weights, coeff, rel_coeff = project(
        tokens, qkv_weight, out_weight, rel_embed, index_rows, factors, scales
    )
    context, p1, p2, p3 = attend_forward(seq_lengths, seq_counts, q, k, v, ekt, eqt)
    mixed, grad_one, context_grad, small, hidden, middle_scale = middle(
        seq_lengths, seq_counts, tokens, context, out_grad, weights, packed, factors, scales, norms
    )
    chunks = packed.shape[0]
    small, hidden = lax.psum(
        (small[:, :RANK], hidden[:, :RANK].reshape(2, chunks, RANK, D)), ("dp", "tensor")
    )
    hidden = hidden[:, lax.axis_index("tensor")]
    gq, gk, gv, gek, gfq = attend_backward(q, k, v, context_grad, ek, fq, p1, p2, p3)
    in_grad, down, up, last_scale = last(
        tokens, gq, gk, gv, grad_one, coeff, weights, rel_embed, index_rows, rel_coeff, gek, gfq, factors, scales
    )
    down_grad, up_grad, scale_grad = share(down, up, last_scale, middle_scale, small)
    return (mixed, in_grad, down_grad, up_grad, hidden[0], hidden[1], scale_grad)


def solution(mesh):
    rows = P(("dp", "tensor"), None)
    return jax.shard_map(
        on_device,
        mesh=mesh,
        in_specs=(
            rows,
            P(),
            P(),
            P(None, "tensor"),
            P("tensor", None),
            P(),
            P(),
            P(),
            P(),
            P(),
            P(),
            P(),
            P(None, "tensor"),
            P(None, "tensor"),
            P(),
            rows,
            rows,
            P(),
            rows,
        ),
        out_specs=(rows, rows, P(), P(), P(None, "tensor"), P(None, "tensor"), P()),
        check_vma=False,
    )
```

```python
import jax
import jax.numpy as jnp
from jax import lax
from jax.experimental import pallas as pl
from jax.experimental.pallas import tpu as pltpu
from jax.sharding import PartitionSpec as P

D = 768
H = 12
DH = 64
PAIR = 2 * DH
SPAN = 256
RANK = 12
PAD = 16
ROWS = 1024
LEN1 = 128
LEN3 = 512
OFFSETS = 2 * LEN3
TILE = 128
BLOCK = 256
SLOTS = ((0, 128), (128, 128), (256, 256), (512, 512))
PACKED = 2 * D + 2 * PAD
norm_epsilon = 1e-07
masked_score = -1e30
bf16 = jnp.bfloat16
f32 = jnp.float32
MEMORY = 60 * 1024 * 1024


def dot_nn(a, b):
    return jnp.dot(a, b, preferred_element_type=f32)


def dot_nt(a, b):
    return lax.dot_general(a, b, (((1,), (1,)), ((), ())), preferred_element_type=f32)


def dot_tn(a, b):
    return lax.dot_general(a, b, (((0,), (0,)), ((), ())), preferred_element_type=f32)


def two_parts(wide):
    high = wide.astype(bf16)
    rest = (wide - high.astype(f32)).astype(bf16)
    return jnp.concatenate([high, rest], axis=0)


def add_parts(stacked):
    return stacked[:PAD] + stacked[PAD:]


def merged(weight, down, up, scale):
    twice = jnp.concatenate([up, up], axis=0)
    extra = dot_tn(two_parts(down.astype(f32) * scale), twice)
    return (weight.astype(f32) + extra).astype(bf16)


def live_counts(lengths_ref, counts_ref):
    ranks = ((0, 0), (0, 1), (1, 0), (2, 0))
    return [
        jnp.where(rank < counts_ref[0, bucket], lengths_ref[0, slot], 0)
        for slot, (bucket, rank) in enumerate(ranks)
    ]


def pack_kernel(in_ref, back_ref, factor_ref, scale_ref, packed_ref):
    packed_ref[:D] = merged(in_ref[...], factor_ref[4], factor_ref[10], scale_ref[:, 4:5])
    packed_ref[D : 2 * D] = merged(back_ref[...], factor_ref[11], factor_ref[9], scale_ref[:, 5:6])
    packed_ref[2 * D : 2 * D + PAD] = factor_ref[10]
    packed_ref[2 * D + PAD :] = factor_ref[11]


def pack_weights(in_weight, back_weight, factors, scales):
    return pl.pallas_call(
        pack_kernel,
        out_shape=jax.ShapeDtypeStruct((PACKED, D), bf16),
        compiler_params=pltpu.CompilerParams(vmem_limit_bytes=MEMORY),
        name="pack_weights",
    )(in_weight, back_weight, factors, scales)


def project_kernel(
    tokens_ref,
    qkv_ref,
    out_ref,
    rel_ref,
    index_ref,
    factor_ref,
    scale_ref,
    q_ref,
    k_ref,
    v_ref,
    ek_ref,
    fq_ref,
    ekt_ref,
    eqt_ref,
    merged_ref,
    coeff_ref,
    rel_coeff_ref,
    pos_scr,
):
    step = pl.program_id(0)

    @pl.when(step == 0)
    def _():
        for member in range(3):
            merged_ref[member] = merged(
                qkv_ref[member],
                factor_ref[member],
                factor_ref[5 + member],
                scale_ref[:, member : member + 1],
            )
        merged_ref[3] = merged(out_ref[...], factor_ref[3], factor_ref[8], scale_ref[:, 3:4])
        rel = rel_ref[...]
        for member in range(2):
            pos_scr[member] = dot_nn(rel, merged_ref[member]).astype(bf16)
            rel_coeff_ref[member] = dot_nt(factor_ref[member], rel)

    tokens = tokens_ref[...]
    for member, ref in enumerate((q_ref, k_ref, v_ref)):
        ref[...] = dot_nn(tokens, merged_ref[member]).astype(bf16)
        coeff_ref[member] = dot_nt(factor_ref[member], tokens)
    bucket = lax.broadcasted_iota(jnp.int32, (2 * SPAN, BLOCK), 0)
    back, forth = (
        jnp.where(bucket == index_ref[row : row + 1, :], 1.0, 0.0).astype(bf16) for row in range(2)
    )
    ek_ref[...] = dot_tn(back, pos_scr[1]).astype(bf16)
    fq_ref[...] = dot_tn(forth, pos_scr[0]).astype(bf16)
    ekt_ref[...] = dot_tn(pos_scr[1], back).astype(bf16)
    eqt_ref[...] = dot_tn(pos_scr[0], back).astype(bf16)


def whole(*shape):
    return pl.BlockSpec(shape, lambda *at: (0,) * len(shape))


def project(tokens, qkv_weight, out_weight, rel_embed, index_rows, factors, scales):
    tile = pl.BlockSpec((BLOCK, D), lambda i: (i, 0))
    rows = jax.ShapeDtypeStruct((ROWS, D), bf16)
    return pl.pallas_call(
        project_kernel,
        grid=(ROWS // BLOCK,),
        in_specs=[
            tile,
            whole(3, D, D),
            whole(D, D),
            whole(2 * SPAN, D),
            pl.BlockSpec((2, BLOCK), lambda i: (0, i)),
            whole(12, PAD, D),
            whole(PAD, 128),
        ],
        out_specs=[tile] * 5
        + [pl.BlockSpec((D, BLOCK), lambda i: (0, i))] * 2
        + [
            whole(4, D, D),
            pl.BlockSpec((3, PAD, BLOCK), lambda i: (0, 0, i)),
            whole(2, PAD, 2 * SPAN),
        ],
        out_shape=[rows] * 5
        + [jax.ShapeDtypeStruct((D, OFFSETS), bf16)] * 2
        + [
            jax.ShapeDtypeStruct((4, D, D), bf16),
            jax.ShapeDtypeStruct((3, PAD, ROWS), f32),
            jax.ShapeDtypeStruct((2, PAD, 2 * SPAN), f32),
        ],
        scratch_shapes=[pltpu.VMEM((2, 2 * SPAN, D), bf16)],
        compiler_params=pltpu.CompilerParams(vmem_limit_bytes=MEMORY),
        name="project",
    )(tokens, qkv_weight, out_weight, rel_embed, index_rows, factors, scales)


def unit_matrix(flipped):
    row = lax.broadcasted_iota(jnp.int32, (TILE, TILE), 0)
    col = lax.broadcasted_iota(jnp.int32, (TILE, TILE), 1)
    return jnp.where(row == (TILE - 1 - col if flipped else col), 1.0, 0.0).astype(bf16)


def head_lanes(member):
    lane = lax.broadcasted_iota(jnp.int32, (1, PAIR), 1)
    return jnp.where(lane // DH == member, 1.0, 0.0).astype(bf16)


def each_head(rows):
    return jnp.concatenate([rows * head_lanes(0), rows * head_lanes(1)], axis=0)


def own_lanes(stacked):
    lane = lax.broadcasted_iota(jnp.int32, (TILE, PAIR), 1)
    return jnp.where(lane < DH, stacked[:TILE], stacked[TILE:])


def lane_and_row():
    lane = lax.broadcasted_iota(jnp.int32, (8, 128), 1)
    return lane, lax.broadcasted_iota(jnp.int32, (8, 128), 0)


def turn(block, shift):
    return pltpu.roll(block, shift % 128, 1, stride=1, stride_axis=0)


def skew(table, length):
    lane, row = lane_and_row()
    count = length // 128
    done = []
    for at in range(0, TILE, 8):
        blocks = [table[at : at + 8, 128 * c : 128 * c + 128] for c in range(count + 1)]
        blocks[0] = jnp.where(lane + row >= 127 - at, blocks[0], blocks[count])
        moved = [turn(block, at + 1) for block in blocks[:count]]
        if count > 1:
            inside = lane - row <= at
            moved = [
                jnp.where(inside, moved[c], moved[(c + 1) % count]) for c in range(count)
            ]
        done.append(jnp.concatenate(moved, axis=1))
    return jnp.concatenate(done, axis=0)


def unskew(scores, length):
    lane, row = lane_and_row()
    zero = jnp.zeros((8, 128), f32)
    done = []
    for at in range(0, TILE, 8):
        moved = [
            turn(scores[at : at + 8, 128 * c : 128 * c + 128], at) for c in range(length // 128)
        ]
        before = lane - row < at
        done.append(
            jnp.concatenate(
                [jnp.where(before, x, y) for x, y in zip([zero] + moved, moved + [zero])], axis=1
            )
        )
    return jnp.concatenate(done, axis=0)


def forward_kernel(
    lengths_ref,
    counts_ref,
    q_ref,
    k_ref,
    v_ref,
    ek_ref,
    eq_ref,
    context_ref,
    p1_ref,
    p2_ref,
    p3_ref,
    shift_scr,
):
    eye = unit_matrix(False)
    anti = unit_matrix(True)
    factor = (3.0 * DH) ** -0.5
    counts = live_counts(lengths_ref, counts_ref)
    for slot, (start, length) in enumerate(SLOTS):
        keys = k_ref[start : start + length, :]
        values = v_ref[start : start + length, :]
        live = lax.broadcasted_iota(jnp.int32, (1, length), 1) < counts[slot]
        for t in range(length // TILE):
            low = LEN3 - TILE - TILE * t
            here = keys[t * TILE : (t + 1) * TILE]
            table = dot_nn(each_head(here), eq_ref[:, low : low + length + TILE])
            for member in range(2):
                shift_scr[member, start + t * TILE : start + (t + 1) * TILE, :length] = skew(
                    table[member * TILE : (member + 1) * TILE], length
                ).astype(bf16)
        for t in range(length // TILE):
            low = LEN3 - TILE - TILE * t
            row = start + t * TILE
            queries = each_head(q_ref[row : row + TILE, :])
            table = dot_nn(queries, ek_ref[:, low : low + length + TILE])
            probs = []
            for member in range(2):
                mine = slice(member * TILE, (member + 1) * TILE)
                left = jnp.concatenate([queries[mine], eye], axis=1)
                shifted = shift_scr[
                    member, start : start + length, t * TILE : (t + 1) * TILE
                ]
                right = jnp.concatenate([keys, shifted], axis=1)
                scores = dot_nt(left, right) + skew(table[mine], length)
                scores = jnp.where(live, scores * factor, masked_score)
                weights = jnp.exp(scores - jnp.max(scores, axis=1, keepdims=True))
                prob = weights * (1.0 / jnp.sum(weights, axis=1, keepdims=True))
                probs.append(prob.astype(bf16))
            context = dot_nn(jnp.concatenate(probs, axis=0), values)
            context_ref[row : row + TILE, :] = own_lanes(context).astype(bf16)
            for member in range(2):
                turned = dot_nn(anti, probs[member]).astype(bf16)
                if length == LEN1:
                    p1_ref[member, row : row + TILE, :] = turned
                elif length == LEN3:
                    p3_ref[member, t * TILE : (t + 1) * TILE, :] = turned
                else:
                    p2_ref[member, t * TILE : (t + 1) * TILE, :] = turned


PAIR_SPEC = pl.BlockSpec((ROWS, PAIR), lambda p: (0, p))
TABLE_SPEC = pl.BlockSpec((PAIR, OFFSETS), lambda p: (p, 0))
PROB_SIZES = ((256, 128), (256, 256), (512, 512))
PROB_SPECS = [pl.BlockSpec((2, *size), lambda p: (p, 0, 0)) for size in PROB_SIZES]


def attend_forward(lengths, counts, q, k, v, ek, eq):
    return pl.pallas_call(
        forward_kernel,
        grid=(H // 2,),
        in_specs=[pl.BlockSpec(memory_space=pltpu.SMEM)] * 2
        + [PAIR_SPEC] * 3
        + [TABLE_SPEC] * 2,
        out_specs=[PAIR_SPEC] + PROB_SPECS,
        out_shape=[jax.ShapeDtypeStruct((ROWS, D), bf16)]
        + [jax.ShapeDtypeStruct((H, *size), bf16) for size in PROB_SIZES],
        scratch_shapes=[pltpu.VMEM((2, ROWS, LEN3), bf16)],
        compiler_params=pltpu.CompilerParams(vmem_limit_bytes=MEMORY),
        name="attention_forward",
    )(lengths, counts, q, k, v, ek, eq)


def backward_kernel(
    q_ref,
    k_ref,
    v_ref,
    g_ref,
    ek_ref,
    fq_ref,
    p1_ref,
    p2_ref,
    p3_ref,
    gq_ref,
    gk_ref,
    gv_ref,
    gek_ref,
    gfq_ref,
    grad_scr,
    turned_scr,
    values_scr,
    gek_scr,
    gfq_scr,
):
    eye = unit_matrix(False)
    anti = unit_matrix(True)
    factor = (3.0 * DH) ** -0.5
    gek_scr[...] = jnp.zeros_like(gek_scr)
    gfq_scr[...] = jnp.zeros_like(gfq_scr)
    for start, length in SLOTS:
        count = length // TILE
        keys = k_ref[start : start + length, :]
        values = v_ref[start : start + length, :]
        value_grad = jnp.zeros((PAIR, length), f32)
        for t in range(count):
            low = LEN3 - TILE - TILE * t
            row = start + t * TILE
            place = start + (count - 1 - t) * TILE
            both = jnp.concatenate([q_ref[row : row + TILE, :], g_ref[row : row + TILE, :]], axis=1)
            both = dot_nn(anti, both).astype(bf16)
            turned_scr[place : place + TILE, :] = both[:, :PAIR]
            queries = each_head(both[:, :PAIR])
            grads = each_head(both[:, PAIR:])
            grad_prob = dot_nt(grads, values)
            probs, raws, spreads = [], [], []
            for member in range(2):
                if length == LEN1:
                    prob = p1_ref[member, row : row + TILE, :]
                elif length == LEN3:
                    prob = p3_ref[member, t * TILE : (t + 1) * TILE, :]
                else:
                    prob = p2_ref[member, t * TILE : (t + 1) * TILE, :]
                mine = grad_prob[member * TILE : (member + 1) * TILE]
                wide = prob.astype(f32)
                delta = jnp.sum(wide * mine, axis=1, keepdims=True)
                raw = (wide * ((mine - delta) * factor)).astype(bf16)
                grad_scr[member, place : place + TILE, :length] = raw
                probs.append(prob)
                raws.append(raw)
                spreads.append(unskew(raw.astype(f32), length).astype(bf16))
            raw = jnp.concatenate(raws, axis=0)
            spread = jnp.concatenate(spreads, axis=0)
            query_grad = own_lanes(
                dot_nn(
                    jnp.concatenate([raw, spread], axis=1),
                    jnp.concatenate([keys, ek_ref[low : low + length + TILE, :]], axis=0),
                )
            )
            gq_ref[row : row + TILE, :] = dot_nn(anti, query_grad.astype(bf16)).astype(bf16)
            gek_scr[:, low : low + length + TILE] += dot_tn(queries, spread)
            value_grad = value_grad + dot_tn(grads, jnp.concatenate(probs, axis=0))
        values_scr[:, start : start + length] = value_grad
        turned = turned_scr[start : start + length, :]
        for t in range(count):
            low = LEN3 - length + TILE * t
            row = start + t * TILE
            raws, spreads = [], []
            for member in range(2):
                raw = dot_nt(
                    eye, grad_scr[member, start : start + length, t * TILE : (t + 1) * TILE]
                )
                raws.append(raw.astype(bf16))
                spreads.append(unskew(raw, length).astype(bf16))
            raw = jnp.concatenate(raws, axis=0)
            spread = jnp.concatenate(spreads, axis=0)
            key_grad = own_lanes(
                dot_nn(
                    jnp.concatenate([raw, spread], axis=1),
                    jnp.concatenate([turned, fq_ref[low : low + length + TILE, :]], axis=0),
                )
            )
            gk_ref[row : row + TILE, :] = key_grad.astype(bf16)
            gfq_scr[:, low : low + length + TILE] += dot_tn(
                each_head(k_ref[row : row + TILE, :]), spread
            )
    gv_ref[...] = values_scr[...].T.astype(bf16)
    gek_ref[...] = gek_scr[...].astype(bf16)
    gfq_ref[...] = gfq_scr[...].astype(bf16)


def attend_backward(q, k, v, g, ek, fq, p1, p2, p3):
    return pl.pallas_call(
        backward_kernel,
        grid=(H // 2,),
        in_specs=[PAIR_SPEC] * 6 + PROB_SPECS,
        out_specs=[PAIR_SPEC] * 3 + [TABLE_SPEC] * 2,
        out_shape=[jax.ShapeDtypeStruct((ROWS, D), bf16)] * 3
        + [jax.ShapeDtypeStruct((D, OFFSETS), bf16)] * 2,
        scratch_shapes=[
            pltpu.VMEM((2, ROWS, LEN3), bf16),
            pltpu.VMEM((ROWS, PAIR), bf16),
            pltpu.VMEM((PAIR, ROWS), f32),
            pltpu.VMEM((PAIR, OFFSETS), f32),
            pltpu.VMEM((PAIR, OFFSETS), f32),
        ],
        compiler_params=pltpu.CompilerParams(vmem_limit_bytes=MEMORY),
        name="attention_backward",
    )(q, k, v, g, ek, fq, p1, p2, p3)


def gelu_pair(hidden):
    z = jnp.abs(hidden) * 0.7071067811865476
    t = 1.0 / (1.0 + 0.3275911 * z)
    poly = t * (
        0.127414796
        + t * (-0.142248368 + t * (0.7107068705 + t * (-0.7265760135 + t * 0.5307027145)))
    )
    bell = jnp.exp(-z * z)
    tail = poly * bell
    below = jnp.where(hidden >= 0, 1.0 - tail, tail)
    return hidden * below, below + hidden * (bell * 0.3989422804014327)


def norm_forward(values, gain, shift):
    centered = values - jnp.mean(values, axis=1, keepdims=True)
    inverse = lax.rsqrt(jnp.mean(centered * centered, axis=1, keepdims=True) + norm_epsilon)
    normal = centered * inverse
    return (normal * gain + shift, normal, inverse)


def norm_backward(grad_out, normal, inverse, gain):
    scaled = grad_out * gain
    return inverse * (
        scaled
        - jnp.mean(scaled, axis=1, keepdims=True)
        - normal * jnp.mean(scaled * normal, axis=1, keepdims=True)
    )


def middle_kernel(
    lengths_ref,
    counts_ref,
    tokens_ref,
    context_ref,
    out_grad_ref,
    weight_ref,
    packed_ref,
    factor_ref,
    scale_ref,
    norm_ref,
    mixed_ref,
    grad_one_ref,
    context_grad_ref,
    small_ref,
    hidden_ref,
    scale_grad_ref,
    active_scr,
    slope_scr,
):
    step = pl.program_id(0)
    chunks = packed_ref.shape[0]

    @pl.when(step == 0)
    def _():
        small_ref[...] = jnp.zeros_like(small_ref)
        hidden_ref[...] = jnp.zeros_like(hidden_ref)
        scale_grad_ref[...] = jnp.zeros_like(scale_grad_ref)

    row = lax.broadcasted_iota(jnp.int32, (BLOCK, 1), 0) + step * BLOCK
    live = jnp.zeros((BLOCK, 1), f32)
    for (start, length), used in zip(SLOTS, live_counts(lengths_ref, counts_ref)):
        live = jnp.where((row >= start) & (row < start + used), 1.0, live)
    gain_one, shift_one, gain_two, shift_two = (norm_ref[i : i + 1, :] for i in range(4))

    context = context_ref[...]
    weight = weight_ref[0]
    attended = dot_nn(context, weight)
    normed, normal_one, inverse_one = norm_forward(
        tokens_ref[...].astype(f32) + attended, gain_one, shift_one
    )
    normed_low = normed.astype(bf16)
    mlp = jnp.zeros((BLOCK, D), f32)
    back_coeff = jnp.zeros((PAD, BLOCK), f32)
    for c in range(chunks):
        hidden = dot_nn(normed_low, packed_ref[c, :D, :])
        active, slope = gelu_pair(hidden)
        active = active.astype(bf16)
        active_scr[c] = active
        slope_scr[c] = slope
        mlp = mlp + dot_nn(active, packed_ref[c, D : 2 * D, :])
        back_coeff = back_coeff + dot_nt(packed_ref[c, 2 * D + PAD :, :], active)
    result, normal_two, inverse_two = norm_forward(normed + mlp, gain_two, shift_two)
    mixed_ref[...] = (result * live).astype(bf16)
    grad_two = norm_backward(
        out_grad_ref[...].astype(f32) * live, normal_two, inverse_two, gain_two
    )
    grad_mlp = grad_two.astype(bf16)

    back_slope = dot_nt(factor_ref[9], grad_mlp)
    small_ref[3] += add_parts(dot_nn(two_parts(back_coeff * scale_ref[:, 5:6]), grad_mlp))
    scale_grad_ref[:, 5:6] += jnp.sum(back_coeff * back_slope, axis=1, keepdims=True)
    back_through = two_parts(back_slope * scale_ref[:, 5:6])
    in_coeff = dot_nt(factor_ref[4], normed_low)
    in_scaled = two_parts(in_coeff * scale_ref[:, 4:5])
    in_slope = jnp.zeros((PAD, BLOCK), f32)
    grad_normed = grad_two
    for c in range(chunks):
        grad_active = dot_nt(grad_mlp, packed_ref[c, D : 2 * D, :])
        grad_hidden = (grad_active * slope_scr[c]).astype(bf16)
        grad_normed = grad_normed + dot_nt(grad_hidden, packed_ref[c, :D, :])
        in_slope = in_slope + dot_nt(packed_ref[c, 2 * D : 2 * D + PAD, :], grad_hidden)
        hidden_ref[c] += add_parts(dot_nn(in_scaled, grad_hidden))
        hidden_ref[chunks + c] += add_parts(dot_nn(back_through, active_scr[c]))
    scale_grad_ref[:, 4:5] += jnp.sum(in_coeff * in_slope, axis=1, keepdims=True)
    small_ref[2] += add_parts(dot_nn(two_parts(in_slope * scale_ref[:, 4:5]), normed_low))

    grad_one = norm_backward(grad_normed, normal_one, inverse_one, gain_one)
    grad_one_ref[...] = grad_one
    grad_attended = grad_one.astype(bf16)
    context_grad_ref[...] = dot_nt(grad_attended, weight).astype(bf16)
    out_coeff = dot_nt(factor_ref[3], context)
    out_slope = dot_nt(factor_ref[8], grad_attended)
    small_ref[1] += add_parts(dot_nn(two_parts(out_coeff * scale_ref[:, 3:4]), grad_attended))
    small_ref[0] += add_parts(dot_nn(two_parts(out_slope * scale_ref[:, 3:4]), context))
    scale_grad_ref[:, 3:4] += jnp.sum(out_coeff * out_slope, axis=1, keepdims=True)


def middle(lengths, counts, tokens, context, out_grad, weights, packed, factors, scales, norms):
    chunks = packed.shape[0]
    tile = pl.BlockSpec((BLOCK, D), lambda i: (i, 0))
    return pl.pallas_call(
        middle_kernel,
        grid=(ROWS // BLOCK,),
        in_specs=[pl.BlockSpec(memory_space=pltpu.SMEM)] * 2
        + [tile] * 3
        + [
            pl.BlockSpec((1, D, D), lambda i: (3, 0, 0)),
            pl.BlockSpec(
                (chunks, PACKED, D), lambda i: (0, 0, 0), pipeline_mode=pl.Buffered(1)
            ),
            whole(12, PAD, D),
            whole(PAD, 128),
            whole(4, D),
        ],
        out_specs=[tile] * 3
        + [whole(4, PAD, D), whole(2 * chunks, PAD, D), whole(PAD, 128)],
        out_shape=[
            jax.ShapeDtypeStruct((ROWS, D), bf16),
            jax.ShapeDtypeStruct((ROWS, D), f32),
            jax.ShapeDtypeStruct((ROWS, D), bf16),
            jax.ShapeDtypeStruct((4, PAD, D), f32),
            jax.ShapeDtypeStruct((2 * chunks, PAD, D), f32),
            jax.ShapeDtypeStruct((PAD, 128), f32),
        ],
        scratch_shapes=[
            pltpu.VMEM((chunks, BLOCK, D), bf16),
            pltpu.VMEM((chunks, BLOCK, D), f32),
        ],
        compiler_params=pltpu.CompilerParams(vmem_limit_bytes=MEMORY),
        name="middle",
    )(lengths, counts, tokens, context, out_grad, weights, packed, factors, scales, norms)


LANES = 128
BLOCKS = D // LANES
MESH = pl.DeviceIdType.MESH


def devices():
    return lax.axis_size("dp") * lax.axis_size("tensor")


def hidden_rows():
    tiles = 2 * BLOCKS
    return PAD * -(-tiles // lax.axis_size("dp"))


def last_kernel(
    tokens_ref,
    gq_ref,
    gk_ref,
    gv_ref,
    grad_one_ref,
    coeff_ref,
    merged_ref,
    index_ref,
    rel_coeff_ref,
    factor_ref,
    scale_ref,
    small_ref,
    hidden_ref,
    middle_scale_ref,
    rel_any,
    gek_any,
    gfq_any,
    in_grad_ref,
    down_out,
    up_out,
    hidden_out,
    scale_out,
    rel_scr,
    gek_scr,
    gfq_scr,
    down_scr,
    up_scr,
    scale_scr,
    stage_scr,
    mine_late,
    land_late,
    mine_small,
    land_small,
    mine_hidden,
    land_hidden,
    all_sums,
    all_hidden,
    load_sem,
    late_out_sem,
    late_in_sem,
    small_out_sem,
    small_in_sem,
    hidden_out_sem,
    hidden_in_sem,
    sums_out_sem,
    sums_in_sem,
    spread_out_sem,
    spread_in_sem,
):
    step = pl.program_id(0)
    final = ROWS // BLOCK - 1
    outer = lax.axis_size("dp")
    inner = lax.axis_size("tensor")
    count = outer * inner
    my_outer = lax.axis_index("dp")
    my_inner = lax.axis_index("tensor")
    me = my_outer * inner + my_inner
    barrier = pltpu.get_barrier_semaphore()

    def partner(off):
        other = lax.rem(me + off, count)
        return other, other // inner, lax.rem(other, inner)

    def send(src, dst, out_sem, in_sem, place):
        return pltpu.make_async_remote_copy(
            src_ref=src,
            dst_ref=dst,
            send_sem=out_sem,
            recv_sem=in_sem,
            device_id=place,
            device_id_type=MESH,
        )

    def late(off):
        other, row, col = partner(off)
        return send(
            mine_late.at[other],
            land_late.at[off],
            late_out_sem.at[off],
            late_in_sem.at[off],
            (row, col),
        )

    def small(off):
        other, row, col = partner(off)
        return send(
            mine_small.at[other],
            land_small.at[off],
            small_out_sem.at[off],
            small_in_sem.at[off],
            (row, col),
        )

    def hidden(off):
        other, row, col = partner(off)
        return send(
            mine_hidden.at[col, row],
            land_hidden.at[off],
            hidden_out_sem.at[off],
            hidden_in_sem.at[off],
            (row, col),
        )

    def sums(off, origin):
        other, row, col = partner(off)
        return send(
            all_sums.at[origin],
            all_sums.at[origin],
            sums_out_sem.at[off],
            sums_in_sem.at[off],
            (row, col),
        )

    def spread(off, origin):
        return send(
            all_hidden.at[origin],
            all_hidden.at[origin],
            spread_out_sem.at[off],
            spread_in_sem.at[off],
            (lax.rem(my_outer + off, outer), my_inner),
        )

    def load(number, src, dst):
        return pltpu.make_async_copy(src, dst, load_sem.at[number])

    loads = ((0, rel_any, rel_scr), (1, gek_any, gek_scr), (2, gfq_any, gfq_scr))

    @pl.when(step == 0)
    def _():
        for piece in loads:
            load(*piece).start()

        @pl.loop(1, count)
        def _(off):
            _, row, col = partner(off)
            pl.semaphore_signal(barrier, inc=1, device_id=(row, col), device_id_type=MESH)

        scale_scr[...] = jnp.zeros_like(scale_scr)
        down_scr[...] = jnp.zeros_like(down_scr)
        up_scr[...] = jnp.zeros_like(up_scr)

    @pl.when(step == 1)
    def _():
        if count > 4 * BLOCKS:
            mine_small[4 * BLOCKS :] = jnp.zeros((count - 4 * BLOCKS, PAD, LANES), bf16)
        for number in range(4):
            for block in range(BLOCKS):
                mine_small[number * BLOCKS + block] = small_ref[
                    number, :, block * LANES : (block + 1) * LANES
                ].astype(bf16)
        mine_hidden[...] = jnp.zeros_like(mine_hidden)
        tiles = mine_hidden.shape[2] // PAD
        for chunk in range(inner):
            for which in range(2):
                for block in range(BLOCKS):
                    tile = which * BLOCKS + block
                    at = tile % tiles * PAD
                    mine_hidden[chunk, tile // tiles, at : at + PAD] = hidden_ref[
                        which * inner + chunk, :, block * LANES : (block + 1) * LANES
                    ].astype(bf16)
        pl.semaphore_wait(barrier, count - 1)

        @pl.loop(1, count)
        def _(off):
            small(off).start()
            hidden(off).start()

        land_small[0] = mine_small[me]
        land_hidden[0] = mine_hidden[my_inner, my_outer]

    @pl.when(step == 2)
    def _():
        for piece in loads:
            load(*piece).wait()
        rel = rel_scr[...]
        bucket = lax.broadcasted_iota(jnp.int32, (2 * SPAN, OFFSETS), 0)
        for member, ref, row in ((0, gfq_scr, 1), (1, gek_scr, 0)):
            scale = scale_ref[:, member : member + 1]
            chosen = jnp.where(bucket == index_ref[row : row + 1, :], 1.0, 0.0).astype(bf16)
            grad = dot_nt(ref[...], chosen).astype(bf16)
            coeff = rel_coeff_ref[member]
            slope = dot_nn(factor_ref[5 + member], grad)
            up_scr[member] += add_parts(dot_nt(two_parts(coeff * scale), grad))
            down_scr[member] += add_parts(dot_nn(two_parts(slope * scale), rel))
            scale_scr[:, member : member + 1] += jnp.sum(coeff * slope, axis=1, keepdims=True)

    tokens = tokens_ref[...]
    in_grad = grad_one_ref[...]
    for member, ref in enumerate((gq_ref, gk_ref, gv_ref)):
        grad = ref[...]
        scale = scale_ref[:, member : member + 1]
        in_grad = in_grad + dot_nt(grad, merged_ref[member])
        coeff = coeff_ref[member]
        slope = dot_nt(factor_ref[5 + member], grad)
        up_scr[member] += add_parts(dot_nn(two_parts(coeff * scale), grad))
        down_scr[member] += add_parts(dot_nn(two_parts(slope * scale), tokens))
        scale_scr[:, member : member + 1] += jnp.sum(coeff * slope, axis=1, keepdims=True)
    in_grad_ref[...] = in_grad

    @pl.when(step == final)
    def _():
        used = 2 * 3 * BLOCKS * RANK
        for number in range(6):
            ref = down_scr if number < 3 else up_scr
            for block in range(BLOCKS):
                at = (number * BLOCKS + block) * RANK
                stage_scr[at : at + RANK, :] = ref[
                    number % 3, :RANK, block * LANES : (block + 1) * LANES
                ]
        stage_scr[used : used + PAD, :] = scale_scr[...] + middle_scale_ref[...]
        stage_scr[used + PAD :, :] = jnp.zeros((count * PAD - used - PAD, LANES), f32)
        mine_late[...] = stage_scr[...].astype(bf16).reshape(count, PAD, LANES)

        @pl.loop(1, count)
        def _(off):
            late(off).start()

        land_late[0] = mine_late[me]

        @pl.loop(1, count)
        def _(off):
            small(off).wait_recv()
            hidden(off).wait_recv()

        all_hidden[my_outer] = jnp.sum(land_hidden[...].astype(f32), axis=0).astype(bf16)

        @pl.loop(1, outer)
        def _(off):
            spread(off, my_outer).start()

        all_sums[me, PAD:] = jnp.sum(land_small[...].astype(f32), axis=0).astype(bf16)

        @pl.loop(1, count)
        def _(off):
            late(off).wait_recv()

        all_sums[me, :PAD] = jnp.sum(land_late[...].astype(f32), axis=0).astype(bf16)

        @pl.loop(1, count)
        def _(off):
            sums(off, me).start()

        @pl.loop(1, outer)
        def _(off):
            spread(off, lax.rem(my_outer + outer - off, outer)).wait_recv()

        tiles = all_hidden.shape[1] // PAD
        for which in range(2):
            for block in range(BLOCKS):
                tile = which * BLOCKS + block
                at = tile % tiles * PAD
                hidden_out[which, :, block * LANES : (block + 1) * LANES] = all_hidden[
                    tile // tiles, at : at + PAD
                ].astype(f32)[:RANK]

        @pl.loop(1, count)
        def _(off):
            sums(off, lax.rem(me + count - off, count)).wait_recv()

        stage_scr[...] = all_sums[:, :PAD].astype(f32).reshape(count * PAD, LANES)
        for number in range(6):
            ref = down_out if number < 3 else up_out
            for block in range(BLOCKS):
                at = (number * BLOCKS + block) * RANK
                ref[number % 3, :, block * LANES : (block + 1) * LANES] = stage_scr[
                    at : at + RANK, :
                ]
        scale_out[...] = stage_scr[used : used + PAD, :].T[:6, :RANK]
        for number, (ref, place) in enumerate(
            ((down_out, 3), (up_out, 3), (down_out, 4), (up_out, 4))
        ):
            for block in range(BLOCKS):
                ref[place, :, block * LANES : (block + 1) * LANES] = all_sums[
                    number * BLOCKS + block, PAD:
                ].astype(f32)[:RANK]

        @pl.loop(1, count)
        def _(off):
            small(off).wait_send()
            hidden(off).wait_send()
            late(off).wait_send()
            sums(off, me).wait_send()

        @pl.loop(1, outer)
        def _(off):
            spread(off, my_outer).wait_send()


def last(
    tokens, gq, gk, gv, grad_one, coeff, weights, index, rel_coeff, factors, scales,
    small, hidden, middle_scale, rel, gek, gfq,
):
    count = devices()
    outer = lax.axis_size("dp")
    inner = lax.axis_size("tensor")
    piece = hidden_rows()
    tile = pl.BlockSpec((BLOCK, D), lambda i: (i, 0))
    factor = jax.ShapeDtypeStruct((5, RANK, D), f32)
    block = pltpu.VMEM((count, PAD, LANES), bf16)
    all_pairs = pltpu.SemaphoreType.DMA((count,))
    return pl.pallas_call(
        last_kernel,
        grid=(ROWS // BLOCK,),
        in_specs=[tile] * 5
        + [
            pl.BlockSpec((3, PAD, BLOCK), lambda i: (0, 0, i)),
            whole(3, D, D),
            whole(2, OFFSETS),
            whole(2, PAD, 2 * SPAN),
            whole(12, PAD, D),
            whole(PAD, LANES),
            whole(4, PAD, D),
            whole(2 * inner, PAD, D),
            whole(PAD, LANES),
        ]
        + [pl.BlockSpec(memory_space=pl.ANY)] * 3,
        out_specs=[
            tile,
            whole(5, RANK, D),
            whole(5, RANK, D),
            whole(2, RANK, D),
            whole(6, RANK),
        ],
        out_shape=[
            jax.ShapeDtypeStruct((ROWS, D), f32),
            factor,
            factor,
            jax.ShapeDtypeStruct((2, RANK, D), f32),
            jax.ShapeDtypeStruct((6, RANK), f32),
        ],
        scratch_shapes=[
            pltpu.VMEM((2 * SPAN, D), bf16),
            pltpu.VMEM((D, OFFSETS), bf16),
            pltpu.VMEM((D, OFFSETS), bf16),
            pltpu.VMEM((3, PAD, D), f32),
            pltpu.VMEM((3, PAD, D), f32),
            pltpu.VMEM((PAD, LANES), f32),
            pltpu.VMEM((count * PAD, LANES), f32),
            block,
            block,
            block,
            block,
            pltpu.VMEM((inner, outer, piece, LANES), bf16),
            pltpu.VMEM((count, piece, LANES), bf16),
            pltpu.VMEM((count, 2 * PAD, LANES), bf16),
            pltpu.VMEM((outer, piece, LANES), bf16),
            pltpu.SemaphoreType.DMA((3,)),
        ]
        + [all_pairs] * 8
        + [pltpu.SemaphoreType.DMA((outer,))] * 2,
        compiler_params=pltpu.CompilerParams(
            collective_id=0, has_side_effects=True, vmem_limit_bytes=MEMORY
        ),
        name="last",
    )(
        tokens, gq, gk, gv, grad_one, coeff, weights, index, rel_coeff, factors, scales,
        small, hidden, middle_scale, rel, gek, gfq,
    )


def on_device(
    tokens,
    qkv_weight,
    out_weight,
    in_weight,
    back_weight,
    rel_embed,
    gain_one,
    shift_one,
    gain_two,
    shift_two,
    adapt_down,
    adapt_up,
    hidden_up,
    hidden_down,
    adapt_scale,
    seq_lengths,
    seq_counts,
    rel_bucket,
    out_grad,
):
    factors = jnp.pad(
        jnp.concatenate([adapt_down, adapt_up, hidden_up[None], hidden_down[None]], axis=0),
        ((0, 0), (0, PAD - RANK), (0, 0)),
    )
    scales = jnp.pad(adapt_scale.T, ((0, PAD - RANK), (0, 128 - 6)))
    index_rows = jnp.pad(
        jnp.stack([rel_bucket[::-1], rel_bucket]), ((0, 0), (0, 1)), constant_values=-1
    )
    norms = jnp.stack([gain_one, shift_one, gain_two, shift_two])
    packed = lax.all_gather(
        pack_weights(in_weight, back_weight, factors, scales), "tensor", axis=0
    )
    q, k, v, ek, fq, ekt, eqt, weights, coeff, rel_coeff = project(
        tokens, qkv_weight, out_weight, rel_embed, index_rows, factors, scales
    )
    context, p1, p2, p3 = attend_forward(seq_lengths, seq_counts, q, k, v, ekt, eqt)
    mixed, grad_one, context_grad, small, hidden, middle_scale = middle(
        seq_lengths, seq_counts, tokens, context, out_grad, weights, packed, factors, scales, norms
    )
    gq, gk, gv, gek, gfq = attend_backward(q, k, v, context_grad, ek, fq, p1, p2, p3)
    in_grad, down_grad, up_grad, hidden_grad, scale_grad = last(
        tokens, gq, gk, gv, grad_one, coeff, weights, index_rows, rel_coeff, factors, scales,
        small, hidden, middle_scale, rel_embed, gek, gfq,
    )
    return (mixed, in_grad, down_grad, up_grad, hidden_grad[0], hidden_grad[1], scale_grad)


def solution(mesh):
    rows = P(("dp", "tensor"), None)
    return jax.shard_map(
        on_device,
        mesh=mesh,
        in_specs=(
            rows,
            P(),
            P(),
            P(None, "tensor"),
            P("tensor", None),
            P(),
            P(),
            P(),
            P(),
            P(),
            P(),
            P(),
            P(None, "tensor"),
            P(None, "tensor"),
            P(),
            rows,
            rows,
            P(),
            rows,
        ),
        out_specs=(rows, rows, P(), P(), P(None, "tensor"), P(None, "tensor"), P()),
        check_vma=False,
    )
```

```python
import jax
import jax.numpy as jnp
from jax import lax
from jax.experimental import pallas as pl
from jax.experimental.pallas import tpu as pltpu
from jax.sharding import PartitionSpec as P

D = 768
H = 12
DH = 64
PAIR = 2 * DH
SPAN = 256
RANK = 12
PAD = 16
ROWS = 1024
LEN1 = 128
LEN3 = 512
OFFSETS = 2 * LEN3
TILE = 128
BLOCK = 256
SLOTS = ((0, 128), (128, 128), (256, 256), (512, 512))
PACKED = 1600
HALF = PACKED // 2
CHUNK = HALF // 5
LANES = 128
BLOCKS = D // LANES
MESH = pl.DeviceIdType.MESH
norm_epsilon = 1e-07
masked_score = -1e30
bf16 = jnp.bfloat16
f32 = jnp.float32
MEMORY = 60 * 1024 * 1024


def dot_nn(a, b):
    return jnp.dot(a, b, preferred_element_type=f32)


def dot_nt(a, b):
    return lax.dot_general(a, b, (((1,), (1,)), ((), ())), preferred_element_type=f32)


def dot_tn(a, b):
    return lax.dot_general(a, b, (((0,), (0,)), ((), ())), preferred_element_type=f32)


def two_parts(wide):
    high = wide.astype(bf16)
    rest = (wide - high.astype(f32)).astype(bf16)
    return jnp.concatenate([high, rest], axis=0)


def add_parts(stacked):
    return stacked[:PAD] + stacked[PAD:]


def merged(weight, down, up, scale):
    twice = jnp.concatenate([up, up], axis=0)
    extra = dot_tn(two_parts(down.astype(f32) * scale), twice)
    return (weight.astype(f32) + extra).astype(bf16)


def live_counts(lengths_ref, counts_ref):
    ranks = ((0, 0), (0, 1), (1, 0), (2, 0))
    return [
        jnp.where(rank < counts_ref[0, bucket], lengths_ref[0, slot], 0)
        for slot, (bucket, rank) in enumerate(ranks)
    ]


def padded(rows):
    return jnp.concatenate([rows.astype(f32), jnp.zeros((PAD - RANK, D), f32)], axis=0).astype(bf16)


def project_kernel(
    tokens_ref,
    qkv_ref,
    rel_ref,
    index_ref,
    down_ref,
    up_ref,
    hidden_up_ref,
    hidden_down_ref,
    adapt_scale_ref,
    out_any,
    in_any,
    back_any,
    q_ref,
    k_ref,
    v_ref,
    eq_ref,
    fk_ref,
    ekt_ref,
    eqt_ref,
    merged_ref,
    packed_ref,
    coeff_ref,
    rel_coeff_ref,
    factor_ref,
    scale_ref,
    pos_scr,
    load_scr,
    load_sem,
):
    step = pl.program_id(0)
    loads = [
        pltpu.make_async_copy(ref, load_scr.at[number], load_sem.at[number])
        for number, ref in enumerate((out_any, in_any, back_any))
    ]

    @pl.when(step == 0)
    def _():
        for load in loads:
            load.start()
        for number in range(5):
            factor_ref[number] = padded(down_ref[number])
            factor_ref[5 + number] = padded(up_ref[number])
        factor_ref[10] = padded(hidden_up_ref[...])
        factor_ref[11] = padded(hidden_down_ref[...])
        wide = jnp.concatenate([adapt_scale_ref[...], jnp.zeros((6, LANES - RANK), f32)], axis=1)
        wide = jnp.concatenate([wide, jnp.zeros((LANES - 6, LANES), f32)], axis=0)
        scale_ref[...] = wide.T[:PAD]
        for member in range(3):
            merged_ref[member] = merged(
                qkv_ref[member],
                factor_ref[member],
                factor_ref[5 + member],
                scale_ref[:, member : member + 1],
            )
        rel = rel_ref[...]
        for member in range(2):
            pos_scr[member] = dot_nn(rel, merged_ref[member]).astype(bf16)
        coeff = dot_nt(factor_ref[:2].reshape(2 * PAD, D), rel)
        rel_coeff_ref[...] = coeff.reshape(2, PAD, 2 * SPAN)

    @pl.when(step == 1)
    def _():
        for load in loads:
            load.wait()
        packed_ref[:D] = merged(load_scr[1], factor_ref[4], factor_ref[10], scale_ref[:, 4:5])
        packed_ref[2 * D : 2 * D + PAD] = factor_ref[10]
        packed_ref[2 * D + PAD : 2 * D + 2 * PAD] = factor_ref[11]
        packed_ref[2 * D + 2 * PAD :] = jnp.zeros((PACKED - 2 * D - 2 * PAD, D), bf16)

    @pl.when(step == 2)
    def _():
        packed_ref[D : 2 * D] = merged(load_scr[2], factor_ref[11], factor_ref[9], scale_ref[:, 5:6])

    @pl.when(step == 3)
    def _():
        merged_ref[3] = merged(load_scr[0], factor_ref[3], factor_ref[8], scale_ref[:, 3:4])

    tokens = tokens_ref[...]
    for member, ref in enumerate((q_ref, k_ref, v_ref)):
        ref[...] = dot_nn(tokens, merged_ref[member]).astype(bf16)
    coeff_ref[...] = dot_nt(factor_ref[:3].reshape(3 * PAD, D), tokens).reshape(3, PAD, BLOCK)
    bucket = lax.broadcasted_iota(jnp.int32, (2 * SPAN, BLOCK), 0)
    back, forth = (
        jnp.where(bucket == index_ref[row : row + 1, :], 1.0, 0.0).astype(bf16) for row in range(2)
    )
    eq_ref[...] = dot_tn(back, pos_scr[0]).astype(bf16)
    fk_ref[...] = dot_tn(forth, pos_scr[1]).astype(bf16)
    ekt_ref[...] = dot_tn(pos_scr[1], back).astype(bf16)
    eqt_ref[...] = dot_tn(pos_scr[0], back).astype(bf16)


def whole(*shape):
    return pl.BlockSpec(shape, lambda *at: (0,) * len(shape))


def once(*shape):
    return pl.BlockSpec(shape, lambda *at: (0,) * len(shape), pipeline_mode=pl.Buffered(1))


def project(
    tokens, qkv_weight, rel_embed, index_rows, down, up, hidden_up, hidden_down, adapt_scale,
    out_weight, in_weight, back_weight,
):
    tile = pl.BlockSpec((BLOCK, D), lambda i: (i, 0))
    rows = jax.ShapeDtypeStruct((ROWS, D), bf16)
    return pl.pallas_call(
        project_kernel,
        grid=(ROWS // BLOCK,),
        in_specs=[
            tile,
            once(3, D, D),
            once(2 * SPAN, D),
            pl.BlockSpec((2, BLOCK), lambda i: (0, i)),
            once(5, RANK, D),
            once(5, RANK, D),
            once(RANK, D),
            once(RANK, D),
            once(6, RANK),
        ]
        + [pl.BlockSpec(memory_space=pl.ANY)] * 3,
        out_specs=[tile] * 5
        + [pl.BlockSpec((D, BLOCK), lambda i: (0, i))] * 2
        + [
            whole(4, D, D),
            whole(PACKED, D),
            pl.BlockSpec((3, PAD, BLOCK), lambda i: (0, 0, i)),
            whole(2, PAD, 2 * SPAN),
            whole(12, PAD, D),
            whole(PAD, LANES),
        ],
        out_shape=[rows] * 5
        + [jax.ShapeDtypeStruct((D, OFFSETS), bf16)] * 2
        + [
            jax.ShapeDtypeStruct((4, D, D), bf16),
            jax.ShapeDtypeStruct((PACKED, D), bf16),
            jax.ShapeDtypeStruct((3, PAD, ROWS), f32),
            jax.ShapeDtypeStruct((2, PAD, 2 * SPAN), f32),
            jax.ShapeDtypeStruct((12, PAD, D), bf16),
            jax.ShapeDtypeStruct((PAD, LANES), f32),
        ],
        scratch_shapes=[
            pltpu.VMEM((2, 2 * SPAN, D), bf16),
            pltpu.VMEM((3, D, D), bf16),
            pltpu.SemaphoreType.DMA((3,)),
        ],
        compiler_params=pltpu.CompilerParams(vmem_limit_bytes=MEMORY),
        name="project",
    )(
        tokens, qkv_weight, rel_embed, index_rows, down, up, hidden_up, hidden_down, adapt_scale,
        out_weight, in_weight, back_weight,
    )


def unit_matrix(flipped):
    row = lax.broadcasted_iota(jnp.int32, (TILE, TILE), 0)
    col = lax.broadcasted_iota(jnp.int32, (TILE, TILE), 1)
    return jnp.where(row == (TILE - 1 - col if flipped else col), 1.0, 0.0).astype(bf16)


def head_lanes(member):
    lane = lax.broadcasted_iota(jnp.int32, (1, PAIR), 1)
    return jnp.where(lane // DH == member, 1.0, 0.0).astype(bf16)


def each_head(rows):
    return jnp.concatenate([rows * head_lanes(0), rows * head_lanes(1)], axis=0)


def own_lanes(stacked):
    lane = lax.broadcasted_iota(jnp.int32, (TILE, PAIR), 1)
    return jnp.where(lane < DH, stacked[:TILE], stacked[TILE:])


def lane_and_row():
    lane = lax.broadcasted_iota(jnp.int32, (8, 128), 1)
    return lane, lax.broadcasted_iota(jnp.int32, (8, 128), 0)


def turn(block, shift):
    return pltpu.roll(block, shift % 128, 1, stride=1, stride_axis=0)


def skew(table, length):
    lane, row = lane_and_row()
    count = length // 128
    done = []
    for at in range(0, TILE, 8):
        blocks = [table[at : at + 8, 128 * c : 128 * c + 128] for c in range(count + 1)]
        blocks[0] = jnp.where(lane + row >= 127 - at, blocks[0], blocks[count])
        moved = [turn(block, at + 1) for block in blocks[:count]]
        if count > 1:
            inside = lane - row <= at
            moved = [
                jnp.where(inside, moved[c], moved[(c + 1) % count]) for c in range(count)
            ]
        done.append(jnp.concatenate(moved, axis=1))
    return jnp.concatenate(done, axis=0)


def flip_rows(block):
    row = lax.broadcasted_iota(jnp.int32, (8, LANES), 0)
    done = []
    for at in range(TILE - 8, -1, -8):
        done.append(
            jnp.concatenate(
                [
                    jnp.take_along_axis(block[at : at + 8, c : c + LANES], 7 - row, axis=0)
                    for c in range(0, block.shape[1], LANES)
                ],
                axis=1,
            )
        )
    return jnp.concatenate(done, axis=0)


def slot_tiles(slot):
    return [(slot, t) for t in range(SLOTS[slot][1] // TILE)]


def prob_block(refs, slot, t, member):
    start, length = SLOTS[slot]
    at = start + t * TILE if length == LEN1 else t * TILE
    ref = refs[{LEN1: 0, LEN3: 2}.get(length, 1)]
    return ref.at[member, at : at + TILE, :]


def unskew(scores, length):
    lane, row = lane_and_row()
    zero = jnp.zeros((8, 128), f32)
    done = []
    for at in range(0, TILE, 8):
        moved = [
            turn(scores[at : at + 8, 128 * c : 128 * c + 128], at) for c in range(length // 128)
        ]
        before = lane - row < at
        done.append(
            jnp.concatenate(
                [jnp.where(before, x, y) for x, y in zip([zero] + moved, moved + [zero])], axis=1
            )
        )
    return jnp.concatenate(done, axis=0)


def gather_moves(packed, gathered, own_sem, sems):
    step = pl.program_id(0)
    final = pl.num_programs(0) - 1
    d = lax.axis_index("dp")
    t = lax.axis_index("tensor")
    near = t + 1 - 2 * lax.rem(t, 2)
    far = t + 2 - 4 * (t // 2)
    mate = d + 1 - 2 * lax.rem(d, 2)
    half = lax.rem(d, 2)
    chunks = HALF // CHUNK
    near_out, near_in, far_out, far_in, mate_out, mate_in, pass_out, pass_in, late_out, late_in = sems
    barrier = pltpu.get_barrier_semaphore()
    places = ((d, near), (d, far), (mate, t))

    def rows(which, chunk):
        return pl.ds(pl.multiple_of(which * HALF + chunk * CHUNK, PAD), CHUNK)

    def send(src, dst, out_sem, in_sem, place):
        return pltpu.make_async_remote_copy(
            src_ref=src, dst_ref=dst, send_sem=out_sem, recv_sem=in_sem, device_id=place, device_id_type=MESH
        )

    def to_near():
        return send(packed, gathered.at[t], near_out.at[0], near_in.at[0], places[0])

    def to_far(chunk):
        here = rows(half, chunk)
        return send(
            packed.at[here], gathered.at[t, here], far_out.at[chunk], far_in.at[chunk], places[1]
        )

    def onward(which, chunk, out_sems, in_sems, place):
        here = gathered.at[far, rows(which, chunk)]
        return send(here, here, out_sems.at[chunk], in_sems.at[chunk], place)

    def to_mate(chunk):
        return onward(half, chunk, mate_out, mate_in, places[2])

    def pass_near(chunk):
        return onward(half, chunk, pass_out, pass_in, places[0])

    def late_near(chunk):
        return onward(1 - half, chunk, late_out, late_in, places[0])

    def own():
        return pltpu.make_async_copy(packed, gathered.at[t], own_sem.at[0])

    def begin():
        @pl.when(step == 0)
        def _():
            for place in places:
                pl.semaphore_signal(barrier, inc=1, device_id=place, device_id_type=MESH)
            own().start()

    def go_on():
        @pl.when(step == 0)
        def _():
            pl.semaphore_wait(barrier, len(places))
            to_far(0).start()
            to_far(1).start()
            to_near().start()

        @pl.when((step > 0) & (step < chunks - 1))
        def _():
            to_far(step + 1).start()

        @pl.when(step > 0)
        def _():
            chunk = step - 1
            to_far(chunk).wait_recv()
            to_mate(chunk).start()
            pass_near(chunk).start()

        @pl.when(step > 2)
        def _():
            chunk = step - 3
            to_mate(chunk).wait_recv()
            late_near(chunk).start()

    def finish():
        @pl.when(step == final)
        def _():
            for chunk in (chunks - 2, chunks - 1):
                to_mate(chunk).wait_recv()
                late_near(chunk).start()
            own().wait()
            to_near().wait()
            for chunk in range(chunks):
                pass_near(chunk).wait_recv()
                late_near(chunk).wait_recv()
                to_far(chunk).wait_send()
                to_mate(chunk).wait_send()
                pass_near(chunk).wait_send()
                late_near(chunk).wait_send()

    return begin, go_on, finish


def forward_kernel(
    lengths_ref,
    counts_ref,
    q_ref,
    k_ref,
    v_ref,
    ek_ref,
    eq_ref,
    packed_any,
    context_ref,
    p1_ref,
    p2_ref,
    p3_ref,
    gathered_any,
    shift_scr,
    score_scr,
    prob_scr,
    own_sem,
    *gather_sems,
):
    gather_start, gather_step, gather_end = gather_moves(
        packed_any, gathered_any, own_sem, gather_sems
    )
    gather_start()
    eye = unit_matrix(False)
    factor = 1.4426950408889634 * (3.0 * DH) ** -0.5
    counts = live_counts(lengths_ref, counts_ref)
    turned_values = v_ref[...].T
    head_rows = [
        jnp.where(
            lax.broadcasted_iota(jnp.int32, (PAIR, 1), 0) // DH == member, 1.0, 0.0
        ).astype(bf16)
        for member in range(2)
    ]

    def place(slot, t):
        start, length = SLOTS[slot]
        low = LEN3 - TILE - TILE * t
        row = start + t * TILE
        return start, length, slice(row, row + TILE), slice(low, low + length + TILE)

    def shift_unit(slot, t):
        start, length, rows, window = place(slot, t)
        table = dot_nn(each_head(q_ref[rows, :]), ek_ref[:, window])
        for member in range(2):
            shift_scr[member, rows, :length] = skew(
                table[member * TILE : (member + 1) * TILE], length
            ).astype(bf16)

    def score_unit(slot, t):
        start, length, rows, window = place(slot, t)
        keys = each_head(k_ref[rows, :])
        table = dot_nn(keys, eq_ref[:, window])
        queries = q_ref[start : start + length, :]
        live = lax.broadcasted_iota(jnp.int32, (TILE, 1), 0) < counts[slot] - t * TILE
        tops = []
        for member in range(2):
            mine = slice(member * TILE, (member + 1) * TILE)
            left = jnp.concatenate([keys[mine], eye], axis=1)
            shifted = shift_scr[member, start : start + length, t * TILE : (t + 1) * TILE]
            right = jnp.concatenate([queries, shifted], axis=1)
            raw = dot_nt(left, right) + skew(table[mine], length)
            raw = jnp.where(live, raw * factor, masked_score)
            score_scr[member, rows, :length] = raw
            tops.append(jnp.max(raw, axis=0, keepdims=True))
        return tops

    def weight_unit(slot, t, tops):
        start, length, rows, window = place(slot, t)
        sums = []
        for member in range(2):
            weights = jnp.exp2(score_scr[member, rows, :length] - tops[member])
            score_scr[member, rows, :length] = weights
            sums.append(jnp.sum(weights, axis=0, keepdims=True))
        return sums

    def prob_unit(slot, t, inverses):
        start, length, rows, window = place(slot, t)
        for member in range(2):
            prob = score_scr[member, rows, :length] * inverses[member]
            prob_scr[member, rows, :length] = prob.astype(bf16)
            prob_block((p1_ref, p2_ref, p3_ref), slot, t, member)[...] = flip_rows(prob).astype(
                bf16
            )

    def context_unit(slot):
        start, length = SLOTS[slot]
        here = slice(start, start + length)
        left = jnp.concatenate([turned_values[:, here] * rows for rows in head_rows], axis=1)
        right = jnp.concatenate([prob_scr[member, here, :length] for member in range(2)], axis=0)
        context_ref[here, :] = dot_nn(left, right).astype(bf16).T

    def both(function, parts):
        return [function(member_parts) for member_parts in zip(*parts)]

    def largest(parts):
        total = parts[0]
        for part in parts[1:]:
            total = jnp.maximum(total, part)
        return total

    groups = ((3,), (2, 1, 0))
    tiles = [[unit for slot in group for unit in slot_tiles(slot)] for group in groups]
    held = {}

    def settle(slot):
        held[slot] = both(largest, [held.pop(unit) for unit in slot_tiles(slot)])

    def invert(slot):
        total = both(sum, [held.pop(unit) for unit in slot_tiles(slot)])
        held[slot] = [1.0 / part for part in total]

    for unit in tiles[0]:
        shift_unit(*unit)
    gather_step()
    for first, second in zip(tiles[0], tiles[1]):
        held[first] = score_unit(*first)
        shift_unit(*second)
    settle(3)
    for first, second in zip(tiles[0], tiles[1]):
        held[second] = score_unit(*second)
        held[first] = weight_unit(*first, held[3])
    invert(3)
    for slot in groups[1]:
        settle(slot)
    for first, second in zip(tiles[0], tiles[1]):
        held[second] = weight_unit(*second, held[second[0]])
        prob_unit(*first, held[3])
    for slot in groups[1]:
        invert(slot)
    context_unit(3)
    for second in tiles[1]:
        prob_unit(*second, held[second[0]])
    for slot in groups[1]:
        context_unit(slot)
    gather_end()


PAIR_SPEC = pl.BlockSpec((ROWS, PAIR), lambda p: (0, p))
TABLE_SPEC = pl.BlockSpec((PAIR, OFFSETS), lambda p: (p, 0))
PROB_SIZES = ((256, 128), (256, 256), (512, 512))
PROB_SPECS = [pl.BlockSpec((2, *size), lambda p: (p, 0, 0)) for size in PROB_SIZES]


def attend_forward(lengths, counts, q, k, v, ek, eq, packed):
    chunks = HALF // CHUNK
    single, several = (pltpu.SemaphoreType.DMA((n,)) for n in (1, chunks))
    inner = lax.axis_size("tensor")
    assert inner == 4 and lax.axis_size("dp") % 2 == 0
    return pl.pallas_call(
        forward_kernel,
        grid=(H // 2,),
        in_specs=[pl.BlockSpec(memory_space=pltpu.SMEM)] * 2
        + [PAIR_SPEC] * 3
        + [TABLE_SPEC] * 2
        + [once(PACKED, D)],
        out_specs=[PAIR_SPEC] + PROB_SPECS + [pl.BlockSpec(memory_space=pl.ANY)],
        out_shape=[jax.ShapeDtypeStruct((ROWS, D), bf16)]
        + [jax.ShapeDtypeStruct((H, *size), bf16) for size in PROB_SIZES]
        + [jax.ShapeDtypeStruct((inner, PACKED, D), bf16)],
        scratch_shapes=[
            pltpu.VMEM((2, ROWS, LEN3), bf16),
            pltpu.VMEM((2, ROWS, LEN3), f32),
            pltpu.VMEM((2, ROWS, LEN3), bf16),
            pltpu.SemaphoreType.DMA((1,)),
        ]
        + [single] * 2
        + [several] * 8,
        compiler_params=pltpu.CompilerParams(
            collective_id=1, has_side_effects=True, vmem_limit_bytes=MEMORY
        ),
        name="attention_forward",
    )(lengths, counts, q, k, v, ek, eq, packed)


def backward_kernel(
    q_ref,
    k_ref,
    v_ref,
    g_ref,
    context_ref,
    eq_ref,
    fk_ref,
    p1_ref,
    p2_ref,
    p3_ref,
    gq_ref,
    gk_ref,
    gv_ref,
    geq_ref,
    gfk_ref,
    grad_scr,
    turned_scr,
    geq_scr,
    gfk_scr,
):
    anti = unit_matrix(True)
    factor = (3.0 * DH) ** -0.5
    geq_scr[...] = jnp.zeros_like(geq_scr)
    gfk_scr[...] = jnp.zeros_like(gfk_scr)
    product = g_ref[...].astype(f32) * context_ref[...].astype(f32)
    high = product.astype(bf16)
    rest = (product - high.astype(f32)).astype(bf16)
    lane = lax.broadcasted_iota(jnp.int32, (PAD, 2 * PAIR), 1) % PAIR
    row = lax.broadcasted_iota(jnp.int32, (PAD, 2 * PAIR), 0)
    summing = jnp.where(lane // DH == row, 1.0, 0.0).astype(bf16)
    delta = dot_nt(summing, jnp.concatenate([high, rest], axis=1))

    def place(slot, t):
        start, length = SLOTS[slot]
        row = start + t * TILE
        return start, length, slice(row, row + TILE)

    def spot(slot, t):
        start, length = SLOTS[slot]
        row = start + length - (t + 1) * TILE
        return slice(row, row + TILE)

    def open_unit(slot, t):
        start, length, rows = place(slot, t)
        both = jnp.concatenate([k_ref[rows, :], v_ref[rows, :]], axis=1)
        both = dot_nn(anti, both).astype(bf16)
        turned_scr[spot(slot, t), :] = both[:, :PAIR]
        return dot_nt(each_head(both[:, PAIR:]), g_ref[start : start + length, :])

    def raw_unit(slot, t, grad_prob):
        start, length, rows = place(slot, t)
        spreads = []
        for member in range(2):
            prob = prob_block((p1_ref, p2_ref, p3_ref), slot, t, member)[...].astype(f32)
            mine = grad_prob[member * TILE : (member + 1) * TILE]
            raw = (prob * (mine - delta[member : member + 1, start : start + length])).astype(bf16)
            grad_scr[member, spot(slot, t), :length] = raw
            spreads.append(unskew(raw.astype(f32), length).astype(bf16))
        return jnp.concatenate(spreads, axis=0)

    def key_unit(slot, t, spread):
        start, length, rows = place(slot, t)
        low = LEN3 - TILE - TILE * t
        window = slice(low, low + length + TILE)
        here = slice(start, start + length)
        raw = jnp.concatenate(
            [grad_scr[member, spot(slot, t), :length] for member in range(2)], axis=0
        )
        probs = jnp.concatenate(
            [prob_block((p1_ref, p2_ref, p3_ref), slot, t, member)[...] for member in range(2)],
            axis=0,
        )
        key_grad = dot_nn(
            jnp.concatenate([raw, spread], axis=1),
            jnp.concatenate([q_ref[here, :], eq_ref[window, :]], axis=0),
        )
        value_grad = dot_nn(probs, g_ref[here, :])
        both = jnp.concatenate([own_lanes(key_grad) * factor, own_lanes(value_grad)], axis=1)
        both = dot_nn(anti, both.astype(bf16)).astype(bf16)
        gk_ref[rows, :] = both[:, :PAIR]
        gv_ref[rows, :] = both[:, PAIR:]
        geq_scr[:, window] += dot_tn(each_head(turned_scr[spot(slot, t), :]), spread)

    def turn_unit(slot, t):
        start, length, rows = place(slot, t)
        raws, spreads = [], []
        for member in range(2):
            raw = grad_scr[member, start : start + length, t * TILE : (t + 1) * TILE].T
            raws.append(raw)
            spreads.append(unskew(raw.astype(f32), length).astype(bf16))
        return jnp.concatenate(raws, axis=0), jnp.concatenate(spreads, axis=0)

    def query_unit(slot, t, raw, spread):
        start, length, rows = place(slot, t)
        low = LEN3 - length + TILE * t
        window = slice(low, low + length + TILE)
        query_grad = dot_nn(
            jnp.concatenate([raw, spread], axis=1),
            jnp.concatenate(
                [turned_scr[start : start + length, :], fk_ref[window, :]], axis=0
            ),
        )
        gq_ref[rows, :] = (own_lanes(query_grad) * factor).astype(bf16)
        gfk_scr[:, window] += dot_tn(each_head(q_ref[rows, :]), spread)

    first, second = slot_tiles(3), slot_tiles(2) + slot_tiles(1) + slot_tiles(0)
    jobs = [("key", unit) for unit in first]
    for one, other in zip(second, first):
        jobs += [("key", one), ("query", other)]
    jobs += [("query", unit) for unit in second]
    held = {}
    for at in range(len(jobs) + 2):
        if at < len(jobs):
            kind, unit = jobs[at]
            held[at] = open_unit(*unit) if kind == "key" else None
        if 0 <= at - 1 < len(jobs):
            kind, unit = jobs[at - 1]
            if kind == "key":
                held[at - 1] = raw_unit(*unit, held[at - 1])
            else:
                held[at - 1] = turn_unit(*unit)
        if 0 <= at - 2 < len(jobs):
            kind, unit = jobs[at - 2]
            if kind == "key":
                key_unit(*unit, held.pop(at - 2))
            else:
                query_unit(*unit, *held.pop(at - 2))
    geq_ref[...] = (geq_scr[...] * factor).astype(bf16)
    gfk_ref[...] = (gfk_scr[...] * factor).astype(bf16)


def attend_backward(q, k, v, g, context, eq, fk, p1, p2, p3):
    return pl.pallas_call(
        backward_kernel,
        grid=(H // 2,),
        in_specs=[PAIR_SPEC] * 7 + PROB_SPECS,
        out_specs=[PAIR_SPEC] * 3 + [TABLE_SPEC] * 2,
        out_shape=[jax.ShapeDtypeStruct((ROWS, D), bf16)] * 3
        + [jax.ShapeDtypeStruct((D, OFFSETS), bf16)] * 2,
        scratch_shapes=[
            pltpu.VMEM((2, ROWS, LEN3), bf16),
            pltpu.VMEM((ROWS, PAIR), bf16),
            pltpu.VMEM((PAIR, OFFSETS), f32),
            pltpu.VMEM((PAIR, OFFSETS), f32),
        ],
        compiler_params=pltpu.CompilerParams(vmem_limit_bytes=MEMORY),
        name="attention_backward",
    )(q, k, v, g, context, eq, fk, p1, p2, p3)


def gelu_pair(hidden):
    z = jnp.abs(hidden) * 0.7071067811865476
    t = 1.0 / (1.0 + 0.3275911 * z)
    poly = t * (
        0.127414796
        + t * (-0.142248368 + t * (0.7107068705 + t * (-0.7265760135 + t * 0.5307027145)))
    )
    bell = jnp.exp(-z * z)
    tail = poly * bell
    below = jnp.where(hidden >= 0, 1.0 - tail, tail)
    return hidden * below, below + hidden * (bell * 0.3989422804014327)


def norm_forward(values, gain, shift):
    centered = values - jnp.mean(values, axis=1, keepdims=True)
    inverse = lax.rsqrt(jnp.mean(centered * centered, axis=1, keepdims=True) + norm_epsilon)
    normal = centered * inverse
    return (normal * gain + shift, normal, inverse)


def norm_backward(grad_out, normal, inverse, gain):
    scaled = grad_out * gain
    return inverse * (
        scaled
        - jnp.mean(scaled, axis=1, keepdims=True)
        - normal * jnp.mean(scaled * normal, axis=1, keepdims=True)
    )


def middle_kernel(
    lengths_ref,
    counts_ref,
    tokens_ref,
    context_ref,
    out_grad_ref,
    weight_ref,
    packed_ref,
    factor_ref,
    scale_ref,
    gain_one_ref,
    shift_one_ref,
    gain_two_ref,
    shift_two_ref,
    mixed_ref,
    grad_one_ref,
    context_grad_ref,
    small_ref,
    hidden_ref,
    scale_grad_ref,
    active_scr,
    slope_scr,
):
    step = pl.program_id(0)
    chunks = packed_ref.shape[0]

    @pl.when(step == 0)
    def _():
        small_ref[...] = jnp.zeros_like(small_ref)
        hidden_ref[...] = jnp.zeros_like(hidden_ref)
        scale_grad_ref[...] = jnp.zeros_like(scale_grad_ref)

    row = lax.broadcasted_iota(jnp.int32, (BLOCK, 1), 0) + step * BLOCK
    live = jnp.zeros((BLOCK, 1), f32)
    for (start, length), used in zip(SLOTS, live_counts(lengths_ref, counts_ref)):
        live = jnp.where((row >= start) & (row < start + used), 1.0, live)
    gain_one, shift_one, gain_two, shift_two = (
        ref[...].reshape(1, D)
        for ref in (gain_one_ref, shift_one_ref, gain_two_ref, shift_two_ref)
    )

    context = context_ref[...]
    weight = weight_ref[0]
    attended = dot_nn(context, weight)
    normed, normal_one, inverse_one = norm_forward(
        tokens_ref[...].astype(f32) + attended, gain_one, shift_one
    )
    normed_low = normed.astype(bf16)
    mlp = jnp.zeros((BLOCK, D), f32)
    back_coeff = jnp.zeros((PAD, BLOCK), f32)
    for c in range(chunks):
        hidden = dot_nn(normed_low, packed_ref[c, :D, :])
        active, slope = gelu_pair(hidden)
        active = active.astype(bf16)
        active_scr[c] = active
        slope_scr[c] = slope
        mlp = mlp + dot_nn(active, packed_ref[c, D : 2 * D, :])
        back_coeff = back_coeff + dot_nt(packed_ref[c, 2 * D + PAD : 2 * D + 2 * PAD, :], active)
    result, normal_two, inverse_two = norm_forward(normed + mlp, gain_two, shift_two)
    mixed_ref[...] = (result * live).astype(bf16)
    grad_two = norm_backward(
        out_grad_ref[...].astype(f32) * live, normal_two, inverse_two, gain_two
    )
    grad_mlp = grad_two.astype(bf16)

    back_slope = dot_nt(factor_ref[9], grad_mlp)
    small_ref[3] += add_parts(dot_nn(two_parts(back_coeff * scale_ref[:, 5:6]), grad_mlp))
    scale_grad_ref[:, 5:6] += jnp.sum(back_coeff * back_slope, axis=1, keepdims=True)
    back_through = two_parts(back_slope * scale_ref[:, 5:6])
    in_coeff = dot_nt(factor_ref[4], normed_low)
    in_scaled = two_parts(in_coeff * scale_ref[:, 4:5])
    in_slope = jnp.zeros((PAD, BLOCK), f32)
    grad_normed = grad_two
    for c in range(chunks):
        grad_active = dot_nt(grad_mlp, packed_ref[c, D : 2 * D, :])
        grad_hidden = (grad_active * slope_scr[c]).astype(bf16)
        grad_normed = grad_normed + dot_nt(grad_hidden, packed_ref[c, :D, :])
        in_slope = in_slope + dot_nt(packed_ref[c, 2 * D : 2 * D + PAD, :], grad_hidden)
        hidden_ref[c] += add_parts(dot_nn(in_scaled, grad_hidden))
        hidden_ref[chunks + c] += add_parts(dot_nn(back_through, active_scr[c]))
    scale_grad_ref[:, 4:5] += jnp.sum(in_coeff * in_slope, axis=1, keepdims=True)
    small_ref[2] += add_parts(dot_nn(two_parts(in_slope * scale_ref[:, 4:5]), normed_low))

    grad_one = norm_backward(grad_normed, normal_one, inverse_one, gain_one)
    grad_one_ref[...] = grad_one
    grad_attended = grad_one.astype(bf16)
    context_grad_ref[...] = dot_nt(grad_attended, weight).astype(bf16)
    out_coeff = dot_nt(factor_ref[3], context)
    out_slope = dot_nt(factor_ref[8], grad_attended)
    small_ref[1] += add_parts(dot_nn(two_parts(out_coeff * scale_ref[:, 3:4]), grad_attended))
    small_ref[0] += add_parts(dot_nn(two_parts(out_slope * scale_ref[:, 3:4]), context))
    scale_grad_ref[:, 3:4] += jnp.sum(out_coeff * out_slope, axis=1, keepdims=True)


def middle(lengths, counts, tokens, context, out_grad, weights, packed, factors, scales, norms):
    chunks = packed.shape[0]
    tile = pl.BlockSpec((BLOCK, D), lambda i: (i, 0))
    return pl.pallas_call(
        middle_kernel,
        grid=(ROWS // BLOCK,),
        in_specs=[pl.BlockSpec(memory_space=pltpu.SMEM)] * 2
        + [tile] * 3
        + [
            pl.BlockSpec((1, D, D), lambda i: (3, 0, 0)),
            pl.BlockSpec(
                (chunks, PACKED, D), lambda i: (0, 0, 0), pipeline_mode=pl.Buffered(1)
            ),
            whole(12, PAD, D),
            whole(PAD, 128),
        ]
        + [whole(D)] * 4,
        out_specs=[tile] * 3
        + [whole(4, PAD, D), whole(2 * chunks, PAD, D), whole(PAD, 128)],
        out_shape=[
            jax.ShapeDtypeStruct((ROWS, D), bf16),
            jax.ShapeDtypeStruct((ROWS, D), f32),
            jax.ShapeDtypeStruct((ROWS, D), bf16),
            jax.ShapeDtypeStruct((4, PAD, D), f32),
            jax.ShapeDtypeStruct((2 * chunks, PAD, D), f32),
            jax.ShapeDtypeStruct((PAD, 128), f32),
        ],
        scratch_shapes=[
            pltpu.VMEM((chunks, BLOCK, D), bf16),
            pltpu.VMEM((chunks, BLOCK, D), f32),
        ],
        compiler_params=pltpu.CompilerParams(vmem_limit_bytes=MEMORY),
        name="middle",
    )(lengths, counts, tokens, context, out_grad, weights, packed, factors, scales, *norms)


def devices():
    return lax.axis_size("dp") * lax.axis_size("tensor")


def hidden_rows():
    tiles = 2 * BLOCKS
    return PAD * -(-tiles // lax.axis_size("dp"))


def last_kernel(
    tokens_ref,
    gq_ref,
    gk_ref,
    gv_ref,
    grad_one_ref,
    coeff_ref,
    merged_ref,
    index_ref,
    rel_coeff_ref,
    factor_ref,
    scale_ref,
    small_ref,
    hidden_ref,
    middle_scale_ref,
    rel_any,
    geq_any,
    gfk_any,
    in_grad_ref,
    down_out,
    up_out,
    hidden_up_out,
    hidden_down_out,
    scale_out,
    rel_scr,
    geq_scr,
    gfk_scr,
    down_scr,
    up_scr,
    scale_scr,
    stage_scr,
    mine_late,
    land_late,
    mine_small,
    land_small,
    mine_hidden,
    land_hidden,
    all_sums,
    all_hidden,
    load_sem,
    late_out_sem,
    late_in_sem,
    small_out_sem,
    small_in_sem,
    hidden_out_sem,
    hidden_in_sem,
    sums_out_sem,
    sums_in_sem,
    spread_out_sem,
    spread_in_sem,
):
    step = pl.program_id(0)
    final = ROWS // BLOCK - 1
    outer = lax.axis_size("dp")
    inner = lax.axis_size("tensor")
    count = outer * inner
    my_outer = lax.axis_index("dp")
    my_inner = lax.axis_index("tensor")
    me = my_outer * inner + my_inner
    barrier = pltpu.get_barrier_semaphore()

    def partner(off):
        other = lax.rem(me + off, count)
        return other, other // inner, lax.rem(other, inner)

    def send(src, dst, out_sem, in_sem, place):
        return pltpu.make_async_remote_copy(
            src_ref=src,
            dst_ref=dst,
            send_sem=out_sem,
            recv_sem=in_sem,
            device_id=place,
            device_id_type=MESH,
        )

    def late(off):
        other, row, col = partner(off)
        return send(
            mine_late.at[other],
            land_late.at[off],
            late_out_sem.at[off],
            late_in_sem.at[off],
            (row, col),
        )

    def small(off):
        other, row, col = partner(off)
        return send(
            mine_small.at[other],
            land_small.at[off],
            small_out_sem.at[off],
            small_in_sem.at[off],
            (row, col),
        )

    def hidden(off):
        other, row, col = partner(off)
        return send(
            mine_hidden.at[col, row],
            land_hidden.at[off],
            hidden_out_sem.at[off],
            hidden_in_sem.at[off],
            (row, col),
        )

    def sums(off, origin):
        other, row, col = partner(off)
        return send(
            all_sums.at[origin],
            all_sums.at[origin],
            sums_out_sem.at[off],
            sums_in_sem.at[off],
            (row, col),
        )

    def spread(off, origin):
        return send(
            all_hidden.at[origin],
            all_hidden.at[origin],
            spread_out_sem.at[off],
            spread_in_sem.at[off],
            (lax.rem(my_outer + off, outer), my_inner),
        )

    def load(number, src, dst):
        return pltpu.make_async_copy(src, dst, load_sem.at[number])

    loads = ((0, rel_any, rel_scr), (1, geq_any, geq_scr), (2, gfk_any, gfk_scr))

    @pl.when(step == 0)
    def _():
        for piece in loads:
            load(*piece).start()

        @pl.loop(1, count)
        def _(off):
            _, row, col = partner(off)
            pl.semaphore_signal(barrier, inc=1, device_id=(row, col), device_id_type=MESH)

        scale_scr[...] = jnp.zeros_like(scale_scr)
        down_scr[...] = jnp.zeros_like(down_scr)
        up_scr[...] = jnp.zeros_like(up_scr)

    @pl.when(step == 1)
    def _():
        if count > 4 * BLOCKS:
            mine_small[4 * BLOCKS :] = jnp.zeros((count - 4 * BLOCKS, PAD, LANES), bf16)
        for number in range(4):
            for block in range(BLOCKS):
                mine_small[number * BLOCKS + block] = small_ref[
                    number, :, block * LANES : (block + 1) * LANES
                ].astype(bf16)
        mine_hidden[...] = jnp.zeros_like(mine_hidden)
        tiles = mine_hidden.shape[2] // PAD
        for chunk in range(inner):
            for which in range(2):
                for block in range(BLOCKS):
                    tile = which * BLOCKS + block
                    at = tile % tiles * PAD
                    mine_hidden[chunk, tile // tiles, at : at + PAD] = hidden_ref[
                        which * inner + chunk, :, block * LANES : (block + 1) * LANES
                    ].astype(bf16)
        pl.semaphore_wait(barrier, count - 1)

        @pl.loop(1, count)
        def _(off):
            small(off).start()
            hidden(off).start()

        land_small[0] = mine_small[me]
        land_hidden[0] = mine_hidden[my_inner, my_outer]

    @pl.when(step == 2)
    def _():
        for piece in loads:
            load(*piece).wait()
        rel = rel_scr[...]
        bucket = lax.broadcasted_iota(jnp.int32, (2 * SPAN, OFFSETS), 0)
        for member, ref, row in ((0, geq_scr, 0), (1, gfk_scr, 1)):
            scale = scale_ref[:, member : member + 1]
            chosen = jnp.where(bucket == index_ref[row : row + 1, :], 1.0, 0.0).astype(bf16)
            grad = dot_nt(ref[...], chosen).astype(bf16)
            coeff = rel_coeff_ref[member]
            slope = dot_nn(factor_ref[5 + member], grad)
            up_scr[member] += add_parts(dot_nt(two_parts(coeff * scale), grad))
            down_scr[member] += add_parts(dot_nn(two_parts(slope * scale), rel))
            scale_scr[:, member : member + 1] += jnp.sum(coeff * slope, axis=1, keepdims=True)

    tokens = tokens_ref[...]
    in_grad = grad_one_ref[...]
    for member, ref in enumerate((gq_ref, gk_ref, gv_ref)):
        grad = ref[...]
        scale = scale_ref[:, member : member + 1]
        in_grad = in_grad + dot_nt(grad, merged_ref[member])
        coeff = coeff_ref[member]
        slope = dot_nt(factor_ref[5 + member], grad)
        up_scr[member] += add_parts(dot_nn(two_parts(coeff * scale), grad))
        down_scr[member] += add_parts(dot_nn(two_parts(slope * scale), tokens))
        scale_scr[:, member : member + 1] += jnp.sum(coeff * slope, axis=1, keepdims=True)
    in_grad_ref[...] = in_grad

    @pl.when(step == final)
    def _():
        used = 2 * 3 * BLOCKS * RANK
        for number in range(6):
            ref = down_scr if number < 3 else up_scr
            for block in range(BLOCKS):
                at = (number * BLOCKS + block) * RANK
                stage_scr[at : at + RANK, :] = ref[
                    number % 3, :RANK, block * LANES : (block + 1) * LANES
                ]
        stage_scr[used : used + PAD, :] = scale_scr[...] + middle_scale_ref[...]
        stage_scr[used + PAD :, :] = jnp.zeros((count * PAD - used - PAD, LANES), f32)
        mine_late[...] = stage_scr[...].astype(bf16).reshape(count, PAD, LANES)

        @pl.loop(1, count)
        def _(off):
            late(off).start()

        land_late[0] = mine_late[me]

        @pl.loop(1, count)
        def _(off):
            small(off).wait_recv()
            hidden(off).wait_recv()

        all_hidden[my_outer] = jnp.sum(land_hidden[...].astype(f32), axis=0).astype(bf16)

        @pl.loop(1, outer)
        def _(off):
            spread(off, my_outer).start()

        all_sums[me, PAD:] = jnp.sum(land_small[...].astype(f32), axis=0).astype(bf16)

        @pl.loop(1, count)
        def _(off):
            late(off).wait_recv()

        all_sums[me, :PAD] = jnp.sum(land_late[...].astype(f32), axis=0).astype(bf16)

        @pl.loop(1, count)
        def _(off):
            sums(off, me).start()

        @pl.loop(1, outer)
        def _(off):
            spread(off, lax.rem(my_outer + outer - off, outer)).wait_recv()

        tiles = all_hidden.shape[1] // PAD
        for which in range(2):
            for block in range(BLOCKS):
                tile = which * BLOCKS + block
                at = tile % tiles * PAD
                out = (hidden_up_out, hidden_down_out)[which]
                out[:, block * LANES : (block + 1) * LANES] = all_hidden[
                    tile // tiles, at : at + PAD
                ].astype(f32)[:RANK]

        @pl.loop(1, count)
        def _(off):
            sums(off, lax.rem(me + count - off, count)).wait_recv()

        stage_scr[...] = all_sums[:, :PAD].astype(f32).reshape(count * PAD, LANES)
        for number in range(6):
            ref = down_out if number < 3 else up_out
            for block in range(BLOCKS):
                at = (number * BLOCKS + block) * RANK
                ref[number % 3, :, block * LANES : (block + 1) * LANES] = stage_scr[
                    at : at + RANK, :
                ]
        scale_out[...] = stage_scr[used : used + PAD, :].T[:6, :RANK]
        for number, (ref, place) in enumerate(
            ((down_out, 3), (up_out, 3), (down_out, 4), (up_out, 4))
        ):
            for block in range(BLOCKS):
                ref[place, :, block * LANES : (block + 1) * LANES] = all_sums[
                    number * BLOCKS + block, PAD:
                ].astype(f32)[:RANK]

        @pl.loop(1, count)
        def _(off):
            small(off).wait_send()
            hidden(off).wait_send()
            late(off).wait_send()
            sums(off, me).wait_send()

        @pl.loop(1, outer)
        def _(off):
            spread(off, my_outer).wait_send()


def last(
    tokens, gq, gk, gv, grad_one, coeff, weights, index, rel_coeff, factors, scales,
    small, hidden, middle_scale, rel, geq, gfk,
):
    count = devices()
    outer = lax.axis_size("dp")
    inner = lax.axis_size("tensor")
    piece = hidden_rows()
    tile = pl.BlockSpec((BLOCK, D), lambda i: (i, 0))
    factor = jax.ShapeDtypeStruct((5, RANK, D), f32)
    block = pltpu.VMEM((count, PAD, LANES), bf16)
    all_pairs = pltpu.SemaphoreType.DMA((count,))
    return pl.pallas_call(
        last_kernel,
        grid=(ROWS // BLOCK,),
        in_specs=[tile] * 5
        + [
            pl.BlockSpec((3, PAD, BLOCK), lambda i: (0, 0, i)),
            whole(3, D, D),
            whole(2, OFFSETS),
            whole(2, PAD, 2 * SPAN),
            whole(12, PAD, D),
            whole(PAD, LANES),
            whole(4, PAD, D),
            whole(2 * inner, PAD, D),
            whole(PAD, LANES),
        ]
        + [pl.BlockSpec(memory_space=pl.ANY)] * 3,
        out_specs=[
            tile,
            whole(5, RANK, D),
            whole(5, RANK, D),
            whole(RANK, D),
            whole(RANK, D),
            whole(6, RANK),
        ],
        out_shape=[
            jax.ShapeDtypeStruct((ROWS, D), f32),
            factor,
            factor,
            jax.ShapeDtypeStruct((RANK, D), f32),
            jax.ShapeDtypeStruct((RANK, D), f32),
            jax.ShapeDtypeStruct((6, RANK), f32),
        ],
        scratch_shapes=[
            pltpu.VMEM((2 * SPAN, D), bf16),
            pltpu.VMEM((D, OFFSETS), bf16),
            pltpu.VMEM((D, OFFSETS), bf16),
            pltpu.VMEM((3, PAD, D), f32),
            pltpu.VMEM((3, PAD, D), f32),
            pltpu.VMEM((PAD, LANES), f32),
            pltpu.VMEM((count * PAD, LANES), f32),
            block,
            block,
            block,
            block,
            pltpu.VMEM((inner, outer, piece, LANES), bf16),
            pltpu.VMEM((count, piece, LANES), bf16),
            pltpu.VMEM((count, 2 * PAD, LANES), bf16),
            pltpu.VMEM((outer, piece, LANES), bf16),
            pltpu.SemaphoreType.DMA((3,)),
        ]
        + [all_pairs] * 8
        + [pltpu.SemaphoreType.DMA((outer,))] * 2,
        compiler_params=pltpu.CompilerParams(
            collective_id=0, has_side_effects=True, vmem_limit_bytes=MEMORY
        ),
        name="last",
    )(
        tokens, gq, gk, gv, grad_one, coeff, weights, index, rel_coeff, factors, scales,
        small, hidden, middle_scale, rel, geq, gfk,
    )


def on_device(
    tokens,
    qkv_weight,
    out_weight,
    in_weight,
    back_weight,
    rel_embed,
    gain_one,
    shift_one,
    gain_two,
    shift_two,
    adapt_down,
    adapt_up,
    hidden_up,
    hidden_down,
    adapt_scale,
    seq_lengths,
    seq_counts,
    rel_bucket,
    out_grad,
):
    index_rows = jnp.pad(
        jnp.stack([rel_bucket[::-1], rel_bucket]), ((0, 0), (0, 1)), constant_values=-1
    )
    norms = (gain_one, shift_one, gain_two, shift_two)
    q, k, v, eq, fk, ekt, eqt, weights, packed, coeff, rel_coeff, factors, scales = project(
        tokens, qkv_weight, rel_embed, index_rows, adapt_down, adapt_up, hidden_up, hidden_down,
        adapt_scale, out_weight, in_weight, back_weight,
    )
    context, p1, p2, p3, gathered = attend_forward(
        seq_lengths, seq_counts, q, k, v, ekt, eqt, packed
    )
    mixed, grad_one, context_grad, small, hidden, middle_scale = middle(
        seq_lengths, seq_counts, tokens, context, out_grad, weights, gathered, factors, scales, norms
    )
    gq, gk, gv, geq, gfk = attend_backward(
        q, k, v, context_grad, context, eq, fk, p1, p2, p3
    )
    in_grad, down_grad, up_grad, hidden_up_grad, hidden_down_grad, scale_grad = last(
        tokens, gq, gk, gv, grad_one, coeff, weights, index_rows, rel_coeff, factors, scales,
        small, hidden, middle_scale, rel_embed, geq, gfk,
    )
    return (mixed, in_grad, down_grad, up_grad, hidden_up_grad, hidden_down_grad, scale_grad)


def solution(mesh):
    rows = P(("dp", "tensor"), None)
    return jax.shard_map(
        on_device,
        mesh=mesh,
        in_specs=(
            rows,
            P(),
            P(),
            P(None, "tensor"),
            P("tensor", None),
            P(),
            P(),
            P(),
            P(),
            P(),
            P(),
            P(),
            P(None, "tensor"),
            P(None, "tensor"),
            P(),
            rows,
            rows,
            P(),
            rows,
        ),
        out_specs=(rows, rows, P(), P(), P(None, "tensor"), P(None, "tensor"), P()),
        check_vma=False,
    )
```

```python
import jax
import jax.numpy as jnp
from jax import lax
from jax.experimental import pallas as pl
from jax.experimental.pallas import tpu as pltpu
from jax.sharding import PartitionSpec as P

D = 768
H = 12
DH = 64
PAIR = 2 * DH
SPAN = 256
RANK = 12
PAD = 16
ROWS = 1024
LEN1 = 128
LEN3 = 512
OFFSETS = 2 * LEN3
TILE = 128
BLOCK = 256
SLOTS = ((0, 128), (128, 128), (256, 256), (512, 512))
PACKED = 1600
HALF = PACKED // 2
CHUNK = HALF // 5
TILES = ROWS // BLOCK
SUMMED = 2
WIDE = 1 * BLOCK
LAG = 1
LANES = 128
BLOCKS = D // LANES
MESH = pl.DeviceIdType.MESH
norm_epsilon = 1e-07
masked_score = -1e30
bf16 = jnp.bfloat16
f32 = jnp.float32
MEMORY = 60 * 1024 * 1024


def dot_nn(a, b):
    return jnp.dot(a, b, preferred_element_type=f32)


def dot_nt(a, b):
    return lax.dot_general(a, b, (((1,), (1,)), ((), ())), preferred_element_type=f32)


def dot_tn(a, b):
    return lax.dot_general(a, b, (((0,), (0,)), ((), ())), preferred_element_type=f32)


def two_parts(wide):
    high = wide.astype(bf16)
    rest = (wide - high.astype(f32)).astype(bf16)
    return jnp.concatenate([high, rest], axis=0)


def add_parts(stacked):
    return stacked[:PAD] + stacked[PAD:]


def merged(weight, down, up, scale):
    twice = jnp.concatenate([up, up], axis=0)
    extra = dot_tn(two_parts(down.astype(f32) * scale), twice)
    return (weight.astype(f32) + extra).astype(bf16)


def live_counts(lengths_ref, counts_ref):
    ranks = ((0, 0), (0, 1), (1, 0), (2, 0))
    return [
        jnp.where(rank < counts_ref[0, bucket], lengths_ref[0, slot], 0)
        for slot, (bucket, rank) in enumerate(ranks)
    ]


def padded(rows):
    return jnp.concatenate([rows.astype(f32), jnp.zeros((PAD - RANK, D), f32)], axis=0).astype(bf16)


def whole(*shape):
    return pl.BlockSpec(shape, lambda *at: (0,) * len(shape))


def once(*shape):
    return pl.BlockSpec(shape, lambda *at: (0,) * len(shape), pipeline_mode=pl.Buffered(1))


def unit_matrix(flipped):
    row = lax.broadcasted_iota(jnp.int32, (TILE, TILE), 0)
    col = lax.broadcasted_iota(jnp.int32, (TILE, TILE), 1)
    return jnp.where(row == (TILE - 1 - col if flipped else col), 1.0, 0.0).astype(bf16)


def head_lanes(member):
    lane = lax.broadcasted_iota(jnp.int32, (1, PAIR), 1)
    return jnp.where(lane // DH == member, 1.0, 0.0).astype(bf16)


def each_head(rows):
    return jnp.concatenate([rows * head_lanes(0), rows * head_lanes(1)], axis=0)


def own_lanes(stacked):
    lane = lax.broadcasted_iota(jnp.int32, (TILE, PAIR), 1)
    return jnp.where(lane < DH, stacked[:TILE], stacked[TILE:])


def lane_and_row():
    lane = lax.broadcasted_iota(jnp.int32, (8, 128), 1)
    return lane, lax.broadcasted_iota(jnp.int32, (8, 128), 0)


def turn(block, shift):
    return pltpu.roll(block, shift % 128, 1, stride=1, stride_axis=0)


def skew(table, length):
    lane, row = lane_and_row()
    count = length // 128
    done = []
    for at in range(0, TILE, 8):
        blocks = [table[at : at + 8, 128 * c : 128 * c + 128] for c in range(count + 1)]
        blocks[0] = jnp.where(lane + row >= 127 - at, blocks[0], blocks[count])
        moved = [turn(block, at + 1) for block in blocks[:count]]
        if count > 1:
            inside = lane - row <= at
            moved = [
                jnp.where(inside, moved[c], moved[(c + 1) % count]) for c in range(count)
            ]
        done.append(jnp.concatenate(moved, axis=1))
    return jnp.concatenate(done, axis=0)


def flip_rows(block):
    row = lax.broadcasted_iota(jnp.int32, (8, LANES), 0)
    done = []
    for at in range(TILE - 8, -1, -8):
        done.append(
            jnp.concatenate(
                [
                    jnp.take_along_axis(block[at : at + 8, c : c + LANES], 7 - row, axis=0)
                    for c in range(0, block.shape[1], LANES)
                ],
                axis=1,
            )
        )
    return jnp.concatenate(done, axis=0)


def slot_tiles(slot):
    return [(slot, t) for t in range(SLOTS[slot][1] // TILE)]


def prob_block(refs, slot, t, member):
    start, length = SLOTS[slot]
    at = start + t * TILE if length == LEN1 else t * TILE
    ref = refs[{LEN1: 0, LEN3: 2}.get(length, 1)]
    return ref.at[member, at : at + TILE, :]


def unskew(scores, length):
    lane, row = lane_and_row()
    zero = jnp.zeros((8, 128), f32)
    done = []
    for at in range(0, TILE, 8):
        moved = [
            turn(scores[at : at + 8, 128 * c : 128 * c + 128], at) for c in range(length // 128)
        ]
        before = lane - row < at
        done.append(
            jnp.concatenate(
                [jnp.where(before, x, y) for x, y in zip([zero] + moved, moved + [zero])], axis=1
            )
        )
    return jnp.concatenate(done, axis=0)


def gather_moves(packed, gathered, own_sem, sems):
    step = pl.program_id(0)
    d = lax.axis_index("dp")
    t = lax.axis_index("tensor")
    near = t + 1 - 2 * lax.rem(t, 2)
    far = t + 2 - 4 * (t // 2)
    mate = d + 1 - 2 * lax.rem(d, 2)
    half = lax.rem(d, 2)
    chunks = HALF // CHUNK
    near_out, near_in, far_out, far_in, mate_out, mate_in, pass_out, pass_in, late_out, late_in = sems
    barrier = pltpu.get_barrier_semaphore()
    places = ((d, near), (d, far), (mate, t))

    def rows(which, chunk):
        return pl.ds(pl.multiple_of(which * HALF + chunk * CHUNK, PAD), CHUNK)

    def send(src, dst, out_sem, in_sem, place):
        return pltpu.make_async_remote_copy(
            src_ref=src, dst_ref=dst, send_sem=out_sem, recv_sem=in_sem, device_id=place, device_id_type=MESH
        )

    def to_near():
        return send(packed, gathered.at[t], near_out.at[0], near_in.at[0], places[0])

    def to_far(chunk):
        here = rows(half, chunk)
        return send(
            packed.at[here], gathered.at[t, here], far_out.at[chunk], far_in.at[chunk], places[1]
        )

    def onward(which, chunk, out_sems, in_sems, place):
        here = gathered.at[far, rows(which, chunk)]
        return send(here, here, out_sems.at[chunk], in_sems.at[chunk], place)

    def to_mate(chunk):
        return onward(half, chunk, mate_out, mate_in, places[2])

    def pass_near(chunk):
        return onward(half, chunk, pass_out, pass_in, places[0])

    def late_near(chunk):
        return onward(1 - half, chunk, late_out, late_in, places[0])

    def own():
        return pltpu.make_async_copy(packed, gathered.at[t], own_sem.at[0])

    def begin():
        for place in places:
            pl.semaphore_signal(barrier, inc=1, device_id=place, device_id_type=MESH)

    def go_on():
        @pl.when(step == 0)
        def _():
            own().start()
            pl.semaphore_wait(barrier, len(places))
            to_far(0).start()
            to_far(1).start()
            to_near().start()

        for chunk, when in ((2, 2), (3, 4), (4, 5)):

            @pl.when(step == when)
            def _(chunk=chunk):
                to_far(chunk).start()

        @pl.when((step >= TILES) & (step < TILES + chunks))
        def _():
            chunk = step - TILES
            to_far(chunk).wait_recv()
            to_mate(chunk).start()
            pass_near(chunk).start()

        @pl.when((step >= TILES + 2) & (step < TILES + 1 + chunks))
        def _():
            chunk = step - TILES - 2
            to_mate(chunk).wait_recv()
            late_near(chunk).start()

    def finish():
        to_mate(chunks - 1).wait_recv()
        late_near(chunks - 1).start()
        own().wait()
        to_near().wait()
        for chunk in range(chunks):
            pass_near(chunk).wait_recv()
            late_near(chunk).wait_recv()
            to_far(chunk).wait_send()
            to_mate(chunk).wait_send()
            pass_near(chunk).wait_send()
            late_near(chunk).wait_send()

    return begin, go_on, finish


def attend(
    lengths_ref, counts_ref, q_ref, k_ref, v_ref, ek_ref, eq_ref, context_ref, p1_ref, p2_ref, p3_ref,
    shift_scr, score_scr, prob_scr,
):
    eye = unit_matrix(False)
    factor = 1.4426950408889634 * (3.0 * DH) ** -0.5
    counts = live_counts(lengths_ref, counts_ref)
    turned_values = v_ref[...].T
    head_rows = [
        jnp.where(
            lax.broadcasted_iota(jnp.int32, (PAIR, 1), 0) // DH == member, 1.0, 0.0
        ).astype(bf16)
        for member in range(2)
    ]

    def place(slot, t):
        start, length = SLOTS[slot]
        low = LEN3 - TILE - TILE * t
        row = start + t * TILE
        return start, length, slice(row, row + TILE), slice(low, low + length + TILE)

    def shift_unit(slot, t):
        start, length, rows, window = place(slot, t)
        table = dot_nn(each_head(q_ref[rows, :]), ek_ref[:, window])
        for member in range(2):
            shift_scr[member, rows, :length] = skew(
                table[member * TILE : (member + 1) * TILE], length
            ).astype(bf16)

    def score_unit(slot, t):
        start, length, rows, window = place(slot, t)
        keys = each_head(k_ref[rows, :])
        table = dot_nn(keys, eq_ref[:, window])
        queries = q_ref[start : start + length, :]
        live = lax.broadcasted_iota(jnp.int32, (TILE, 1), 0) < counts[slot] - t * TILE
        tops = []
        for member in range(2):
            mine = slice(member * TILE, (member + 1) * TILE)
            left = jnp.concatenate([keys[mine], eye], axis=1)
            shifted = shift_scr[member, start : start + length, t * TILE : (t + 1) * TILE]
            right = jnp.concatenate([queries, shifted], axis=1)
            raw = dot_nt(left, right) + skew(table[mine], length)
            raw = jnp.where(live, raw * factor, masked_score)
            score_scr[member, rows, :length] = raw
            tops.append(jnp.max(raw, axis=0, keepdims=True))
        return tops

    def weight_unit(slot, t, tops):
        start, length, rows, window = place(slot, t)
        sums = []
        for member in range(2):
            weights = jnp.exp2(score_scr[member, rows, :length] - tops[member])
            score_scr[member, rows, :length] = weights
            sums.append(jnp.sum(weights, axis=0, keepdims=True))
        return sums

    def prob_unit(slot, t, inverses):
        start, length, rows, window = place(slot, t)
        for member in range(2):
            prob = score_scr[member, rows, :length] * inverses[member]
            prob_scr[member, rows, :length] = prob.astype(bf16)
            prob_block((p1_ref, p2_ref, p3_ref), slot, t, member)[...] = flip_rows(prob).astype(
                bf16
            )

    def context_unit(slot):
        start, length = SLOTS[slot]
        here = slice(start, start + length)
        left = jnp.concatenate([turned_values[:, here] * rows for rows in head_rows], axis=1)
        right = jnp.concatenate([prob_scr[member, here, :length] for member in range(2)], axis=0)
        context_ref[here, :] = dot_nn(left, right).astype(bf16).T

    def both(function, parts):
        return [function(member_parts) for member_parts in zip(*parts)]

    def largest(parts):
        total = parts[0]
        for part in parts[1:]:
            total = jnp.maximum(total, part)
        return total

    groups = ((3,), (2, 1, 0))
    tiles = [[unit for slot in group for unit in slot_tiles(slot)] for group in groups]
    held = {}

    def settle(slot):
        held[slot] = both(largest, [held.pop(unit) for unit in slot_tiles(slot)])

    def invert(slot):
        total = both(sum, [held.pop(unit) for unit in slot_tiles(slot)])
        held[slot] = [1.0 / part for part in total]

    for unit in tiles[0]:
        shift_unit(*unit)
    for first, second in zip(tiles[0], tiles[1]):
        held[first] = score_unit(*first)
        shift_unit(*second)
    settle(3)
    for first, second in zip(tiles[0], tiles[1]):
        held[second] = score_unit(*second)
        held[first] = weight_unit(*first, held[3])
    invert(3)
    for slot in groups[1]:
        settle(slot)
    for first, second in zip(tiles[0], tiles[1]):
        held[second] = weight_unit(*second, held[second[0]])
        prob_unit(*first, held[3])
    for slot in groups[1]:
        invert(slot)
    context_unit(3)
    for second in tiles[1]:
        prob_unit(*second, held[second[0]])
    for slot in groups[1]:
        context_unit(slot)


def front_kernel(
    lengths_ref,
    counts_ref,
    tokens_ref,
    index_ref,
    down_ref,
    up_ref,
    hidden_up_ref,
    hidden_down_ref,
    adapt_scale_ref,
    in_any,
    back_any,
    qkv_any,
    rel_any,
    out_any,
    eq_ref,
    fk_ref,
    coeff_ref,
    rel_coeff_ref,
    factor_ref,
    scale_ref,
    context_ref,
    p1_ref,
    p2_ref,
    p3_ref,
    q_any,
    k_any,
    v_any,
    merged_any,
    gathered_any,
    q_scr,
    k_scr,
    v_scr,
    ekt_scr,
    eqt_scr,
    merged_scr,
    packed_scr,
    pos_scr,
    in_scr,
    back_scr,
    qkv_scr,
    rel_scr,
    out_scr,
    shift_scr,
    score_scr,
    prob_scr,
    load_sem,
    store_sem,
    own_sem,
    *gather_sems,
):
    step = pl.program_id(0)
    gather_start, gather_step, gather_end = gather_moves(
        packed_scr, gathered_any, own_sem, gather_sems
    )
    loads = [
        pltpu.make_async_copy(src, dst, load_sem.at[number])
        for number, (src, dst) in enumerate(
            (
                (in_any, in_scr),
                (back_any, back_scr),
                (qkv_any, qkv_scr),
                (rel_any, rel_scr),
                (out_any, out_scr),
            )
        )
    ]
    stores = [
        pltpu.make_async_copy(src, dst, store_sem.at[number])
        for number, (src, dst) in enumerate(
            ((q_scr, q_any), (k_scr, k_any), (v_scr, v_any), (merged_scr, merged_any))
        )
    ]

    @pl.when(step == 0)
    def _():
        gather_start()
        for load in loads:
            load.start()
        for number in range(5):
            factor_ref[number] = padded(down_ref[number])
            factor_ref[5 + number] = padded(up_ref[number])
        factor_ref[10] = padded(hidden_up_ref[...])
        factor_ref[11] = padded(hidden_down_ref[...])
        wide = jnp.concatenate([adapt_scale_ref[...], jnp.zeros((6, LANES - RANK), f32)], axis=1)
        wide = jnp.concatenate([wide, jnp.zeros((LANES - 6, LANES), f32)], axis=0)
        scale_ref[...] = wide.T[:PAD]
        packed_scr[2 * D : 2 * D + PAD] = factor_ref[10]
        packed_scr[2 * D + PAD : 2 * D + 2 * PAD] = factor_ref[11]
        packed_scr[2 * D + 2 * PAD :] = jnp.zeros((PACKED - 2 * D - 2 * PAD, D), bf16)
        loads[0].wait()
        packed_scr[:D] = merged(in_scr[...], factor_ref[4], factor_ref[10], scale_ref[:, 4:5])
        loads[1].wait()
        packed_scr[D : 2 * D] = merged(back_scr[...], factor_ref[11], factor_ref[9], scale_ref[:, 5:6])

    gather_step()

    @pl.when(step == 0)
    def _():
        loads[2].wait()
        for member in range(3):
            merged_scr[member] = merged(
                qkv_scr[member],
                factor_ref[member],
                factor_ref[5 + member],
                scale_ref[:, member : member + 1],
            )
        loads[3].wait()
        rel = rel_scr[...]
        for member in range(2):
            pos_scr[member] = dot_nn(rel, merged_scr[member]).astype(bf16)
        coeff = dot_nt(factor_ref[:2].reshape(2 * PAD, D), rel)
        rel_coeff_ref[...] = coeff.reshape(2, PAD, 2 * SPAN)

    @pl.when(step == 1)
    def _():
        loads[4].wait()
        merged_scr[3] = merged(out_scr[...], factor_ref[3], factor_ref[8], scale_ref[:, 3:4])

    @pl.when(step < TILES)
    def _():
        rows = pl.ds(pl.multiple_of(step * BLOCK, BLOCK), BLOCK)
        tokens = tokens_ref[...]
        for member, ref in enumerate((q_scr, k_scr, v_scr)):
            ref[rows, :] = dot_nn(tokens, merged_scr[member]).astype(bf16)
        coeff = dot_nt(factor_ref[:3].reshape(3 * PAD, D), tokens)
        coeff_ref[...] = coeff.reshape(3, PAD, BLOCK)
        bucket = lax.broadcasted_iota(jnp.int32, (2 * SPAN, BLOCK), 0)
        back, forth = (
            jnp.where(bucket == index_ref[row : row + 1, :], 1.0, 0.0).astype(bf16)
            for row in range(2)
        )
        eq_ref[...] = dot_tn(back, pos_scr[0]).astype(bf16)
        fk_ref[...] = dot_tn(forth, pos_scr[1]).astype(bf16)
        ekt_scr[:, rows] = dot_tn(pos_scr[1], back).astype(bf16)
        eqt_scr[:, rows] = dot_tn(pos_scr[0], back).astype(bf16)

    @pl.when(step == TILES)
    def _():
        for store in stores:
            store.start()

    @pl.when(step >= TILES)
    def _():
        lanes = pl.ds(pl.multiple_of((step - TILES) * PAIR, PAIR), PAIR)
        attend(
            lengths_ref,
            counts_ref,
            q_scr.at[:, lanes],
            k_scr.at[:, lanes],
            v_scr.at[:, lanes],
            ekt_scr.at[lanes, :],
            eqt_scr.at[lanes, :],
            context_ref,
            p1_ref,
            p2_ref,
            p3_ref,
            shift_scr,
            score_scr,
            prob_scr,
        )

    @pl.when(step == pl.num_programs(0) - 1)
    def _():
        for store in stores:
            store.wait()
        gather_end()


PAIR_SPEC = pl.BlockSpec((ROWS, PAIR), lambda p: (0, p))
TABLE_SPEC = pl.BlockSpec((PAIR, OFFSETS), lambda p: (p, 0))
PROB_SIZES = ((256, 128), (256, 256), (512, 512))
PROB_SPECS = [pl.BlockSpec((2, *size), lambda p: (p, 0, 0)) for size in PROB_SIZES]


def front(
    lengths, counts, tokens, qkv_weight, rel_embed, index_rows, down, up, hidden_up, hidden_down,
    adapt_scale, out_weight, in_weight, back_weight,
):
    chunks = HALF // CHUNK
    single, several = (pltpu.SemaphoreType.DMA((n,)) for n in (1, chunks))
    inner = lax.axis_size("tensor")
    assert inner == 4 and lax.axis_size("dp") % 2 == 0

    def tile_at(i):
        return jnp.minimum(i, TILES - 1)

    def pair_at(i):
        return jnp.maximum(i - TILES, 0)

    tile = pl.BlockSpec((BLOCK, D), lambda i: (tile_at(i), 0))
    rows = jax.ShapeDtypeStruct((ROWS, D), bf16)
    anywhere = pl.BlockSpec(memory_space=pl.ANY)
    return pl.pallas_call(
        front_kernel,
        grid=(TILES + H // 2,),
        in_specs=[pl.BlockSpec(memory_space=pltpu.SMEM)] * 2
        + [
            tile,
            pl.BlockSpec((2, BLOCK), lambda i: (0, tile_at(i))),
            once(5, RANK, D),
            once(5, RANK, D),
            once(RANK, D),
            once(RANK, D),
            once(6, RANK),
        ]
        + [anywhere] * 5,
        out_specs=[tile] * 2
        + [
            pl.BlockSpec((3, PAD, BLOCK), lambda i: (0, 0, tile_at(i))),
            whole(2, PAD, 2 * SPAN),
            whole(12, PAD, D),
            whole(PAD, LANES),
            pl.BlockSpec((ROWS, PAIR), lambda i: (0, pair_at(i))),
        ]
        + [pl.BlockSpec((2, *size), lambda i: (pair_at(i), 0, 0)) for size in PROB_SIZES]
        + [anywhere] * 5,
        out_shape=[rows] * 2
        + [
            jax.ShapeDtypeStruct((3, PAD, ROWS), f32),
            jax.ShapeDtypeStruct((2, PAD, 2 * SPAN), f32),
            jax.ShapeDtypeStruct((12, PAD, D), bf16),
            jax.ShapeDtypeStruct((PAD, LANES), f32),
            rows,
        ]
        + [jax.ShapeDtypeStruct((H, *size), bf16) for size in PROB_SIZES]
        + [rows] * 3
        + [
            jax.ShapeDtypeStruct((4, D, D), bf16),
            jax.ShapeDtypeStruct((inner, PACKED, D), bf16),
        ],
        scratch_shapes=[pltpu.VMEM((ROWS, D), bf16)] * 3
        + [pltpu.VMEM((D, OFFSETS), bf16)] * 2
        + [
            pltpu.VMEM((4, D, D), bf16),
            pltpu.VMEM((PACKED, D), bf16),
            pltpu.VMEM((2, 2 * SPAN, D), bf16),
            pltpu.VMEM((D, D), bf16),
            pltpu.VMEM((D, D), bf16),
            pltpu.VMEM((3, D, D), bf16),
            pltpu.VMEM((2 * SPAN, D), bf16),
            pltpu.VMEM((D, D), bf16),
            pltpu.VMEM((2, ROWS, LEN3), bf16),
            pltpu.VMEM((2, ROWS, LEN3), f32),
            pltpu.VMEM((2, ROWS, LEN3), bf16),
            pltpu.SemaphoreType.DMA((5,)),
            pltpu.SemaphoreType.DMA((4,)),
            pltpu.SemaphoreType.DMA((1,)),
        ]
        + [single] * 2
        + [several] * 8,
        compiler_params=pltpu.CompilerParams(
            collective_id=1, has_side_effects=True, vmem_limit_bytes=MEMORY
        ),
        name="front",
    )(
        lengths, counts, tokens, index_rows, down, up, hidden_up, hidden_down, adapt_scale,
        in_weight, back_weight, qkv_weight, rel_embed, out_weight,
    )


def backward_kernel(
    q_ref,
    k_ref,
    v_ref,
    g_ref,
    context_ref,
    eq_ref,
    fk_ref,
    p1_ref,
    p2_ref,
    p3_ref,
    gq_ref,
    gk_ref,
    gv_ref,
    geq_ref,
    gfk_ref,
    grad_scr,
    turned_scr,
    geq_scr,
    gfk_scr,
):
    anti = unit_matrix(True)
    factor = (3.0 * DH) ** -0.5
    geq_scr[...] = jnp.zeros_like(geq_scr)
    gfk_scr[...] = jnp.zeros_like(gfk_scr)
    product = g_ref[...].astype(f32) * context_ref[...].astype(f32)
    high = product.astype(bf16)
    rest = (product - high.astype(f32)).astype(bf16)
    lane = lax.broadcasted_iota(jnp.int32, (PAD, 2 * PAIR), 1) % PAIR
    row = lax.broadcasted_iota(jnp.int32, (PAD, 2 * PAIR), 0)
    summing = jnp.where(lane // DH == row, 1.0, 0.0).astype(bf16)
    delta = dot_nt(summing, jnp.concatenate([high, rest], axis=1))

    def place(slot, t):
        start, length = SLOTS[slot]
        row = start + t * TILE
        return start, length, slice(row, row + TILE)

    def spot(slot, t):
        start, length = SLOTS[slot]
        row = start + length - (t + 1) * TILE
        return slice(row, row + TILE)

    def open_unit(slot, t):
        start, length, rows = place(slot, t)
        both = jnp.concatenate([k_ref[rows, :], v_ref[rows, :]], axis=1)
        both = dot_nn(anti, both).astype(bf16)
        turned_scr[spot(slot, t), :] = both[:, :PAIR]
        return dot_nt(each_head(both[:, PAIR:]), g_ref[start : start + length, :])

    def raw_unit(slot, t, grad_prob):
        start, length, rows = place(slot, t)
        spreads = []
        for member in range(2):
            prob = prob_block((p1_ref, p2_ref, p3_ref), slot, t, member)[...].astype(f32)
            mine = grad_prob[member * TILE : (member + 1) * TILE]
            raw = (prob * (mine - delta[member : member + 1, start : start + length])).astype(bf16)
            grad_scr[member, spot(slot, t), :length] = raw
            spreads.append(unskew(raw.astype(f32), length).astype(bf16))
        return jnp.concatenate(spreads, axis=0)

    def key_unit(slot, t, spread):
        start, length, rows = place(slot, t)
        low = LEN3 - TILE - TILE * t
        window = slice(low, low + length + TILE)
        here = slice(start, start + length)
        raw = jnp.concatenate(
            [grad_scr[member, spot(slot, t), :length] for member in range(2)], axis=0
        )
        probs = jnp.concatenate(
            [prob_block((p1_ref, p2_ref, p3_ref), slot, t, member)[...] for member in range(2)],
            axis=0,
        )
        key_grad = dot_nn(
            jnp.concatenate([raw, spread], axis=1),
            jnp.concatenate([q_ref[here, :], eq_ref[window, :]], axis=0),
        )
        value_grad = dot_nn(probs, g_ref[here, :])
        both = jnp.concatenate([own_lanes(key_grad) * factor, own_lanes(value_grad)], axis=1)
        both = dot_nn(anti, both.astype(bf16)).astype(bf16)
        gk_ref[rows, :] = both[:, :PAIR]
        gv_ref[rows, :] = both[:, PAIR:]
        geq_scr[:, window] += dot_tn(each_head(turned_scr[spot(slot, t), :]), spread)

    def turn_unit(slot, t):
        start, length, rows = place(slot, t)
        raws, spreads = [], []
        for member in range(2):
            raw = grad_scr[member, start : start + length, t * TILE : (t + 1) * TILE].T
            raws.append(raw)
            spreads.append(unskew(raw.astype(f32), length).astype(bf16))
        return jnp.concatenate(raws, axis=0), jnp.concatenate(spreads, axis=0)

    def query_unit(slot, t, raw, spread):
        start, length, rows = place(slot, t)
        low = LEN3 - length + TILE * t
        window = slice(low, low + length + TILE)
        query_grad = dot_nn(
            jnp.concatenate([raw, spread], axis=1),
            jnp.concatenate(
                [turned_scr[start : start + length, :], fk_ref[window, :]], axis=0
            ),
        )
        gq_ref[rows, :] = (own_lanes(query_grad) * factor).astype(bf16)
        gfk_scr[:, window] += dot_tn(each_head(q_ref[rows, :]), spread)

    first, second = slot_tiles(3), slot_tiles(2) + slot_tiles(1) + slot_tiles(0)
    jobs = [("key", unit) for unit in first]
    for one, other in zip(second, first):
        jobs += [("key", one), ("query", other)]
    jobs += [("query", unit) for unit in second]
    held = {}
    for at in range(len(jobs) + 2):
        if at < len(jobs):
            kind, unit = jobs[at]
            held[at] = open_unit(*unit) if kind == "key" else None
        if 0 <= at - 1 < len(jobs):
            kind, unit = jobs[at - 1]
            if kind == "key":
                held[at - 1] = raw_unit(*unit, held[at - 1])
            else:
                held[at - 1] = turn_unit(*unit)
        if 0 <= at - 2 < len(jobs):
            kind, unit = jobs[at - 2]
            if kind == "key":
                key_unit(*unit, held.pop(at - 2))
            else:
                query_unit(*unit, *held.pop(at - 2))
    geq_ref[...] = (geq_scr[...] * factor).astype(bf16)
    gfk_ref[...] = (gfk_scr[...] * factor).astype(bf16)


def attend_backward(q, k, v, g, context, eq, fk, p1, p2, p3):
    return pl.pallas_call(
        backward_kernel,
        grid=(H // 2,),
        in_specs=[PAIR_SPEC] * 7 + PROB_SPECS,
        out_specs=[PAIR_SPEC] * 3 + [TABLE_SPEC] * 2,
        out_shape=[jax.ShapeDtypeStruct((ROWS, D), bf16)] * 3
        + [jax.ShapeDtypeStruct((D, OFFSETS), bf16)] * 2,
        scratch_shapes=[
            pltpu.VMEM((2, ROWS, LEN3), bf16),
            pltpu.VMEM((ROWS, PAIR), bf16),
            pltpu.VMEM((PAIR, OFFSETS), f32),
            pltpu.VMEM((PAIR, OFFSETS), f32),
        ],
        compiler_params=pltpu.CompilerParams(vmem_limit_bytes=MEMORY),
        name="attention_backward",
    )(q, k, v, g, context, eq, fk, p1, p2, p3)


def gelu_pair(hidden):
    z = jnp.abs(hidden) * 0.7071067811865476
    t = 1.0 / (1.0 + 0.3275911 * z)
    poly = t * (
        0.127414796
        + t * (-0.142248368 + t * (0.7107068705 + t * (-0.7265760135 + t * 0.5307027145)))
    )
    bell = jnp.exp(-z * z)
    tail = poly * bell
    below = jnp.where(hidden >= 0, 1.0 - tail, tail)
    return hidden * below, below + hidden * (bell * 0.3989422804014327)


def norm_forward(values, gain, shift):
    centered = values - jnp.mean(values, axis=1, keepdims=True)
    inverse = lax.rsqrt(jnp.mean(centered * centered, axis=1, keepdims=True) + norm_epsilon)
    normal = centered * inverse
    return (normal * gain + shift, normal, inverse)


def norm_backward(grad_out, normal, inverse, gain):
    scaled = grad_out * gain
    return inverse * (
        scaled
        - jnp.mean(scaled, axis=1, keepdims=True)
        - normal * jnp.mean(scaled * normal, axis=1, keepdims=True)
    )


def middle_kernel(
    lengths_ref,
    counts_ref,
    tokens_ref,
    context_ref,
    out_grad_ref,
    weight_ref,
    packed_ref,
    factor_ref,
    scale_ref,
    gain_one_ref,
    shift_one_ref,
    gain_two_ref,
    shift_two_ref,
    mixed_ref,
    grad_one_ref,
    context_grad_ref,
    small_ref,
    hidden_ref,
    scale_grad_ref,
    active_scr,
    slope_scr,
):
    step = pl.program_id(0)
    chunks = packed_ref.shape[0]

    @pl.when(step == 0)
    def _():
        small_ref[...] = jnp.zeros_like(small_ref)
        hidden_ref[...] = jnp.zeros_like(hidden_ref)
        scale_grad_ref[...] = jnp.zeros_like(scale_grad_ref)

    gain_one, shift_one, gain_two, shift_two = (
        ref[...].reshape(1, D)
        for ref in (gain_one_ref, shift_one_ref, gain_two_ref, shift_two_ref)
    )
    used_rows = live_counts(lengths_ref, counts_ref)
    weight = weight_ref[0]

    def work(number):
        rows = slice(number * BLOCK, (number + 1) * BLOCK)
        row = lax.broadcasted_iota(jnp.int32, (BLOCK, 1), 0) + step * WIDE + number * BLOCK
        live = jnp.zeros((BLOCK, 1), f32)
        for (start, length), used in zip(SLOTS, used_rows):
            live = jnp.where((row >= start) & (row < start + used), 1.0, live)
        context = context_ref[rows, :]
        attended = dot_nn(context, weight)
        normed, normal_one, inverse_one = norm_forward(
            tokens_ref[rows, :].astype(f32) + attended, gain_one, shift_one
        )
        normed_low = normed.astype(bf16)
        yield
        mlp = jnp.zeros((BLOCK, D), f32)
        back_coeff = jnp.zeros((PAD, BLOCK), f32)
        ahead = dot_nn(normed_low, packed_ref[0, :D, :])
        for c in range(chunks):
            hidden = ahead
            if c + 1 < chunks:
                ahead = dot_nn(normed_low, packed_ref[c + 1, :D, :])
            active, slope = gelu_pair(hidden)
            active = active.astype(bf16)
            active_scr[c, rows, :] = active
            slope_scr[c, rows, :] = slope
            mlp = mlp + dot_nn(active, packed_ref[c, D : 2 * D, :])
            back_coeff = back_coeff + dot_nt(
                packed_ref[c, 2 * D + PAD : 2 * D + 2 * PAD, :], active
            )
            yield
        result, normal_two, inverse_two = norm_forward(normed + mlp, gain_two, shift_two)
        mixed_ref[rows, :] = (result * live).astype(bf16)
        grad_two = norm_backward(
            out_grad_ref[rows, :].astype(f32) * live, normal_two, inverse_two, gain_two
        )
        grad_mlp = grad_two.astype(bf16)
        yield
        back_slope = dot_nt(factor_ref[9], grad_mlp)
        small_ref[3] += add_parts(dot_nn(two_parts(back_coeff * scale_ref[:, 5:6]), grad_mlp))
        scale_grad_ref[:, 5:6] += jnp.sum(back_coeff * back_slope, axis=1, keepdims=True)
        back_through = two_parts(back_slope * scale_ref[:, 5:6])
        in_coeff = dot_nt(factor_ref[4], normed_low)
        in_scaled = two_parts(in_coeff * scale_ref[:, 4:5])
        in_slope = jnp.zeros((PAD, BLOCK), f32)
        grad_normed = grad_two
        ahead = dot_nt(grad_mlp, packed_ref[0, D : 2 * D, :])
        for c in range(chunks):
            grad_active = ahead
            if c + 1 < chunks:
                ahead = dot_nt(grad_mlp, packed_ref[c + 1, D : 2 * D, :])
            grad_hidden = (grad_active * slope_scr[c, rows, :]).astype(bf16)
            grad_normed = grad_normed + dot_nt(grad_hidden, packed_ref[c, :D, :])
            in_slope = in_slope + dot_nt(packed_ref[c, 2 * D : 2 * D + PAD, :], grad_hidden)
            hidden_ref[c] += add_parts(dot_nn(in_scaled, grad_hidden))
            hidden_ref[chunks + c] += add_parts(dot_nn(back_through, active_scr[c, rows, :]))
            yield
        scale_grad_ref[:, 4:5] += jnp.sum(in_coeff * in_slope, axis=1, keepdims=True)
        small_ref[2] += add_parts(dot_nn(two_parts(in_slope * scale_ref[:, 4:5]), normed_low))
        grad_one = norm_backward(grad_normed, normal_one, inverse_one, gain_one)
        grad_one_ref[rows, :] = grad_one
        grad_attended = grad_one.astype(bf16)
        yield
        context_grad_ref[rows, :] = dot_nt(grad_attended, weight).astype(bf16)
        out_coeff = dot_nt(factor_ref[3], context)
        out_slope = dot_nt(factor_ref[8], grad_attended)
        small_ref[1] += add_parts(dot_nn(two_parts(out_coeff * scale_ref[:, 3:4]), grad_attended))
        small_ref[0] += add_parts(dot_nn(two_parts(out_slope * scale_ref[:, 3:4]), context))
        scale_grad_ref[:, 3:4] += jnp.sum(out_coeff * out_slope, axis=1, keepdims=True)

    waiting = [work(number) for number in range(WIDE // BLOCK)]
    running = []
    turn_number = 0
    while waiting or running:
        if waiting and turn_number % LAG == 0:
            running.append(waiting.pop(0))
        turn_number += 1
        for job in list(running):
            try:
                next(job)
            except StopIteration:
                running.remove(job)


def middle(lengths, counts, tokens, context, out_grad, weights, packed, factors, scales, norms):
    chunks = packed.shape[0]
    tile = pl.BlockSpec((WIDE, D), lambda i: (i, 0))
    return pl.pallas_call(
        middle_kernel,
        grid=(ROWS // WIDE,),
        in_specs=[pl.BlockSpec(memory_space=pltpu.SMEM)] * 2
        + [tile] * 3
        + [
            pl.BlockSpec((1, D, D), lambda i: (3, 0, 0)),
            pl.BlockSpec(
                (chunks, PACKED, D), lambda i: (0, 0, 0), pipeline_mode=pl.Buffered(1)
            ),
            whole(12, PAD, D),
            whole(PAD, 128),
        ]
        + [whole(D)] * 4,
        out_specs=[tile] * 3
        + [whole(4, PAD, D), whole(2 * chunks, PAD, D), whole(PAD, 128)],
        out_shape=[
            jax.ShapeDtypeStruct((ROWS, D), bf16),
            jax.ShapeDtypeStruct((ROWS, D), f32),
            jax.ShapeDtypeStruct((ROWS, D), bf16),
            jax.ShapeDtypeStruct((4, PAD, D), f32),
            jax.ShapeDtypeStruct((2 * chunks, PAD, D), f32),
            jax.ShapeDtypeStruct((PAD, 128), f32),
        ],
        scratch_shapes=[
            pltpu.VMEM((chunks, WIDE, D), bf16),
            pltpu.VMEM((chunks, WIDE, D), f32),
        ],
        compiler_params=pltpu.CompilerParams(vmem_limit_bytes=MEMORY),
        name="middle",
    )(lengths, counts, tokens, context, out_grad, weights, packed, factors, scales, *norms)


def devices():
    return lax.axis_size("dp") * lax.axis_size("tensor")


def hidden_rows():
    tiles = 2 * BLOCKS
    return PAD * -(-tiles // lax.axis_size("dp"))


def last_kernel(
    grad_one_ref,
    coeff_ref,
    index_ref,
    rel_coeff_ref,
    factor_ref,
    scale_ref,
    small_ref,
    hidden_ref,
    middle_scale_ref,
    tokens_any,
    gq_any,
    gk_any,
    gv_any,
    rel_any,
    geq_any,
    gfk_any,
    merged_any,
    in_grad_ref,
    down_out,
    up_out,
    hidden_up_out,
    hidden_down_out,
    scale_out,
    tokens_scr,
    grads_scr,
    rel_scr,
    geq_scr,
    gfk_scr,
    merged_scr,
    down_scr,
    up_scr,
    scale_scr,
    stage_scr,
    mine_late,
    land_late,
    mine_small,
    land_small,
    mine_hidden,
    land_hidden,
    all_sums,
    all_hidden,
    load_sem,
    late_out_sem,
    late_in_sem,
    small_out_sem,
    small_in_sem,
    hidden_out_sem,
    hidden_in_sem,
    sums_out_sem,
    sums_in_sem,
    spread_out_sem,
    spread_in_sem,
):
    step = pl.program_id(0)
    final = TILES
    used = 2 * 3 * BLOCKS * RANK
    outer = lax.axis_size("dp")
    inner = lax.axis_size("tensor")
    count = outer * inner
    my_outer = lax.axis_index("dp")
    my_inner = lax.axis_index("tensor")
    me = my_outer * inner + my_inner
    barrier = pltpu.get_barrier_semaphore()

    def partner(off):
        other = lax.rem(me + off, count)
        return other, other // inner, lax.rem(other, inner)

    def send(src, dst, out_sem, in_sem, place):
        return pltpu.make_async_remote_copy(
            src_ref=src,
            dst_ref=dst,
            send_sem=out_sem,
            recv_sem=in_sem,
            device_id=place,
            device_id_type=MESH,
        )

    def late(off):
        other, row, col = partner(off)
        return send(
            mine_late.at[other],
            land_late.at[off],
            late_out_sem.at[off],
            late_in_sem.at[off],
            (row, col),
        )

    def small(off):
        other, row, col = partner(off)
        return send(
            mine_small.at[other],
            land_small.at[off],
            small_out_sem.at[off],
            small_in_sem.at[off],
            (row, col),
        )

    def hidden(off):
        other, row, col = partner(off)
        return send(
            mine_hidden.at[col, row],
            land_hidden.at[off],
            hidden_out_sem.at[off],
            hidden_in_sem.at[off],
            (row, col),
        )

    def sums(off, origin):
        other, row, col = partner(off)
        return send(
            all_sums.at[origin],
            all_sums.at[origin],
            sums_out_sem.at[off],
            sums_in_sem.at[off],
            (row, col),
        )

    def spread(off, origin):
        return send(
            all_hidden.at[origin],
            all_hidden.at[origin],
            spread_out_sem.at[off],
            spread_in_sem.at[off],
            (lax.rem(my_outer + off, outer), my_inner),
        )

    loads = [
        pltpu.make_async_copy(src, dst, load_sem.at[number])
        for number, (src, dst) in enumerate(
            (
                (tokens_any, tokens_scr),
                (gq_any, grads_scr.at[0]),
                (gk_any, grads_scr.at[1]),
                (gv_any, grads_scr.at[2]),
                (rel_any, rel_scr),
                (geq_any, geq_scr),
                (gfk_any, gfk_scr),
                (merged_any.at[pl.ds(0, 3)], merged_scr),
            )
        )
    ]

    @pl.when(step == 0)
    def _():
        for load in loads:
            load.start()

        @pl.loop(1, count)
        def _(off):
            _, row, col = partner(off)
            pl.semaphore_signal(barrier, inc=1, device_id=(row, col), device_id_type=MESH)

        scale_scr[...] = jnp.zeros_like(scale_scr)
        if count > 4 * BLOCKS:
            mine_small[4 * BLOCKS :] = jnp.zeros((count - 4 * BLOCKS, PAD, LANES), bf16)
        for number in range(4):
            for block in range(BLOCKS):
                mine_small[number * BLOCKS + block] = small_ref[
                    number, :, block * LANES : (block + 1) * LANES
                ].astype(bf16)
        mine_hidden[...] = jnp.zeros_like(mine_hidden)
        tiles = mine_hidden.shape[2] // PAD
        for chunk in range(inner):
            for which in range(2):
                for block in range(BLOCKS):
                    tile = which * BLOCKS + block
                    at = tile % tiles * PAD
                    mine_hidden[chunk, tile // tiles, at : at + PAD] = hidden_ref[
                        which * inner + chunk, :, block * LANES : (block + 1) * LANES
                    ].astype(bf16)
        pl.semaphore_wait(barrier, count - 1)

        @pl.loop(1, count)
        def _(off):
            small(off).start()
            hidden(off).start()

        land_small[0] = mine_small[me]
        land_hidden[0] = mine_hidden[my_inner, my_outer]
        loads[0].wait()
        tokens = tokens_scr[...]
        for member in range(3):
            loads[1 + member].wait()
            grad = grads_scr[member]
            scale = scale_ref[:, member : member + 1]
            coeff = coeff_ref[member]
            slope = dot_nt(factor_ref[5 + member], grad)
            up_scr[member] = add_parts(dot_nn(two_parts(coeff * scale), grad))
            down_scr[member] = add_parts(dot_nn(two_parts(slope * scale), tokens))
            scale_scr[:, member : member + 1] += jnp.sum(coeff * slope, axis=1, keepdims=True)
        for load in loads[4:7]:
            load.wait()
        rel = rel_scr[...]
        bucket = lax.broadcasted_iota(jnp.int32, (2 * SPAN, OFFSETS), 0)
        for member, ref, row in ((0, geq_scr, 0), (1, gfk_scr, 1)):
            scale = scale_ref[:, member : member + 1]
            chosen = jnp.where(bucket == index_ref[row : row + 1, :], 1.0, 0.0).astype(bf16)
            grad = dot_nt(ref[...], chosen).astype(bf16)
            coeff = rel_coeff_ref[member]
            slope = dot_nn(factor_ref[5 + member], grad)
            up_scr[member] += add_parts(dot_nt(two_parts(coeff * scale), grad))
            down_scr[member] += add_parts(dot_nn(two_parts(slope * scale), rel))
            scale_scr[:, member : member + 1] += jnp.sum(coeff * slope, axis=1, keepdims=True)
        for number in range(6):
            ref = down_scr if number < 3 else up_scr
            for block in range(BLOCKS):
                at = (number * BLOCKS + block) * RANK
                stage_scr[at : at + RANK, :] = ref[
                    number % 3, :RANK, block * LANES : (block + 1) * LANES
                ]
        stage_scr[used : used + PAD, :] = scale_scr[...] + middle_scale_ref[...]
        stage_scr[used + PAD :, :] = jnp.zeros((count * PAD - used - PAD, LANES), f32)
        mine_late[...] = stage_scr[...].astype(bf16).reshape(count, PAD, LANES)

        @pl.loop(1, count)
        def _(off):
            late(off).start()

        land_late[0] = mine_late[me]
        loads[7].wait()

    @pl.when(step > 0)
    def _():
        rows = pl.ds(pl.multiple_of((step - 1) * BLOCK, BLOCK), BLOCK)
        in_grad = grad_one_ref[...]
        for member in range(3):
            in_grad = in_grad + dot_nt(grads_scr[member, rows, :], merged_scr[member])
        in_grad_ref[...] = in_grad

    @pl.when(step == SUMMED)
    def _():
        @pl.loop(1, count)
        def _(off):
            small(off).wait_recv()
            hidden(off).wait_recv()

        all_hidden[my_outer] = jnp.sum(land_hidden[...].astype(f32), axis=0).astype(bf16)

        @pl.loop(1, outer)
        def _(off):
            spread(off, my_outer).start()

        all_sums[me, PAD:] = jnp.sum(land_small[...].astype(f32), axis=0).astype(bf16)

        @pl.loop(1, count)
        def _(off):
            late(off).wait_recv()

        all_sums[me, :PAD] = jnp.sum(land_late[...].astype(f32), axis=0).astype(bf16)

        @pl.loop(1, count)
        def _(off):
            sums(off, me).start()

    @pl.when(step == final)
    def _():
        @pl.loop(1, outer)
        def _(off):
            spread(off, lax.rem(my_outer + outer - off, outer)).wait_recv()

        tiles = all_hidden.shape[1] // PAD
        for which in range(2):
            for block in range(BLOCKS):
                tile = which * BLOCKS + block
                at = tile % tiles * PAD
                out = (hidden_up_out, hidden_down_out)[which]
                out[:, block * LANES : (block + 1) * LANES] = all_hidden[
                    tile // tiles, at : at + PAD
                ].astype(f32)[:RANK]

        @pl.loop(1, count)
        def _(off):
            sums(off, lax.rem(me + count - off, count)).wait_recv()

        stage_scr[...] = all_sums[:, :PAD].astype(f32).reshape(count * PAD, LANES)
        for number in range(6):
            ref = down_out if number < 3 else up_out
            for block in range(BLOCKS):
                at = (number * BLOCKS + block) * RANK
                ref[number % 3, :, block * LANES : (block + 1) * LANES] = stage_scr[
                    at : at + RANK, :
                ]
        scale_out[...] = stage_scr[used : used + PAD, :].T[:6, :RANK]
        for number, (ref, place) in enumerate(
            ((down_out, 3), (up_out, 3), (down_out, 4), (up_out, 4))
        ):
            for block in range(BLOCKS):
                ref[place, :, block * LANES : (block + 1) * LANES] = all_sums[
                    number * BLOCKS + block, PAD:
                ].astype(f32)[:RANK]

        @pl.loop(1, count)
        def _(off):
            small(off).wait_send()
            hidden(off).wait_send()
            late(off).wait_send()
            sums(off, me).wait_send()

        @pl.loop(1, outer)
        def _(off):
            spread(off, my_outer).wait_send()


def last(
    tokens, gq, gk, gv, grad_one, coeff, weights, index, rel_coeff, factors, scales,
    small, hidden, middle_scale, rel, geq, gfk,
):
    count = devices()
    outer = lax.axis_size("dp")
    inner = lax.axis_size("tensor")
    piece = hidden_rows()
    tile = pl.BlockSpec((BLOCK, D), lambda i: (jnp.maximum(i - 1, 0), 0))
    factor = jax.ShapeDtypeStruct((5, RANK, D), f32)
    block = pltpu.VMEM((count, PAD, LANES), bf16)
    all_pairs = pltpu.SemaphoreType.DMA((count,))
    return pl.pallas_call(
        last_kernel,
        grid=(1 + TILES,),
        in_specs=[
            tile,
            once(3, PAD, ROWS),
            once(2, OFFSETS),
            once(2, PAD, 2 * SPAN),
            once(12, PAD, D),
            once(PAD, LANES),
            once(4, PAD, D),
            once(2 * inner, PAD, D),
            once(PAD, LANES),
        ]
        + [pl.BlockSpec(memory_space=pl.ANY)] * 8,
        out_specs=[
            tile,
            whole(5, RANK, D),
            whole(5, RANK, D),
            whole(RANK, D),
            whole(RANK, D),
            whole(6, RANK),
        ],
        out_shape=[
            jax.ShapeDtypeStruct((ROWS, D), f32),
            factor,
            factor,
            jax.ShapeDtypeStruct((RANK, D), f32),
            jax.ShapeDtypeStruct((RANK, D), f32),
            jax.ShapeDtypeStruct((6, RANK), f32),
        ],
        scratch_shapes=[
            pltpu.VMEM((ROWS, D), bf16),
            pltpu.VMEM((3, ROWS, D), bf16),
            pltpu.VMEM((2 * SPAN, D), bf16),
            pltpu.VMEM((D, OFFSETS), bf16),
            pltpu.VMEM((D, OFFSETS), bf16),
            pltpu.VMEM((3, D, D), bf16),
            pltpu.VMEM((3, PAD, D), f32),
            pltpu.VMEM((3, PAD, D), f32),
            pltpu.VMEM((PAD, LANES), f32),
            pltpu.VMEM((count * PAD, LANES), f32),
            block,
            block,
            block,
            block,
            pltpu.VMEM((inner, outer, piece, LANES), bf16),
            pltpu.VMEM((count, piece, LANES), bf16),
            pltpu.VMEM((count, 2 * PAD, LANES), bf16),
            pltpu.VMEM((outer, piece, LANES), bf16),
            pltpu.SemaphoreType.DMA((8,)),
        ]
        + [all_pairs] * 8
        + [pltpu.SemaphoreType.DMA((outer,))] * 2,
        compiler_params=pltpu.CompilerParams(
            collective_id=0, has_side_effects=True, vmem_limit_bytes=MEMORY
        ),
        name="last",
    )(
        grad_one, coeff, index, rel_coeff, factors, scales, small, hidden, middle_scale,
        tokens, gq, gk, gv, rel, geq, gfk, weights,
    )


def on_device(
    tokens,
    qkv_weight,
    out_weight,
    in_weight,
    back_weight,
    rel_embed,
    gain_one,
    shift_one,
    gain_two,
    shift_two,
    adapt_down,
    adapt_up,
    hidden_up,
    hidden_down,
    adapt_scale,
    seq_lengths,
    seq_counts,
    rel_bucket,
    out_grad,
):
    index_rows = jnp.pad(
        jnp.stack([rel_bucket[::-1], rel_bucket]), ((0, 0), (0, 1)), constant_values=-1
    )
    norms = (gain_one, shift_one, gain_two, shift_two)
    eq, fk, coeff, rel_coeff, factors, scales, context, p1, p2, p3, q, k, v, weights, gathered = front(
        seq_lengths, seq_counts, tokens, qkv_weight, rel_embed, index_rows, adapt_down, adapt_up,
        hidden_up, hidden_down, adapt_scale, out_weight, in_weight, back_weight,
    )
    mixed, grad_one, context_grad, small, hidden, middle_scale = middle(
        seq_lengths, seq_counts, tokens, context, out_grad, weights, gathered, factors, scales, norms
    )
    gq, gk, gv, geq, gfk = attend_backward(
        q, k, v, context_grad, context, eq, fk, p1, p2, p3
    )
    in_grad, down_grad, up_grad, hidden_up_grad, hidden_down_grad, scale_grad = last(
        tokens, gq, gk, gv, grad_one, coeff, weights, index_rows, rel_coeff, factors, scales,
        small, hidden, middle_scale, rel_embed, geq, gfk,
    )
    return (mixed, in_grad, down_grad, up_grad, hidden_up_grad, hidden_down_grad, scale_grad)


def solution(mesh):
    rows = P(("dp", "tensor"), None)
    return jax.shard_map(
        on_device,
        mesh=mesh,
        in_specs=(
            rows,
            P(),
            P(),
            P(None, "tensor"),
            P("tensor", None),
            P(),
            P(),
            P(),
            P(),
            P(),
            P(),
            P(),
            P(None, "tensor"),
            P(None, "tensor"),
            P(),
            rows,
            rows,
            P(),
            rows,
        ),
        out_specs=(rows, rows, P(), P(), P(None, "tensor"), P(None, "tensor"), P()),
        check_vma=False,
    )
```

```python
import jax
import jax.numpy as jnp
from jax import lax
from jax.experimental import pallas as pl
from jax.experimental.pallas import tpu as pltpu
from jax.sharding import PartitionSpec as P

D = 768
H = 12
DH = 64
PAIR = 2 * DH
SPAN = 256
RANK = 12
PAD = 16
ROWS = 1024
LEN1 = 128
LEN3 = 512
OFFSETS = 2 * LEN3
TILE = 128
BLOCK = 256
SLOTS = ((0, 128), (128, 128), (256, 256), (512, 512))
PACKED = 1600
HALF = PACKED // 2
CHUNK = HALF // 5
TILES = ROWS // BLOCK
SUMMED = 2
WIDE = 1 * BLOCK
LAG = 1
LANES = 128
BLOCKS = D // LANES
MESH = pl.DeviceIdType.MESH
norm_epsilon = 1e-07
masked_score = -1e30
bf16 = jnp.bfloat16
f32 = jnp.float32
MEMORY = 60 * 1024 * 1024


def dot_nn(a, b):
    return jnp.dot(a, b, preferred_element_type=f32)


def dot_nt(a, b):
    return lax.dot_general(a, b, (((1,), (1,)), ((), ())), preferred_element_type=f32)


def dot_tn(a, b):
    return lax.dot_general(a, b, (((0,), (0,)), ((), ())), preferred_element_type=f32)


def two_parts(wide):
    high = wide.astype(bf16)
    rest = (wide - high.astype(f32)).astype(bf16)
    return jnp.concatenate([high, rest], axis=0)


def add_parts(stacked):
    return stacked[:PAD] + stacked[PAD:]


def merged(weight, down, up, scale):
    twice = jnp.concatenate([up, up], axis=0)
    extra = dot_tn(two_parts(down.astype(f32) * scale), twice)
    return (weight.astype(f32) + extra).astype(bf16)


def live_counts(lengths_ref, counts_ref):
    ranks = ((0, 0), (0, 1), (1, 0), (2, 0))
    return [
        jnp.where(rank < counts_ref[0, bucket], lengths_ref[0, slot], 0)
        for slot, (bucket, rank) in enumerate(ranks)
    ]


def padded(rows):
    return jnp.concatenate([rows.astype(f32), jnp.zeros((PAD - RANK, D), f32)], axis=0).astype(bf16)


def whole(*shape):
    return pl.BlockSpec(shape, lambda *at: (0,) * len(shape))


def once(*shape):
    return pl.BlockSpec(shape, lambda *at: (0,) * len(shape), pipeline_mode=pl.Buffered(1))


def unit_matrix(flipped):
    row = lax.broadcasted_iota(jnp.int32, (TILE, TILE), 0)
    col = lax.broadcasted_iota(jnp.int32, (TILE, TILE), 1)
    return jnp.where(row == (TILE - 1 - col if flipped else col), 1.0, 0.0).astype(bf16)


def head_lanes(member):
    lane = lax.broadcasted_iota(jnp.int32, (1, PAIR), 1)
    return jnp.where(lane // DH == member, 1.0, 0.0).astype(bf16)


def each_head(rows):
    return jnp.concatenate([rows * head_lanes(0), rows * head_lanes(1)], axis=0)


def own_lanes(stacked):
    lane = lax.broadcasted_iota(jnp.int32, (TILE, PAIR), 1)
    return jnp.where(lane < DH, stacked[:TILE], stacked[TILE:])


def lane_and_row():
    lane = lax.broadcasted_iota(jnp.int32, (8, 128), 1)
    return lane, lax.broadcasted_iota(jnp.int32, (8, 128), 0)


def turn(block, shift):
    return pltpu.roll(block, shift % 128, 1, stride=1, stride_axis=0)


def skew(table, length):
    lane, row = lane_and_row()
    count = length // 128
    done = []
    for at in range(0, TILE, 8):
        blocks = [table[at : at + 8, 128 * c : 128 * c + 128] for c in range(count + 1)]
        blocks[0] = jnp.where(lane + row >= 127 - at, blocks[0], blocks[count])
        moved = [turn(block, at + 1) for block in blocks[:count]]
        if count > 1:
            inside = lane - row <= at
            moved = [
                jnp.where(inside, moved[c], moved[(c + 1) % count]) for c in range(count)
            ]
        done.append(jnp.concatenate(moved, axis=1))
    return jnp.concatenate(done, axis=0)


def flip_rows(block):
    row = lax.broadcasted_iota(jnp.int32, (8, LANES), 0)
    done = []
    for at in range(TILE - 8, -1, -8):
        done.append(
            jnp.concatenate(
                [
                    jnp.take_along_axis(block[at : at + 8, c : c + LANES], 7 - row, axis=0)
                    for c in range(0, block.shape[1], LANES)
                ],
                axis=1,
            )
        )
    return jnp.concatenate(done, axis=0)


def slot_tiles(slot):
    return [(slot, t) for t in range(SLOTS[slot][1] // TILE)]


def prob_block(refs, slot, t, member):
    start, length = SLOTS[slot]
    at = start + t * TILE if length == LEN1 else t * TILE
    ref = refs[{LEN1: 0, LEN3: 2}.get(length, 1)]
    return ref.at[member, at : at + TILE, :]


def unskew(scores, length):
    lane, row = lane_and_row()
    zero = jnp.zeros((8, 128), f32)
    done = []
    for at in range(0, TILE, 8):
        moved = [
            turn(scores[at : at + 8, 128 * c : 128 * c + 128], at) for c in range(length // 128)
        ]
        before = lane - row < at
        done.append(
            jnp.concatenate(
                [jnp.where(before, x, y) for x, y in zip([zero] + moved, moved + [zero])], axis=1
            )
        )
    return jnp.concatenate(done, axis=0)


def gather_moves(packed, gathered, own_sem, sems):
    step = pl.program_id(0)
    d = lax.axis_index("dp")
    t = lax.axis_index("tensor")
    near = t + 1 - 2 * lax.rem(t, 2)
    far = t + 2 - 4 * (t // 2)
    mate = d + 1 - 2 * lax.rem(d, 2)
    half = lax.rem(d, 2)
    chunks = HALF // CHUNK
    near_out, near_in, far_out, far_in, mate_out, mate_in, pass_out, pass_in, late_out, late_in = sems
    barrier = pltpu.get_barrier_semaphore()
    places = ((d, near), (d, far), (mate, t))

    def rows(which, chunk):
        return pl.ds(pl.multiple_of(which * HALF + chunk * CHUNK, PAD), CHUNK)

    def send(src, dst, out_sem, in_sem, place):
        return pltpu.make_async_remote_copy(
            src_ref=src, dst_ref=dst, send_sem=out_sem, recv_sem=in_sem, device_id=place, device_id_type=MESH
        )

    def to_near():
        return send(packed, gathered.at[t], near_out.at[0], near_in.at[0], places[0])

    def to_far(chunk):
        here = rows(half, chunk)
        return send(
            packed.at[here], gathered.at[t, here], far_out.at[chunk], far_in.at[chunk], places[1]
        )

    def onward(which, chunk, out_sems, in_sems, place):
        here = gathered.at[far, rows(which, chunk)]
        return send(here, here, out_sems.at[chunk], in_sems.at[chunk], place)

    def to_mate(chunk):
        return onward(half, chunk, mate_out, mate_in, places[2])

    def pass_near(chunk):
        return onward(half, chunk, pass_out, pass_in, places[0])

    def late_near(chunk):
        return onward(1 - half, chunk, late_out, late_in, places[0])

    def own():
        return pltpu.make_async_copy(packed, gathered.at[t], own_sem.at[0])

    def begin():
        for place in places:
            pl.semaphore_signal(barrier, inc=1, device_id=place, device_id_type=MESH)

    def go_on():
        @pl.when(step == 0)
        def _():
            own().start()
            pl.semaphore_wait(barrier, len(places))
            to_far(0).start()
            to_far(1).start()
            to_near().start()

        for chunk, when in ((2, 2), (3, 4), (4, 5)):

            @pl.when(step == when)
            def _(chunk=chunk):
                to_far(chunk).start()

        @pl.when((step >= TILES) & (step < TILES + chunks))
        def _():
            chunk = step - TILES
            to_far(chunk).wait_recv()
            to_mate(chunk).start()
            pass_near(chunk).start()

        @pl.when((step >= TILES + 2) & (step < TILES + 1 + chunks))
        def _():
            chunk = step - TILES - 2
            to_mate(chunk).wait_recv()
            late_near(chunk).start()

    def finish():
        to_mate(chunks - 1).wait_recv()
        late_near(chunks - 1).start()
        own().wait()
        to_near().wait()
        for chunk in range(chunks):
            pass_near(chunk).wait_recv()
            late_near(chunk).wait_recv()
            to_far(chunk).wait_send()
            to_mate(chunk).wait_send()
            pass_near(chunk).wait_send()
            late_near(chunk).wait_send()

    return begin, go_on, finish


def attend(
    lengths_ref, counts_ref, q_ref, k_ref, v_ref, ek_ref, eq_ref, context_ref, p1_ref, p2_ref, p3_ref,
    shift_scr, score_scr, prob_scr,
):
    eye = unit_matrix(False)
    factor = 1.4426950408889634 * (3.0 * DH) ** -0.5
    counts = live_counts(lengths_ref, counts_ref)
    turned_values = v_ref[...].T
    head_rows = [
        jnp.where(
            lax.broadcasted_iota(jnp.int32, (PAIR, 1), 0) // DH == member, 1.0, 0.0
        ).astype(bf16)
        for member in range(2)
    ]

    def place(slot, t):
        start, length = SLOTS[slot]
        low = LEN3 - TILE - TILE * t
        row = start + t * TILE
        return start, length, slice(row, row + TILE), slice(low, low + length + TILE)

    def shift_unit(slot, t):
        start, length, rows, window = place(slot, t)
        table = dot_nn(each_head(q_ref[rows, :]), ek_ref[:, window])
        for member in range(2):
            shift_scr[member, rows, :length] = skew(
                table[member * TILE : (member + 1) * TILE], length
            ).astype(bf16)

    def score_unit(slot, t):
        start, length, rows, window = place(slot, t)
        keys = each_head(k_ref[rows, :])
        table = dot_nn(keys, eq_ref[:, window])
        queries = q_ref[start : start + length, :]
        live = lax.broadcasted_iota(jnp.int32, (TILE, 1), 0) < counts[slot] - t * TILE
        tops = []
        for member in range(2):
            mine = slice(member * TILE, (member + 1) * TILE)
            left = jnp.concatenate([keys[mine], eye], axis=1)
            shifted = shift_scr[member, start : start + length, t * TILE : (t + 1) * TILE]
            right = jnp.concatenate([queries, shifted], axis=1)
            raw = dot_nt(left, right) + skew(table[mine], length)
            raw = jnp.where(live, raw * factor, masked_score)
            score_scr[member, rows, :length] = raw
            tops.append(jnp.max(raw, axis=0, keepdims=True))
        return tops

    def weight_unit(slot, t, tops):
        start, length, rows, window = place(slot, t)
        sums = []
        for member in range(2):
            weights = jnp.exp2(score_scr[member, rows, :length] - tops[member])
            score_scr[member, rows, :length] = weights
            sums.append(jnp.sum(weights, axis=0, keepdims=True))
        return sums

    def prob_unit(slot, t, inverses):
        start, length, rows, window = place(slot, t)
        for member in range(2):
            prob = score_scr[member, rows, :length] * inverses[member]
            prob_scr[member, rows, :length] = prob.astype(bf16)
            prob_block((p1_ref, p2_ref, p3_ref), slot, t, member)[...] = flip_rows(prob).astype(
                bf16
            )

    def context_unit(slot):
        start, length = SLOTS[slot]
        here = slice(start, start + length)
        left = jnp.concatenate([turned_values[:, here] * rows for rows in head_rows], axis=1)
        right = jnp.concatenate([prob_scr[member, here, :length] for member in range(2)], axis=0)
        context_ref[here, :] = dot_nn(left, right).astype(bf16).T

    def both(function, parts):
        return [function(member_parts) for member_parts in zip(*parts)]

    def largest(parts):
        total = parts[0]
        for part in parts[1:]:
            total = jnp.maximum(total, part)
        return total

    groups = ((3,), (2, 1, 0))
    tiles = [[unit for slot in group for unit in slot_tiles(slot)] for group in groups]
    held = {}

    def settle(slot):
        held[slot] = both(largest, [held.pop(unit) for unit in slot_tiles(slot)])

    def invert(slot):
        total = both(sum, [held.pop(unit) for unit in slot_tiles(slot)])
        held[slot] = [1.0 / part for part in total]

    for unit in tiles[0]:
        shift_unit(*unit)
    for first, second in zip(tiles[0], tiles[1]):
        held[first] = score_unit(*first)
        shift_unit(*second)
    settle(3)
    for first, second in zip(tiles[0], tiles[1]):
        held[second] = score_unit(*second)
        held[first] = weight_unit(*first, held[3])
    invert(3)
    for slot in groups[1]:
        settle(slot)
    for first, second in zip(tiles[0], tiles[1]):
        held[second] = weight_unit(*second, held[second[0]])
        prob_unit(*first, held[3])
    for slot in groups[1]:
        invert(slot)
    context_unit(3)
    for second in tiles[1]:
        prob_unit(*second, held[second[0]])
    for slot in groups[1]:
        context_unit(slot)


def front_kernel(
    lengths_ref,
    counts_ref,
    tokens_ref,
    index_ref,
    down_ref,
    up_ref,
    hidden_up_ref,
    hidden_down_ref,
    adapt_scale_ref,
    in_any,
    back_any,
    qkv_any,
    rel_any,
    out_any,
    eq_ref,
    fk_ref,
    coeff_ref,
    rel_coeff_ref,
    factor_ref,
    scale_ref,
    context_ref,
    p1_ref,
    p2_ref,
    p3_ref,
    q_any,
    k_any,
    v_any,
    merged_any,
    gathered_any,
    q_scr,
    k_scr,
    v_scr,
    ekt_scr,
    eqt_scr,
    merged_scr,
    packed_scr,
    pos_scr,
    in_scr,
    back_scr,
    qkv_scr,
    rel_scr,
    out_scr,
    shift_scr,
    score_scr,
    prob_scr,
    load_sem,
    store_sem,
    own_sem,
    *gather_sems,
):
    step = pl.program_id(0)
    gather_start, gather_step, gather_end = gather_moves(
        packed_scr, gathered_any, own_sem, gather_sems
    )
    loads = [
        pltpu.make_async_copy(src, dst, load_sem.at[number])
        for number, (src, dst) in enumerate(
            (
                (in_any, in_scr),
                (back_any, back_scr),
                (qkv_any, qkv_scr),
                (rel_any, rel_scr),
                (out_any, out_scr),
            )
        )
    ]
    stores = [
        pltpu.make_async_copy(src, dst, store_sem.at[number])
        for number, (src, dst) in enumerate(
            ((q_scr, q_any), (k_scr, k_any), (v_scr, v_any), (merged_scr, merged_any))
        )
    ]

    @pl.when(step == 0)
    def _():
        gather_start()
        for load in loads:
            load.start()
        for number in range(5):
            factor_ref[number] = padded(down_ref[number])
            factor_ref[5 + number] = padded(up_ref[number])
        factor_ref[10] = padded(hidden_up_ref[...])
        factor_ref[11] = padded(hidden_down_ref[...])
        wide = jnp.concatenate([adapt_scale_ref[...], jnp.zeros((6, LANES - RANK), f32)], axis=1)
        wide = jnp.concatenate([wide, jnp.zeros((LANES - 6, LANES), f32)], axis=0)
        scale_ref[...] = wide.T[:PAD]
        packed_scr[2 * D : 2 * D + PAD] = factor_ref[10]
        packed_scr[2 * D + PAD : 2 * D + 2 * PAD] = factor_ref[11]
        packed_scr[2 * D + 2 * PAD :] = jnp.zeros((PACKED - 2 * D - 2 * PAD, D), bf16)
        loads[0].wait()
        packed_scr[:D] = merged(in_scr[...], factor_ref[4], factor_ref[10], scale_ref[:, 4:5])
        loads[1].wait()
        packed_scr[D : 2 * D] = merged(back_scr[...], factor_ref[11], factor_ref[9], scale_ref[:, 5:6])

    gather_step()

    @pl.when(step == 0)
    def _():
        loads[2].wait()
        for member in range(3):
            merged_scr[member] = merged(
                qkv_scr[member],
                factor_ref[member],
                factor_ref[5 + member],
                scale_ref[:, member : member + 1],
            )
        loads[3].wait()
        rel = rel_scr[...]
        for member in range(2):
            pos_scr[member] = dot_nn(rel, merged_scr[member]).astype(bf16)
        coeff = dot_nt(factor_ref[:2].reshape(2 * PAD, D), rel)
        rel_coeff_ref[...] = coeff.reshape(2, PAD, 2 * SPAN)

    @pl.when(step == 1)
    def _():
        loads[4].wait()
        merged_scr[3] = merged(out_scr[...], factor_ref[3], factor_ref[8], scale_ref[:, 3:4])

    @pl.when(step < TILES)
    def _():
        rows = pl.ds(pl.multiple_of(step * BLOCK, BLOCK), BLOCK)
        tokens = tokens_ref[...]
        for member, ref in enumerate((q_scr, k_scr, v_scr)):
            ref[rows, :] = dot_nn(tokens, merged_scr[member]).astype(bf16)
        coeff = dot_nt(factor_ref[:3].reshape(3 * PAD, D), tokens)
        coeff_ref[...] = coeff.reshape(3, PAD, BLOCK)
        bucket = lax.broadcasted_iota(jnp.int32, (2 * SPAN, BLOCK), 0)
        back, forth = (
            jnp.where(bucket == index_ref[row : row + 1, :], 1.0, 0.0).astype(bf16)
            for row in range(2)
        )
        eq_ref[...] = dot_tn(back, pos_scr[0]).astype(bf16)
        fk_ref[...] = dot_tn(forth, pos_scr[1]).astype(bf16)
        ekt_scr[:, rows] = dot_tn(pos_scr[1], back).astype(bf16)
        eqt_scr[:, rows] = dot_tn(pos_scr[0], back).astype(bf16)

    @pl.when(step == TILES)
    def _():
        for store in stores:
            store.start()

    @pl.when(step >= TILES)
    def _():
        lanes = pl.ds(pl.multiple_of((step - TILES) * PAIR, PAIR), PAIR)
        attend(
            lengths_ref,
            counts_ref,
            q_scr.at[:, lanes],
            k_scr.at[:, lanes],
            v_scr.at[:, lanes],
            ekt_scr.at[lanes, :],
            eqt_scr.at[lanes, :],
            context_ref,
            p1_ref,
            p2_ref,
            p3_ref,
            shift_scr,
            score_scr,
            prob_scr,
        )

    @pl.when(step == pl.num_programs(0) - 1)
    def _():
        for store in stores:
            store.wait()
        gather_end()


PAIR_SPEC = pl.BlockSpec((ROWS, PAIR), lambda p: (0, p))
TABLE_SPEC = pl.BlockSpec((PAIR, OFFSETS), lambda p: (p, 0))
PROB_SIZES = ((256, 128), (256, 256), (512, 512))
PROB_SPECS = [pl.BlockSpec((2, *size), lambda p: (p, 0, 0)) for size in PROB_SIZES]


def front(
    lengths, counts, tokens, qkv_weight, rel_embed, index_rows, down, up, hidden_up, hidden_down,
    adapt_scale, out_weight, in_weight, back_weight,
):
    chunks = HALF // CHUNK
    single, several = (pltpu.SemaphoreType.DMA((n,)) for n in (1, chunks))
    inner = lax.axis_size("tensor")
    assert inner == 4 and lax.axis_size("dp") % 2 == 0

    def tile_at(i):
        return jnp.minimum(i, TILES - 1)

    def pair_at(i):
        return jnp.maximum(i - TILES, 0)

    tile = pl.BlockSpec((BLOCK, D), lambda i: (tile_at(i), 0))
    rows = jax.ShapeDtypeStruct((ROWS, D), bf16)
    anywhere = pl.BlockSpec(memory_space=pl.ANY)
    return pl.pallas_call(
        front_kernel,
        grid=(TILES + H // 2,),
        in_specs=[pl.BlockSpec(memory_space=pltpu.SMEM)] * 2
        + [
            tile,
            pl.BlockSpec((2, BLOCK), lambda i: (0, tile_at(i))),
            once(5, RANK, D),
            once(5, RANK, D),
            once(RANK, D),
            once(RANK, D),
            once(6, RANK),
        ]
        + [anywhere] * 5,
        out_specs=[tile] * 2
        + [
            pl.BlockSpec((3, PAD, BLOCK), lambda i: (0, 0, tile_at(i))),
            whole(2, PAD, 2 * SPAN),
            whole(12, PAD, D),
            whole(PAD, LANES),
            pl.BlockSpec((ROWS, PAIR), lambda i: (0, pair_at(i))),
        ]
        + [pl.BlockSpec((2, *size), lambda i: (pair_at(i), 0, 0)) for size in PROB_SIZES]
        + [anywhere] * 5,
        out_shape=[rows] * 2
        + [
            jax.ShapeDtypeStruct((3, PAD, ROWS), f32),
            jax.ShapeDtypeStruct((2, PAD, 2 * SPAN), f32),
            jax.ShapeDtypeStruct((12, PAD, D), bf16),
            jax.ShapeDtypeStruct((PAD, LANES), f32),
            rows,
        ]
        + [jax.ShapeDtypeStruct((H, *size), bf16) for size in PROB_SIZES]
        + [rows] * 3
        + [
            jax.ShapeDtypeStruct((4, D, D), bf16),
            jax.ShapeDtypeStruct((inner, PACKED, D), bf16),
        ],
        scratch_shapes=[pltpu.VMEM((ROWS, D), bf16)] * 3
        + [pltpu.VMEM((D, OFFSETS), bf16)] * 2
        + [
            pltpu.VMEM((4, D, D), bf16),
            pltpu.VMEM((PACKED, D), bf16),
            pltpu.VMEM((2, 2 * SPAN, D), bf16),
            pltpu.VMEM((D, D), bf16),
            pltpu.VMEM((D, D), bf16),
            pltpu.VMEM((3, D, D), bf16),
            pltpu.VMEM((2 * SPAN, D), bf16),
            pltpu.VMEM((D, D), bf16),
            pltpu.VMEM((2, ROWS, LEN3), bf16),
            pltpu.VMEM((2, ROWS, LEN3), f32),
            pltpu.VMEM((2, ROWS, LEN3), bf16),
            pltpu.SemaphoreType.DMA((5,)),
            pltpu.SemaphoreType.DMA((4,)),
            pltpu.SemaphoreType.DMA((1,)),
        ]
        + [single] * 2
        + [several] * 8,
        compiler_params=pltpu.CompilerParams(
            collective_id=1, has_side_effects=True, vmem_limit_bytes=MEMORY
        ),
        name="front",
    )(
        lengths, counts, tokens, index_rows, down, up, hidden_up, hidden_down, adapt_scale,
        in_weight, back_weight, qkv_weight, rel_embed, out_weight,
    )


def backward_kernel(
    q_ref,
    k_ref,
    v_ref,
    g_ref,
    context_ref,
    eq_ref,
    fk_ref,
    p1_ref,
    p2_ref,
    p3_ref,
    gq_ref,
    gk_ref,
    gv_ref,
    geq_ref,
    gfk_ref,
    grad_scr,
    turned_scr,
    geq_scr,
    gfk_scr,
):
    anti = unit_matrix(True)
    factor = (3.0 * DH) ** -0.5
    geq_scr[...] = jnp.zeros_like(geq_scr)
    gfk_scr[...] = jnp.zeros_like(gfk_scr)
    product = g_ref[...].astype(f32) * context_ref[...].astype(f32)
    high = product.astype(bf16)
    rest = (product - high.astype(f32)).astype(bf16)
    lane = lax.broadcasted_iota(jnp.int32, (PAD, 2 * PAIR), 1) % PAIR
    row = lax.broadcasted_iota(jnp.int32, (PAD, 2 * PAIR), 0)
    summing = jnp.where(lane // DH == row, 1.0, 0.0).astype(bf16)
    delta = dot_nt(summing, jnp.concatenate([high, rest], axis=1))

    def place(slot, t):
        start, length = SLOTS[slot]
        row = start + t * TILE
        return start, length, slice(row, row + TILE)

    def spot(slot, t):
        start, length = SLOTS[slot]
        row = start + length - (t + 1) * TILE
        return slice(row, row + TILE)

    def open_unit(slot, t):
        start, length, rows = place(slot, t)
        both = jnp.concatenate([k_ref[rows, :], v_ref[rows, :]], axis=1)
        both = dot_nn(anti, both).astype(bf16)
        turned_scr[spot(slot, t), :] = both[:, :PAIR]
        return dot_nt(each_head(both[:, PAIR:]), g_ref[start : start + length, :])

    def raw_unit(slot, t, grad_prob):
        start, length, rows = place(slot, t)
        spreads = []
        for member in range(2):
            prob = prob_block((p1_ref, p2_ref, p3_ref), slot, t, member)[...].astype(f32)
            mine = grad_prob[member * TILE : (member + 1) * TILE]
            raw = (prob * (mine - delta[member : member + 1, start : start + length])).astype(bf16)
            grad_scr[member, spot(slot, t), :length] = raw
            spreads.append(unskew(raw.astype(f32), length).astype(bf16))
        return jnp.concatenate(spreads, axis=0)

    def key_unit(slot, t, spread):
        start, length, rows = place(slot, t)
        low = LEN3 - TILE - TILE * t
        window = slice(low, low + length + TILE)
        here = slice(start, start + length)
        raw = jnp.concatenate(
            [grad_scr[member, spot(slot, t), :length] for member in range(2)], axis=0
        )
        probs = jnp.concatenate(
            [prob_block((p1_ref, p2_ref, p3_ref), slot, t, member)[...] for member in range(2)],
            axis=0,
        )
        key_grad = dot_nn(
            jnp.concatenate([raw, spread], axis=1),
            jnp.concatenate([q_ref[here, :], eq_ref[window, :]], axis=0),
        )
        value_grad = dot_nn(probs, g_ref[here, :])
        both = jnp.concatenate([own_lanes(key_grad) * factor, own_lanes(value_grad)], axis=1)
        both = dot_nn(anti, both.astype(bf16)).astype(bf16)
        gk_ref[rows, :] = both[:, :PAIR]
        gv_ref[rows, :] = both[:, PAIR:]
        geq_scr[:, window] += dot_tn(each_head(turned_scr[spot(slot, t), :]), spread)

    def turn_unit(slot, t):
        start, length, rows = place(slot, t)
        raws, spreads = [], []
        for member in range(2):
            raw = grad_scr[member, start : start + length, t * TILE : (t + 1) * TILE].T
            raws.append(raw)
            spreads.append(unskew(raw.astype(f32), length).astype(bf16))
        return jnp.concatenate(raws, axis=0), jnp.concatenate(spreads, axis=0)

    def query_unit(slot, t, raw, spread):
        start, length, rows = place(slot, t)
        low = LEN3 - length + TILE * t
        window = slice(low, low + length + TILE)
        query_grad = dot_nn(
            jnp.concatenate([raw, spread], axis=1),
            jnp.concatenate(
                [turned_scr[start : start + length, :], fk_ref[window, :]], axis=0
            ),
        )
        gq_ref[rows, :] = (own_lanes(query_grad) * factor).astype(bf16)
        gfk_scr[:, window] += dot_tn(each_head(q_ref[rows, :]), spread)

    first, second = slot_tiles(3), slot_tiles(2) + slot_tiles(1) + slot_tiles(0)
    jobs = [("key", unit) for unit in first]
    for one, other in zip(second, first):
        jobs += [("key", one), ("query", other)]
    jobs += [("query", unit) for unit in second]
    held = {}
    for at in range(len(jobs) + 2):
        if at < len(jobs):
            kind, unit = jobs[at]
            held[at] = open_unit(*unit) if kind == "key" else None
        if 0 <= at - 1 < len(jobs):
            kind, unit = jobs[at - 1]
            if kind == "key":
                held[at - 1] = raw_unit(*unit, held[at - 1])
            else:
                held[at - 1] = turn_unit(*unit)
        if 0 <= at - 2 < len(jobs):
            kind, unit = jobs[at - 2]
            if kind == "key":
                key_unit(*unit, held.pop(at - 2))
            else:
                query_unit(*unit, *held.pop(at - 2))
    geq_ref[...] = (geq_scr[...] * factor).astype(bf16)
    gfk_ref[...] = (gfk_scr[...] * factor).astype(bf16)


def attend_backward(q, k, v, g, context, eq, fk, p1, p2, p3):
    return pl.pallas_call(
        backward_kernel,
        grid=(H // 2,),
        in_specs=[PAIR_SPEC] * 7 + PROB_SPECS,
        out_specs=[PAIR_SPEC] * 3 + [TABLE_SPEC] * 2,
        out_shape=[jax.ShapeDtypeStruct((ROWS, D), bf16)] * 3
        + [jax.ShapeDtypeStruct((D, OFFSETS), bf16)] * 2,
        scratch_shapes=[
            pltpu.VMEM((2, ROWS, LEN3), bf16),
            pltpu.VMEM((ROWS, PAIR), bf16),
            pltpu.VMEM((PAIR, OFFSETS), f32),
            pltpu.VMEM((PAIR, OFFSETS), f32),
        ],
        compiler_params=pltpu.CompilerParams(vmem_limit_bytes=MEMORY),
        name="attention_backward",
    )(q, k, v, g, context, eq, fk, p1, p2, p3)


def gelu_pair(hidden):
    z = jnp.abs(hidden) * 0.7071067811865476
    t = 1.0 / (1.0 + 0.3275911 * z)
    poly = t * (
        0.127414796
        + t * (-0.142248368 + t * (0.7107068705 + t * (-0.7265760135 + t * 0.5307027145)))
    )
    bell = jnp.exp(-z * z)
    tail = poly * bell
    below = jnp.where(hidden >= 0, 1.0 - tail, tail)
    return hidden * below, below + hidden * (bell * 0.3989422804014327)


def norm_forward(values, gain, shift):
    centered = values - jnp.mean(values, axis=1, keepdims=True)
    inverse = lax.rsqrt(jnp.mean(centered * centered, axis=1, keepdims=True) + norm_epsilon)
    normal = centered * inverse
    return (normal * gain + shift, normal, inverse)


def norm_backward(grad_out, normal, inverse, gain):
    scaled = grad_out * gain
    return inverse * (
        scaled
        - jnp.mean(scaled, axis=1, keepdims=True)
        - normal * jnp.mean(scaled * normal, axis=1, keepdims=True)
    )


def middle_kernel(
    lengths_ref,
    counts_ref,
    tokens_ref,
    context_ref,
    out_grad_ref,
    weight_ref,
    packed_ref,
    factor_ref,
    scale_ref,
    gain_one_ref,
    shift_one_ref,
    gain_two_ref,
    shift_two_ref,
    mixed_ref,
    grad_one_ref,
    context_grad_ref,
    small_ref,
    hidden_ref,
    scale_grad_ref,
    active_scr,
    slope_scr,
):
    step = pl.program_id(0)
    chunks = packed_ref.shape[0]

    @pl.when(step == 0)
    def _():
        small_ref[...] = jnp.zeros_like(small_ref)
        hidden_ref[...] = jnp.zeros_like(hidden_ref)
        scale_grad_ref[...] = jnp.zeros_like(scale_grad_ref)

    gain_one, shift_one, gain_two, shift_two = (
        ref[...].reshape(1, D)
        for ref in (gain_one_ref, shift_one_ref, gain_two_ref, shift_two_ref)
    )
    used_rows = live_counts(lengths_ref, counts_ref)
    weight = weight_ref[0]

    def work(number):
        rows = slice(number * BLOCK, (number + 1) * BLOCK)
        row = lax.broadcasted_iota(jnp.int32, (BLOCK, 1), 0) + step * WIDE + number * BLOCK
        live = jnp.zeros((BLOCK, 1), f32)
        for (start, length), used in zip(SLOTS, used_rows):
            live = jnp.where((row >= start) & (row < start + used), 1.0, live)
        context = context_ref[rows, :]
        attended = dot_nn(context, weight)
        normed, normal_one, inverse_one = norm_forward(
            tokens_ref[rows, :].astype(f32) + attended, gain_one, shift_one
        )
        normed_low = normed.astype(bf16)
        yield
        mlp = jnp.zeros((BLOCK, D), f32)
        back_coeff = jnp.zeros((PAD, BLOCK), f32)
        ahead = dot_nn(normed_low, packed_ref[0, :D, :])
        for c in range(chunks):
            hidden = ahead
            if c + 1 < chunks:
                ahead = dot_nn(normed_low, packed_ref[c + 1, :D, :])
            active, slope = gelu_pair(hidden)
            active = active.astype(bf16)
            active_scr[c, rows, :] = active
            slope_scr[c, rows, :] = slope
            mlp = mlp + dot_nn(active, packed_ref[c, D : 2 * D, :])
            back_coeff = back_coeff + dot_nt(
                packed_ref[c, 2 * D + PAD : 2 * D + 2 * PAD, :], active
            )
            yield
        result, normal_two, inverse_two = norm_forward(normed + mlp, gain_two, shift_two)
        mixed_ref[rows, :] = (result * live).astype(bf16)
        grad_two = norm_backward(
            out_grad_ref[rows, :].astype(f32) * live, normal_two, inverse_two, gain_two
        )
        grad_mlp = grad_two.astype(bf16)
        yield
        back_slope = dot_nt(factor_ref[9], grad_mlp)
        small_ref[3] += add_parts(dot_nn(two_parts(back_coeff * scale_ref[:, 5:6]), grad_mlp))
        scale_grad_ref[:, 5:6] += jnp.sum(back_coeff * back_slope, axis=1, keepdims=True)
        back_through = two_parts(back_slope * scale_ref[:, 5:6])
        in_coeff = dot_nt(factor_ref[4], normed_low)
        in_scaled = two_parts(in_coeff * scale_ref[:, 4:5])
        in_slope = jnp.zeros((PAD, BLOCK), f32)
        grad_normed = grad_two
        ahead = dot_nt(grad_mlp, packed_ref[0, D : 2 * D, :])
        for c in range(chunks):
            grad_active = ahead
            if c + 1 < chunks:
                ahead = dot_nt(grad_mlp, packed_ref[c + 1, D : 2 * D, :])
            grad_hidden = (grad_active * slope_scr[c, rows, :]).astype(bf16)
            grad_normed = grad_normed + dot_nt(grad_hidden, packed_ref[c, :D, :])
            in_slope = in_slope + dot_nt(packed_ref[c, 2 * D : 2 * D + PAD, :], grad_hidden)
            hidden_ref[c] += add_parts(dot_nn(in_scaled, grad_hidden))
            hidden_ref[chunks + c] += add_parts(dot_nn(back_through, active_scr[c, rows, :]))
            yield
        scale_grad_ref[:, 4:5] += jnp.sum(in_coeff * in_slope, axis=1, keepdims=True)
        small_ref[2] += add_parts(dot_nn(two_parts(in_slope * scale_ref[:, 4:5]), normed_low))
        grad_one = norm_backward(grad_normed, normal_one, inverse_one, gain_one)
        grad_one_ref[rows, :] = grad_one
        grad_attended = grad_one.astype(bf16)
        yield
        context_grad_ref[rows, :] = dot_nt(grad_attended, weight).astype(bf16)
        out_coeff = dot_nt(factor_ref[3], context)
        out_slope = dot_nt(factor_ref[8], grad_attended)
        small_ref[1] += add_parts(dot_nn(two_parts(out_coeff * scale_ref[:, 3:4]), grad_attended))
        small_ref[0] += add_parts(dot_nn(two_parts(out_slope * scale_ref[:, 3:4]), context))
        scale_grad_ref[:, 3:4] += jnp.sum(out_coeff * out_slope, axis=1, keepdims=True)

    waiting = [work(number) for number in range(WIDE // BLOCK)]
    running = []
    turn_number = 0
    while waiting or running:
        if waiting and turn_number % LAG == 0:
            running.append(waiting.pop(0))
        turn_number += 1
        for job in list(running):
            try:
                next(job)
            except StopIteration:
                running.remove(job)


def middle(lengths, counts, tokens, context, out_grad, weights, packed, factors, scales, norms):
    chunks = packed.shape[0]
    tile = pl.BlockSpec((WIDE, D), lambda i: (i, 0))
    return pl.pallas_call(
        middle_kernel,
        grid=(ROWS // WIDE,),
        in_specs=[pl.BlockSpec(memory_space=pltpu.SMEM)] * 2
        + [tile] * 3
        + [
            pl.BlockSpec((1, D, D), lambda i: (3, 0, 0)),
            pl.BlockSpec(
                (chunks, PACKED, D), lambda i: (0, 0, 0), pipeline_mode=pl.Buffered(1)
            ),
            whole(12, PAD, D),
            whole(PAD, 128),
        ]
        + [whole(D)] * 4,
        out_specs=[tile] * 3
        + [whole(4, PAD, D), whole(2 * chunks, PAD, D), whole(PAD, 128)],
        out_shape=[
            jax.ShapeDtypeStruct((ROWS, D), bf16),
            jax.ShapeDtypeStruct((ROWS, D), f32),
            jax.ShapeDtypeStruct((ROWS, D), bf16),
            jax.ShapeDtypeStruct((4, PAD, D), f32),
            jax.ShapeDtypeStruct((2 * chunks, PAD, D), f32),
            jax.ShapeDtypeStruct((PAD, 128), f32),
        ],
        scratch_shapes=[
            pltpu.VMEM((chunks, WIDE, D), bf16),
            pltpu.VMEM((chunks, WIDE, D), f32),
        ],
        compiler_params=pltpu.CompilerParams(vmem_limit_bytes=MEMORY),
        name="middle",
    )(lengths, counts, tokens, context, out_grad, weights, packed, factors, scales, *norms)


def devices():
    return lax.axis_size("dp") * lax.axis_size("tensor")


def hidden_rows():
    tiles = 2 * BLOCKS
    return PAD * -(-tiles // lax.axis_size("dp"))


def last_kernel(
    grad_one_ref,
    coeff_ref,
    index_ref,
    rel_coeff_ref,
    factor_ref,
    scale_ref,
    small_ref,
    hidden_ref,
    middle_scale_ref,
    tokens_any,
    gq_any,
    gk_any,
    gv_any,
    rel_any,
    geq_any,
    gfk_any,
    merged_any,
    in_grad_ref,
    down_out,
    up_out,
    hidden_up_out,
    hidden_down_out,
    scale_out,
    tokens_scr,
    grads_scr,
    rel_scr,
    geq_scr,
    gfk_scr,
    merged_scr,
    down_scr,
    up_scr,
    scale_scr,
    stage_scr,
    mine_late,
    land_late,
    mine_early,
    land_early,
    part_early,
    land_part,
    all_sums,
    all_hidden,
    load_sem,
    late_out_sem,
    late_in_sem,
    sums_out_sem,
    sums_in_sem,
    early_out_sem,
    early_in_sem,
    part_out_sem,
    part_in_sem,
    spread_out_sem,
    spread_in_sem,
):
    step = pl.program_id(0)
    final = TILES
    used = 2 * 3 * BLOCKS * RANK
    outer = lax.axis_size("dp")
    inner = lax.axis_size("tensor")
    count = outer * inner
    my_outer = lax.axis_index("dp")
    my_inner = lax.axis_index("tensor")
    me = my_outer * inner + my_inner
    barrier = pltpu.get_barrier_semaphore()

    def partner(off):
        other = lax.rem(me + off, count)
        return other, other // inner, lax.rem(other, inner)

    def send(src, dst, out_sem, in_sem, place):
        return pltpu.make_async_remote_copy(
            src_ref=src,
            dst_ref=dst,
            send_sem=out_sem,
            recv_sem=in_sem,
            device_id=place,
            device_id_type=MESH,
        )

    def late(off):
        other, row, col = partner(off)
        return send(
            mine_late.at[other], land_late.at[off], late_out_sem.at[0], late_in_sem.at[0], (row, col)
        )

    def sums(off):
        other, row, col = partner(off)
        return send(
            all_sums.at[0], all_sums.at[off], sums_out_sem.at[0], sums_in_sem.at[0], (row, col)
        )

    def every_late():
        others = pl.ds(1, count - 1)
        return send(
            mine_late.at[others],
            land_late.at[others],
            late_out_sem.at[0],
            late_in_sem.at[0],
            (my_outer, my_inner),
        )

    def every_sums():
        others = pl.ds(1, count - 1)
        return send(
            all_sums.at[others],
            all_sums.at[others],
            sums_out_sem.at[0],
            sums_in_sem.at[0],
            (my_outer, my_inner),
        )

    def early(off):
        col = lax.rem(my_inner + off, inner)
        return send(
            mine_early.at[col],
            land_early.at[off],
            early_out_sem.at[off],
            early_in_sem.at[off],
            (my_outer, col),
        )

    def part(off):
        row = lax.rem(my_outer + off, outer)
        return send(
            part_early.at[row],
            land_part.at[off],
            part_out_sem.at[off],
            part_in_sem.at[off],
            (row, my_inner),
        )

    def spread(off, origin):
        return send(
            all_hidden.at[origin],
            all_hidden.at[origin],
            spread_out_sem.at[off],
            spread_in_sem.at[off],
            (lax.rem(my_outer + off, outer), my_inner),
        )

    loads = [
        pltpu.make_async_copy(src, dst, load_sem.at[number])
        for number, (src, dst) in enumerate(
            (
                (tokens_any, tokens_scr),
                (gq_any, grads_scr.at[0]),
                (gk_any, grads_scr.at[1]),
                (gv_any, grads_scr.at[2]),
                (rel_any, rel_scr),
                (geq_any, geq_scr),
                (gfk_any, gfk_scr),
                (merged_any.at[pl.ds(0, 3)], merged_scr),
            )
        )
    ]

    @pl.when(step == 0)
    def _():
        for load in loads:
            load.start()

        @pl.loop(1, count)
        def _(off):
            _, row, col = partner(off)
            pl.semaphore_signal(barrier, inc=1, device_id=(row, col), device_id_type=MESH)

        scale_scr[...] = jnp.zeros_like(scale_scr)
        mine_early[...] = jnp.zeros_like(mine_early)
        for number in range(4):
            for block in range(BLOCKS):
                piece = number * BLOCKS + block
                mine_early[piece % inner, piece // inner, :PAD] = small_ref[
                    number, :, block * LANES : (block + 1) * LANES
                ].astype(bf16)
        tiles = mine_early.shape[2] // PAD - 1
        for chunk in range(inner):
            for which in range(2):
                for block in range(BLOCKS):
                    tile = which * BLOCKS + block
                    at = (tile % tiles + 1) * PAD
                    mine_early[chunk, tile // tiles, at : at + PAD] = hidden_ref[
                        which * inner + chunk, :, block * LANES : (block + 1) * LANES
                    ].astype(bf16)
        pl.semaphore_wait(barrier, count - 1)

        @pl.loop(1, inner)
        def _(off):
            early(off).start()

        land_early[0] = mine_early[my_inner]
        loads[0].wait()
        tokens = tokens_scr[...]
        for member in range(3):
            loads[1 + member].wait()
            grad = grads_scr[member]
            scale = scale_ref[:, member : member + 1]
            coeff = coeff_ref[member]
            slope = dot_nt(factor_ref[5 + member], grad)
            up_scr[member] = add_parts(dot_nn(two_parts(coeff * scale), grad))
            down_scr[member] = add_parts(dot_nn(two_parts(slope * scale), tokens))
            scale_scr[:, member : member + 1] += jnp.sum(coeff * slope, axis=1, keepdims=True)

        @pl.loop(1, inner)
        def _(off):
            early(off).wait_recv()

        part_early[...] = jnp.sum(land_early[...].astype(f32), axis=0).astype(bf16)

        @pl.loop(1, outer)
        def _(off):
            part(off).start()

        land_part[0] = part_early[my_outer]
        for load in loads[4:7]:
            load.wait()
        rel = rel_scr[...]
        bucket = lax.broadcasted_iota(jnp.int32, (2 * SPAN, OFFSETS), 0)
        for member, ref, row in ((0, geq_scr, 0), (1, gfk_scr, 1)):
            scale = scale_ref[:, member : member + 1]
            chosen = jnp.where(bucket == index_ref[row : row + 1, :], 1.0, 0.0).astype(bf16)
            grad = dot_nt(ref[...], chosen).astype(bf16)
            coeff = rel_coeff_ref[member]
            slope = dot_nn(factor_ref[5 + member], grad)
            up_scr[member] += add_parts(dot_nt(two_parts(coeff * scale), grad))
            down_scr[member] += add_parts(dot_nn(two_parts(slope * scale), rel))
            scale_scr[:, member : member + 1] += jnp.sum(coeff * slope, axis=1, keepdims=True)
        for number in range(6):
            ref = down_scr if number < 3 else up_scr
            for block in range(BLOCKS):
                at = (number * BLOCKS + block) * RANK
                stage_scr[at : at + RANK, :] = ref[
                    number % 3, :RANK, block * LANES : (block + 1) * LANES
                ]
        stage_scr[used : used + PAD, :] = scale_scr[...] + middle_scale_ref[...]
        stage_scr[used + PAD :, :] = jnp.zeros((count * PAD - used - PAD, LANES), f32)
        mine_late[...] = stage_scr[...].astype(bf16).reshape(count, PAD, LANES)

        @pl.loop(1, count)
        def _(off):
            late(off).start()

        land_late[0] = mine_late[me]
        loads[7].wait()

    @pl.when(step > 0)
    def _():
        rows = pl.ds(pl.multiple_of((step - 1) * BLOCK, BLOCK), BLOCK)
        in_grad = grad_one_ref[...]
        for member in range(3):
            in_grad = in_grad + dot_nt(grads_scr[member, rows, :], merged_scr[member])
        in_grad_ref[...] = in_grad

    @pl.when(step == SUMMED)
    def _():
        @pl.loop(1, outer)
        def _(off):
            part(off).wait_recv()

        summed = jnp.sum(land_part[...].astype(f32), axis=0).astype(bf16)
        all_hidden[my_outer] = summed[PAD:]
        all_sums[0, PAD:] = summed[:PAD]

        @pl.loop(1, outer)
        def _(off):
            spread(off, my_outer).start()

        every_late().wait_recv()
        all_sums[0, :PAD] = jnp.sum(land_late[...].astype(f32), axis=0).astype(bf16)

        @pl.loop(1, count)
        def _(off):
            sums(off).start()

    @pl.when(step == final)
    def _():
        @pl.loop(1, outer)
        def _(off):
            spread(off, lax.rem(my_outer + outer - off, outer)).wait_recv()

        tiles = all_hidden.shape[1] // PAD
        for which in range(2):
            for block in range(BLOCKS):
                tile = which * BLOCKS + block
                at = tile % tiles * PAD
                out = (hidden_up_out, hidden_down_out)[which]
                out[:, block * LANES : (block + 1) * LANES] = all_hidden[
                    tile // tiles, at : at + PAD
                ].astype(f32)[:RANK]

        every_sums().wait_recv()

        def summed_by(owner):
            return all_sums.at[lax.rem(me + count - owner, count)]

        for owner in range(count):
            stage_scr[owner * PAD : (owner + 1) * PAD, :] = summed_by(owner)[:PAD].astype(f32)
        for number in range(6):
            ref = down_out if number < 3 else up_out
            for block in range(BLOCKS):
                at = (number * BLOCKS + block) * RANK
                ref[number % 3, :, block * LANES : (block + 1) * LANES] = stage_scr[
                    at : at + RANK, :
                ]
        scale_out[...] = stage_scr[used : used + PAD, :].T[:6, :RANK]
        for number, (ref, place) in enumerate(
            ((down_out, 3), (up_out, 3), (down_out, 4), (up_out, 4))
        ):
            for block in range(BLOCKS):
                ref[place, :, block * LANES : (block + 1) * LANES] = summed_by(
                    number * BLOCKS + block
                )[PAD:].astype(f32)[:RANK]
        every_late().wait_send()
        every_sums().wait_send()

        @pl.loop(1, inner)
        def _(off):
            early(off).wait_send()

        @pl.loop(1, outer)
        def _(off):
            part(off).wait_send()
            spread(off, my_outer).wait_send()


def last(
    tokens, gq, gk, gv, grad_one, coeff, weights, index, rel_coeff, factors, scales,
    small, hidden, middle_scale, rel, geq, gfk,
):
    count = devices()
    outer = lax.axis_size("dp")
    inner = lax.axis_size("tensor")
    piece = hidden_rows()
    tile = pl.BlockSpec((BLOCK, D), lambda i: (jnp.maximum(i - 1, 0), 0))
    factor = jax.ShapeDtypeStruct((5, RANK, D), f32)
    block = pltpu.VMEM((count, PAD, LANES), bf16)
    return pl.pallas_call(
        last_kernel,
        grid=(1 + TILES,),
        in_specs=[
            tile,
            once(3, PAD, ROWS),
            once(2, OFFSETS),
            once(2, PAD, 2 * SPAN),
            once(12, PAD, D),
            once(PAD, LANES),
            once(4, PAD, D),
            once(2 * inner, PAD, D),
            once(PAD, LANES),
        ]
        + [pl.BlockSpec(memory_space=pl.ANY)] * 8,
        out_specs=[
            tile,
            whole(5, RANK, D),
            whole(5, RANK, D),
            whole(RANK, D),
            whole(RANK, D),
            whole(6, RANK),
        ],
        out_shape=[
            jax.ShapeDtypeStruct((ROWS, D), f32),
            factor,
            factor,
            jax.ShapeDtypeStruct((RANK, D), f32),
            jax.ShapeDtypeStruct((RANK, D), f32),
            jax.ShapeDtypeStruct((6, RANK), f32),
        ],
        scratch_shapes=[
            pltpu.VMEM((ROWS, D), bf16),
            pltpu.VMEM((3, ROWS, D), bf16),
            pltpu.VMEM((2 * SPAN, D), bf16),
            pltpu.VMEM((D, OFFSETS), bf16),
            pltpu.VMEM((D, OFFSETS), bf16),
            pltpu.VMEM((3, D, D), bf16),
            pltpu.VMEM((3, PAD, D), f32),
            pltpu.VMEM((3, PAD, D), f32),
            pltpu.VMEM((PAD, LANES), f32),
            pltpu.VMEM((count * PAD, LANES), f32),
            block,
            block,
            pltpu.VMEM((inner, outer, PAD + piece, LANES), bf16),
            pltpu.VMEM((inner, outer, PAD + piece, LANES), bf16),
            pltpu.VMEM((outer, PAD + piece, LANES), bf16),
            pltpu.VMEM((outer, PAD + piece, LANES), bf16),
            pltpu.VMEM((count, 2 * PAD, LANES), bf16),
            pltpu.VMEM((outer, piece, LANES), bf16),
            pltpu.SemaphoreType.DMA((8,)),
        ]
        + [pltpu.SemaphoreType.DMA((1,))] * 4
        + [pltpu.SemaphoreType.DMA((inner,))] * 2
        + [pltpu.SemaphoreType.DMA((outer,))] * 4,
        compiler_params=pltpu.CompilerParams(
            collective_id=0, has_side_effects=True, vmem_limit_bytes=MEMORY
        ),
        name="last",
    )(
        grad_one, coeff, index, rel_coeff, factors, scales, small, hidden, middle_scale,
        tokens, gq, gk, gv, rel, geq, gfk, weights,
    )


def on_device(
    tokens,
    qkv_weight,
    out_weight,
    in_weight,
    back_weight,
    rel_embed,
    gain_one,
    shift_one,
    gain_two,
    shift_two,
    adapt_down,
    adapt_up,
    hidden_up,
    hidden_down,
    adapt_scale,
    seq_lengths,
    seq_counts,
    rel_bucket,
    out_grad,
):
    index_rows = jnp.pad(
        jnp.stack([rel_bucket[::-1], rel_bucket]), ((0, 0), (0, 1)), constant_values=-1
    )
    norms = (gain_one, shift_one, gain_two, shift_two)
    eq, fk, coeff, rel_coeff, factors, scales, context, p1, p2, p3, q, k, v, weights, gathered = front(
        seq_lengths, seq_counts, tokens, qkv_weight, rel_embed, index_rows, adapt_down, adapt_up,
        hidden_up, hidden_down, adapt_scale, out_weight, in_weight, back_weight,
    )
    mixed, grad_one, context_grad, small, hidden, middle_scale = middle(
        seq_lengths, seq_counts, tokens, context, out_grad, weights, gathered, factors, scales, norms
    )
    gq, gk, gv, geq, gfk = attend_backward(
        q, k, v, context_grad, context, eq, fk, p1, p2, p3
    )
    in_grad, down_grad, up_grad, hidden_up_grad, hidden_down_grad, scale_grad = last(
        tokens, gq, gk, gv, grad_one, coeff, weights, index_rows, rel_coeff, factors, scales,
        small, hidden, middle_scale, rel_embed, geq, gfk,
    )
    return (mixed, in_grad, down_grad, up_grad, hidden_up_grad, hidden_down_grad, scale_grad)


def solution(mesh):
    rows = P(("dp", "tensor"), None)
    return jax.shard_map(
        on_device,
        mesh=mesh,
        in_specs=(
            rows,
            P(),
            P(),
            P(None, "tensor"),
            P("tensor", None),
            P(),
            P(),
            P(),
            P(),
            P(),
            P(),
            P(),
            P(None, "tensor"),
            P(None, "tensor"),
            P(),
            rows,
            rows,
            P(),
            rows,
        ),
        out_specs=(rows, rows, P(), P(), P(None, "tensor"), P(None, "tensor"), P()),
        check_vma=False,
    )
```

```python
import jax
import jax.numpy as jnp
from jax import lax
from jax.experimental import pallas as pl
from jax.experimental.pallas import tpu as pltpu
from jax.sharding import PartitionSpec as P

D = 768
H = 12
DH = 64
PAIR = 2 * DH
SPAN = 256
RANK = 12
PAD = 16
ROWS = 1024
LEN1 = 128
LEN3 = 512
OFFSETS = 2 * LEN3
TILE = 128
BLOCK = 256
SLOTS = ((0, 128), (128, 128), (256, 256), (512, 512))
PACKED = 1600
QUARTER = PACKED // 4
CHUNKS = 5
CHUNK = QUARTER // CHUNKS
TILES = ROWS // BLOCK
SUMMED = 2
WIDE = 1 * BLOCK
LAG = 1
LANES = 128
BLOCKS = D // LANES
MESH = pl.DeviceIdType.MESH
norm_epsilon = 1e-07
masked_score = -1e30
bf16 = jnp.bfloat16
f32 = jnp.float32
MEMORY = 60 * 1024 * 1024


def dot_nn(a, b):
    return jnp.dot(a, b, preferred_element_type=f32)


def dot_nt(a, b):
    return lax.dot_general(a, b, (((1,), (1,)), ((), ())), preferred_element_type=f32)


def dot_tn(a, b):
    return lax.dot_general(a, b, (((0,), (0,)), ((), ())), preferred_element_type=f32)


def two_parts(wide):
    high = wide.astype(bf16)
    rest = (wide - high.astype(f32)).astype(bf16)
    return jnp.concatenate([high, rest], axis=0)


def add_parts(stacked):
    return stacked[:PAD] + stacked[PAD:]


def merged(weight, down, up, scale):
    twice = jnp.concatenate([up, up], axis=0)
    extra = dot_tn(two_parts(down.astype(f32) * scale), twice)
    return (weight.astype(f32) + extra).astype(bf16)


def live_counts(lengths_ref, counts_ref):
    ranks = ((0, 0), (0, 1), (1, 0), (2, 0))
    return [
        jnp.where(rank < counts_ref[0, bucket], lengths_ref[0, slot], 0)
        for slot, (bucket, rank) in enumerate(ranks)
    ]


def padded(rows):
    return jnp.concatenate([rows.astype(f32), jnp.zeros((PAD - RANK, D), f32)], axis=0).astype(bf16)


def whole(*shape):
    return pl.BlockSpec(shape, lambda *at: (0,) * len(shape))


def once(*shape):
    return pl.BlockSpec(shape, lambda *at: (0,) * len(shape), pipeline_mode=pl.Buffered(1))


def unit_matrix(flipped):
    row = lax.broadcasted_iota(jnp.int32, (TILE, TILE), 0)
    col = lax.broadcasted_iota(jnp.int32, (TILE, TILE), 1)
    return jnp.where(row == (TILE - 1 - col if flipped else col), 1.0, 0.0).astype(bf16)


def head_lanes(member):
    lane = lax.broadcasted_iota(jnp.int32, (1, PAIR), 1)
    return jnp.where(lane // DH == member, 1.0, 0.0).astype(bf16)


def each_head(rows):
    return jnp.concatenate([rows * head_lanes(0), rows * head_lanes(1)], axis=0)


def own_lanes(stacked):
    lane = lax.broadcasted_iota(jnp.int32, (TILE, PAIR), 1)
    return jnp.where(lane < DH, stacked[:TILE], stacked[TILE:])


def lane_and_row():
    lane = lax.broadcasted_iota(jnp.int32, (8, 128), 1)
    return lane, lax.broadcasted_iota(jnp.int32, (8, 128), 0)


def turn(block, shift):
    return pltpu.roll(block, shift % 128, 1, stride=1, stride_axis=0)


def skew(table, length):
    lane, row = lane_and_row()
    count = length // 128
    done = []
    for at in range(0, TILE, 8):
        blocks = [table[at : at + 8, 128 * c : 128 * c + 128] for c in range(count + 1)]
        blocks[0] = jnp.where(lane + row >= 127 - at, blocks[0], blocks[count])
        moved = [turn(block, at + 1) for block in blocks[:count]]
        if count > 1:
            inside = lane - row <= at
            moved = [
                jnp.where(inside, moved[c], moved[(c + 1) % count]) for c in range(count)
            ]
        done.append(jnp.concatenate(moved, axis=1))
    return jnp.concatenate(done, axis=0)


def flip_rows(block):
    row = lax.broadcasted_iota(jnp.int32, (8, LANES), 0)
    done = []
    for at in range(TILE - 8, -1, -8):
        done.append(
            jnp.concatenate(
                [
                    jnp.take_along_axis(block[at : at + 8, c : c + LANES], 7 - row, axis=0)
                    for c in range(0, block.shape[1], LANES)
                ],
                axis=1,
            )
        )
    return jnp.concatenate(done, axis=0)


def slot_tiles(slot):
    return [(slot, t) for t in range(SLOTS[slot][1] // TILE)]


def prob_block(refs, slot, t, member):
    start, length = SLOTS[slot]
    at = start + t * TILE if length == LEN1 else t * TILE
    ref = refs[{LEN1: 0, LEN3: 2}.get(length, 1)]
    return ref.at[member, at : at + TILE, :]


def unskew(scores, length):
    lane, row = lane_and_row()
    zero = jnp.zeros((8, 128), f32)
    done = []
    for at in range(0, TILE, 8):
        moved = [
            turn(scores[at : at + 8, 128 * c : 128 * c + 128], at) for c in range(length // 128)
        ]
        before = lane - row < at
        done.append(
            jnp.concatenate(
                [jnp.where(before, x, y) for x, y in zip([zero] + moved, moved + [zero])], axis=1
            )
        )
    return jnp.concatenate(done, axis=0)


def gather_moves(packed, gathered, own_sem, sems):
    step = pl.program_id(0)
    d = lax.axis_index("dp")
    t = lax.axis_index("tensor")
    near = t + 1 - 2 * lax.rem(t, 2)
    far = t + 2 - 4 * (t // 2)
    mate = d + 1 - 2 * lax.rem(d, 2)
    other = d + 2 - 4 * lax.rem(d // 2, 2)
    mine = lax.rem(d, 4)
    mates = mine + 1 - 2 * lax.rem(mine, 2)
    others = mine + 2 - 4 * (mine // 2)
    across = 3 - mine
    near_out, near_in, own_sems = sems[0], sems[1], sems[2:]
    pairs = [own_sems[2 * i : 2 * i + 2] for i in range(8)]
    far_sems, mate_sems, other_sems, relay_sems, *pass_sems = pairs
    barrier = pltpu.get_barrier_semaphore()
    places = ((d, near), (d, far), (mate, t), (other, t))

    def rows(which, chunk):
        return pl.ds(pl.multiple_of(which * QUARTER + chunk * CHUNK, PAD), CHUNK)

    def send(src, dst, out_sem, in_sem, place):
        return pltpu.make_async_remote_copy(
            src_ref=src, dst_ref=dst, send_sem=out_sem, recv_sem=in_sem, device_id=place, device_id_type=MESH
        )

    def to_near():
        return send(packed, gathered.at[t], near_out.at[0], near_in.at[0], places[0])

    def to_far(chunk):
        here = rows(mine, chunk)
        return send(
            packed.at[here],
            gathered.at[t, here],
            far_sems[0].at[chunk],
            far_sems[1].at[chunk],
            places[1],
        )

    def onward(which, chunk, pair, place):
        here = gathered.at[far, rows(which, chunk)]
        return send(here, here, pair[0].at[chunk], pair[1].at[chunk], place)

    def to_mate(chunk):
        return onward(mine, chunk, mate_sems, places[2])

    def to_other(chunk):
        return onward(mine, chunk, other_sems, places[3])

    def relay(chunk):
        if chunk % 2 == 0:
            return onward(others, chunk, relay_sems, places[2])
        return onward(mates, chunk, relay_sems, places[3])

    def passing(number, chunk):
        which = (mine, mates, others, across)[number]
        return onward(which, chunk, pass_sems[number], places[0])

    def own():
        return pltpu.make_async_copy(packed, gathered.at[t], own_sem.at[0])

    def begin():
        for place in places:
            pl.semaphore_signal(barrier, inc=1, device_id=place, device_id_type=MESH)

    def forward(chunk):
        to_far(chunk).wait_recv()
        to_mate(chunk).start()
        to_other(chunk).start()
        passing(0, chunk).start()

    def cross(chunk):
        to_mate(chunk).wait_recv()
        to_other(chunk).wait_recv()
        relay(chunk).start()
        passing(1, chunk).start()
        passing(2, chunk).start()

    def close(chunk):
        relay(chunk).wait_recv()
        passing(3, chunk).start()

    plan = {
        3: ((forward, 0),),
        4: ((forward, 1),),
        5: ((forward, 2), (forward, 3)),
        6: ((cross, 0), (forward, 4)),
        7: ((cross, 1), (cross, 2)),
        8: ((cross, 3), (close, 0), (close, 1)),
        9: ((cross, 4), (close, 2), (close, 3)),
    }

    def go_on():
        @pl.when(step == 0)
        def _():
            own().start()
            pl.semaphore_wait(barrier, len(places))
            for chunk in range(CHUNKS):
                to_far(chunk).start()
            to_near().start()

        for when, moves in plan.items():

            @pl.when(step == when)
            def _(moves=moves):
                for move, chunk in moves:
                    move(chunk)

    def finish():
        close(CHUNKS - 1)
        own().wait()
        to_near().wait()
        for chunk in range(CHUNKS):
            for number in range(4):
                passing(number, chunk).wait()
            to_far(chunk).wait_send()
            to_mate(chunk).wait_send()
            to_other(chunk).wait_send()
            relay(chunk).wait_send()

    return begin, go_on, finish


def attend(
    lengths_ref, counts_ref, q_ref, k_ref, v_ref, ek_ref, eq_ref, context_ref, p1_ref, p2_ref, p3_ref,
    shift_scr, score_scr, prob_scr,
):
    eye = unit_matrix(False)
    factor = 1.4426950408889634 * (3.0 * DH) ** -0.5
    counts = live_counts(lengths_ref, counts_ref)
    turned_values = v_ref[...].T
    head_rows = [
        jnp.where(
            lax.broadcasted_iota(jnp.int32, (PAIR, 1), 0) // DH == member, 1.0, 0.0
        ).astype(bf16)
        for member in range(2)
    ]

    def place(slot, t):
        start, length = SLOTS[slot]
        low = LEN3 - TILE - TILE * t
        row = start + t * TILE
        return start, length, slice(row, row + TILE), slice(low, low + length + TILE)

    def shift_unit(slot, t):
        start, length, rows, window = place(slot, t)
        table = dot_nn(each_head(q_ref[rows, :]), ek_ref[:, window])
        for member in range(2):
            shift_scr[member, rows, :length] = skew(
                table[member * TILE : (member + 1) * TILE], length
            ).astype(bf16)

    def score_unit(slot, t):
        start, length, rows, window = place(slot, t)
        keys = each_head(k_ref[rows, :])
        table = dot_nn(keys, eq_ref[:, window])
        queries = q_ref[start : start + length, :]
        live = lax.broadcasted_iota(jnp.int32, (TILE, 1), 0) < counts[slot] - t * TILE
        tops = []
        for member in range(2):
            mine = slice(member * TILE, (member + 1) * TILE)
            left = jnp.concatenate([keys[mine], eye], axis=1)
            shifted = shift_scr[member, start : start + length, t * TILE : (t + 1) * TILE]
            right = jnp.concatenate([queries, shifted], axis=1)
            raw = dot_nt(left, right) + skew(table[mine], length)
            raw = jnp.where(live, raw * factor, masked_score)
            score_scr[member, rows, :length] = raw
            tops.append(jnp.max(raw, axis=0, keepdims=True))
        return tops

    def weight_unit(slot, t, tops):
        start, length, rows, window = place(slot, t)
        sums = []
        for member in range(2):
            weights = jnp.exp2(score_scr[member, rows, :length] - tops[member])
            score_scr[member, rows, :length] = weights
            sums.append(jnp.sum(weights, axis=0, keepdims=True))
        return sums

    def prob_unit(slot, t, inverses):
        start, length, rows, window = place(slot, t)
        for member in range(2):
            prob = score_scr[member, rows, :length] * inverses[member]
            prob_scr[member, rows, :length] = prob.astype(bf16)
            prob_block((p1_ref, p2_ref, p3_ref), slot, t, member)[...] = flip_rows(prob).astype(
                bf16
            )

    def context_unit(slot):
        start, length = SLOTS[slot]
        here = slice(start, start + length)
        left = jnp.concatenate([turned_values[:, here] * rows for rows in head_rows], axis=1)
        right = jnp.concatenate([prob_scr[member, here, :length] for member in range(2)], axis=0)
        context_ref[here, :] = dot_nn(left, right).astype(bf16).T

    def both(function, parts):
        return [function(member_parts) for member_parts in zip(*parts)]

    def largest(parts):
        total = parts[0]
        for part in parts[1:]:
            total = jnp.maximum(total, part)
        return total

    groups = ((3,), (2, 1, 0))
    tiles = [[unit for slot in group for unit in slot_tiles(slot)] for group in groups]
    held = {}

    def settle(slot):
        held[slot] = both(largest, [held.pop(unit) for unit in slot_tiles(slot)])

    def invert(slot):
        total = both(sum, [held.pop(unit) for unit in slot_tiles(slot)])
        held[slot] = [1.0 / part for part in total]

    for unit in tiles[0]:
        shift_unit(*unit)
    for first, second in zip(tiles[0], tiles[1]):
        held[first] = score_unit(*first)
        shift_unit(*second)
    settle(3)
    for first, second in zip(tiles[0], tiles[1]):
        held[second] = score_unit(*second)
        held[first] = weight_unit(*first, held[3])
    invert(3)
    for slot in groups[1]:
        settle(slot)
    for first, second in zip(tiles[0], tiles[1]):
        held[second] = weight_unit(*second, held[second[0]])
        prob_unit(*first, held[3])
    for slot in groups[1]:
        invert(slot)
    context_unit(3)
    for second in tiles[1]:
        prob_unit(*second, held[second[0]])
    for slot in groups[1]:
        context_unit(slot)


def front_kernel(
    lengths_ref,
    counts_ref,
    tokens_ref,
    index_ref,
    down_ref,
    up_ref,
    hidden_up_ref,
    hidden_down_ref,
    adapt_scale_ref,
    in_any,
    back_any,
    qkv_any,
    rel_any,
    out_any,
    eq_ref,
    fk_ref,
    coeff_ref,
    rel_coeff_ref,
    factor_ref,
    scale_ref,
    context_ref,
    p1_ref,
    p2_ref,
    p3_ref,
    q_any,
    k_any,
    v_any,
    merged_any,
    gathered_any,
    q_scr,
    k_scr,
    v_scr,
    ekt_scr,
    eqt_scr,
    merged_scr,
    packed_scr,
    pos_scr,
    in_scr,
    back_scr,
    qkv_scr,
    rel_scr,
    out_scr,
    shift_scr,
    score_scr,
    prob_scr,
    load_sem,
    store_sem,
    own_sem,
    *gather_sems,
):
    step = pl.program_id(0)
    gather_start, gather_step, gather_end = gather_moves(
        packed_scr, gathered_any, own_sem, gather_sems
    )
    loads = [
        pltpu.make_async_copy(src, dst, load_sem.at[number])
        for number, (src, dst) in enumerate(
            (
                (in_any, in_scr),
                (back_any, back_scr),
                (qkv_any, qkv_scr),
                (rel_any, rel_scr),
                (out_any, out_scr),
            )
        )
    ]
    stores = [
        pltpu.make_async_copy(src, dst, store_sem.at[number])
        for number, (src, dst) in enumerate(
            ((q_scr, q_any), (k_scr, k_any), (v_scr, v_any), (merged_scr, merged_any))
        )
    ]

    @pl.when(step == 0)
    def _():
        gather_start()
        for load in loads:
            load.start()
        for number in range(5):
            factor_ref[number] = padded(down_ref[number])
            factor_ref[5 + number] = padded(up_ref[number])
        factor_ref[10] = padded(hidden_up_ref[...])
        factor_ref[11] = padded(hidden_down_ref[...])
        wide = jnp.concatenate([adapt_scale_ref[...], jnp.zeros((6, LANES - RANK), f32)], axis=1)
        wide = jnp.concatenate([wide, jnp.zeros((LANES - 6, LANES), f32)], axis=0)
        scale_ref[...] = wide.T[:PAD]
        packed_scr[2 * D : 2 * D + PAD] = factor_ref[10]
        packed_scr[2 * D + PAD : 2 * D + 2 * PAD] = factor_ref[11]
        packed_scr[2 * D + 2 * PAD :] = jnp.zeros((PACKED - 2 * D - 2 * PAD, D), bf16)
        loads[0].wait()
        packed_scr[:D] = merged(in_scr[...], factor_ref[4], factor_ref[10], scale_ref[:, 4:5])
        loads[1].wait()
        packed_scr[D : 2 * D] = merged(back_scr[...], factor_ref[11], factor_ref[9], scale_ref[:, 5:6])

    gather_step()

    @pl.when(step == 0)
    def _():
        loads[2].wait()
        for member in range(3):
            merged_scr[member] = merged(
                qkv_scr[member],
                factor_ref[member],
                factor_ref[5 + member],
                scale_ref[:, member : member + 1],
            )
        loads[3].wait()
        rel = rel_scr[...]
        for member in range(2):
            pos_scr[member] = dot_nn(rel, merged_scr[member]).astype(bf16)
        coeff = dot_nt(factor_ref[:2].reshape(2 * PAD, D), rel)
        rel_coeff_ref[...] = coeff.reshape(2, PAD, 2 * SPAN)

    @pl.when(step == 1)
    def _():
        loads[4].wait()
        merged_scr[3] = merged(out_scr[...], factor_ref[3], factor_ref[8], scale_ref[:, 3:4])

    @pl.when(step < TILES)
    def _():
        rows = pl.ds(pl.multiple_of(step * BLOCK, BLOCK), BLOCK)
        tokens = tokens_ref[...]
        for member, ref in enumerate((q_scr, k_scr, v_scr)):
            ref[rows, :] = dot_nn(tokens, merged_scr[member]).astype(bf16)
        coeff = dot_nt(factor_ref[:3].reshape(3 * PAD, D), tokens)
        coeff_ref[...] = coeff.reshape(3, PAD, BLOCK)
        bucket = lax.broadcasted_iota(jnp.int32, (2 * SPAN, BLOCK), 0)
        back, forth = (
            jnp.where(bucket == index_ref[row : row + 1, :], 1.0, 0.0).astype(bf16)
            for row in range(2)
        )
        eq_ref[...] = dot_tn(back, pos_scr[0]).astype(bf16)
        fk_ref[...] = dot_tn(forth, pos_scr[1]).astype(bf16)
        ekt_scr[:, rows] = dot_tn(pos_scr[1], back).astype(bf16)
        eqt_scr[:, rows] = dot_tn(pos_scr[0], back).astype(bf16)

    @pl.when(step == TILES)
    def _():
        for store in stores:
            store.start()

    @pl.when(step >= TILES)
    def _():
        lanes = pl.ds(pl.multiple_of((step - TILES) * PAIR, PAIR), PAIR)
        attend(
            lengths_ref,
            counts_ref,
            q_scr.at[:, lanes],
            k_scr.at[:, lanes],
            v_scr.at[:, lanes],
            ekt_scr.at[lanes, :],
            eqt_scr.at[lanes, :],
            context_ref,
            p1_ref,
            p2_ref,
            p3_ref,
            shift_scr,
            score_scr,
            prob_scr,
        )

    @pl.when(step == pl.num_programs(0) - 1)
    def _():
        for store in stores:
            store.wait()
        gather_end()


PAIR_SPEC = pl.BlockSpec((ROWS, PAIR), lambda p: (0, p))
TABLE_SPEC = pl.BlockSpec((PAIR, OFFSETS), lambda p: (p, 0))
PROB_SIZES = ((256, 128), (256, 256), (512, 512))
PROB_SPECS = [pl.BlockSpec((2, *size), lambda p: (p, 0, 0)) for size in PROB_SIZES]


def front(
    lengths, counts, tokens, qkv_weight, rel_embed, index_rows, down, up, hidden_up, hidden_down,
    adapt_scale, out_weight, in_weight, back_weight,
):
    single, several = (pltpu.SemaphoreType.DMA((n,)) for n in (1, CHUNKS))
    inner = lax.axis_size("tensor")
    assert inner == 4 and lax.axis_size("dp") % 4 == 0

    def tile_at(i):
        return jnp.minimum(i, TILES - 1)

    def pair_at(i):
        return jnp.maximum(i - TILES, 0)

    tile = pl.BlockSpec((BLOCK, D), lambda i: (tile_at(i), 0))
    rows = jax.ShapeDtypeStruct((ROWS, D), bf16)
    anywhere = pl.BlockSpec(memory_space=pl.ANY)
    return pl.pallas_call(
        front_kernel,
        grid=(TILES + H // 2,),
        in_specs=[pl.BlockSpec(memory_space=pltpu.SMEM)] * 2
        + [
            tile,
            pl.BlockSpec((2, BLOCK), lambda i: (0, tile_at(i))),
            once(5, RANK, D),
            once(5, RANK, D),
            once(RANK, D),
            once(RANK, D),
            once(6, RANK),
        ]
        + [anywhere] * 5,
        out_specs=[tile] * 2
        + [
            pl.BlockSpec((3, PAD, BLOCK), lambda i: (0, 0, tile_at(i))),
            whole(2, PAD, 2 * SPAN),
            whole(12, PAD, D),
            whole(PAD, LANES),
            pl.BlockSpec((ROWS, PAIR), lambda i: (0, pair_at(i))),
        ]
        + [pl.BlockSpec((2, *size), lambda i: (pair_at(i), 0, 0)) for size in PROB_SIZES]
        + [anywhere] * 5,
        out_shape=[rows] * 2
        + [
            jax.ShapeDtypeStruct((3, PAD, ROWS), f32),
            jax.ShapeDtypeStruct((2, PAD, 2 * SPAN), f32),
            jax.ShapeDtypeStruct((12, PAD, D), bf16),
            jax.ShapeDtypeStruct((PAD, LANES), f32),
            rows,
        ]
        + [jax.ShapeDtypeStruct((H, *size), bf16) for size in PROB_SIZES]
        + [rows] * 3
        + [
            jax.ShapeDtypeStruct((4, D, D), bf16),
            jax.ShapeDtypeStruct((inner, PACKED, D), bf16),
        ],
        scratch_shapes=[pltpu.VMEM((ROWS, D), bf16)] * 3
        + [pltpu.VMEM((D, OFFSETS), bf16)] * 2
        + [
            pltpu.VMEM((4, D, D), bf16),
            pltpu.VMEM((PACKED, D), bf16),
            pltpu.VMEM((2, 2 * SPAN, D), bf16),
            pltpu.VMEM((D, D), bf16),
            pltpu.VMEM((D, D), bf16),
            pltpu.VMEM((3, D, D), bf16),
            pltpu.VMEM((2 * SPAN, D), bf16),
            pltpu.VMEM((D, D), bf16),
            pltpu.VMEM((2, ROWS, LEN3), bf16),
            pltpu.VMEM((2, ROWS, LEN3), f32),
            pltpu.VMEM((2, ROWS, LEN3), bf16),
            pltpu.SemaphoreType.DMA((5,)),
            pltpu.SemaphoreType.DMA((4,)),
            pltpu.SemaphoreType.DMA((1,)),
        ]
        + [single] * 2
        + [several] * 16,
        compiler_params=pltpu.CompilerParams(
            collective_id=1, has_side_effects=True, vmem_limit_bytes=MEMORY
        ),
        name="front",
    )(
        lengths, counts, tokens, index_rows, down, up, hidden_up, hidden_down, adapt_scale,
        in_weight, back_weight, qkv_weight, rel_embed, out_weight,
    )


def backward_kernel(
    q_ref,
    k_ref,
    v_ref,
    g_ref,
    context_ref,
    eq_ref,
    fk_ref,
    p1_ref,
    p2_ref,
    p3_ref,
    gq_ref,
    gk_ref,
    gv_ref,
    geq_ref,
    gfk_ref,
    grad_scr,
    turned_scr,
    geq_scr,
    gfk_scr,
):
    anti = unit_matrix(True)
    factor = (3.0 * DH) ** -0.5
    geq_scr[...] = jnp.zeros_like(geq_scr)
    gfk_scr[...] = jnp.zeros_like(gfk_scr)
    product = g_ref[...].astype(f32) * context_ref[...].astype(f32)
    high = product.astype(bf16)
    rest = (product - high.astype(f32)).astype(bf16)
    lane = lax.broadcasted_iota(jnp.int32, (PAD, 2 * PAIR), 1) % PAIR
    row = lax.broadcasted_iota(jnp.int32, (PAD, 2 * PAIR), 0)
    summing = jnp.where(lane // DH == row, 1.0, 0.0).astype(bf16)
    delta = dot_nt(summing, jnp.concatenate([high, rest], axis=1))

    def place(slot, t):
        start, length = SLOTS[slot]
        row = start + t * TILE
        return start, length, slice(row, row + TILE)

    def spot(slot, t):
        start, length = SLOTS[slot]
        row = start + length - (t + 1) * TILE
        return slice(row, row + TILE)

    def open_unit(slot, t):
        start, length, rows = place(slot, t)
        both = jnp.concatenate([k_ref[rows, :], v_ref[rows, :]], axis=1)
        both = dot_nn(anti, both).astype(bf16)
        turned_scr[spot(slot, t), :] = both[:, :PAIR]
        return dot_nt(each_head(both[:, PAIR:]), g_ref[start : start + length, :])

    def raw_unit(slot, t, grad_prob):
        start, length, rows = place(slot, t)
        spreads = []
        for member in range(2):
            prob = prob_block((p1_ref, p2_ref, p3_ref), slot, t, member)[...].astype(f32)
            mine = grad_prob[member * TILE : (member + 1) * TILE]
            raw = (prob * (mine - delta[member : member + 1, start : start + length])).astype(bf16)
            grad_scr[member, spot(slot, t), :length] = raw
            spreads.append(unskew(raw.astype(f32), length).astype(bf16))
        return jnp.concatenate(spreads, axis=0)

    def key_unit(slot, t, spread):
        start, length, rows = place(slot, t)
        low = LEN3 - TILE - TILE * t
        window = slice(low, low + length + TILE)
        here = slice(start, start + length)
        raw = jnp.concatenate(
            [grad_scr[member, spot(slot, t), :length] for member in range(2)], axis=0
        )
        probs = jnp.concatenate(
            [prob_block((p1_ref, p2_ref, p3_ref), slot, t, member)[...] for member in range(2)],
            axis=0,
        )
        key_grad = dot_nn(
            jnp.concatenate([raw, spread], axis=1),
            jnp.concatenate([q_ref[here, :], eq_ref[window, :]], axis=0),
        )
        value_grad = dot_nn(probs, g_ref[here, :])
        both = jnp.concatenate([own_lanes(key_grad) * factor, own_lanes(value_grad)], axis=1)
        both = dot_nn(anti, both.astype(bf16)).astype(bf16)
        gk_ref[rows, :] = both[:, :PAIR]
        gv_ref[rows, :] = both[:, PAIR:]
        geq_scr[:, window] += dot_tn(each_head(turned_scr[spot(slot, t), :]), spread)

    def turn_unit(slot, t):
        start, length, rows = place(slot, t)
        raws, spreads = [], []
        for member in range(2):
            raw = grad_scr[member, start : start + length, t * TILE : (t + 1) * TILE].T
            raws.append(raw)
            spreads.append(unskew(raw.astype(f32), length).astype(bf16))
        return jnp.concatenate(raws, axis=0), jnp.concatenate(spreads, axis=0)

    def query_unit(slot, t, raw, spread):
        start, length, rows = place(slot, t)
        low = LEN3 - length + TILE * t
        window = slice(low, low + length + TILE)
        query_grad = dot_nn(
            jnp.concatenate([raw, spread], axis=1),
            jnp.concatenate(
                [turned_scr[start : start + length, :], fk_ref[window, :]], axis=0
            ),
        )
        gq_ref[rows, :] = (own_lanes(query_grad) * factor).astype(bf16)
        gfk_scr[:, window] += dot_tn(each_head(q_ref[rows, :]), spread)

    first, second = slot_tiles(3), slot_tiles(2) + slot_tiles(1) + slot_tiles(0)
    jobs = [("key", unit) for unit in first]
    for one, other in zip(second, first):
        jobs += [("key", one), ("query", other)]
    jobs += [("query", unit) for unit in second]
    held = {}
    for at in range(len(jobs) + 2):
        if at < len(jobs):
            kind, unit = jobs[at]
            held[at] = open_unit(*unit) if kind == "key" else None
        if 0 <= at - 1 < len(jobs):
            kind, unit = jobs[at - 1]
            if kind == "key":
                held[at - 1] = raw_unit(*unit, held[at - 1])
            else:
                held[at - 1] = turn_unit(*unit)
        if 0 <= at - 2 < len(jobs):
            kind, unit = jobs[at - 2]
            if kind == "key":
                key_unit(*unit, held.pop(at - 2))
            else:
                query_unit(*unit, *held.pop(at - 2))
    geq_ref[...] = (geq_scr[...] * factor).astype(bf16)
    gfk_ref[...] = (gfk_scr[...] * factor).astype(bf16)


def attend_backward(q, k, v, g, context, eq, fk, p1, p2, p3):
    return pl.pallas_call(
        backward_kernel,
        grid=(H // 2,),
        in_specs=[PAIR_SPEC] * 7 + PROB_SPECS,
        out_specs=[PAIR_SPEC] * 3 + [TABLE_SPEC] * 2,
        out_shape=[jax.ShapeDtypeStruct((ROWS, D), bf16)] * 3
        + [jax.ShapeDtypeStruct((D, OFFSETS), bf16)] * 2,
        scratch_shapes=[
            pltpu.VMEM((2, ROWS, LEN3), bf16),
            pltpu.VMEM((ROWS, PAIR), bf16),
            pltpu.VMEM((PAIR, OFFSETS), f32),
            pltpu.VMEM((PAIR, OFFSETS), f32),
        ],
        compiler_params=pltpu.CompilerParams(vmem_limit_bytes=MEMORY),
        name="attention_backward",
    )(q, k, v, g, context, eq, fk, p1, p2, p3)


def gelu_pair(hidden):
    z = jnp.abs(hidden) * 0.7071067811865476
    t = 1.0 / (1.0 + 0.3275911 * z)
    poly = t * (
        0.127414796
        + t * (-0.142248368 + t * (0.7107068705 + t * (-0.7265760135 + t * 0.5307027145)))
    )
    bell = jnp.exp(-z * z)
    tail = poly * bell
    below = jnp.where(hidden >= 0, 1.0 - tail, tail)
    return hidden * below, below + hidden * (bell * 0.3989422804014327)


def norm_forward(values, gain, shift):
    centered = values - jnp.mean(values, axis=1, keepdims=True)
    inverse = lax.rsqrt(jnp.mean(centered * centered, axis=1, keepdims=True) + norm_epsilon)
    normal = centered * inverse
    return (normal * gain + shift, normal, inverse)


def norm_backward(grad_out, normal, inverse, gain):
    scaled = grad_out * gain
    return inverse * (
        scaled
        - jnp.mean(scaled, axis=1, keepdims=True)
        - normal * jnp.mean(scaled * normal, axis=1, keepdims=True)
    )


def middle_kernel(
    lengths_ref,
    counts_ref,
    tokens_ref,
    context_ref,
    out_grad_ref,
    weight_ref,
    packed_ref,
    factor_ref,
    scale_ref,
    gain_one_ref,
    shift_one_ref,
    gain_two_ref,
    shift_two_ref,
    mixed_ref,
    grad_one_ref,
    context_grad_ref,
    small_ref,
    hidden_ref,
    scale_grad_ref,
    active_scr,
    slope_scr,
):
    step = pl.program_id(0)
    chunks = packed_ref.shape[0]

    @pl.when(step == 0)
    def _():
        small_ref[...] = jnp.zeros_like(small_ref)
        hidden_ref[...] = jnp.zeros_like(hidden_ref)
        scale_grad_ref[...] = jnp.zeros_like(scale_grad_ref)

    gain_one, shift_one, gain_two, shift_two = (
        ref[...].reshape(1, D)
        for ref in (gain_one_ref, shift_one_ref, gain_two_ref, shift_two_ref)
    )
    used_rows = live_counts(lengths_ref, counts_ref)
    weight = weight_ref[0]

    def work(number):
        rows = slice(number * BLOCK, (number + 1) * BLOCK)
        row = lax.broadcasted_iota(jnp.int32, (BLOCK, 1), 0) + step * WIDE + number * BLOCK
        live = jnp.zeros((BLOCK, 1), f32)
        for (start, length), used in zip(SLOTS, used_rows):
            live = jnp.where((row >= start) & (row < start + used), 1.0, live)
        context = context_ref[rows, :]
        attended = dot_nn(context, weight)
        normed, normal_one, inverse_one = norm_forward(
            tokens_ref[rows, :].astype(f32) + attended, gain_one, shift_one
        )
        normed_low = normed.astype(bf16)
        yield
        mlp = jnp.zeros((BLOCK, D), f32)
        back_coeff = jnp.zeros((PAD, BLOCK), f32)
        ahead = dot_nn(normed_low, packed_ref[0, :D, :])
        for c in range(chunks):
            hidden = ahead
            if c + 1 < chunks:
                ahead = dot_nn(normed_low, packed_ref[c + 1, :D, :])
            active, slope = gelu_pair(hidden)
            active = active.astype(bf16)
            active_scr[c, rows, :] = active
            slope_scr[c, rows, :] = slope
            mlp = mlp + dot_nn(active, packed_ref[c, D : 2 * D, :])
            back_coeff = back_coeff + dot_nt(
                packed_ref[c, 2 * D + PAD : 2 * D + 2 * PAD, :], active
            )
            yield
        result, normal_two, inverse_two = norm_forward(normed + mlp, gain_two, shift_two)
        mixed_ref[rows, :] = (result * live).astype(bf16)
        grad_two = norm_backward(
            out_grad_ref[rows, :].astype(f32) * live, normal_two, inverse_two, gain_two
        )
        grad_mlp = grad_two.astype(bf16)
        yield
        back_slope = dot_nt(factor_ref[9], grad_mlp)
        small_ref[3] += add_parts(dot_nn(two_parts(back_coeff * scale_ref[:, 5:6]), grad_mlp))
        scale_grad_ref[:, 5:6] += jnp.sum(back_coeff * back_slope, axis=1, keepdims=True)
        back_through = two_parts(back_slope * scale_ref[:, 5:6])
        in_coeff = dot_nt(factor_ref[4], normed_low)
        in_scaled = two_parts(in_coeff * scale_ref[:, 4:5])
        in_slope = jnp.zeros((PAD, BLOCK), f32)
        grad_normed = grad_two
        ahead = dot_nt(grad_mlp, packed_ref[0, D : 2 * D, :])
        for c in range(chunks):
            grad_active = ahead
            if c + 1 < chunks:
                ahead = dot_nt(grad_mlp, packed_ref[c + 1, D : 2 * D, :])
            grad_hidden = (grad_active * slope_scr[c, rows, :]).astype(bf16)
            grad_normed = grad_normed + dot_nt(grad_hidden, packed_ref[c, :D, :])
            in_slope = in_slope + dot_nt(packed_ref[c, 2 * D : 2 * D + PAD, :], grad_hidden)
            hidden_ref[c] += add_parts(dot_nn(in_scaled, grad_hidden))
            hidden_ref[chunks + c] += add_parts(dot_nn(back_through, active_scr[c, rows, :]))
            yield
        scale_grad_ref[:, 4:5] += jnp.sum(in_coeff * in_slope, axis=1, keepdims=True)
        small_ref[2] += add_parts(dot_nn(two_parts(in_slope * scale_ref[:, 4:5]), normed_low))
        grad_one = norm_backward(grad_normed, normal_one, inverse_one, gain_one)
        grad_one_ref[rows, :] = grad_one
        grad_attended = grad_one.astype(bf16)
        yield
        context_grad_ref[rows, :] = dot_nt(grad_attended, weight).astype(bf16)
        out_coeff = dot_nt(factor_ref[3], context)
        out_slope = dot_nt(factor_ref[8], grad_attended)
        small_ref[1] += add_parts(dot_nn(two_parts(out_coeff * scale_ref[:, 3:4]), grad_attended))
        small_ref[0] += add_parts(dot_nn(two_parts(out_slope * scale_ref[:, 3:4]), context))
        scale_grad_ref[:, 3:4] += jnp.sum(out_coeff * out_slope, axis=1, keepdims=True)

    waiting = [work(number) for number in range(WIDE // BLOCK)]
    running = []
    turn_number = 0
    while waiting or running:
        if waiting and turn_number % LAG == 0:
            running.append(waiting.pop(0))
        turn_number += 1
        for job in list(running):
            try:
                next(job)
            except StopIteration:
                running.remove(job)


def middle(lengths, counts, tokens, context, out_grad, weights, packed, factors, scales, norms):
    chunks = packed.shape[0]
    tile = pl.BlockSpec((WIDE, D), lambda i: (i, 0))
    return pl.pallas_call(
        middle_kernel,
        grid=(ROWS // WIDE,),
        in_specs=[pl.BlockSpec(memory_space=pltpu.SMEM)] * 2
        + [tile] * 3
        + [
            pl.BlockSpec((1, D, D), lambda i: (3, 0, 0)),
            pl.BlockSpec(
                (chunks, PACKED, D), lambda i: (0, 0, 0), pipeline_mode=pl.Buffered(1)
            ),
            whole(12, PAD, D),
            whole(PAD, 128),
        ]
        + [whole(D)] * 4,
        out_specs=[tile] * 3
        + [whole(4, PAD, D), whole(2 * chunks, PAD, D), whole(PAD, 128)],
        out_shape=[
            jax.ShapeDtypeStruct((ROWS, D), bf16),
            jax.ShapeDtypeStruct((ROWS, D), f32),
            jax.ShapeDtypeStruct((ROWS, D), bf16),
            jax.ShapeDtypeStruct((4, PAD, D), f32),
            jax.ShapeDtypeStruct((2 * chunks, PAD, D), f32),
            jax.ShapeDtypeStruct((PAD, 128), f32),
        ],
        scratch_shapes=[
            pltpu.VMEM((chunks, WIDE, D), bf16),
            pltpu.VMEM((chunks, WIDE, D), f32),
        ],
        compiler_params=pltpu.CompilerParams(vmem_limit_bytes=MEMORY),
        name="middle",
    )(lengths, counts, tokens, context, out_grad, weights, packed, factors, scales, *norms)


def devices():
    return lax.axis_size("dp") * lax.axis_size("tensor")


def hidden_rows():
    tiles = 2 * BLOCKS
    return PAD * -(-tiles // lax.axis_size("dp"))


def last_kernel(
    grad_one_ref,
    coeff_ref,
    index_ref,
    rel_coeff_ref,
    factor_ref,
    scale_ref,
    small_ref,
    hidden_ref,
    middle_scale_ref,
    tokens_any,
    gq_any,
    gk_any,
    gv_any,
    rel_any,
    geq_any,
    gfk_any,
    merged_any,
    in_grad_ref,
    down_out,
    up_out,
    hidden_up_out,
    hidden_down_out,
    scale_out,
    tokens_scr,
    grads_scr,
    rel_scr,
    geq_scr,
    gfk_scr,
    merged_scr,
    down_scr,
    up_scr,
    scale_scr,
    stage_scr,
    mine_late,
    land_late,
    mine_early,
    land_early,
    part_early,
    land_part,
    all_sums,
    all_hidden,
    load_sem,
    late_out_sem,
    late_in_sem,
    sums_out_sem,
    sums_in_sem,
    early_out_sem,
    early_in_sem,
    part_out_sem,
    part_in_sem,
    spread_out_sem,
    spread_in_sem,
):
    step = pl.program_id(0)
    final = TILES
    used = 2 * 3 * BLOCKS * RANK
    outer = lax.axis_size("dp")
    inner = lax.axis_size("tensor")
    count = outer * inner
    my_outer = lax.axis_index("dp")
    my_inner = lax.axis_index("tensor")
    me = my_outer * inner + my_inner
    barrier = pltpu.get_barrier_semaphore()

    def partner(off):
        other = lax.rem(me + off, count)
        return other, other // inner, lax.rem(other, inner)

    def send(src, dst, out_sem, in_sem, place):
        return pltpu.make_async_remote_copy(
            src_ref=src,
            dst_ref=dst,
            send_sem=out_sem,
            recv_sem=in_sem,
            device_id=place,
            device_id_type=MESH,
        )

    def late(off):
        other, row, col = partner(off)
        return send(
            mine_late.at[other], land_late.at[off], late_out_sem.at[0], late_in_sem.at[0], (row, col)
        )

    def sums(off):
        other, row, col = partner(off)
        return send(
            all_sums.at[0], all_sums.at[off], sums_out_sem.at[0], sums_in_sem.at[0], (row, col)
        )

    def every_late():
        others = pl.ds(1, count - 1)
        return send(
            mine_late.at[others],
            land_late.at[others],
            late_out_sem.at[0],
            late_in_sem.at[0],
            (my_outer, my_inner),
        )

    def every_sums():
        others = pl.ds(1, count - 1)
        return send(
            all_sums.at[others],
            all_sums.at[others],
            sums_out_sem.at[0],
            sums_in_sem.at[0],
            (my_outer, my_inner),
        )

    def early(off):
        col = lax.rem(my_inner + off, inner)
        return send(
            mine_early.at[col],
            land_early.at[off],
            early_out_sem.at[off],
            early_in_sem.at[off],
            (my_outer, col),
        )

    def part(off):
        row = lax.rem(my_outer + off, outer)
        return send(
            part_early.at[row],
            land_part.at[off],
            part_out_sem.at[off],
            part_in_sem.at[off],
            (row, my_inner),
        )

    def spread(off, origin):
        return send(
            all_hidden.at[origin],
            all_hidden.at[origin],
            spread_out_sem.at[off],
            spread_in_sem.at[off],
            (lax.rem(my_outer + off, outer), my_inner),
        )

    loads = [
        pltpu.make_async_copy(src, dst, load_sem.at[number])
        for number, (src, dst) in enumerate(
            (
                (tokens_any, tokens_scr),
                (gq_any, grads_scr.at[0]),
                (gk_any, grads_scr.at[1]),
                (gv_any, grads_scr.at[2]),
                (rel_any, rel_scr),
                (geq_any, geq_scr),
                (gfk_any, gfk_scr),
                (merged_any.at[pl.ds(0, 3)], merged_scr),
            )
        )
    ]

    @pl.when(step == 0)
    def _():
        for load in loads:
            load.start()

        @pl.loop(1, count)
        def _(off):
            _, row, col = partner(off)
            pl.semaphore_signal(barrier, inc=1, device_id=(row, col), device_id_type=MESH)

        scale_scr[...] = jnp.zeros_like(scale_scr)
        mine_early[...] = jnp.zeros_like(mine_early)
        for number in range(4):
            for block in range(BLOCKS):
                piece = number * BLOCKS + block
                mine_early[piece % inner, piece // inner, :PAD] = small_ref[
                    number, :, block * LANES : (block + 1) * LANES
                ].astype(bf16)
        tiles = mine_early.shape[2] // PAD - 1
        for chunk in range(inner):
            for which in range(2):
                for block in range(BLOCKS):
                    tile = which * BLOCKS + block
                    at = (tile % tiles + 1) * PAD
                    mine_early[chunk, tile // tiles, at : at + PAD] = hidden_ref[
                        which * inner + chunk, :, block * LANES : (block + 1) * LANES
                    ].astype(bf16)
        pl.semaphore_wait(barrier, count - 1)

        @pl.loop(1, inner)
        def _(off):
            early(off).start()

        land_early[0] = mine_early[my_inner]
        loads[0].wait()
        tokens = tokens_scr[...]
        for member in range(3):
            loads[1 + member].wait()
            grad = grads_scr[member]
            scale = scale_ref[:, member : member + 1]
            coeff = coeff_ref[member]
            slope = dot_nt(factor_ref[5 + member], grad)
            up_scr[member] = add_parts(dot_nn(two_parts(coeff * scale), grad))
            down_scr[member] = add_parts(dot_nn(two_parts(slope * scale), tokens))
            scale_scr[:, member : member + 1] += jnp.sum(coeff * slope, axis=1, keepdims=True)

        @pl.loop(1, inner)
        def _(off):
            early(off).wait_recv()

        part_early[...] = jnp.sum(land_early[...].astype(f32), axis=0).astype(bf16)

        @pl.loop(1, outer)
        def _(off):
            part(off).start()

        land_part[0] = part_early[my_outer]
        for load in loads[4:7]:
            load.wait()
        rel = rel_scr[...]
        bucket = lax.broadcasted_iota(jnp.int32, (2 * SPAN, OFFSETS), 0)
        for member, ref, row in ((0, geq_scr, 0), (1, gfk_scr, 1)):
            scale = scale_ref[:, member : member + 1]
            chosen = jnp.where(bucket == index_ref[row : row + 1, :], 1.0, 0.0).astype(bf16)
            grad = dot_nt(ref[...], chosen).astype(bf16)
            coeff = rel_coeff_ref[member]
            slope = dot_nn(factor_ref[5 + member], grad)
            up_scr[member] += add_parts(dot_nt(two_parts(coeff * scale), grad))
            down_scr[member] += add_parts(dot_nn(two_parts(slope * scale), rel))
            scale_scr[:, member : member + 1] += jnp.sum(coeff * slope, axis=1, keepdims=True)
        for number in range(6):
            ref = down_scr if number < 3 else up_scr
            for block in range(BLOCKS):
                at = (number * BLOCKS + block) * RANK
                stage_scr[at : at + RANK, :] = ref[
                    number % 3, :RANK, block * LANES : (block + 1) * LANES
                ]
        stage_scr[used : used + PAD, :] = scale_scr[...] + middle_scale_ref[...]
        stage_scr[used + PAD :, :] = jnp.zeros((count * PAD - used - PAD, LANES), f32)
        mine_late[...] = stage_scr[...].astype(bf16).reshape(count, PAD, LANES)

        @pl.loop(1, count)
        def _(off):
            late(off).start()

        land_late[0] = mine_late[me]
        loads[7].wait()

    @pl.when(step > 0)
    def _():
        rows = pl.ds(pl.multiple_of((step - 1) * BLOCK, BLOCK), BLOCK)
        in_grad = grad_one_ref[...]
        for member in range(3):
            in_grad = in_grad + dot_nt(grads_scr[member, rows, :], merged_scr[member])
        in_grad_ref[...] = in_grad

    @pl.when(step == SUMMED)
    def _():
        @pl.loop(1, outer)
        def _(off):
            part(off).wait_recv()

        summed = jnp.sum(land_part[...].astype(f32), axis=0).astype(bf16)
        all_hidden[my_outer] = summed[PAD:]
        all_sums[0, PAD:] = summed[:PAD]

        @pl.loop(1, outer)
        def _(off):
            spread(off, my_outer).start()

        every_late().wait_recv()
        all_sums[0, :PAD] = jnp.sum(land_late[...].astype(f32), axis=0).astype(bf16)

        @pl.loop(1, count)
        def _(off):
            sums(off).start()

    @pl.when(step == final)
    def _():
        @pl.loop(1, outer)
        def _(off):
            spread(off, lax.rem(my_outer + outer - off, outer)).wait_recv()

        tiles = all_hidden.shape[1] // PAD
        for which in range(2):
            for block in range(BLOCKS):
                tile = which * BLOCKS + block
                at = tile % tiles * PAD
                out = (hidden_up_out, hidden_down_out)[which]
                out[:, block * LANES : (block + 1) * LANES] = all_hidden[
                    tile // tiles, at : at + PAD
                ].astype(f32)[:RANK]

        every_sums().wait_recv()

        def summed_by(owner):
            return all_sums.at[lax.rem(me + count - owner, count)]

        for owner in range(count):
            stage_scr[owner * PAD : (owner + 1) * PAD, :] = summed_by(owner)[:PAD].astype(f32)
        for number in range(6):
            ref = down_out if number < 3 else up_out
            for block in range(BLOCKS):
                at = (number * BLOCKS + block) * RANK
                ref[number % 3, :, block * LANES : (block + 1) * LANES] = stage_scr[
                    at : at + RANK, :
                ]
        scale_out[...] = stage_scr[used : used + PAD, :].T[:6, :RANK]
        for number, (ref, place) in enumerate(
            ((down_out, 3), (up_out, 3), (down_out, 4), (up_out, 4))
        ):
            for block in range(BLOCKS):
                ref[place, :, block * LANES : (block + 1) * LANES] = summed_by(
                    number * BLOCKS + block
                )[PAD:].astype(f32)[:RANK]
        every_late().wait_send()
        every_sums().wait_send()

        @pl.loop(1, inner)
        def _(off):
            early(off).wait_send()

        @pl.loop(1, outer)
        def _(off):
            part(off).wait_send()
            spread(off, my_outer).wait_send()


def last(
    tokens, gq, gk, gv, grad_one, coeff, weights, index, rel_coeff, factors, scales,
    small, hidden, middle_scale, rel, geq, gfk,
):
    count = devices()
    outer = lax.axis_size("dp")
    inner = lax.axis_size("tensor")
    piece = hidden_rows()
    tile = pl.BlockSpec((BLOCK, D), lambda i: (jnp.maximum(i - 1, 0), 0))
    factor = jax.ShapeDtypeStruct((5, RANK, D), f32)
    block = pltpu.VMEM((count, PAD, LANES), bf16)
    return pl.pallas_call(
        last_kernel,
        grid=(1 + TILES,),
        in_specs=[
            tile,
            once(3, PAD, ROWS),
            once(2, OFFSETS),
            once(2, PAD, 2 * SPAN),
            once(12, PAD, D),
            once(PAD, LANES),
            once(4, PAD, D),
            once(2 * inner, PAD, D),
            once(PAD, LANES),
        ]
        + [pl.BlockSpec(memory_space=pl.ANY)] * 8,
        out_specs=[
            tile,
            whole(5, RANK, D),
            whole(5, RANK, D),
            whole(RANK, D),
            whole(RANK, D),
            whole(6, RANK),
        ],
        out_shape=[
            jax.ShapeDtypeStruct((ROWS, D), f32),
            factor,
            factor,
            jax.ShapeDtypeStruct((RANK, D), f32),
            jax.ShapeDtypeStruct((RANK, D), f32),
            jax.ShapeDtypeStruct((6, RANK), f32),
        ],
        scratch_shapes=[
            pltpu.VMEM((ROWS, D), bf16),
            pltpu.VMEM((3, ROWS, D), bf16),
            pltpu.VMEM((2 * SPAN, D), bf16),
            pltpu.VMEM((D, OFFSETS), bf16),
            pltpu.VMEM((D, OFFSETS), bf16),
            pltpu.VMEM((3, D, D), bf16),
            pltpu.VMEM((3, PAD, D), f32),
            pltpu.VMEM((3, PAD, D), f32),
            pltpu.VMEM((PAD, LANES), f32),
            pltpu.VMEM((count * PAD, LANES), f32),
            block,
            block,
            pltpu.VMEM((inner, outer, PAD + piece, LANES), bf16),
            pltpu.VMEM((inner, outer, PAD + piece, LANES), bf16),
            pltpu.VMEM((outer, PAD + piece, LANES), bf16),
            pltpu.VMEM((outer, PAD + piece, LANES), bf16),
            pltpu.VMEM((count, 2 * PAD, LANES), bf16),
            pltpu.VMEM((outer, piece, LANES), bf16),
            pltpu.SemaphoreType.DMA((8,)),
        ]
        + [pltpu.SemaphoreType.DMA((1,))] * 4
        + [pltpu.SemaphoreType.DMA((inner,))] * 2
        + [pltpu.SemaphoreType.DMA((outer,))] * 4,
        compiler_params=pltpu.CompilerParams(
            collective_id=0, has_side_effects=True, vmem_limit_bytes=MEMORY
        ),
        name="last",
    )(
        grad_one, coeff, index, rel_coeff, factors, scales, small, hidden, middle_scale,
        tokens, gq, gk, gv, rel, geq, gfk, weights,
    )


def finish_kernel(*refs):
    half = len(refs) // 2
    refs[half][...] = refs[0][...]

    @pl.when(pl.program_id(0) == 0)
    def _():
        for src, dst in zip(refs[1:half], refs[half + 1 :]):
            dst[...] = src[...]


def finish(in_grad, *small):
    tile = pl.BlockSpec((BLOCK, D), lambda i: (i, 0))
    specs = [tile] + [whole(*part.shape) for part in small]
    return pl.pallas_call(
        finish_kernel,
        grid=(ROWS // BLOCK,),
        in_specs=specs,
        out_specs=specs,
        out_shape=[jax.ShapeDtypeStruct(part.shape, part.dtype) for part in (in_grad, *small)],
        compiler_params=pltpu.CompilerParams(vmem_limit_bytes=MEMORY),
        name="finish",
    )(in_grad, *small)


def on_device(
    tokens,
    qkv_weight,
    out_weight,
    in_weight,
    back_weight,
    rel_embed,
    gain_one,
    shift_one,
    gain_two,
    shift_two,
    adapt_down,
    adapt_up,
    hidden_up,
    hidden_down,
    adapt_scale,
    seq_lengths,
    seq_counts,
    rel_bucket,
    out_grad,
):
    index_rows = jnp.pad(
        jnp.stack([rel_bucket[::-1], rel_bucket]), ((0, 0), (0, 1)), constant_values=-1
    )
    norms = (gain_one, shift_one, gain_two, shift_two)
    eq, fk, coeff, rel_coeff, factors, scales, context, p1, p2, p3, q, k, v, weights, gathered = front(
        seq_lengths, seq_counts, tokens, qkv_weight, rel_embed, index_rows, adapt_down, adapt_up,
        hidden_up, hidden_down, adapt_scale, out_weight, in_weight, back_weight,
    )
    mixed, grad_one, context_grad, small, hidden, middle_scale = middle(
        seq_lengths, seq_counts, tokens, context, out_grad, weights, gathered, factors, scales, norms
    )
    gq, gk, gv, geq, gfk = attend_backward(
        q, k, v, context_grad, context, eq, fk, p1, p2, p3
    )
    sums = last(
        tokens, gq, gk, gv, grad_one, coeff, weights, index_rows, rel_coeff, factors, scales,
        small, hidden, middle_scale, rel_embed, geq, gfk,
    )
    return (mixed, *finish(*sums))


def solution(mesh):
    rows = P(("dp", "tensor"), None)
    return jax.shard_map(
        on_device,
        mesh=mesh,
        in_specs=(
            rows,
            P(),
            P(),
            P(None, "tensor"),
            P("tensor", None),
            P(),
            P(),
            P(),
            P(),
            P(),
            P(),
            P(),
            P(None, "tensor"),
            P(None, "tensor"),
            P(),
            rows,
            rows,
            P(),
            rows,
        ),
        out_specs=(rows, rows, P(), P(), P(None, "tensor"), P(None, "tensor"), P()),
        check_vma=False,
    )
```

```python
import jax
import jax.numpy as jnp
from jax import lax
from jax.experimental import pallas as pl
from jax.experimental.pallas import tpu as pltpu
from jax.sharding import PartitionSpec as P

D = 768
H = 12
DH = 64
PAIR = 2 * DH
SPAN = 256
RANK = 12
PAD = 16
ROWS = 1024
LEN1 = 128
LEN3 = 512
OFFSETS = 2 * LEN3
TILE = 128
BLOCK = 256
SLOTS = ((0, 128), (128, 128), (256, 256), (512, 512))
PACKED = 1600
QUARTER = PACKED // 4
CHUNKS = 5
CHUNK = QUARTER // CHUNKS
TILES = ROWS // BLOCK
SUMMED = 2
WIDE = 1 * BLOCK
LAG = 1
LANES = 128
BLOCKS = D // LANES
MESH = pl.DeviceIdType.MESH
norm_epsilon = 1e-07
masked_score = -1e30
bf16 = jnp.bfloat16
f32 = jnp.float32
MEMORY = 60 * 1024 * 1024


def dot_nn(a, b):
    return jnp.dot(a, b, preferred_element_type=f32)


def dot_nt(a, b):
    return lax.dot_general(a, b, (((1,), (1,)), ((), ())), preferred_element_type=f32)


def dot_tn(a, b):
    return lax.dot_general(a, b, (((0,), (0,)), ((), ())), preferred_element_type=f32)


def two_parts(wide):
    high = wide.astype(bf16)
    rest = (wide - high.astype(f32)).astype(bf16)
    return jnp.concatenate([high, rest], axis=0)


def add_parts(stacked):
    return stacked[:PAD] + stacked[PAD:]


def merged(weight, down, up, scale):
    twice = jnp.concatenate([up, up], axis=0)
    extra = dot_tn(two_parts(down.astype(f32) * scale), twice)
    return (weight.astype(f32) + extra).astype(bf16)


def live_counts(lengths_ref, counts_ref):
    ranks = ((0, 0), (0, 1), (1, 0), (2, 0))
    return [
        jnp.where(rank < counts_ref[0, bucket], lengths_ref[0, slot], 0)
        for slot, (bucket, rank) in enumerate(ranks)
    ]


def padded(rows):
    return jnp.concatenate([rows.astype(f32), jnp.zeros((PAD - RANK, D), f32)], axis=0).astype(bf16)


def whole(*shape):
    return pl.BlockSpec(shape, lambda *at: (0,) * len(shape))


def once(*shape):
    return pl.BlockSpec(shape, lambda *at: (0,) * len(shape), pipeline_mode=pl.Buffered(1))


def unit_matrix(flipped):
    row = lax.broadcasted_iota(jnp.int32, (TILE, TILE), 0)
    col = lax.broadcasted_iota(jnp.int32, (TILE, TILE), 1)
    return jnp.where(row == (TILE - 1 - col if flipped else col), 1.0, 0.0).astype(bf16)


def head_lanes(member):
    lane = lax.broadcasted_iota(jnp.int32, (1, PAIR), 1)
    return jnp.where(lane // DH == member, 1.0, 0.0).astype(bf16)


def each_head(rows):
    return jnp.concatenate([rows * head_lanes(0), rows * head_lanes(1)], axis=0)


def own_lanes(stacked):
    lane = lax.broadcasted_iota(jnp.int32, (TILE, PAIR), 1)
    return jnp.where(lane < DH, stacked[:TILE], stacked[TILE:])


def lane_and_row():
    lane = lax.broadcasted_iota(jnp.int32, (8, 128), 1)
    return lane, lax.broadcasted_iota(jnp.int32, (8, 128), 0)


def turn(block, shift):
    return pltpu.roll(block, shift % 128, 1, stride=1, stride_axis=0)


def skew(table, length):
    lane, row = lane_and_row()
    count = length // 128
    done = []
    for at in range(0, TILE, 8):
        blocks = [table[at : at + 8, 128 * c : 128 * c + 128] for c in range(count + 1)]
        blocks[0] = jnp.where(lane + row >= 127 - at, blocks[0], blocks[count])
        moved = [turn(block, at + 1) for block in blocks[:count]]
        if count > 1:
            inside = lane - row <= at
            moved = [
                jnp.where(inside, moved[c], moved[(c + 1) % count]) for c in range(count)
            ]
        done.append(jnp.concatenate(moved, axis=1))
    return jnp.concatenate(done, axis=0)


def flip_rows(block):
    row = lax.broadcasted_iota(jnp.int32, (8, LANES), 0)
    done = []
    for at in range(TILE - 8, -1, -8):
        done.append(
            jnp.concatenate(
                [
                    jnp.take_along_axis(block[at : at + 8, c : c + LANES], 7 - row, axis=0)
                    for c in range(0, block.shape[1], LANES)
                ],
                axis=1,
            )
        )
    return jnp.concatenate(done, axis=0)


def slot_tiles(slot):
    return [(slot, t) for t in range(SLOTS[slot][1] // TILE)]


def prob_block(refs, slot, t, member):
    start, length = SLOTS[slot]
    at = start + t * TILE if length == LEN1 else t * TILE
    ref = refs[{LEN1: 0, LEN3: 2}.get(length, 1)]
    return ref.at[member, at : at + TILE, :]


def unskew(scores, length):
    lane, row = lane_and_row()
    zero = jnp.zeros((8, 128), f32)
    done = []
    for at in range(0, TILE, 8):
        moved = [
            turn(scores[at : at + 8, 128 * c : 128 * c + 128], at) for c in range(length // 128)
        ]
        before = lane - row < at
        done.append(
            jnp.concatenate(
                [jnp.where(before, x, y) for x, y in zip([zero] + moved, moved + [zero])], axis=1
            )
        )
    return jnp.concatenate(done, axis=0)


def gather_moves(packed, gathered, own_sem, sems):
    step = pl.program_id(0)
    d = lax.axis_index("dp")
    t = lax.axis_index("tensor")
    near = t + 1 - 2 * lax.rem(t, 2)
    far = t + 2 - 4 * (t // 2)
    mate = d + 1 - 2 * lax.rem(d, 2)
    other = d + 2 - 4 * lax.rem(d // 2, 2)
    mine = lax.rem(d, 4)
    mates = mine + 1 - 2 * lax.rem(mine, 2)
    others = mine + 2 - 4 * (mine // 2)
    across = 3 - mine
    near_out, near_in, own_sems = sems[0], sems[1], sems[2:]
    pairs = [own_sems[2 * i : 2 * i + 2] for i in range(8)]
    far_sems, mate_sems, other_sems, relay_sems, *pass_sems = pairs
    barrier = pltpu.get_barrier_semaphore()
    places = ((d, near), (d, far), (mate, t), (other, t))

    def rows(which, chunk):
        return pl.ds(pl.multiple_of(which * QUARTER + chunk * CHUNK, PAD), CHUNK)

    def send(src, dst, out_sem, in_sem, place):
        return pltpu.make_async_remote_copy(
            src_ref=src, dst_ref=dst, send_sem=out_sem, recv_sem=in_sem, device_id=place, device_id_type=MESH
        )

    def to_near():
        return send(packed, gathered.at[t], near_out.at[0], near_in.at[0], places[0])

    def to_far(chunk):
        here = rows(mine, chunk)
        return send(
            packed.at[here],
            gathered.at[t, here],
            far_sems[0].at[chunk],
            far_sems[1].at[chunk],
            places[1],
        )

    def onward(which, chunk, pair, place):
        here = gathered.at[far, rows(which, chunk)]
        return send(here, here, pair[0].at[chunk], pair[1].at[chunk], place)

    def to_mate(chunk):
        return onward(mine, chunk, mate_sems, places[2])

    def to_other(chunk):
        return onward(mine, chunk, other_sems, places[3])

    def relay(chunk):
        if chunk % 2 == 0:
            return onward(others, chunk, relay_sems, places[2])
        return onward(mates, chunk, relay_sems, places[3])

    def passing(number, chunk):
        which = (mine, mates, others, across)[number]
        return onward(which, chunk, pass_sems[number], places[0])

    def own():
        return pltpu.make_async_copy(packed, gathered.at[t], own_sem.at[0])

    def begin():
        for place in places:
            pl.semaphore_signal(barrier, inc=1, device_id=place, device_id_type=MESH)

    def forward(chunk):
        to_far(chunk).wait_recv()
        to_mate(chunk).start()
        to_other(chunk).start()
        passing(0, chunk).start()

    def cross(chunk):
        to_mate(chunk).wait_recv()
        to_other(chunk).wait_recv()
        relay(chunk).start()
        passing(1, chunk).start()
        passing(2, chunk).start()

    def close(chunk):
        relay(chunk).wait_recv()
        passing(3, chunk).start()

    plan = {
        3: ((forward, 0),),
        4: ((forward, 1),),
        5: ((forward, 2), (forward, 3)),
        6: ((cross, 0), (forward, 4)),
        7: ((cross, 1), (cross, 2)),
        8: ((cross, 3), (close, 0), (close, 1)),
        9: ((cross, 4), (close, 2), (close, 3)),
    }

    def go_on():
        @pl.when(step == 0)
        def _():
            own().start()
            pl.semaphore_wait(barrier, len(places))
            for chunk in range(CHUNKS):
                to_far(chunk).start()
            to_near().start()

        for when, moves in plan.items():

            @pl.when(step == when)
            def _(moves=moves):
                for move, chunk in moves:
                    move(chunk)

    def finish():
        close(CHUNKS - 1)
        own().wait()
        to_near().wait()
        for chunk in range(CHUNKS):
            for number in range(4):
                passing(number, chunk).wait()
            to_far(chunk).wait_send()
            to_mate(chunk).wait_send()
            to_other(chunk).wait_send()
            relay(chunk).wait_send()

    return begin, go_on, finish


def attend(
    lengths_ref, counts_ref, q_ref, k_ref, v_ref, ek_ref, eq_ref, context_ref, p1_ref, p2_ref, p3_ref,
    shift_scr, score_scr, prob_scr,
):
    eye = unit_matrix(False)
    factor = 1.4426950408889634 * (3.0 * DH) ** -0.5
    counts = live_counts(lengths_ref, counts_ref)
    turned_values = v_ref[...].T
    head_rows = [
        jnp.where(
            lax.broadcasted_iota(jnp.int32, (PAIR, 1), 0) // DH == member, 1.0, 0.0
        ).astype(bf16)
        for member in range(2)
    ]

    def place(slot, t):
        start, length = SLOTS[slot]
        low = LEN3 - TILE - TILE * t
        row = start + t * TILE
        return start, length, slice(row, row + TILE), slice(low, low + length + TILE)

    def shift_unit(slot, t):
        start, length, rows, window = place(slot, t)
        table = dot_nn(each_head(q_ref[rows, :]), ek_ref[:, window])
        for member in range(2):
            shift_scr[member, rows, :length] = skew(
                table[member * TILE : (member + 1) * TILE], length
            ).astype(bf16)

    def score_unit(slot, t):
        start, length, rows, window = place(slot, t)
        keys = each_head(k_ref[rows, :])
        table = dot_nn(keys, eq_ref[:, window])
        queries = q_ref[start : start + length, :]
        live = lax.broadcasted_iota(jnp.int32, (TILE, 1), 0) < counts[slot] - t * TILE
        tops = []
        for member in range(2):
            mine = slice(member * TILE, (member + 1) * TILE)
            left = jnp.concatenate([keys[mine], eye], axis=1)
            shifted = shift_scr[member, start : start + length, t * TILE : (t + 1) * TILE]
            right = jnp.concatenate([queries, shifted], axis=1)
            raw = dot_nt(left, right) + skew(table[mine], length)
            raw = jnp.where(live, raw * factor, masked_score)
            score_scr[member, rows, :length] = raw
            tops.append(jnp.max(raw, axis=0, keepdims=True))
        return tops

    def weight_unit(slot, t, tops):
        start, length, rows, window = place(slot, t)
        sums = []
        for member in range(2):
            weights = jnp.exp2(score_scr[member, rows, :length] - tops[member])
            score_scr[member, rows, :length] = weights
            sums.append(jnp.sum(weights, axis=0, keepdims=True))
        return sums

    def prob_unit(slot, t, inverses):
        start, length, rows, window = place(slot, t)
        for member in range(2):
            prob = score_scr[member, rows, :length] * inverses[member]
            prob_scr[member, rows, :length] = prob.astype(bf16)
            prob_block((p1_ref, p2_ref, p3_ref), slot, t, member)[...] = flip_rows(prob).astype(
                bf16
            )

    def context_unit(slot):
        start, length = SLOTS[slot]
        here = slice(start, start + length)
        left = jnp.concatenate([turned_values[:, here] * rows for rows in head_rows], axis=1)
        right = jnp.concatenate([prob_scr[member, here, :length] for member in range(2)], axis=0)
        context_ref[here, :] = dot_nn(left, right).astype(bf16).T

    def both(function, parts):
        return [function(member_parts) for member_parts in zip(*parts)]

    def largest(parts):
        total = parts[0]
        for part in parts[1:]:
            total = jnp.maximum(total, part)
        return total

    groups = ((3,), (2, 1, 0))
    tiles = [[unit for slot in group for unit in slot_tiles(slot)] for group in groups]
    held = {}

    def settle(slot):
        held[slot] = both(largest, [held.pop(unit) for unit in slot_tiles(slot)])

    def invert(slot):
        total = both(sum, [held.pop(unit) for unit in slot_tiles(slot)])
        held[slot] = [1.0 / part for part in total]

    for unit in tiles[0]:
        shift_unit(*unit)
    for first, second in zip(tiles[0], tiles[1]):
        held[first] = score_unit(*first)
        shift_unit(*second)
    settle(3)
    for first, second in zip(tiles[0], tiles[1]):
        held[second] = score_unit(*second)
        held[first] = weight_unit(*first, held[3])
    invert(3)
    for slot in groups[1]:
        settle(slot)
    for first, second in zip(tiles[0], tiles[1]):
        held[second] = weight_unit(*second, held[second[0]])
        prob_unit(*first, held[3])
    for slot in groups[1]:
        invert(slot)
    context_unit(3)
    for second in tiles[1]:
        prob_unit(*second, held[second[0]])
    for slot in groups[1]:
        context_unit(slot)


def reversed_buckets(row):
    wide = row.astype(f32) + 1.0
    blocks = jnp.concatenate(
        [wide[:, at : at + LANES] for at in range(OFFSETS - LANES, -1, -LANES)], axis=0
    )
    high = jnp.floor(blocks * 0.5)
    both = jnp.concatenate([high, blocks - 2.0 * high], axis=0).astype(bf16)
    turned = dot_nn(both, unit_matrix(True))
    count = OFFSETS // LANES
    value = 2.0 * turned[:count] + turned[count:]
    line = jnp.concatenate([value[at : at + 1, :] for at in range(count)], axis=1)
    line = pltpu.roll(jnp.broadcast_to(line, (8, OFFSETS)), OFFSETS - 1, 1)[:1]
    return (line - 1.0).astype(jnp.int32)


def front_kernel(
    lengths_ref,
    counts_ref,
    tokens_ref,
    bucket_ref,
    down_ref,
    up_ref,
    hidden_up_ref,
    hidden_down_ref,
    adapt_scale_ref,
    in_any,
    back_any,
    qkv_any,
    rel_any,
    out_any,
    eq_ref,
    fk_ref,
    coeff_ref,
    rel_coeff_ref,
    factor_ref,
    scale_ref,
    index_ref,
    context_ref,
    p1_ref,
    p2_ref,
    p3_ref,
    q_any,
    k_any,
    v_any,
    merged_any,
    gathered_any,
    q_scr,
    k_scr,
    v_scr,
    ekt_scr,
    eqt_scr,
    merged_scr,
    packed_scr,
    pos_scr,
    in_scr,
    back_scr,
    qkv_scr,
    rel_scr,
    out_scr,
    shift_scr,
    score_scr,
    prob_scr,
    load_sem,
    store_sem,
    own_sem,
    *gather_sems,
):
    step = pl.program_id(0)
    gather_start, gather_step, gather_end = gather_moves(
        packed_scr, gathered_any, own_sem, gather_sems
    )
    loads = [
        pltpu.make_async_copy(src, dst, load_sem.at[number])
        for number, (src, dst) in enumerate(
            (
                (in_any, in_scr),
                (back_any, back_scr),
                (qkv_any, qkv_scr),
                (rel_any, rel_scr),
                (out_any, out_scr),
            )
        )
    ]
    stores = [
        pltpu.make_async_copy(src, dst, store_sem.at[number])
        for number, (src, dst) in enumerate(
            ((q_scr, q_any), (k_scr, k_any), (v_scr, v_any), (merged_scr, merged_any))
        )
    ]

    @pl.when(step == 0)
    def _():
        gather_start()
        for load in loads:
            load.start()
        for number in range(5):
            factor_ref[number] = padded(down_ref[number])
            factor_ref[5 + number] = padded(up_ref[number])
        factor_ref[10] = padded(hidden_up_ref[...])
        factor_ref[11] = padded(hidden_down_ref[...])
        wide = jnp.concatenate([adapt_scale_ref[...], jnp.zeros((6, LANES - RANK), f32)], axis=1)
        wide = jnp.concatenate([wide, jnp.zeros((LANES - 6, LANES), f32)], axis=0)
        scale_ref[...] = wide.T[:PAD]
        packed_scr[2 * D : 2 * D + PAD] = factor_ref[10]
        packed_scr[2 * D + PAD : 2 * D + 2 * PAD] = factor_ref[11]
        packed_scr[2 * D + 2 * PAD :] = jnp.zeros((PACKED - 2 * D - 2 * PAD, D), bf16)
        loads[0].wait()
        packed_scr[:D] = merged(in_scr[...], factor_ref[4], factor_ref[10], scale_ref[:, 4:5])
        loads[1].wait()
        packed_scr[D : 2 * D] = merged(back_scr[...], factor_ref[11], factor_ref[9], scale_ref[:, 5:6])

    gather_step()

    @pl.when(step == 0)
    def _():
        index_ref[0:1, :] = reversed_buckets(bucket_ref[...].reshape(1, OFFSETS))
        index_ref[1:2, :] = bucket_ref[...].reshape(1, OFFSETS)
        loads[2].wait()
        for member in range(3):
            merged_scr[member] = merged(
                qkv_scr[member],
                factor_ref[member],
                factor_ref[5 + member],
                scale_ref[:, member : member + 1],
            )
        loads[3].wait()
        rel = rel_scr[...]
        for member in range(2):
            pos_scr[member] = dot_nn(rel, merged_scr[member]).astype(bf16)
        coeff = dot_nt(factor_ref[:2].reshape(2 * PAD, D), rel)
        rel_coeff_ref[...] = coeff.reshape(2, PAD, 2 * SPAN)

    @pl.when(step == 1)
    def _():
        loads[4].wait()
        merged_scr[3] = merged(out_scr[...], factor_ref[3], factor_ref[8], scale_ref[:, 3:4])

    @pl.when(step < TILES)
    def _():
        rows = pl.ds(pl.multiple_of(step * BLOCK, BLOCK), BLOCK)
        tokens = tokens_ref[...]
        for member, ref in enumerate((q_scr, k_scr, v_scr)):
            ref[rows, :] = dot_nn(tokens, merged_scr[member]).astype(bf16)
        coeff = dot_nt(factor_ref[:3].reshape(3 * PAD, D), tokens)
        coeff_ref[...] = coeff.reshape(3, PAD, BLOCK)
        bucket = lax.broadcasted_iota(jnp.int32, (2 * SPAN, BLOCK), 0)
        back, forth = (
            jnp.where(bucket == index_ref[row : row + 1, rows], 1.0, 0.0).astype(bf16)
            for row in range(2)
        )
        eq_ref[...] = dot_tn(back, pos_scr[0]).astype(bf16)
        fk_ref[...] = dot_tn(forth, pos_scr[1]).astype(bf16)
        ekt_scr[:, rows] = dot_tn(pos_scr[1], back).astype(bf16)
        eqt_scr[:, rows] = dot_tn(pos_scr[0], back).astype(bf16)

    @pl.when(step == TILES)
    def _():
        for store in stores:
            store.start()

    @pl.when(step >= TILES)
    def _():
        lanes = pl.ds(pl.multiple_of((step - TILES) * PAIR, PAIR), PAIR)
        attend(
            lengths_ref,
            counts_ref,
            q_scr.at[:, lanes],
            k_scr.at[:, lanes],
            v_scr.at[:, lanes],
            ekt_scr.at[lanes, :],
            eqt_scr.at[lanes, :],
            context_ref,
            p1_ref,
            p2_ref,
            p3_ref,
            shift_scr,
            score_scr,
            prob_scr,
        )

    @pl.when(step == pl.num_programs(0) - 1)
    def _():
        for store in stores:
            store.wait()
        gather_end()


PAIR_SPEC = pl.BlockSpec((ROWS, PAIR), lambda p: (0, p))
TABLE_SPEC = pl.BlockSpec((PAIR, OFFSETS), lambda p: (p, 0))
PROB_SIZES = ((256, 128), (256, 256), (512, 512))
PROB_SPECS = [pl.BlockSpec((2, *size), lambda p: (p, 0, 0)) for size in PROB_SIZES]


def front(
    lengths, counts, tokens, qkv_weight, rel_embed, buckets, down, up, hidden_up, hidden_down,
    adapt_scale, out_weight, in_weight, back_weight,
):
    single, several = (pltpu.SemaphoreType.DMA((n,)) for n in (1, CHUNKS))
    inner = lax.axis_size("tensor")
    assert inner == 4 and lax.axis_size("dp") % 4 == 0

    def tile_at(i):
        return jnp.minimum(i, TILES - 1)

    def pair_at(i):
        return jnp.maximum(i - TILES, 0)

    tile = pl.BlockSpec((BLOCK, D), lambda i: (tile_at(i), 0))
    rows = jax.ShapeDtypeStruct((ROWS, D), bf16)
    anywhere = pl.BlockSpec(memory_space=pl.ANY)
    return pl.pallas_call(
        front_kernel,
        grid=(TILES + H // 2,),
        in_specs=[pl.BlockSpec(memory_space=pltpu.SMEM)] * 2
        + [
            tile,
            once(OFFSETS),
            once(5, RANK, D),
            once(5, RANK, D),
            once(RANK, D),
            once(RANK, D),
            once(6, RANK),
        ]
        + [anywhere] * 5,
        out_specs=[tile] * 2
        + [
            pl.BlockSpec((3, PAD, BLOCK), lambda i: (0, 0, tile_at(i))),
            whole(2, PAD, 2 * SPAN),
            whole(12, PAD, D),
            whole(PAD, LANES),
            whole(2, OFFSETS),
            pl.BlockSpec((ROWS, PAIR), lambda i: (0, pair_at(i))),
        ]
        + [pl.BlockSpec((2, *size), lambda i: (pair_at(i), 0, 0)) for size in PROB_SIZES]
        + [anywhere] * 5,
        out_shape=[rows] * 2
        + [
            jax.ShapeDtypeStruct((3, PAD, ROWS), f32),
            jax.ShapeDtypeStruct((2, PAD, 2 * SPAN), f32),
            jax.ShapeDtypeStruct((12, PAD, D), bf16),
            jax.ShapeDtypeStruct((PAD, LANES), f32),
            jax.ShapeDtypeStruct((2, OFFSETS), jnp.int32),
            rows,
        ]
        + [jax.ShapeDtypeStruct((H, *size), bf16) for size in PROB_SIZES]
        + [rows] * 3
        + [
            jax.ShapeDtypeStruct((4, D, D), bf16),
            jax.ShapeDtypeStruct((inner, PACKED, D), bf16),
        ],
        scratch_shapes=[pltpu.VMEM((ROWS, D), bf16)] * 3
        + [pltpu.VMEM((D, OFFSETS), bf16)] * 2
        + [
            pltpu.VMEM((4, D, D), bf16),
            pltpu.VMEM((PACKED, D), bf16),
            pltpu.VMEM((2, 2 * SPAN, D), bf16),
            pltpu.VMEM((D, D), bf16),
            pltpu.VMEM((D, D), bf16),
            pltpu.VMEM((3, D, D), bf16),
            pltpu.VMEM((2 * SPAN, D), bf16),
            pltpu.VMEM((D, D), bf16),
            pltpu.VMEM((2, ROWS, LEN3), bf16),
            pltpu.VMEM((2, ROWS, LEN3), f32),
            pltpu.VMEM((2, ROWS, LEN3), bf16),
            pltpu.SemaphoreType.DMA((5,)),
            pltpu.SemaphoreType.DMA((4,)),
            pltpu.SemaphoreType.DMA((1,)),
        ]
        + [single] * 2
        + [several] * 16,
        compiler_params=pltpu.CompilerParams(
            collective_id=1, has_side_effects=True, vmem_limit_bytes=MEMORY
        ),
        name="front",
    )(
        lengths, counts, tokens, buckets, down, up, hidden_up, hidden_down, adapt_scale,
        in_weight, back_weight, qkv_weight, rel_embed, out_weight,
    )


def backward_kernel(
    q_ref,
    k_ref,
    v_ref,
    g_ref,
    context_ref,
    eq_ref,
    fk_ref,
    p1_ref,
    p2_ref,
    p3_ref,
    gq_ref,
    gk_ref,
    gv_ref,
    geq_ref,
    gfk_ref,
    grad_scr,
    turned_scr,
    geq_scr,
    gfk_scr,
):
    anti = unit_matrix(True)
    factor = (3.0 * DH) ** -0.5
    geq_scr[...] = jnp.zeros_like(geq_scr)
    gfk_scr[...] = jnp.zeros_like(gfk_scr)
    product = g_ref[...].astype(f32) * context_ref[...].astype(f32)
    high = product.astype(bf16)
    rest = (product - high.astype(f32)).astype(bf16)
    lane = lax.broadcasted_iota(jnp.int32, (PAD, 2 * PAIR), 1) % PAIR
    row = lax.broadcasted_iota(jnp.int32, (PAD, 2 * PAIR), 0)
    summing = jnp.where(lane // DH == row, 1.0, 0.0).astype(bf16)
    delta = dot_nt(summing, jnp.concatenate([high, rest], axis=1))

    def place(slot, t):
        start, length = SLOTS[slot]
        row = start + t * TILE
        return start, length, slice(row, row + TILE)

    def spot(slot, t):
        start, length = SLOTS[slot]
        row = start + length - (t + 1) * TILE
        return slice(row, row + TILE)

    def open_unit(slot, t):
        start, length, rows = place(slot, t)
        both = jnp.concatenate([k_ref[rows, :], v_ref[rows, :]], axis=1)
        both = dot_nn(anti, both).astype(bf16)
        turned_scr[spot(slot, t), :] = both[:, :PAIR]
        return dot_nt(each_head(both[:, PAIR:]), g_ref[start : start + length, :])

    def raw_unit(slot, t, grad_prob):
        start, length, rows = place(slot, t)
        spreads = []
        for member in range(2):
            prob = prob_block((p1_ref, p2_ref, p3_ref), slot, t, member)[...].astype(f32)
            mine = grad_prob[member * TILE : (member + 1) * TILE]
            raw = (prob * (mine - delta[member : member + 1, start : start + length])).astype(bf16)
            grad_scr[member, spot(slot, t), :length] = raw
            spreads.append(unskew(raw.astype(f32), length).astype(bf16))
        return jnp.concatenate(spreads, axis=0)

    def key_unit(slot, t, spread):
        start, length, rows = place(slot, t)
        low = LEN3 - TILE - TILE * t
        window = slice(low, low + length + TILE)
        here = slice(start, start + length)
        raw = jnp.concatenate(
            [grad_scr[member, spot(slot, t), :length] for member in range(2)], axis=0
        )
        probs = jnp.concatenate(
            [prob_block((p1_ref, p2_ref, p3_ref), slot, t, member)[...] for member in range(2)],
            axis=0,
        )
        key_grad = dot_nn(
            jnp.concatenate([raw, spread], axis=1),
            jnp.concatenate([q_ref[here, :], eq_ref[window, :]], axis=0),
        )
        value_grad = dot_nn(probs, g_ref[here, :])
        both = jnp.concatenate([own_lanes(key_grad) * factor, own_lanes(value_grad)], axis=1)
        both = dot_nn(anti, both.astype(bf16)).astype(bf16)
        gk_ref[rows, :] = both[:, :PAIR]
        gv_ref[rows, :] = both[:, PAIR:]
        geq_scr[:, window] += dot_tn(each_head(turned_scr[spot(slot, t), :]), spread)

    def turn_unit(slot, t):
        start, length, rows = place(slot, t)
        raws, spreads = [], []
        for member in range(2):
            raw = grad_scr[member, start : start + length, t * TILE : (t + 1) * TILE].T
            raws.append(raw)
            spreads.append(unskew(raw.astype(f32), length).astype(bf16))
        return jnp.concatenate(raws, axis=0), jnp.concatenate(spreads, axis=0)

    def query_unit(slot, t, raw, spread):
        start, length, rows = place(slot, t)
        low = LEN3 - length + TILE * t
        window = slice(low, low + length + TILE)
        query_grad = dot_nn(
            jnp.concatenate([raw, spread], axis=1),
            jnp.concatenate(
                [turned_scr[start : start + length, :], fk_ref[window, :]], axis=0
            ),
        )
        gq_ref[rows, :] = (own_lanes(query_grad) * factor).astype(bf16)
        gfk_scr[:, window] += dot_tn(each_head(q_ref[rows, :]), spread)

    first, second = slot_tiles(3), slot_tiles(2) + slot_tiles(1) + slot_tiles(0)
    jobs = [("key", unit) for unit in second]
    for one, other in zip(first, second):
        jobs += [("key", one), ("query", other)]
    jobs += [("query", unit) for unit in first]
    held = {}
    for at in range(len(jobs) + 2):
        if at < len(jobs):
            kind, unit = jobs[at]
            held[at] = open_unit(*unit) if kind == "key" else None
        if 0 <= at - 1 < len(jobs):
            kind, unit = jobs[at - 1]
            if kind == "key":
                held[at - 1] = raw_unit(*unit, held[at - 1])
            else:
                held[at - 1] = turn_unit(*unit)
        if 0 <= at - 2 < len(jobs):
            kind, unit = jobs[at - 2]
            if kind == "key":
                key_unit(*unit, held.pop(at - 2))
            else:
                query_unit(*unit, *held.pop(at - 2))
    geq_ref[...] = (geq_scr[...] * factor).astype(bf16)
    gfk_ref[...] = (gfk_scr[...] * factor).astype(bf16)


def attend_backward(q, k, v, g, context, eq, fk, p1, p2, p3):
    return pl.pallas_call(
        backward_kernel,
        grid=(H // 2,),
        in_specs=[PAIR_SPEC] * 7 + PROB_SPECS,
        out_specs=[PAIR_SPEC] * 3 + [TABLE_SPEC] * 2,
        out_shape=[jax.ShapeDtypeStruct((ROWS, D), bf16)] * 3
        + [jax.ShapeDtypeStruct((D, OFFSETS), bf16)] * 2,
        scratch_shapes=[
            pltpu.VMEM((2, ROWS, LEN3), bf16),
            pltpu.VMEM((ROWS, PAIR), bf16),
            pltpu.VMEM((PAIR, OFFSETS), f32),
            pltpu.VMEM((PAIR, OFFSETS), f32),
        ],
        compiler_params=pltpu.CompilerParams(vmem_limit_bytes=MEMORY),
        name="attention_backward",
    )(q, k, v, g, context, eq, fk, p1, p2, p3)


def gelu_pair(hidden):
    z = jnp.abs(hidden) * 0.7071067811865476
    t = 1.0 / (1.0 + 0.3275911 * z)
    poly = t * (
        0.127414796
        + t * (-0.142248368 + t * (0.7107068705 + t * (-0.7265760135 + t * 0.5307027145)))
    )
    bell = jnp.exp(-z * z)
    tail = poly * bell
    below = jnp.where(hidden >= 0, 1.0 - tail, tail)
    return hidden * below, below + hidden * (bell * 0.3989422804014327)


def norm_forward(values, gain, shift):
    centered = values - jnp.mean(values, axis=1, keepdims=True)
    inverse = lax.rsqrt(jnp.mean(centered * centered, axis=1, keepdims=True) + norm_epsilon)
    normal = centered * inverse
    return (normal * gain + shift, normal, inverse)


def norm_backward(grad_out, normal, inverse, gain):
    scaled = grad_out * gain
    return inverse * (
        scaled
        - jnp.mean(scaled, axis=1, keepdims=True)
        - normal * jnp.mean(scaled * normal, axis=1, keepdims=True)
    )


def middle_kernel(
    lengths_ref,
    counts_ref,
    tokens_ref,
    context_ref,
    out_grad_ref,
    weight_ref,
    packed_ref,
    factor_ref,
    scale_ref,
    gain_one_ref,
    shift_one_ref,
    gain_two_ref,
    shift_two_ref,
    mixed_ref,
    grad_one_ref,
    context_grad_ref,
    small_ref,
    hidden_ref,
    scale_grad_ref,
    active_scr,
    slope_scr,
):
    step = pl.program_id(0)
    chunks = packed_ref.shape[0]

    @pl.when(step == 0)
    def _():
        small_ref[...] = jnp.zeros_like(small_ref)
        hidden_ref[...] = jnp.zeros_like(hidden_ref)
        scale_grad_ref[...] = jnp.zeros_like(scale_grad_ref)

    gain_one, shift_one, gain_two, shift_two = (
        ref[...].reshape(1, D)
        for ref in (gain_one_ref, shift_one_ref, gain_two_ref, shift_two_ref)
    )
    used_rows = live_counts(lengths_ref, counts_ref)
    weight = weight_ref[0]

    def work(number):
        rows = slice(number * BLOCK, (number + 1) * BLOCK)
        row = lax.broadcasted_iota(jnp.int32, (BLOCK, 1), 0) + step * WIDE + number * BLOCK
        live = jnp.zeros((BLOCK, 1), f32)
        for (start, length), used in zip(SLOTS, used_rows):
            live = jnp.where((row >= start) & (row < start + used), 1.0, live)
        context = context_ref[rows, :]
        attended = dot_nn(context, weight)
        normed, normal_one, inverse_one = norm_forward(
            tokens_ref[rows, :].astype(f32) + attended, gain_one, shift_one
        )
        normed_low = normed.astype(bf16)
        yield
        mlp = jnp.zeros((BLOCK, D), f32)
        back_coeff = jnp.zeros((PAD, BLOCK), f32)
        ahead = dot_nn(normed_low, packed_ref[0, :D, :])
        for c in range(chunks):
            hidden = ahead
            if c + 1 < chunks:
                ahead = dot_nn(normed_low, packed_ref[c + 1, :D, :])
            active, slope = gelu_pair(hidden)
            active = active.astype(bf16)
            active_scr[c, rows, :] = active
            slope_scr[c, rows, :] = slope
            mlp = mlp + dot_nn(active, packed_ref[c, D : 2 * D, :])
            back_coeff = back_coeff + dot_nt(
                packed_ref[c, 2 * D + PAD : 2 * D + 2 * PAD, :], active
            )
            yield
        result, normal_two, inverse_two = norm_forward(normed + mlp, gain_two, shift_two)
        mixed_ref[rows, :] = (result * live).astype(bf16)
        grad_two = norm_backward(
            out_grad_ref[rows, :].astype(f32) * live, normal_two, inverse_two, gain_two
        )
        grad_mlp = grad_two.astype(bf16)
        yield
        back_slope = dot_nt(factor_ref[9], grad_mlp)
        small_ref[3] += add_parts(dot_nn(two_parts(back_coeff * scale_ref[:, 5:6]), grad_mlp))
        scale_grad_ref[:, 5:6] += jnp.sum(back_coeff * back_slope, axis=1, keepdims=True)
        back_through = two_parts(back_slope * scale_ref[:, 5:6])
        in_coeff = dot_nt(factor_ref[4], normed_low)
        in_scaled = two_parts(in_coeff * scale_ref[:, 4:5])
        in_slope = jnp.zeros((PAD, BLOCK), f32)
        grad_normed = grad_two
        ahead = dot_nt(grad_mlp, packed_ref[0, D : 2 * D, :])
        for c in range(chunks):
            grad_active = ahead
            if c + 1 < chunks:
                ahead = dot_nt(grad_mlp, packed_ref[c + 1, D : 2 * D, :])
            grad_hidden = (grad_active * slope_scr[c, rows, :]).astype(bf16)
            grad_normed = grad_normed + dot_nt(grad_hidden, packed_ref[c, :D, :])
            in_slope = in_slope + dot_nt(packed_ref[c, 2 * D : 2 * D + PAD, :], grad_hidden)
            hidden_ref[c] += add_parts(dot_nn(in_scaled, grad_hidden))
            hidden_ref[chunks + c] += add_parts(dot_nn(back_through, active_scr[c, rows, :]))
            yield
        scale_grad_ref[:, 4:5] += jnp.sum(in_coeff * in_slope, axis=1, keepdims=True)
        small_ref[2] += add_parts(dot_nn(two_parts(in_slope * scale_ref[:, 4:5]), normed_low))
        grad_one = norm_backward(grad_normed, normal_one, inverse_one, gain_one)
        grad_one_ref[rows, :] = grad_one
        grad_attended = grad_one.astype(bf16)
        yield
        context_grad_ref[rows, :] = dot_nt(grad_attended, weight).astype(bf16)
        out_coeff = dot_nt(factor_ref[3], context)
        out_slope = dot_nt(factor_ref[8], grad_attended)
        small_ref[1] += add_parts(dot_nn(two_parts(out_coeff * scale_ref[:, 3:4]), grad_attended))
        small_ref[0] += add_parts(dot_nn(two_parts(out_slope * scale_ref[:, 3:4]), context))
        scale_grad_ref[:, 3:4] += jnp.sum(out_coeff * out_slope, axis=1, keepdims=True)

    waiting = [work(number) for number in range(WIDE // BLOCK)]
    running = []
    turn_number = 0
    while waiting or running:
        if waiting and turn_number % LAG == 0:
            running.append(waiting.pop(0))
        turn_number += 1
        for job in list(running):
            try:
                next(job)
            except StopIteration:
                running.remove(job)


def middle(lengths, counts, tokens, context, out_grad, weights, packed, factors, scales, norms):
    chunks = packed.shape[0]
    tile = pl.BlockSpec((WIDE, D), lambda i: (i, 0))
    return pl.pallas_call(
        middle_kernel,
        grid=(ROWS // WIDE,),
        in_specs=[pl.BlockSpec(memory_space=pltpu.SMEM)] * 2
        + [tile] * 3
        + [
            pl.BlockSpec((1, D, D), lambda i: (3, 0, 0)),
            pl.BlockSpec(
                (chunks, PACKED, D), lambda i: (0, 0, 0), pipeline_mode=pl.Buffered(1)
            ),
            whole(12, PAD, D),
            whole(PAD, 128),
        ]
        + [whole(D)] * 4,
        out_specs=[tile] * 3
        + [whole(4, PAD, D), whole(2 * chunks, PAD, D), whole(PAD, 128)],
        out_shape=[
            jax.ShapeDtypeStruct((ROWS, D), bf16),
            jax.ShapeDtypeStruct((ROWS, D), f32),
            jax.ShapeDtypeStruct((ROWS, D), bf16),
            jax.ShapeDtypeStruct((4, PAD, D), f32),
            jax.ShapeDtypeStruct((2 * chunks, PAD, D), f32),
            jax.ShapeDtypeStruct((PAD, 128), f32),
        ],
        scratch_shapes=[
            pltpu.VMEM((chunks, WIDE, D), bf16),
            pltpu.VMEM((chunks, WIDE, D), f32),
        ],
        compiler_params=pltpu.CompilerParams(vmem_limit_bytes=MEMORY),
        name="middle",
    )(lengths, counts, tokens, context, out_grad, weights, packed, factors, scales, *norms)


def devices():
    return lax.axis_size("dp") * lax.axis_size("tensor")


def hidden_rows():
    tiles = 2 * BLOCKS
    return PAD * -(-tiles // lax.axis_size("dp"))


def last_kernel(
    grad_one_ref,
    coeff_ref,
    index_ref,
    rel_coeff_ref,
    factor_ref,
    scale_ref,
    small_ref,
    hidden_ref,
    middle_scale_ref,
    tokens_any,
    gq_any,
    gk_any,
    gv_any,
    rel_any,
    geq_any,
    gfk_any,
    merged_any,
    in_grad_ref,
    down_out,
    up_out,
    hidden_up_out,
    hidden_down_out,
    scale_out,
    tokens_scr,
    grads_scr,
    rel_scr,
    geq_scr,
    gfk_scr,
    merged_scr,
    down_scr,
    up_scr,
    scale_scr,
    stage_scr,
    mine_late,
    land_late,
    mine_early,
    land_early,
    part_early,
    land_part,
    all_sums,
    all_hidden,
    load_sem,
    late_out_sem,
    late_in_sem,
    sums_out_sem,
    sums_in_sem,
    early_out_sem,
    early_in_sem,
    part_out_sem,
    part_in_sem,
    spread_out_sem,
    spread_in_sem,
):
    step = pl.program_id(0)
    final = TILES
    used = 2 * 3 * BLOCKS * RANK
    outer = lax.axis_size("dp")
    inner = lax.axis_size("tensor")
    count = outer * inner
    my_outer = lax.axis_index("dp")
    my_inner = lax.axis_index("tensor")
    me = my_outer * inner + my_inner
    barrier = pltpu.get_barrier_semaphore()

    def partner(off):
        other = lax.rem(me + off, count)
        return other, other // inner, lax.rem(other, inner)

    def send(src, dst, out_sem, in_sem, place):
        return pltpu.make_async_remote_copy(
            src_ref=src,
            dst_ref=dst,
            send_sem=out_sem,
            recv_sem=in_sem,
            device_id=place,
            device_id_type=MESH,
        )

    def late(off):
        other, row, col = partner(off)
        return send(
            mine_late.at[other], land_late.at[off], late_out_sem.at[0], late_in_sem.at[0], (row, col)
        )

    def sums(off):
        other, row, col = partner(off)
        return send(
            all_sums.at[0], all_sums.at[off], sums_out_sem.at[0], sums_in_sem.at[0], (row, col)
        )

    def every_late():
        others = pl.ds(1, count - 1)
        return send(
            mine_late.at[others],
            land_late.at[others],
            late_out_sem.at[0],
            late_in_sem.at[0],
            (my_outer, my_inner),
        )

    def every_sums():
        others = pl.ds(1, count - 1)
        return send(
            all_sums.at[others],
            all_sums.at[others],
            sums_out_sem.at[0],
            sums_in_sem.at[0],
            (my_outer, my_inner),
        )

    def early(off):
        col = lax.rem(my_inner + off, inner)
        return send(
            mine_early.at[col],
            land_early.at[off],
            early_out_sem.at[off],
            early_in_sem.at[off],
            (my_outer, col),
        )

    def part(off):
        row = lax.rem(my_outer + off, outer)
        return send(
            part_early.at[row],
            land_part.at[off],
            part_out_sem.at[off],
            part_in_sem.at[off],
            (row, my_inner),
        )

    def spread(off, origin):
        return send(
            all_hidden.at[origin],
            all_hidden.at[origin],
            spread_out_sem.at[off],
            spread_in_sem.at[off],
            (lax.rem(my_outer + off, outer), my_inner),
        )

    loads = [
        pltpu.make_async_copy(src, dst, load_sem.at[number])
        for number, (src, dst) in enumerate(
            (
                (tokens_any, tokens_scr),
                (gq_any, grads_scr.at[0]),
                (gk_any, grads_scr.at[1]),
                (gv_any, grads_scr.at[2]),
                (rel_any, rel_scr),
                (geq_any, geq_scr),
                (gfk_any, gfk_scr),
                (merged_any.at[pl.ds(0, 3)], merged_scr),
            )
        )
    ]

    @pl.when(step == 0)
    def _():
        for load in loads:
            load.start()

        @pl.loop(1, count)
        def _(off):
            _, row, col = partner(off)
            pl.semaphore_signal(barrier, inc=1, device_id=(row, col), device_id_type=MESH)

        scale_scr[...] = jnp.zeros_like(scale_scr)
        mine_early[...] = jnp.zeros_like(mine_early)
        for number in range(4):
            for block in range(BLOCKS):
                piece = number * BLOCKS + block
                mine_early[piece % inner, piece // inner, :PAD] = small_ref[
                    number, :, block * LANES : (block + 1) * LANES
                ].astype(bf16)
        tiles = mine_early.shape[2] // PAD - 1
        for chunk in range(inner):
            for which in range(2):
                for block in range(BLOCKS):
                    tile = which * BLOCKS + block
                    at = (tile % tiles + 1) * PAD
                    mine_early[chunk, tile // tiles, at : at + PAD] = hidden_ref[
                        which * inner + chunk, :, block * LANES : (block + 1) * LANES
                    ].astype(bf16)
        pl.semaphore_wait(barrier, count - 1)

        @pl.loop(1, inner)
        def _(off):
            early(off).start()

        land_early[0] = mine_early[my_inner]
        loads[0].wait()
        tokens = tokens_scr[...]
        for member in range(3):
            loads[1 + member].wait()
            grad = grads_scr[member]
            scale = scale_ref[:, member : member + 1]
            coeff = coeff_ref[member]
            slope = dot_nt(factor_ref[5 + member], grad)
            up_scr[member] = add_parts(dot_nn(two_parts(coeff * scale), grad))
            down_scr[member] = add_parts(dot_nn(two_parts(slope * scale), tokens))
            scale_scr[:, member : member + 1] += jnp.sum(coeff * slope, axis=1, keepdims=True)

        @pl.loop(1, inner)
        def _(off):
            early(off).wait_recv()

        part_early[...] = jnp.sum(land_early[...].astype(f32), axis=0).astype(bf16)

        @pl.loop(1, outer)
        def _(off):
            part(off).start()

        land_part[0] = part_early[my_outer]
        for load in loads[4:7]:
            load.wait()
        rel = rel_scr[...]
        bucket = lax.broadcasted_iota(jnp.int32, (2 * SPAN, OFFSETS), 0)
        for member, ref, row in ((0, geq_scr, 0), (1, gfk_scr, 1)):
            scale = scale_ref[:, member : member + 1]
            chosen = jnp.where(bucket == index_ref[row : row + 1, :], 1.0, 0.0).astype(bf16)
            grad = dot_nt(ref[...], chosen).astype(bf16)
            coeff = rel_coeff_ref[member]
            slope = dot_nn(factor_ref[5 + member], grad)
            up_scr[member] += add_parts(dot_nt(two_parts(coeff * scale), grad))
            down_scr[member] += add_parts(dot_nn(two_parts(slope * scale), rel))
            scale_scr[:, member : member + 1] += jnp.sum(coeff * slope, axis=1, keepdims=True)
        for number in range(6):
            ref = down_scr if number < 3 else up_scr
            for block in range(BLOCKS):
                at = (number * BLOCKS + block) * RANK
                stage_scr[at : at + RANK, :] = ref[
                    number % 3, :RANK, block * LANES : (block + 1) * LANES
                ]
        stage_scr[used : used + PAD, :] = scale_scr[...] + middle_scale_ref[...]
        stage_scr[used + PAD :, :] = jnp.zeros((count * PAD - used - PAD, LANES), f32)
        mine_late[...] = stage_scr[...].astype(bf16).reshape(count, PAD, LANES)

        @pl.loop(1, count)
        def _(off):
            late(off).start()

        land_late[0] = mine_late[me]
        loads[7].wait()

    @pl.when(step > 0)
    def _():
        rows = pl.ds(pl.multiple_of((step - 1) * BLOCK, BLOCK), BLOCK)
        in_grad = grad_one_ref[...]
        for member in range(3):
            in_grad = in_grad + dot_nt(grads_scr[member, rows, :], merged_scr[member])
        in_grad_ref[...] = in_grad

    @pl.when(step == SUMMED)
    def _():
        @pl.loop(1, outer)
        def _(off):
            part(off).wait_recv()

        summed = jnp.sum(land_part[...].astype(f32), axis=0).astype(bf16)
        all_hidden[my_outer] = summed[PAD:]
        all_sums[0, PAD:] = summed[:PAD]

        @pl.loop(1, outer)
        def _(off):
            spread(off, my_outer).start()

        every_late().wait_recv()
        all_sums[0, :PAD] = jnp.sum(land_late[...].astype(f32), axis=0).astype(bf16)

        @pl.loop(1, count)
        def _(off):
            sums(off).start()

    @pl.when(step == final)
    def _():
        @pl.loop(1, outer)
        def _(off):
            spread(off, lax.rem(my_outer + outer - off, outer)).wait_recv()

        tiles = all_hidden.shape[1] // PAD
        for which in range(2):
            for block in range(BLOCKS):
                tile = which * BLOCKS + block
                at = tile % tiles * PAD
                out = (hidden_up_out, hidden_down_out)[which]
                out[:, block * LANES : (block + 1) * LANES] = all_hidden[
                    tile // tiles, at : at + PAD
                ].astype(f32)[:RANK]

        every_sums().wait_recv()

        def summed_by(owner):
            return all_sums.at[lax.rem(me + count - owner, count)]

        for owner in range(count):
            stage_scr[owner * PAD : (owner + 1) * PAD, :] = summed_by(owner)[:PAD].astype(f32)
        for number in range(6):
            ref = down_out if number < 3 else up_out
            for block in range(BLOCKS):
                at = (number * BLOCKS + block) * RANK
                ref[number % 3, :, block * LANES : (block + 1) * LANES] = stage_scr[
                    at : at + RANK, :
                ]
        scale_out[...] = stage_scr[used : used + PAD, :].T[:6, :RANK]
        for number, (ref, place) in enumerate(
            ((down_out, 3), (up_out, 3), (down_out, 4), (up_out, 4))
        ):
            for block in range(BLOCKS):
                ref[place, :, block * LANES : (block + 1) * LANES] = summed_by(
                    number * BLOCKS + block
                )[PAD:].astype(f32)[:RANK]
        every_late().wait_send()
        every_sums().wait_send()

        @pl.loop(1, inner)
        def _(off):
            early(off).wait_send()

        @pl.loop(1, outer)
        def _(off):
            part(off).wait_send()
            spread(off, my_outer).wait_send()


def last(
    tokens, gq, gk, gv, grad_one, coeff, weights, index, rel_coeff, factors, scales,
    small, hidden, middle_scale, rel, geq, gfk,
):
    count = devices()
    outer = lax.axis_size("dp")
    inner = lax.axis_size("tensor")
    piece = hidden_rows()
    tile = pl.BlockSpec((BLOCK, D), lambda i: (jnp.maximum(i - 1, 0), 0))
    factor = jax.ShapeDtypeStruct((5, RANK, D), f32)
    block = pltpu.VMEM((count, PAD, LANES), bf16)
    return pl.pallas_call(
        last_kernel,
        grid=(1 + TILES,),
        in_specs=[
            tile,
            once(3, PAD, ROWS),
            once(2, OFFSETS),
            once(2, PAD, 2 * SPAN),
            once(12, PAD, D),
            once(PAD, LANES),
            once(4, PAD, D),
            once(2 * inner, PAD, D),
            once(PAD, LANES),
        ]
        + [pl.BlockSpec(memory_space=pl.ANY)] * 8,
        out_specs=[
            tile,
            whole(5, RANK, D),
            whole(5, RANK, D),
            whole(RANK, D),
            whole(RANK, D),
            whole(6, RANK),
        ],
        out_shape=[
            jax.ShapeDtypeStruct((ROWS, D), f32),
            factor,
            factor,
            jax.ShapeDtypeStruct((RANK, D), f32),
            jax.ShapeDtypeStruct((RANK, D), f32),
            jax.ShapeDtypeStruct((6, RANK), f32),
        ],
        scratch_shapes=[
            pltpu.VMEM((ROWS, D), bf16),
            pltpu.VMEM((3, ROWS, D), bf16),
            pltpu.VMEM((2 * SPAN, D), bf16),
            pltpu.VMEM((D, OFFSETS), bf16),
            pltpu.VMEM((D, OFFSETS), bf16),
            pltpu.VMEM((3, D, D), bf16),
            pltpu.VMEM((3, PAD, D), f32),
            pltpu.VMEM((3, PAD, D), f32),
            pltpu.VMEM((PAD, LANES), f32),
            pltpu.VMEM((count * PAD, LANES), f32),
            block,
            block,
            pltpu.VMEM((inner, outer, PAD + piece, LANES), bf16),
            pltpu.VMEM((inner, outer, PAD + piece, LANES), bf16),
            pltpu.VMEM((outer, PAD + piece, LANES), bf16),
            pltpu.VMEM((outer, PAD + piece, LANES), bf16),
            pltpu.VMEM((count, 2 * PAD, LANES), bf16),
            pltpu.VMEM((outer, piece, LANES), bf16),
            pltpu.SemaphoreType.DMA((8,)),
        ]
        + [pltpu.SemaphoreType.DMA((1,))] * 4
        + [pltpu.SemaphoreType.DMA((inner,))] * 2
        + [pltpu.SemaphoreType.DMA((outer,))] * 4,
        compiler_params=pltpu.CompilerParams(
            collective_id=0, has_side_effects=True, vmem_limit_bytes=MEMORY
        ),
        name="last",
    )(
        grad_one, coeff, index, rel_coeff, factors, scales, small, hidden, middle_scale,
        tokens, gq, gk, gv, rel, geq, gfk, weights,
    )


def finish_kernel(*refs):
    half = len(refs) // 2
    refs[half][...] = refs[0][...]

    @pl.when(pl.program_id(0) == 0)
    def _():
        for src, dst in zip(refs[1:half], refs[half + 1 :]):
            dst[...] = src[...]


def finish(in_grad, *small):
    tile = pl.BlockSpec((BLOCK, D), lambda i: (i, 0))
    specs = [tile] + [whole(*part.shape) for part in small]
    return pl.pallas_call(
        finish_kernel,
        grid=(ROWS // BLOCK,),
        in_specs=specs,
        out_specs=specs,
        out_shape=[jax.ShapeDtypeStruct(part.shape, part.dtype) for part in (in_grad, *small)],
        compiler_params=pltpu.CompilerParams(vmem_limit_bytes=MEMORY),
        name="finish",
    )(in_grad, *small)


def on_device(
    tokens,
    qkv_weight,
    out_weight,
    in_weight,
    back_weight,
    rel_embed,
    gain_one,
    shift_one,
    gain_two,
    shift_two,
    adapt_down,
    adapt_up,
    hidden_up,
    hidden_down,
    adapt_scale,
    seq_lengths,
    seq_counts,
    rel_bucket,
    out_grad,
):
    buckets = jnp.pad(rel_bucket, (0, 1), constant_values=-1)
    norms = (gain_one, shift_one, gain_two, shift_two)
    (
        eq, fk, coeff, rel_coeff, factors, scales, index_rows, context, p1, p2, p3, q, k, v, weights,
        gathered,
    ) = front(
        seq_lengths, seq_counts, tokens, qkv_weight, rel_embed, buckets, adapt_down, adapt_up,
        hidden_up, hidden_down, adapt_scale, out_weight, in_weight, back_weight,
    )
    mixed, grad_one, context_grad, small, hidden, middle_scale = middle(
        seq_lengths, seq_counts, tokens, context, out_grad, weights, gathered, factors, scales, norms
    )
    gq, gk, gv, geq, gfk = attend_backward(
        q, k, v, context_grad, context, eq, fk, p1, p2, p3
    )
    sums = last(
        tokens, gq, gk, gv, grad_one, coeff, weights, index_rows, rel_coeff, factors, scales,
        small, hidden, middle_scale, rel_embed, geq, gfk,
    )
    return (mixed, *finish(*sums))


def solution(mesh):
    rows = P(("dp", "tensor"), None)
    return jax.shard_map(
        on_device,
        mesh=mesh,
        in_specs=(
            rows,
            P(),
            P(),
            P(None, "tensor"),
            P("tensor", None),
            P(),
            P(),
            P(),
            P(),
            P(),
            P(),
            P(),
            P(None, "tensor"),
            P(None, "tensor"),
            P(),
            rows,
            rows,
            P(),
            rows,
        ),
        out_specs=(rows, rows, P(), P(), P(None, "tensor"), P(None, "tensor"), P()),
        check_vma=False,
    )
```

```python
import jax
import jax.numpy as jnp
from jax import lax
from jax.experimental import pallas as pl
from jax.experimental.pallas import tpu as pltpu
from jax.sharding import PartitionSpec as P

D = 768
H = 12
DH = 64
PAIR = 2 * DH
SPAN = 256
RANK = 12
PAD = 16
ROWS = 1024
LEN1 = 128
LEN3 = 512
OFFSETS = 2 * LEN3
TILE = 128
BLOCK = 256
SLOTS = ((0, 128), (128, 128), (256, 256), (512, 512))
PACKED = 1600
QUARTER = PACKED // 4
CHUNKS = 5
CHUNK = QUARTER // CHUNKS
TILES = ROWS // BLOCK
SUMMED = 1
WIDE = 1 * BLOCK
LAG = 1
LANES = 128
BLOCKS = D // LANES
MESH = pl.DeviceIdType.MESH
norm_epsilon = 1e-07
masked_score = -1e30
bf16 = jnp.bfloat16
f32 = jnp.float32
MEMORY = 60 * 1024 * 1024


def dot_nn(a, b):
    return jnp.dot(a, b, preferred_element_type=f32)


def dot_nt(a, b):
    return lax.dot_general(a, b, (((1,), (1,)), ((), ())), preferred_element_type=f32)


def dot_tn(a, b):
    return lax.dot_general(a, b, (((0,), (0,)), ((), ())), preferred_element_type=f32)


def two_parts(wide):
    high = wide.astype(bf16)
    rest = (wide - high.astype(f32)).astype(bf16)
    return jnp.concatenate([high, rest], axis=0)


def add_parts(stacked):
    return stacked[:PAD] + stacked[PAD:]


def merged(weight, down, up, scale):
    twice = jnp.concatenate([up, up], axis=0)
    extra = dot_tn(two_parts(down.astype(f32) * scale), twice)
    return (weight.astype(f32) + extra).astype(bf16)


def live_counts(lengths_ref, counts_ref):
    ranks = ((0, 0), (0, 1), (1, 0), (2, 0))
    return [
        jnp.where(rank < counts_ref[0, bucket], lengths_ref[0, slot], 0)
        for slot, (bucket, rank) in enumerate(ranks)
    ]


def padded(rows):
    return jnp.concatenate([rows.astype(f32), jnp.zeros((PAD - RANK, D), f32)], axis=0).astype(bf16)


def whole(*shape):
    return pl.BlockSpec(shape, lambda *at: (0,) * len(shape))


def once(*shape):
    return pl.BlockSpec(shape, lambda *at: (0,) * len(shape), pipeline_mode=pl.Buffered(1))


def unit_matrix(flipped):
    row = lax.broadcasted_iota(jnp.int32, (TILE, TILE), 0)
    col = lax.broadcasted_iota(jnp.int32, (TILE, TILE), 1)
    return jnp.where(row == (TILE - 1 - col if flipped else col), 1.0, 0.0).astype(bf16)


def head_lanes(member):
    lane = lax.broadcasted_iota(jnp.int32, (1, PAIR), 1)
    return jnp.where(lane // DH == member, 1.0, 0.0).astype(bf16)


def each_head(rows):
    return jnp.concatenate([rows * head_lanes(0), rows * head_lanes(1)], axis=0)


def own_lanes(stacked):
    lane = lax.broadcasted_iota(jnp.int32, (TILE, PAIR), 1)
    return jnp.where(lane < DH, stacked[:TILE], stacked[TILE:])


def lane_and_row():
    lane = lax.broadcasted_iota(jnp.int32, (8, 128), 1)
    return lane, lax.broadcasted_iota(jnp.int32, (8, 128), 0)


def turn(block, shift):
    return pltpu.roll(block, shift % 128, 1, stride=1, stride_axis=0)


def skew(table, length):
    lane, row = lane_and_row()
    count = length // 128
    done = []
    for at in range(0, TILE, 8):
        blocks = [table[at : at + 8, 128 * c : 128 * c + 128] for c in range(count + 1)]
        blocks[0] = jnp.where(lane + row >= 127 - at, blocks[0], blocks[count])
        moved = [turn(block, at + 1) for block in blocks[:count]]
        if count > 1:
            inside = lane - row <= at
            moved = [
                jnp.where(inside, moved[c], moved[(c + 1) % count]) for c in range(count)
            ]
        done.append(jnp.concatenate(moved, axis=1))
    return jnp.concatenate(done, axis=0)


def flip_rows(block):
    row = lax.broadcasted_iota(jnp.int32, (8, LANES), 0)
    done = []
    for at in range(TILE - 8, -1, -8):
        done.append(
            jnp.concatenate(
                [
                    jnp.take_along_axis(block[at : at + 8, c : c + LANES], 7 - row, axis=0)
                    for c in range(0, block.shape[1], LANES)
                ],
                axis=1,
            )
        )
    return jnp.concatenate(done, axis=0)


def slot_tiles(slot):
    return [(slot, t) for t in range(SLOTS[slot][1] // TILE)]


def prob_block(refs, slot, t, member):
    start, length = SLOTS[slot]
    at = start + t * TILE if length == LEN1 else t * TILE
    ref = refs[{LEN1: 0, LEN3: 2}.get(length, 1)]
    return ref.at[member, at : at + TILE, :]


def unskew(scores, length):
    lane, row = lane_and_row()
    zero = jnp.zeros((8, 128), f32)
    done = []
    for at in range(0, TILE, 8):
        moved = [
            turn(scores[at : at + 8, 128 * c : 128 * c + 128], at) for c in range(length // 128)
        ]
        before = lane - row < at
        done.append(
            jnp.concatenate(
                [jnp.where(before, x, y) for x, y in zip([zero] + moved, moved + [zero])], axis=1
            )
        )
    return jnp.concatenate(done, axis=0)


def gather_moves(packed, gathered, own_sem, sems):
    step = pl.program_id(0)
    d = lax.axis_index("dp")
    t = lax.axis_index("tensor")
    near = t + 1 - 2 * lax.rem(t, 2)
    far = t + 2 - 4 * (t // 2)
    mate = d + 1 - 2 * lax.rem(d, 2)
    other = d + 2 - 4 * lax.rem(d // 2, 2)
    mine = lax.rem(d, 4)
    mates = mine + 1 - 2 * lax.rem(mine, 2)
    others = mine + 2 - 4 * (mine // 2)
    across = 3 - mine
    near_out, near_in, own_sems = sems[0], sems[1], sems[2:]
    pairs = [own_sems[2 * i : 2 * i + 2] for i in range(8)]
    far_sems, mate_sems, other_sems, relay_sems, *pass_sems = pairs
    barrier = pltpu.get_barrier_semaphore()
    places = ((d, near), (d, far), (mate, t), (other, t))

    def rows(which, chunk):
        return pl.ds(pl.multiple_of(which * QUARTER + chunk * CHUNK, PAD), CHUNK)

    def send(src, dst, out_sem, in_sem, place):
        return pltpu.make_async_remote_copy(
            src_ref=src, dst_ref=dst, send_sem=out_sem, recv_sem=in_sem, device_id=place, device_id_type=MESH
        )

    def to_near():
        return send(packed, gathered.at[t], near_out.at[0], near_in.at[0], places[0])

    def to_far(chunk):
        here = rows(mine, chunk)
        return send(
            packed.at[here],
            gathered.at[t, here],
            far_sems[0].at[chunk],
            far_sems[1].at[chunk],
            places[1],
        )

    def onward(which, chunk, pair, place):
        here = gathered.at[far, rows(which, chunk)]
        return send(here, here, pair[0].at[chunk], pair[1].at[chunk], place)

    def to_mate(chunk):
        return onward(mine, chunk, mate_sems, places[2])

    def to_other(chunk):
        return onward(mine, chunk, other_sems, places[3])

    def relay(chunk):
        if chunk % 2 == 0:
            return onward(others, chunk, relay_sems, places[2])
        return onward(mates, chunk, relay_sems, places[3])

    def passing(number, chunk):
        which = (mine, mates, others, across)[number]
        return onward(which, chunk, pass_sems[number], places[0])

    def own():
        return pltpu.make_async_copy(packed, gathered.at[t], own_sem.at[0])

    def begin():
        for place in places:
            pl.semaphore_signal(barrier, inc=1, device_id=place, device_id_type=MESH)

    def forward(chunk):
        to_far(chunk).wait_recv()
        to_mate(chunk).start()
        to_other(chunk).start()
        passing(0, chunk).start()

    def cross(chunk):
        to_mate(chunk).wait_recv()
        to_other(chunk).wait_recv()
        relay(chunk).start()
        passing(1, chunk).start()
        passing(2, chunk).start()

    def close(chunk):
        relay(chunk).wait_recv()
        passing(3, chunk).start()

    plan = {
        3: ((forward, 0),),
        4: ((forward, 1),),
        5: ((forward, 2), (forward, 3)),
        6: ((cross, 0), (forward, 4)),
        7: ((cross, 1), (cross, 2)),
        8: ((cross, 3), (close, 0), (close, 1)),
        9: ((cross, 4), (close, 2), (close, 3)),
    }

    def go_on():
        @pl.when(step == 0)
        def _():
            own().start()
            pl.semaphore_wait(barrier, len(places))
            for chunk in range(CHUNKS):
                to_far(chunk).start()
            to_near().start()

        for when, moves in plan.items():

            @pl.when(step == when)
            def _(moves=moves):
                for move, chunk in moves:
                    move(chunk)

    def finish():
        close(CHUNKS - 1)
        own().wait()
        to_near().wait()
        for chunk in range(CHUNKS):
            for number in range(4):
                passing(number, chunk).wait()
            to_far(chunk).wait_send()
            to_mate(chunk).wait_send()
            to_other(chunk).wait_send()
            relay(chunk).wait_send()

    return begin, go_on, finish


def attend(
    lengths_ref, counts_ref, q_ref, k_ref, v_ref, ek_ref, eq_ref, context_ref, p1_ref, p2_ref, p3_ref,
    shift_scr, score_scr, prob_scr,
):
    eye = unit_matrix(False)
    factor = 1.4426950408889634 * (3.0 * DH) ** -0.5
    counts = live_counts(lengths_ref, counts_ref)
    turned_values = v_ref[...].T
    head_rows = [
        jnp.where(
            lax.broadcasted_iota(jnp.int32, (PAIR, 1), 0) // DH == member, 1.0, 0.0
        ).astype(bf16)
        for member in range(2)
    ]

    def place(slot, t):
        start, length = SLOTS[slot]
        low = LEN3 - TILE - TILE * t
        row = start + t * TILE
        return start, length, slice(row, row + TILE), slice(low, low + length + TILE)

    def shift_unit(slot, t):
        start, length, rows, window = place(slot, t)
        table = dot_nn(each_head(q_ref[rows, :]), ek_ref[:, window])
        for member in range(2):
            shift_scr[member, rows, :length] = skew(
                table[member * TILE : (member + 1) * TILE], length
            ).astype(bf16)

    def score_unit(slot, t):
        start, length, rows, window = place(slot, t)
        keys = each_head(k_ref[rows, :])
        table = dot_nn(keys, eq_ref[:, window])
        queries = q_ref[start : start + length, :]
        live = lax.broadcasted_iota(jnp.int32, (TILE, 1), 0) < counts[slot] - t * TILE
        tops = []
        for member in range(2):
            mine = slice(member * TILE, (member + 1) * TILE)
            left = jnp.concatenate([keys[mine], eye], axis=1)
            shifted = shift_scr[member, start : start + length, t * TILE : (t + 1) * TILE]
            right = jnp.concatenate([queries, shifted], axis=1)
            raw = dot_nt(left, right) + skew(table[mine], length)
            raw = jnp.where(live, raw * factor, masked_score)
            score_scr[member, rows, :length] = raw
            tops.append(jnp.max(raw, axis=0, keepdims=True))
        return tops

    def weight_unit(slot, t, tops):
        start, length, rows, window = place(slot, t)
        sums = []
        for member in range(2):
            weights = jnp.exp2(score_scr[member, rows, :length] - tops[member])
            score_scr[member, rows, :length] = weights
            sums.append(jnp.sum(weights, axis=0, keepdims=True))
        return sums

    def prob_unit(slot, t, inverses):
        start, length, rows, window = place(slot, t)
        for member in range(2):
            prob = score_scr[member, rows, :length] * inverses[member]
            prob_scr[member, rows, :length] = prob.astype(bf16)
            prob_block((p1_ref, p2_ref, p3_ref), slot, t, member)[...] = flip_rows(prob).astype(
                bf16
            )

    def context_unit(slot):
        start, length = SLOTS[slot]
        here = slice(start, start + length)
        left = jnp.concatenate([turned_values[:, here] * rows for rows in head_rows], axis=1)
        right = jnp.concatenate([prob_scr[member, here, :length] for member in range(2)], axis=0)
        context_ref[here, :] = dot_nn(left, right).astype(bf16).T

    def both(function, parts):
        return [function(member_parts) for member_parts in zip(*parts)]

    def largest(parts):
        total = parts[0]
        for part in parts[1:]:
            total = jnp.maximum(total, part)
        return total

    groups = ((3,), (2, 1, 0))
    tiles = [[unit for slot in group for unit in slot_tiles(slot)] for group in groups]
    held = {}

    def settle(slot):
        held[slot] = both(largest, [held.pop(unit) for unit in slot_tiles(slot)])

    def invert(slot):
        total = both(sum, [held.pop(unit) for unit in slot_tiles(slot)])
        held[slot] = [1.0 / part for part in total]

    for unit in tiles[0]:
        shift_unit(*unit)
    for first, second in zip(tiles[0], tiles[1]):
        held[first] = score_unit(*first)
        shift_unit(*second)
    settle(3)
    for first, second in zip(tiles[0], tiles[1]):
        held[second] = score_unit(*second)
        held[first] = weight_unit(*first, held[3])
    invert(3)
    for slot in groups[1]:
        settle(slot)
    for first, second in zip(tiles[0], tiles[1]):
        held[second] = weight_unit(*second, held[second[0]])
        prob_unit(*first, held[3])
    for slot in groups[1]:
        invert(slot)
    context_unit(3)
    for second in tiles[1]:
        prob_unit(*second, held[second[0]])
    for slot in groups[1]:
        context_unit(slot)


def reversed_buckets(row):
    wide = row.astype(f32) + 1.0
    blocks = jnp.concatenate(
        [wide[:, at : at + LANES] for at in range(OFFSETS - LANES, -1, -LANES)], axis=0
    )
    high = jnp.floor(blocks * 0.5)
    both = jnp.concatenate([high, blocks - 2.0 * high], axis=0).astype(bf16)
    turned = dot_nn(both, unit_matrix(True))
    count = OFFSETS // LANES
    value = 2.0 * turned[:count] + turned[count:]
    line = jnp.concatenate([value[at : at + 1, :] for at in range(count)], axis=1)
    line = pltpu.roll(jnp.broadcast_to(line, (8, OFFSETS)), OFFSETS - 1, 1)[:1]
    return (line - 1.0).astype(jnp.int32)


def front_kernel(
    lengths_ref,
    counts_ref,
    tokens_ref,
    bucket_ref,
    down_ref,
    up_ref,
    hidden_up_ref,
    hidden_down_ref,
    adapt_scale_ref,
    in_any,
    back_any,
    qkv_any,
    rel_any,
    out_any,
    eq_ref,
    fk_ref,
    coeff_ref,
    rel_coeff_ref,
    factor_ref,
    scale_ref,
    index_ref,
    context_ref,
    p1_ref,
    p2_ref,
    p3_ref,
    q_any,
    k_any,
    v_any,
    merged_any,
    gathered_any,
    q_scr,
    k_scr,
    v_scr,
    ekt_scr,
    eqt_scr,
    merged_scr,
    packed_scr,
    pos_scr,
    in_scr,
    back_scr,
    qkv_scr,
    rel_scr,
    out_scr,
    shift_scr,
    score_scr,
    prob_scr,
    load_sem,
    store_sem,
    own_sem,
    *gather_sems,
):
    step = pl.program_id(0)
    gather_start, gather_step, gather_end = gather_moves(
        packed_scr, gathered_any, own_sem, gather_sems
    )
    loads = [
        pltpu.make_async_copy(src, dst, load_sem.at[number])
        for number, (src, dst) in enumerate(
            (
                (in_any, in_scr),
                (back_any, back_scr),
                (qkv_any, qkv_scr),
                (rel_any, rel_scr),
                (out_any, out_scr),
            )
        )
    ]
    stores = [
        pltpu.make_async_copy(src, dst, store_sem.at[number])
        for number, (src, dst) in enumerate(
            ((q_scr, q_any), (k_scr, k_any), (v_scr, v_any), (merged_scr, merged_any))
        )
    ]

    @pl.when(step == 0)
    def _():
        gather_start()
        for load in loads:
            load.start()
        for number in range(5):
            factor_ref[number] = padded(down_ref[number])
            factor_ref[5 + number] = padded(up_ref[number])
        factor_ref[10] = padded(hidden_up_ref[...])
        factor_ref[11] = padded(hidden_down_ref[...])
        wide = jnp.concatenate([adapt_scale_ref[...], jnp.zeros((6, LANES - RANK), f32)], axis=1)
        wide = jnp.concatenate([wide, jnp.zeros((LANES - 6, LANES), f32)], axis=0)
        scale_ref[...] = wide.T[:PAD]
        packed_scr[2 * D : 2 * D + PAD] = factor_ref[10]
        packed_scr[2 * D + PAD : 2 * D + 2 * PAD] = factor_ref[11]
        packed_scr[2 * D + 2 * PAD :] = jnp.zeros((PACKED - 2 * D - 2 * PAD, D), bf16)
        loads[0].wait()
        packed_scr[:D] = merged(in_scr[...], factor_ref[4], factor_ref[10], scale_ref[:, 4:5])
        loads[1].wait()
        packed_scr[D : 2 * D] = merged(back_scr[...], factor_ref[11], factor_ref[9], scale_ref[:, 5:6])

    gather_step()

    @pl.when(step == 0)
    def _():
        index_ref[0:1, :] = reversed_buckets(bucket_ref[...].reshape(1, OFFSETS))
        index_ref[1:2, :] = bucket_ref[...].reshape(1, OFFSETS)
        loads[2].wait()
        for member in range(3):
            merged_scr[member] = merged(
                qkv_scr[member],
                factor_ref[member],
                factor_ref[5 + member],
                scale_ref[:, member : member + 1],
            )
        loads[3].wait()
        rel = rel_scr[...]
        for member in range(2):
            pos_scr[member] = dot_nn(rel, merged_scr[member]).astype(bf16)
        coeff = dot_nt(factor_ref[:2].reshape(2 * PAD, D), rel)
        rel_coeff_ref[...] = coeff.reshape(2, PAD, 2 * SPAN)

    @pl.when(step == 1)
    def _():
        loads[4].wait()
        merged_scr[3] = merged(out_scr[...], factor_ref[3], factor_ref[8], scale_ref[:, 3:4])

    @pl.when(step < TILES)
    def _():
        rows = pl.ds(pl.multiple_of(step * BLOCK, BLOCK), BLOCK)
        tokens = tokens_ref[...]
        for member, ref in enumerate((q_scr, k_scr, v_scr)):
            ref[rows, :] = dot_nn(tokens, merged_scr[member]).astype(bf16)
        coeff = dot_nt(factor_ref[:3].reshape(3 * PAD, D), tokens)
        coeff_ref[...] = coeff.reshape(3, PAD, BLOCK)
        bucket = lax.broadcasted_iota(jnp.int32, (2 * SPAN, BLOCK), 0)
        back, forth = (
            jnp.where(bucket == index_ref[row : row + 1, rows], 1.0, 0.0).astype(bf16)
            for row in range(2)
        )
        eq_ref[...] = dot_tn(back, pos_scr[0]).astype(bf16)
        fk_ref[...] = dot_tn(forth, pos_scr[1]).astype(bf16)
        ekt_scr[:, rows] = dot_tn(pos_scr[1], back).astype(bf16)
        eqt_scr[:, rows] = dot_tn(pos_scr[0], back).astype(bf16)

    @pl.when(step == TILES)
    def _():
        for store in stores:
            store.start()

    @pl.when(step >= TILES)
    def _():
        lanes = pl.ds(pl.multiple_of((step - TILES) * PAIR, PAIR), PAIR)
        attend(
            lengths_ref,
            counts_ref,
            q_scr.at[:, lanes],
            k_scr.at[:, lanes],
            v_scr.at[:, lanes],
            ekt_scr.at[lanes, :],
            eqt_scr.at[lanes, :],
            context_ref,
            p1_ref,
            p2_ref,
            p3_ref,
            shift_scr,
            score_scr,
            prob_scr,
        )

    @pl.when(step == pl.num_programs(0) - 1)
    def _():
        for store in stores:
            store.wait()
        gather_end()


PAIR_SPEC = pl.BlockSpec((ROWS, PAIR), lambda p: (0, p))
TABLE_SPEC = pl.BlockSpec((PAIR, OFFSETS), lambda p: (p, 0))
PROB_SIZES = ((256, 128), (256, 256), (512, 512))
PROB_SPECS = [pl.BlockSpec((2, *size), lambda p: (p, 0, 0)) for size in PROB_SIZES]


def front(
    lengths, counts, tokens, qkv_weight, rel_embed, buckets, down, up, hidden_up, hidden_down,
    adapt_scale, out_weight, in_weight, back_weight,
):
    single, several = (pltpu.SemaphoreType.DMA((n,)) for n in (1, CHUNKS))
    inner = lax.axis_size("tensor")
    assert inner == 4 and lax.axis_size("dp") % 4 == 0

    def tile_at(i):
        return jnp.minimum(i, TILES - 1)

    def pair_at(i):
        return jnp.maximum(i - TILES, 0)

    tile = pl.BlockSpec((BLOCK, D), lambda i: (tile_at(i), 0))
    rows = jax.ShapeDtypeStruct((ROWS, D), bf16)
    anywhere = pl.BlockSpec(memory_space=pl.ANY)
    return pl.pallas_call(
        front_kernel,
        grid=(TILES + H // 2,),
        in_specs=[pl.BlockSpec(memory_space=pltpu.SMEM)] * 2
        + [
            tile,
            once(OFFSETS),
            once(5, RANK, D),
            once(5, RANK, D),
            once(RANK, D),
            once(RANK, D),
            once(6, RANK),
        ]
        + [anywhere] * 5,
        out_specs=[tile] * 2
        + [
            pl.BlockSpec((3, PAD, BLOCK), lambda i: (0, 0, tile_at(i))),
            whole(2, PAD, 2 * SPAN),
            whole(12, PAD, D),
            whole(PAD, LANES),
            whole(2, OFFSETS),
            pl.BlockSpec((ROWS, PAIR), lambda i: (0, pair_at(i))),
        ]
        + [pl.BlockSpec((2, *size), lambda i: (pair_at(i), 0, 0)) for size in PROB_SIZES]
        + [anywhere] * 5,
        out_shape=[rows] * 2
        + [
            jax.ShapeDtypeStruct((3, PAD, ROWS), f32),
            jax.ShapeDtypeStruct((2, PAD, 2 * SPAN), f32),
            jax.ShapeDtypeStruct((12, PAD, D), bf16),
            jax.ShapeDtypeStruct((PAD, LANES), f32),
            jax.ShapeDtypeStruct((2, OFFSETS), jnp.int32),
            rows,
        ]
        + [jax.ShapeDtypeStruct((H, *size), bf16) for size in PROB_SIZES]
        + [rows] * 3
        + [
            jax.ShapeDtypeStruct((4, D, D), bf16),
            jax.ShapeDtypeStruct((inner, PACKED, D), bf16),
        ],
        scratch_shapes=[pltpu.VMEM((ROWS, D), bf16)] * 3
        + [pltpu.VMEM((D, OFFSETS), bf16)] * 2
        + [
            pltpu.VMEM((4, D, D), bf16),
            pltpu.VMEM((PACKED, D), bf16),
            pltpu.VMEM((2, 2 * SPAN, D), bf16),
            pltpu.VMEM((D, D), bf16),
            pltpu.VMEM((D, D), bf16),
            pltpu.VMEM((3, D, D), bf16),
            pltpu.VMEM((2 * SPAN, D), bf16),
            pltpu.VMEM((D, D), bf16),
            pltpu.VMEM((2, ROWS, LEN3), bf16),
            pltpu.VMEM((2, ROWS, LEN3), f32),
            pltpu.VMEM((2, ROWS, LEN3), bf16),
            pltpu.SemaphoreType.DMA((5,)),
            pltpu.SemaphoreType.DMA((4,)),
            pltpu.SemaphoreType.DMA((1,)),
        ]
        + [single] * 2
        + [several] * 16,
        compiler_params=pltpu.CompilerParams(
            collective_id=1, has_side_effects=True, vmem_limit_bytes=MEMORY
        ),
        name="front",
    )(
        lengths, counts, tokens, buckets, down, up, hidden_up, hidden_down, adapt_scale,
        in_weight, back_weight, qkv_weight, rel_embed, out_weight,
    )


def backward_kernel(
    q_ref,
    k_ref,
    v_ref,
    g_ref,
    context_ref,
    eq_ref,
    fk_ref,
    p1_ref,
    p2_ref,
    p3_ref,
    gq_ref,
    gk_ref,
    gv_ref,
    geq_ref,
    gfk_ref,
    grad_scr,
    turned_scr,
    geq_scr,
    gfk_scr,
):
    anti = unit_matrix(True)
    factor = (3.0 * DH) ** -0.5
    geq_scr[...] = jnp.zeros_like(geq_scr)
    gfk_scr[...] = jnp.zeros_like(gfk_scr)
    product = g_ref[...].astype(f32) * context_ref[...].astype(f32)
    high = product.astype(bf16)
    rest = (product - high.astype(f32)).astype(bf16)
    lane = lax.broadcasted_iota(jnp.int32, (PAD, 2 * PAIR), 1) % PAIR
    row = lax.broadcasted_iota(jnp.int32, (PAD, 2 * PAIR), 0)
    summing = jnp.where(lane // DH == row, 1.0, 0.0).astype(bf16)
    delta = dot_nt(summing, jnp.concatenate([high, rest], axis=1))

    def place(slot, t):
        start, length = SLOTS[slot]
        row = start + t * TILE
        return start, length, slice(row, row + TILE)

    def spot(slot, t):
        start, length = SLOTS[slot]
        row = start + length - (t + 1) * TILE
        return slice(row, row + TILE)

    def open_unit(slot, t):
        start, length, rows = place(slot, t)
        both = jnp.concatenate([k_ref[rows, :], v_ref[rows, :]], axis=1)
        both = dot_nn(anti, both).astype(bf16)
        turned_scr[spot(slot, t), :] = both[:, :PAIR]
        return dot_nt(each_head(both[:, PAIR:]), g_ref[start : start + length, :])

    def raw_unit(slot, t, grad_prob):
        start, length, rows = place(slot, t)
        spreads = []
        for member in range(2):
            prob = prob_block((p1_ref, p2_ref, p3_ref), slot, t, member)[...].astype(f32)
            mine = grad_prob[member * TILE : (member + 1) * TILE]
            raw = (prob * (mine - delta[member : member + 1, start : start + length])).astype(bf16)
            grad_scr[member, spot(slot, t), :length] = raw
            spreads.append(unskew(raw.astype(f32), length).astype(bf16))
        return jnp.concatenate(spreads, axis=0)

    def key_unit(slot, t, spread):
        start, length, rows = place(slot, t)
        low = LEN3 - TILE - TILE * t
        window = slice(low, low + length + TILE)
        here = slice(start, start + length)
        raw = jnp.concatenate(
            [grad_scr[member, spot(slot, t), :length] for member in range(2)], axis=0
        )
        probs = jnp.concatenate(
            [prob_block((p1_ref, p2_ref, p3_ref), slot, t, member)[...] for member in range(2)],
            axis=0,
        )
        key_grad = dot_nn(
            jnp.concatenate([raw, spread], axis=1),
            jnp.concatenate([q_ref[here, :], eq_ref[window, :]], axis=0),
        )
        value_grad = dot_nn(probs, g_ref[here, :])
        both = jnp.concatenate([own_lanes(key_grad) * factor, own_lanes(value_grad)], axis=1)
        both = dot_nn(anti, both.astype(bf16)).astype(bf16)
        gk_ref[rows, :] = both[:, :PAIR]
        gv_ref[rows, :] = both[:, PAIR:]
        geq_scr[:, window] += dot_tn(each_head(turned_scr[spot(slot, t), :]), spread)

    def turn_unit(slot, t):
        start, length, rows = place(slot, t)
        raws, spreads = [], []
        for member in range(2):
            raw = grad_scr[member, start : start + length, t * TILE : (t + 1) * TILE].T
            raws.append(raw)
            spreads.append(unskew(raw.astype(f32), length).astype(bf16))
        return jnp.concatenate(raws, axis=0), jnp.concatenate(spreads, axis=0)

    def query_unit(slot, t, raw, spread):
        start, length, rows = place(slot, t)
        low = LEN3 - length + TILE * t
        window = slice(low, low + length + TILE)
        query_grad = dot_nn(
            jnp.concatenate([raw, spread], axis=1),
            jnp.concatenate(
                [turned_scr[start : start + length, :], fk_ref[window, :]], axis=0
            ),
        )
        gq_ref[rows, :] = (own_lanes(query_grad) * factor).astype(bf16)
        gfk_scr[:, window] += dot_tn(each_head(q_ref[rows, :]), spread)

    first, second = slot_tiles(3), slot_tiles(2) + slot_tiles(1) + slot_tiles(0)
    jobs = [("key", unit) for unit in second]
    for one, other in zip(first, second):
        jobs += [("key", one), ("query", other)]
    jobs += [("query", unit) for unit in first]
    held = {}
    for at in range(len(jobs) + 2):
        if at < len(jobs):
            kind, unit = jobs[at]
            held[at] = open_unit(*unit) if kind == "key" else None
        if 0 <= at - 1 < len(jobs):
            kind, unit = jobs[at - 1]
            if kind == "key":
                held[at - 1] = raw_unit(*unit, held[at - 1])
            else:
                held[at - 1] = turn_unit(*unit)
        if 0 <= at - 2 < len(jobs):
            kind, unit = jobs[at - 2]
            if kind == "key":
                key_unit(*unit, held.pop(at - 2))
            else:
                query_unit(*unit, *held.pop(at - 2))
    geq_ref[...] = (geq_scr[...] * factor).astype(bf16)
    gfk_ref[...] = (gfk_scr[...] * factor).astype(bf16)


def attend_backward(q, k, v, g, context, eq, fk, p1, p2, p3):
    return pl.pallas_call(
        backward_kernel,
        grid=(H // 2,),
        in_specs=[PAIR_SPEC] * 7 + PROB_SPECS,
        out_specs=[PAIR_SPEC] * 3 + [TABLE_SPEC] * 2,
        out_shape=[jax.ShapeDtypeStruct((ROWS, D), bf16)] * 3
        + [jax.ShapeDtypeStruct((D, OFFSETS), bf16)] * 2,
        scratch_shapes=[
            pltpu.VMEM((2, ROWS, LEN3), bf16),
            pltpu.VMEM((ROWS, PAIR), bf16),
            pltpu.VMEM((PAIR, OFFSETS), f32),
            pltpu.VMEM((PAIR, OFFSETS), f32),
        ],
        compiler_params=pltpu.CompilerParams(vmem_limit_bytes=MEMORY),
        name="attention_backward",
    )(q, k, v, g, context, eq, fk, p1, p2, p3)


def gelu_pair(hidden):
    z = jnp.abs(hidden) * 0.7071067811865476
    t = 1.0 / (1.0 + 0.3275911 * z)
    poly = t * (
        0.127414796
        + t * (-0.142248368 + t * (0.7107068705 + t * (-0.7265760135 + t * 0.5307027145)))
    )
    bell = jnp.exp(-z * z)
    tail = poly * bell
    below = jnp.where(hidden >= 0, 1.0 - tail, tail)
    return hidden * below, below + hidden * (bell * 0.3989422804014327)


def norm_forward(values, gain, shift):
    centered = values - jnp.mean(values, axis=1, keepdims=True)
    inverse = lax.rsqrt(jnp.mean(centered * centered, axis=1, keepdims=True) + norm_epsilon)
    normal = centered * inverse
    return (normal * gain + shift, normal, inverse)


def norm_backward(grad_out, normal, inverse, gain):
    scaled = grad_out * gain
    return inverse * (
        scaled
        - jnp.mean(scaled, axis=1, keepdims=True)
        - normal * jnp.mean(scaled * normal, axis=1, keepdims=True)
    )


def middle_kernel(
    lengths_ref,
    counts_ref,
    tokens_ref,
    context_ref,
    out_grad_ref,
    weight_ref,
    packed_ref,
    factor_ref,
    scale_ref,
    gain_one_ref,
    shift_one_ref,
    gain_two_ref,
    shift_two_ref,
    mixed_ref,
    grad_one_ref,
    context_grad_ref,
    small_ref,
    hidden_ref,
    scale_grad_ref,
    active_scr,
    slope_scr,
):
    step = pl.program_id(0)
    chunks = packed_ref.shape[0]

    @pl.when(step == 0)
    def _():
        small_ref[...] = jnp.zeros_like(small_ref)
        hidden_ref[...] = jnp.zeros_like(hidden_ref)
        scale_grad_ref[...] = jnp.zeros_like(scale_grad_ref)

    gain_one, shift_one, gain_two, shift_two = (
        ref[...].reshape(1, D)
        for ref in (gain_one_ref, shift_one_ref, gain_two_ref, shift_two_ref)
    )
    used_rows = live_counts(lengths_ref, counts_ref)
    weight = weight_ref[0]

    def work(number):
        rows = slice(number * BLOCK, (number + 1) * BLOCK)
        row = lax.broadcasted_iota(jnp.int32, (BLOCK, 1), 0) + step * WIDE + number * BLOCK
        live = jnp.zeros((BLOCK, 1), f32)
        for (start, length), used in zip(SLOTS, used_rows):
            live = jnp.where((row >= start) & (row < start + used), 1.0, live)
        context = context_ref[rows, :]
        attended = dot_nn(context, weight)
        normed, normal_one, inverse_one = norm_forward(
            tokens_ref[rows, :].astype(f32) + attended, gain_one, shift_one
        )
        normed_low = normed.astype(bf16)
        yield
        mlp = jnp.zeros((BLOCK, D), f32)
        back_coeff = jnp.zeros((PAD, BLOCK), f32)
        ahead = dot_nn(normed_low, packed_ref[0, :D, :])
        for c in range(chunks):
            hidden = ahead
            if c + 1 < chunks:
                ahead = dot_nn(normed_low, packed_ref[c + 1, :D, :])
            active, slope = gelu_pair(hidden)
            active = active.astype(bf16)
            active_scr[c, rows, :] = active
            slope_scr[c, rows, :] = slope
            mlp = mlp + dot_nn(active, packed_ref[c, D : 2 * D, :])
            back_coeff = back_coeff + dot_nt(
                packed_ref[c, 2 * D + PAD : 2 * D + 2 * PAD, :], active
            )
            yield
        result, normal_two, inverse_two = norm_forward(normed + mlp, gain_two, shift_two)
        mixed_ref[rows, :] = (result * live).astype(bf16)
        grad_two = norm_backward(
            out_grad_ref[rows, :].astype(f32) * live, normal_two, inverse_two, gain_two
        )
        grad_mlp = grad_two.astype(bf16)
        yield
        back_slope = dot_nt(factor_ref[9], grad_mlp)
        small_ref[3] += add_parts(dot_nn(two_parts(back_coeff * scale_ref[:, 5:6]), grad_mlp))
        scale_grad_ref[:, 5:6] += jnp.sum(back_coeff * back_slope, axis=1, keepdims=True)
        back_through = two_parts(back_slope * scale_ref[:, 5:6])
        in_coeff = dot_nt(factor_ref[4], normed_low)
        in_scaled = two_parts(in_coeff * scale_ref[:, 4:5])
        in_slope = jnp.zeros((PAD, BLOCK), f32)
        grad_normed = grad_two
        ahead = dot_nt(grad_mlp, packed_ref[0, D : 2 * D, :])
        for c in range(chunks):
            grad_active = ahead
            if c + 1 < chunks:
                ahead = dot_nt(grad_mlp, packed_ref[c + 1, D : 2 * D, :])
            grad_hidden = (grad_active * slope_scr[c, rows, :]).astype(bf16)
            grad_normed = grad_normed + dot_nt(grad_hidden, packed_ref[c, :D, :])
            in_slope = in_slope + dot_nt(packed_ref[c, 2 * D : 2 * D + PAD, :], grad_hidden)
            hidden_ref[c] += add_parts(dot_nn(in_scaled, grad_hidden))
            hidden_ref[chunks + c] += add_parts(dot_nn(back_through, active_scr[c, rows, :]))
            yield
        scale_grad_ref[:, 4:5] += jnp.sum(in_coeff * in_slope, axis=1, keepdims=True)
        small_ref[2] += add_parts(dot_nn(two_parts(in_slope * scale_ref[:, 4:5]), normed_low))
        grad_one = norm_backward(grad_normed, normal_one, inverse_one, gain_one)
        grad_one_ref[rows, :] = grad_one
        grad_attended = grad_one.astype(bf16)
        yield
        context_grad_ref[rows, :] = dot_nt(grad_attended, weight).astype(bf16)
        out_coeff = dot_nt(factor_ref[3], context)
        out_slope = dot_nt(factor_ref[8], grad_attended)
        small_ref[1] += add_parts(dot_nn(two_parts(out_coeff * scale_ref[:, 3:4]), grad_attended))
        small_ref[0] += add_parts(dot_nn(two_parts(out_slope * scale_ref[:, 3:4]), context))
        scale_grad_ref[:, 3:4] += jnp.sum(out_coeff * out_slope, axis=1, keepdims=True)

    waiting = [work(number) for number in range(WIDE // BLOCK)]
    running = []
    turn_number = 0
    while waiting or running:
        if waiting and turn_number % LAG == 0:
            running.append(waiting.pop(0))
        turn_number += 1
        for job in list(running):
            try:
                next(job)
            except StopIteration:
                running.remove(job)


def middle(lengths, counts, tokens, context, out_grad, weights, packed, factors, scales, norms):
    chunks = packed.shape[0]
    tile = pl.BlockSpec((WIDE, D), lambda i: (i, 0))
    return pl.pallas_call(
        middle_kernel,
        grid=(ROWS // WIDE,),
        in_specs=[pl.BlockSpec(memory_space=pltpu.SMEM)] * 2
        + [tile] * 3
        + [
            pl.BlockSpec((1, D, D), lambda i: (3, 0, 0)),
            pl.BlockSpec(
                (chunks, PACKED, D), lambda i: (0, 0, 0), pipeline_mode=pl.Buffered(1)
            ),
            whole(12, PAD, D),
            whole(PAD, 128),
        ]
        + [whole(D)] * 4,
        out_specs=[tile] * 3
        + [whole(4, PAD, D), whole(2 * chunks, PAD, D), whole(PAD, 128)],
        out_shape=[
            jax.ShapeDtypeStruct((ROWS, D), bf16),
            jax.ShapeDtypeStruct((ROWS, D), f32),
            jax.ShapeDtypeStruct((ROWS, D), bf16),
            jax.ShapeDtypeStruct((4, PAD, D), f32),
            jax.ShapeDtypeStruct((2 * chunks, PAD, D), f32),
            jax.ShapeDtypeStruct((PAD, 128), f32),
        ],
        scratch_shapes=[
            pltpu.VMEM((chunks, WIDE, D), bf16),
            pltpu.VMEM((chunks, WIDE, D), f32),
        ],
        compiler_params=pltpu.CompilerParams(vmem_limit_bytes=MEMORY),
        name="middle",
    )(lengths, counts, tokens, context, out_grad, weights, packed, factors, scales, *norms)


def devices():
    return lax.axis_size("dp") * lax.axis_size("tensor")


def hidden_rows():
    tiles = 2 * BLOCKS
    return PAD * -(-tiles // lax.axis_size("dp"))


def last_kernel(
    grad_one_ref,
    coeff_ref,
    index_ref,
    rel_coeff_ref,
    factor_ref,
    scale_ref,
    small_ref,
    hidden_ref,
    middle_scale_ref,
    tokens_any,
    gq_any,
    gk_any,
    gv_any,
    rel_any,
    geq_any,
    gfk_any,
    merged_any,
    in_grad_ref,
    down_out,
    up_out,
    hidden_up_out,
    hidden_down_out,
    scale_out,
    tokens_scr,
    grads_scr,
    rel_scr,
    geq_scr,
    gfk_scr,
    merged_scr,
    down_scr,
    up_scr,
    scale_scr,
    stage_scr,
    mine_late,
    land_late,
    mine_early,
    land_early,
    part_early,
    land_part,
    all_sums,
    all_hidden,
    load_sem,
    late_out_sem,
    late_in_sem,
    sums_out_sem,
    sums_in_sem,
    early_out_sem,
    early_in_sem,
    part_out_sem,
    part_in_sem,
    spread_out_sem,
    spread_in_sem,
):
    step = pl.program_id(0)
    final = TILES
    used = 2 * 3 * BLOCKS * RANK
    outer = lax.axis_size("dp")
    inner = lax.axis_size("tensor")
    count = outer * inner
    my_outer = lax.axis_index("dp")
    my_inner = lax.axis_index("tensor")
    me = my_outer * inner + my_inner
    barrier = pltpu.get_barrier_semaphore()

    def partner(off):
        other = lax.rem(me + off, count)
        return other, other // inner, lax.rem(other, inner)

    def send(src, dst, out_sem, in_sem, place):
        return pltpu.make_async_remote_copy(
            src_ref=src,
            dst_ref=dst,
            send_sem=out_sem,
            recv_sem=in_sem,
            device_id=place,
            device_id_type=MESH,
        )

    def late(off):
        other, row, col = partner(off)
        return send(
            mine_late.at[other], land_late.at[off], late_out_sem.at[0], late_in_sem.at[0], (row, col)
        )

    def sums(off):
        other, row, col = partner(off)
        return send(
            all_sums.at[0], all_sums.at[off], sums_out_sem.at[0], sums_in_sem.at[0], (row, col)
        )

    def every_late():
        others = pl.ds(1, count - 1)
        return send(
            mine_late.at[others],
            land_late.at[others],
            late_out_sem.at[0],
            late_in_sem.at[0],
            (my_outer, my_inner),
        )

    def every_sums():
        others = pl.ds(1, count - 1)
        return send(
            all_sums.at[others],
            all_sums.at[others],
            sums_out_sem.at[0],
            sums_in_sem.at[0],
            (my_outer, my_inner),
        )

    def early(off):
        col = lax.rem(my_inner + off, inner)
        return send(
            mine_early.at[col],
            land_early.at[off],
            early_out_sem.at[off],
            early_in_sem.at[off],
            (my_outer, col),
        )

    def part(off):
        row = lax.rem(my_outer + off, outer)
        return send(
            part_early.at[row],
            land_part.at[off],
            part_out_sem.at[off],
            part_in_sem.at[off],
            (row, my_inner),
        )

    def spread(off, origin):
        return send(
            all_hidden.at[origin],
            all_hidden.at[origin],
            spread_out_sem.at[off],
            spread_in_sem.at[off],
            (lax.rem(my_outer + off, outer), my_inner),
        )

    loads = [
        pltpu.make_async_copy(src, dst, load_sem.at[number])
        for number, (src, dst) in enumerate(
            (
                (tokens_any, tokens_scr),
                (gq_any, grads_scr.at[0]),
                (gk_any, grads_scr.at[1]),
                (gv_any, grads_scr.at[2]),
                (rel_any, rel_scr),
                (geq_any, geq_scr),
                (gfk_any, gfk_scr),
                (merged_any.at[pl.ds(0, 3)], merged_scr),
            )
        )
    ]

    @pl.when(step == 0)
    def _():
        for load in loads:
            load.start()

        @pl.loop(1, count)
        def _(off):
            _, row, col = partner(off)
            pl.semaphore_signal(barrier, inc=1, device_id=(row, col), device_id_type=MESH)

        scale_scr[...] = jnp.zeros_like(scale_scr)
        mine_early[...] = jnp.zeros_like(mine_early)
        for number in range(4):
            for block in range(BLOCKS):
                piece = number * BLOCKS + block
                mine_early[piece % inner, piece // inner, :PAD] = small_ref[
                    number, :, block * LANES : (block + 1) * LANES
                ].astype(bf16)
        tiles = mine_early.shape[2] // PAD - 1
        for chunk in range(inner):
            for which in range(2):
                for block in range(BLOCKS):
                    tile = which * BLOCKS + block
                    at = (tile % tiles + 1) * PAD
                    mine_early[chunk, tile // tiles, at : at + PAD] = hidden_ref[
                        which * inner + chunk, :, block * LANES : (block + 1) * LANES
                    ].astype(bf16)
        pl.semaphore_wait(barrier, count - 1)

        @pl.loop(1, inner)
        def _(off):
            early(off).start()

        land_early[0] = mine_early[my_inner]
        loads[0].wait()
        tokens = tokens_scr[...]
        for member in range(3):
            loads[1 + member].wait()
            grad = grads_scr[member]
            scale = scale_ref[:, member : member + 1]
            coeff = coeff_ref[member]
            slope = dot_nt(factor_ref[5 + member], grad)
            up_scr[member] = add_parts(dot_nn(two_parts(coeff * scale), grad))
            down_scr[member] = add_parts(dot_nn(two_parts(slope * scale), tokens))
            scale_scr[:, member : member + 1] += jnp.sum(coeff * slope, axis=1, keepdims=True)

        @pl.loop(1, inner)
        def _(off):
            early(off).wait_recv()

        part_early[...] = jnp.sum(land_early[...].astype(f32), axis=0).astype(bf16)

        @pl.loop(1, outer)
        def _(off):
            part(off).start()

        land_part[0] = part_early[my_outer]
        for load in loads[4:7]:
            load.wait()
        rel = rel_scr[...]
        bucket = lax.broadcasted_iota(jnp.int32, (2 * SPAN, OFFSETS), 0)
        for member, ref, row in ((0, geq_scr, 0), (1, gfk_scr, 1)):
            scale = scale_ref[:, member : member + 1]
            chosen = jnp.where(bucket == index_ref[row : row + 1, :], 1.0, 0.0).astype(bf16)
            grad = dot_nt(ref[...], chosen).astype(bf16)
            coeff = rel_coeff_ref[member]
            slope = dot_nn(factor_ref[5 + member], grad)
            up_scr[member] += add_parts(dot_nt(two_parts(coeff * scale), grad))
            down_scr[member] += add_parts(dot_nn(two_parts(slope * scale), rel))
            scale_scr[:, member : member + 1] += jnp.sum(coeff * slope, axis=1, keepdims=True)
        for number in range(6):
            ref = down_scr if number < 3 else up_scr
            for block in range(BLOCKS):
                at = (number * BLOCKS + block) * RANK
                stage_scr[at : at + RANK, :] = ref[
                    number % 3, :RANK, block * LANES : (block + 1) * LANES
                ]
        stage_scr[used : used + PAD, :] = scale_scr[...] + middle_scale_ref[...]
        stage_scr[used + PAD :, :] = jnp.zeros((count * PAD - used - PAD, LANES), f32)
        mine_late[...] = stage_scr[...].astype(bf16).reshape(count, PAD, LANES)

        @pl.loop(1, count)
        def _(off):
            late(off).start()

        land_late[0] = mine_late[me]
        loads[7].wait()

    @pl.when(step > 0)
    def _():
        rows = pl.ds(pl.multiple_of((step - 1) * BLOCK, BLOCK), BLOCK)
        in_grad = grad_one_ref[...]
        for member in range(3):
            in_grad = in_grad + dot_nt(grads_scr[member, rows, :], merged_scr[member])
        in_grad_ref[...] = in_grad

    @pl.when(step == SUMMED)
    def _():
        @pl.loop(1, outer)
        def _(off):
            part(off).wait_recv()

        summed = jnp.sum(land_part[...].astype(f32), axis=0).astype(bf16)
        all_hidden[my_outer] = summed[PAD:]
        all_sums[0, PAD:] = summed[:PAD]

        @pl.loop(1, outer)
        def _(off):
            spread(off, my_outer).start()

        every_late().wait_recv()
        all_sums[0, :PAD] = jnp.sum(land_late[...].astype(f32), axis=0).astype(bf16)

        @pl.loop(1, count)
        def _(off):
            sums(off).start()

    @pl.when(step == final)
    def _():
        @pl.loop(1, outer)
        def _(off):
            spread(off, lax.rem(my_outer + outer - off, outer)).wait_recv()

        tiles = all_hidden.shape[1] // PAD
        for which in range(2):
            for block in range(BLOCKS):
                tile = which * BLOCKS + block
                at = tile % tiles * PAD
                out = (hidden_up_out, hidden_down_out)[which]
                out[:, block * LANES : (block + 1) * LANES] = all_hidden[
                    tile // tiles, at : at + PAD
                ].astype(f32)[:RANK]

        every_sums().wait_recv()

        def summed_by(owner):
            return all_sums.at[lax.rem(me + count - owner, count)]

        for owner in range(count):
            stage_scr[owner * PAD : (owner + 1) * PAD, :] = summed_by(owner)[:PAD].astype(f32)
        for number in range(6):
            ref = down_out if number < 3 else up_out
            for block in range(BLOCKS):
                at = (number * BLOCKS + block) * RANK
                ref[number % 3, :, block * LANES : (block + 1) * LANES] = stage_scr[
                    at : at + RANK, :
                ]
        scale_out[...] = stage_scr[used : used + PAD, :].T[:6, :RANK]
        for number, (ref, place) in enumerate(
            ((down_out, 3), (up_out, 3), (down_out, 4), (up_out, 4))
        ):
            for block in range(BLOCKS):
                ref[place, :, block * LANES : (block + 1) * LANES] = summed_by(
                    number * BLOCKS + block
                )[PAD:].astype(f32)[:RANK]
        every_late().wait_send()
        every_sums().wait_send()

        @pl.loop(1, inner)
        def _(off):
            early(off).wait_send()

        @pl.loop(1, outer)
        def _(off):
            part(off).wait_send()
            spread(off, my_outer).wait_send()


def last(
    tokens, gq, gk, gv, grad_one, coeff, weights, index, rel_coeff, factors, scales,
    small, hidden, middle_scale, rel, geq, gfk,
):
    count = devices()
    outer = lax.axis_size("dp")
    inner = lax.axis_size("tensor")
    piece = hidden_rows()
    tile = pl.BlockSpec((BLOCK, D), lambda i: (jnp.maximum(i - 1, 0), 0))
    factor = jax.ShapeDtypeStruct((5, RANK, D), f32)
    block = pltpu.VMEM((count, PAD, LANES), bf16)
    return pl.pallas_call(
        last_kernel,
        grid=(1 + TILES,),
        in_specs=[
            tile,
            once(3, PAD, ROWS),
            once(2, OFFSETS),
            once(2, PAD, 2 * SPAN),
            once(12, PAD, D),
            once(PAD, LANES),
            once(4, PAD, D),
            once(2 * inner, PAD, D),
            once(PAD, LANES),
        ]
        + [pl.BlockSpec(memory_space=pl.ANY)] * 8,
        out_specs=[
            tile,
            whole(5, RANK, D),
            whole(5, RANK, D),
            whole(RANK, D),
            whole(RANK, D),
            whole(6, RANK),
        ],
        out_shape=[
            jax.ShapeDtypeStruct((ROWS, D), f32),
            factor,
            factor,
            jax.ShapeDtypeStruct((RANK, D), f32),
            jax.ShapeDtypeStruct((RANK, D), f32),
            jax.ShapeDtypeStruct((6, RANK), f32),
        ],
        scratch_shapes=[
            pltpu.VMEM((ROWS, D), bf16),
            pltpu.VMEM((3, ROWS, D), bf16),
            pltpu.VMEM((2 * SPAN, D), bf16),
            pltpu.VMEM((D, OFFSETS), bf16),
            pltpu.VMEM((D, OFFSETS), bf16),
            pltpu.VMEM((3, D, D), bf16),
            pltpu.VMEM((3, PAD, D), f32),
            pltpu.VMEM((3, PAD, D), f32),
            pltpu.VMEM((PAD, LANES), f32),
            pltpu.VMEM((count * PAD, LANES), f32),
            block,
            block,
            pltpu.VMEM((inner, outer, PAD + piece, LANES), bf16),
            pltpu.VMEM((inner, outer, PAD + piece, LANES), bf16),
            pltpu.VMEM((outer, PAD + piece, LANES), bf16),
            pltpu.VMEM((outer, PAD + piece, LANES), bf16),
            pltpu.VMEM((count, 2 * PAD, LANES), bf16),
            pltpu.VMEM((outer, piece, LANES), bf16),
            pltpu.SemaphoreType.DMA((8,)),
        ]
        + [pltpu.SemaphoreType.DMA((1,))] * 4
        + [pltpu.SemaphoreType.DMA((inner,))] * 2
        + [pltpu.SemaphoreType.DMA((outer,))] * 4,
        compiler_params=pltpu.CompilerParams(
            collective_id=0, has_side_effects=True, vmem_limit_bytes=MEMORY
        ),
        name="last",
    )(
        grad_one, coeff, index, rel_coeff, factors, scales, small, hidden, middle_scale,
        tokens, gq, gk, gv, rel, geq, gfk, weights,
    )


def finish_kernel(*refs):
    half = len(refs) // 2
    refs[half][...] = refs[0][...]

    @pl.when(pl.program_id(0) == 0)
    def _():
        for src, dst in zip(refs[1:half], refs[half + 1 :]):
            dst[...] = src[...]


def finish(in_grad, *small):
    tile = pl.BlockSpec((BLOCK, D), lambda i: (i, 0))
    specs = [tile] + [whole(*part.shape) for part in small]
    return pl.pallas_call(
        finish_kernel,
        grid=(ROWS // BLOCK,),
        in_specs=specs,
        out_specs=specs,
        out_shape=[jax.ShapeDtypeStruct(part.shape, part.dtype) for part in (in_grad, *small)],
        compiler_params=pltpu.CompilerParams(vmem_limit_bytes=MEMORY),
        name="finish",
    )(in_grad, *small)


def on_device(
    tokens,
    qkv_weight,
    out_weight,
    in_weight,
    back_weight,
    rel_embed,
    gain_one,
    shift_one,
    gain_two,
    shift_two,
    adapt_down,
    adapt_up,
    hidden_up,
    hidden_down,
    adapt_scale,
    seq_lengths,
    seq_counts,
    rel_bucket,
    out_grad,
):
    buckets = jnp.pad(rel_bucket, (0, 1), constant_values=-1)
    norms = (gain_one, shift_one, gain_two, shift_two)
    (
        eq, fk, coeff, rel_coeff, factors, scales, index_rows, context, p1, p2, p3, q, k, v, weights,
        gathered,
    ) = front(
        seq_lengths, seq_counts, tokens, qkv_weight, rel_embed, buckets, adapt_down, adapt_up,
        hidden_up, hidden_down, adapt_scale, out_weight, in_weight, back_weight,
    )
    mixed, grad_one, context_grad, small, hidden, middle_scale = middle(
        seq_lengths, seq_counts, tokens, context, out_grad, weights, gathered, factors, scales, norms
    )
    gq, gk, gv, geq, gfk = attend_backward(
        q, k, v, context_grad, context, eq, fk, p1, p2, p3
    )
    sums = last(
        tokens, gq, gk, gv, grad_one, coeff, weights, index_rows, rel_coeff, factors, scales,
        small, hidden, middle_scale, rel_embed, geq, gfk,
    )
    return (mixed, *finish(*sums))


def solution(mesh):
    rows = P(("dp", "tensor"), None)
    return jax.shard_map(
        on_device,
        mesh=mesh,
        in_specs=(
            rows,
            P(),
            P(),
            P(None, "tensor"),
            P("tensor", None),
            P(),
            P(),
            P(),
            P(),
            P(),
            P(),
            P(),
            P(None, "tensor"),
            P(None, "tensor"),
            P(),
            rows,
            rows,
            P(),
            rows,
        ),
        out_specs=(rows, rows, P(), P(), P(None, "tensor"), P(None, "tensor"), P()),
        check_vma=False,
    )
```
